32 devices in a mesh: batch: 8 (over z, y), proto: 4 (over x, core).
Axes of the slice: x: 2, y: 2, z: 4, core: 2. Of those that a mesh axis runs over, the one named last changes fastest.
Arguments:
- crops: bfloat16 [1536, 1536], P(('batch', 'proto')), may hold values from -6 to 6
- teacher_emb: bfloat16 [1536, 256], P('batch'), may hold values from -4 to 4
- w_first: bfloat16 [1536, 2048], P(None, 'proto'), may hold values from -0.15625 to 0.15625
- b_first: float32 [2048], replicated, may hold values from -3 to 3
- w_second: bfloat16 [2048, 2048], P('proto'), may hold values from -0.125 to 0.125
- b_second: float32 [2048], replicated, may hold values from -3 to 3
- w_third: bfloat16 [2048, 256], P('proto'), may hold values from -0.125 to 0.125
- b_third: float32 [256], replicated, may hold values from -3 to 3
- protos: bfloat16 [65536, 256], P('proto'), may hold values from -60 to 60
Outputs:
- crop_grad: float32 [1536, 256], P(('batch', 'proto'))
The draws below stay inside these ranges and needn't reach their ends.
All inputs are finite; a program needn't handle non-finite values.
Results may differ from the reference program's by a relative error of at most 0.018.
The reference program's roundings to bfloat16 on the way (of `h_first`, `h_second`, `student_emb`, `teacher_unit` and `difference`) count: a program that leaves them out, or rounds other values in their place, can miss the bound.
Values may be sent and summed in bfloat16 or wider, within the bound.
No kernel may reach another device: no remote copies, remote signals or barrier semaphores. Data moves between devices by JAX's collectives and lax.ppermute only.
A program may use at most 128 MiB of HBM per device.

```python
import math
import jax
import jax.numpy as jnp
from jax import lax

D_IN = 1536
HID_UNITS = 2048
BOTTLE = 256
PROTOS = 65536
CROPS_DEV = 192
ITERS = 3
CROPS = 1536


def pair_total():
    return max(1, min(CROPS // CROPS_DEV // 2, BOTTLE // 8))


def drawn_pairs(key, count):
    key_list = jax.random.split(key, 2)
    half_width = BOTTLE // 2
    sign_table = 2.0 * jax.random.randint(key_list[0], (2, count, half_width), 0, 2).astype(jnp.float32) - 1.0
    strength = jnp.exp(jax.random.uniform(key_list[1], (count,), minval=math.log(30.0), maxval=math.log(50.0)))
    return (sign_table, strength)


def draw_teacher_emb(key, part):
    count = pair_total()
    sign_table, strength = drawn_pairs(key, count)
    key = jax.random.fold_in(key, 11)
    key_list = jax.random.split(key, 3)
    half_width = BOTTLE // 2
    shard_total = CROPS // CROPS_DEV
    mixed_shards = max(shard_total // 2, 1)
    shard_index = jnp.arange(CROPS) // CROPS_DEV
    pair_index = shard_index % count
    mixed_rows = (shard_index < mixed_shards)[:, None]
    planted = (jax.random.randint(key_list[0], (CROPS,), 0, 4) == 0)[:, None]
    noise = jnp.clip(jax.random.normal(key_list[1], (CROPS, BOTTLE)), -4.0, 4.0)
    logit_gap = jax.random.uniform(key_list[2], (CROPS,), minval=0.0, maxval=3.0)
    first_dirs = sign_table[0][pair_index]
    second_dirs = sign_table[1][pair_index]
    offset_weight = (0.07 * logit_gap / (math.sqrt(2.0) * strength[pair_index]))[:, None]
    tied = first_dirs + second_dirs + offset_weight * (first_dirs - second_dirs)
    aligned = jnp.where(mixed_rows, tied, first_dirs)
    background = jnp.concatenate([0.05 * noise[:, :half_width], noise[:, half_width:]], axis=1)
    planted_rows = jnp.concatenate([aligned, 0.05 * noise[:, half_width:]], axis=1)
    values = jnp.where(planted, planted_rows, background)
    return jnp.clip(values, -4.0, 4.0).astype(jnp.bfloat16)


def draw_protos(key, part):
    count = pair_total()
    sign_table, strength = drawn_pairs(key, count)
    key = jax.random.fold_in(key, 7)
    key_list = jax.random.split(key, 3)
    half_width = BOTTLE // 2
    scales = jnp.exp(jax.random.uniform(key_list[0], (PROTOS, 1), minval=math.log(0.5), maxval=math.log(5.0)))
    noise = jnp.clip(jax.random.normal(key_list[1], (PROTOS, BOTTLE)), -4.0, 4.0)
    values = 0.15 * scales * noise
    row_order = jax.random.permutation(key_list[2], PROTOS)
    row_scale = (strength / math.sqrt(half_width))[:, None]
    zero_block = jnp.zeros((count, BOTTLE - half_width), jnp.float32)
    first_rows = jnp.concatenate([sign_table[0] * row_scale, zero_block], axis=1)
    second_rows = jnp.concatenate([sign_table[1] * row_scale, zero_block], axis=1)
    values = values.at[row_order[:count]].set(first_rows).at[row_order[count:2 * count]].set(second_rows)
    return jnp.clip(values, -60.0, 60.0).astype(jnp.bfloat16)


def block_scale(own_key, shape, shards, least, high):
    level = 1.0
    for dim, shards_of in shards:
        steps = jax.random.uniform(jax.random.fold_in(jax.random.fold_in(own_key, 6), dim), (shards_of,), jnp.float32, least / len(shards), high / len(shards))
        level = level * jnp.repeat(jnp.exp(steps), shape[dim] // shards_of).reshape((-1,) + (1,) * (len(shape) - 1 - dim))
    return level


def centred(stream_key, extent, width, bound, cuts=(), dtype=jnp.bfloat16):
    loudness = block_scale(stream_key, extent, cuts, -0.22, 0.18) if cuts else 1.0
    entries = jax.random.normal(stream_key, extent, jnp.float32) * width * loudness
    return jnp.minimum(jnp.maximum(entries, -bound), bound).astype(dtype)


def setup_inputs(seed: int = 0) -> dict:
    keys = jax.random.split(jax.random.key(seed), 10)
    crops = centred(keys[0], (CROPS, D_IN), 1.0, 6.0, ((0, 32),))
    teacher_emb = draw_teacher_emb(jax.random.fold_in(keys[9], 71), 0)
    w_first = centred(keys[2], (D_IN, HID_UNITS), D_IN ** -0.5, 0.15625, ((1, 4),))
    b_first = centred(keys[3], (HID_UNITS,), 0.5, 3.0, (), jnp.float32)
    w_second = centred(keys[4], (HID_UNITS, HID_UNITS), HID_UNITS ** -0.5, 0.125, ((0, 4),))
    b_second = centred(keys[5], (HID_UNITS,), 0.5, 3.0, (), jnp.float32)
    w_third = centred(keys[6], (HID_UNITS, BOTTLE), HID_UNITS ** -0.5, 0.125, ((0, 4),))
    b_third = centred(keys[7], (BOTTLE,), 0.5, 3.0, (), jnp.float32)
    protos = draw_protos(jax.random.fold_in(keys[9], 71), 0)
    return {"crops": crops, "teacher_emb": teacher_emb, "w_first": w_first, "b_first": b_first, "w_second": w_second, "b_second": b_second, "w_third": w_third, "b_third": b_third, "protos": protos}


student_temp = 0.1
teacher_temp = 0.07
norm_eps = 1e-06

def scores(left_rows, right_rows):
    return lax.dot_general(left_rows, right_rows, (((1,), (1,)), ((), ())), preferred_element_type=jnp.float32)

def unit_rows(values):
    lengths = jnp.sqrt(lax.optimization_barrier(jnp.sum(values * values, axis=1, keepdims=True)) + norm_eps)
    return (values / lengths, lengths)

def reference(crops, teacher_emb, w_first, b_first, w_second, b_second, w_third, b_third, protos):
    h_first = jax.nn.gelu(jnp.dot(crops, w_first, preferred_element_type=jnp.float32) + b_first, approximate=False).astype(jnp.bfloat16)
    h_second = jax.nn.gelu(jnp.dot(h_first, w_second, preferred_element_type=jnp.float32) + b_second, approximate=False).astype(jnp.bfloat16)
    bottleneck = jnp.dot(h_second, w_third, preferred_element_type=jnp.float32) + b_third
    unit, lengths = unit_rows(bottleneck)
    student_emb = unit.astype(jnp.bfloat16)
    teacher_unit = unit_rows(teacher_emb.astype(jnp.float32))[0].astype(jnp.bfloat16)
    crops_total = teacher_emb.shape[0]
    protos_total = protos.shape[0]
    block_rows = math.gcd(crops_total, 512)
    block_count = crops_total // block_rows
    teacher_blocks = teacher_unit.reshape(block_count, block_rows, -1)
    student_blocks = student_emb.reshape(block_count, block_rows, -1)

    def exponent(row_block):
        logits = scores(row_block, protos) / teacher_temp
        return jnp.exp(logits - lax.optimization_barrier(jnp.max(logits, axis=1, keepdims=True)))

    def first_pass(running, row_block):
        return (running + lax.optimization_barrier(jnp.sum(exponent(row_block), axis=0)), None)
    empty = jnp.zeros((protos_total,), jnp.float32)
    row_total, _ = lax.scan(first_pass, empty, teacher_blocks)
    proto_scale = 1.0 / (protos_total * row_total)
    for sweep_step in range(ITERS):
        proto_scale = 1.0 / (protos_total * row_total)
        if sweep_step + 1 < ITERS:

            def sweep(running, row_block):
                weights_e = exponent(row_block)
                crop_scale = 1.0 / (crops_total * jnp.dot(weights_e, proto_scale, precision=lax.Precision.HIGHEST))
                return (running + jnp.dot(crop_scale, weights_e, precision=lax.Precision.HIGHEST), None)
            row_total, _ = lax.scan(sweep, empty, teacher_blocks)

    def finish(blocks):
        teacher_block, student_block = blocks
        weights_e = exponent(teacher_block)
        crop_scale = 1.0 / (crops_total * jnp.dot(weights_e, proto_scale, precision=lax.Precision.HIGHEST))
        targets = crops_total * weights_e * proto_scale[None, :] * crop_scale[:, None]
        logits = scores(student_block, protos) / student_temp
        row_top = lax.optimization_barrier(jnp.max(logits, axis=1, keepdims=True))
        shifted = jnp.exp(logits - row_top)
        row_sum = lax.optimization_barrier(jnp.sum(shifted, axis=1, keepdims=True))
        probs = shifted / row_sum
        difference = (probs - targets).astype(jnp.bfloat16)
        return jnp.dot(difference, protos, preferred_element_type=jnp.float32) / student_temp
    grad_blocks = lax.map(finish, (teacher_blocks, student_blocks))
    emb_grad = grad_blocks.reshape(crops_total, -1)
    crop_grad = (emb_grad - unit * lax.optimization_barrier(jnp.sum(unit * emb_grad, axis=1, keepdims=True))) / lengths
    return crop_grad
```

```python
import jax
import jax.numpy as jnp
from jax import lax
from jax.sharding import PartitionSpec as P

ITERS = 3

student_temp = 0.1
teacher_temp = 0.07
norm_eps = 1e-06


def scores(left_rows, right_rows):
    return lax.dot_general(
        left_rows, right_rows, (((1,), (1,)), ((), ())), preferred_element_type=jnp.float32
    )


def unit_rows(values):
    lengths = jnp.sqrt(jnp.sum(values * values, axis=1, keepdims=True) + norm_eps)
    return (values / lengths, lengths)


def exchange_rows(blocks, axis):
    count = lax.axis_size(axis)
    own = lax.axis_index(axis)
    rows = blocks.shape[0] // count
    parts = [lax.dynamic_slice_in_dim(blocks, own * rows, rows, 0)]
    for step in range(1, count):
        target = lax.rem(own + step, count)
        sent = lax.dynamic_slice_in_dim(blocks, target * rows, rows, 0)
        parts.append(lax.ppermute(sent, axis, [(i, (i + step) % count) for i in range(count)]))
    return parts


def body(crops, teacher_emb, w_first, b_first, w_second, b_second, w_third, b_third, protos):
    batch_index = lax.axis_index("batch")
    proto_index = lax.axis_index("proto")
    batch_size = lax.axis_size("batch")
    proto_size = lax.axis_size("proto")
    share_rows = crops.shape[0]
    group_rows = teacher_emb.shape[0]
    crops_total = group_rows * batch_size
    protos_total = protos.shape[0] * proto_size
    thin = protos.shape[0] // batch_size
    hidden_share = w_first.shape[1]

    all_crops = lax.all_gather(crops, "proto", axis=0, tiled=True)
    w_third_all = lax.all_gather(w_third, "proto", axis=0, tiled=True)
    first_bias = lax.dynamic_slice_in_dim(b_first, proto_index * hidden_share, hidden_share)
    h_first = jax.nn.gelu(
        jnp.dot(all_crops, w_first, preferred_element_type=jnp.float32) + first_bias,
        approximate=False,
    ).astype(jnp.bfloat16)
    partial_value = jnp.dot(h_first, w_second, preferred_element_type=jnp.float32)

    teacher_unit = unit_rows(teacher_emb.astype(jnp.float32))[0].astype(jnp.bfloat16)
    unit_share = lax.dynamic_slice_in_dim(teacher_unit, proto_index * share_rows, share_rows, 0)
    all_unit = lax.all_gather(unit_share, ("batch", "proto"), axis=0, tiled=True)
    thin_protos = lax.dynamic_slice_in_dim(protos, batch_index * thin, thin, 0)
    thin_logits = scores(thin_protos, all_unit) / teacher_temp
    teacher_top = lax.pmax(jnp.max(thin_logits, axis=0), ("batch", "proto"))
    thin_weights = jnp.exp(thin_logits - teacher_top[None, :])

    pre_second = sum(exchange_rows(partial_value, "proto"))
    h_second = jax.nn.gelu(pre_second + b_second, approximate=False).astype(jnp.bfloat16)
    bottleneck = jnp.dot(h_second, w_third_all, preferred_element_type=jnp.float32) + b_third
    unit, lengths = unit_rows(bottleneck)
    student_emb = lax.all_gather(unit.astype(jnp.bfloat16), "proto", axis=0, tiled=True)
    logits = scores(student_emb, protos) / student_temp
    local_top = jnp.max(logits, axis=1, keepdims=True)
    shifted = jnp.exp(logits - local_top)
    local_total = jnp.sum(shifted, axis=1, keepdims=True)
    attract = jnp.dot(shifted.astype(jnp.bfloat16), protos, preferred_element_type=jnp.float32)
    attract = jnp.concatenate(
        [attract, jnp.broadcast_to(local_total, (group_rows, 128)), jnp.broadcast_to(local_top, (group_rows, 128))],
        axis=1,
    )
    attract_parts = exchange_rows(attract, "proto")

    row_total = jnp.sum(thin_weights, axis=1)
    for sweep_step in range(ITERS):
        proto_scale = 1.0 / (protos_total * row_total)
        if sweep_step + 1 < ITERS:
            column_total = lax.psum(
                jnp.sum(thin_weights * proto_scale[:, None], axis=0), ("batch", "proto")
            )
            crop_scale = 1.0 / (crops_total * column_total)
            row_total = jnp.sum(thin_weights * crop_scale[None, :], axis=1)
    all_scale = lax.all_gather(proto_scale, "batch", axis=0, tiled=True)

    own_top = lax.dynamic_slice_in_dim(teacher_top, batch_index * group_rows, group_rows, 0)
    weights_e = jnp.exp(scores(teacher_unit, protos) / teacher_temp - own_top[:, None])
    scaled = weights_e * all_scale[None, :]
    column_part = jnp.sum(scaled, axis=1, keepdims=True)
    repel = jnp.dot(scaled.astype(jnp.bfloat16), protos, preferred_element_type=jnp.float32)
    repel = jnp.concatenate([repel, jnp.broadcast_to(column_part, (group_rows, 128))], axis=1)
    repel_sum = sum(exchange_rows(repel, "proto"))

    width = protos.shape[1]
    tops = [part[:, width + 128 : width + 129] for part in attract_parts]
    row_top = tops[0]
    for top in tops[1:]:
        row_top = jnp.maximum(row_top, top)
    attract_sum = sum(part[:, :width] * jnp.exp(top - row_top) for part, top in zip(attract_parts, tops))
    row_sum = sum(part[:, width : width + 1] * jnp.exp(top - row_top) for part, top in zip(attract_parts, tops))
    emb_grad = (
        attract_sum / row_sum - repel_sum[:, :width] / repel_sum[:, width : width + 1]
    ) / student_temp
    crop_grad = (emb_grad - unit * jnp.sum(unit * emb_grad, axis=1, keepdims=True)) / lengths
    return crop_grad


def solution(mesh):
    in_specs = (
        P(("batch", "proto"), None),
        P("batch", None),
        P(None, "proto"),
        P(),
        P("proto", None),
        P(),
        P("proto", None),
        P(),
        P("proto", None),
    )
    out_specs = P(("batch", "proto"), None)
    return jax.shard_map(body, mesh=mesh, in_specs=in_specs, out_specs=out_specs, check_vma=False)
```

```python
import jax
import jax.numpy as jnp
from jax import lax
from jax.sharding import PartitionSpec as P

ITERS = 3

student_temp = 0.1
teacher_temp = 0.07
norm_eps = 1e-06


def scores(left_rows, right_rows):
    return lax.dot_general(
        left_rows, right_rows, (((1,), (1,)), ((), ())), preferred_element_type=jnp.float32
    )


def unit_rows(values):
    lengths = jnp.sqrt(jnp.sum(values * values, axis=1, keepdims=True) + norm_eps)
    return (values / lengths, lengths)


def exchange_rows(blocks, axis):
    count = lax.axis_size(axis)
    own = lax.axis_index(axis)
    rows = blocks.shape[0] // count
    parts = [lax.dynamic_slice_in_dim(blocks, own * rows, rows, 0)]
    for step in range(1, count):
        target = lax.rem(own + step, count)
        sent = lax.dynamic_slice_in_dim(blocks, target * rows, rows, 0)
        parts.append(lax.ppermute(sent, axis, [(i, (i + step) % count) for i in range(count)]))
    return parts


def spread(values, axes):
    count = lax.axis_size(axes)
    copies = jnp.broadcast_to(values[None], (count,) + values.shape)
    return lax.all_to_all(copies, axes, 0, 0, tiled=True)


def butterfly(values, axis, combine):
    count = lax.axis_size(axis)
    step = 1
    while step < count:
        other = lax.ppermute(values, axis, [(i, i ^ step) for i in range(count)])
        values = combine(values, other, (lax.axis_index(axis) // step) % 2)
        step *= 2
    return values


def in_order(mine, other, upper):
    return jnp.where(upper == 0, jnp.concatenate([mine, other]), jnp.concatenate([other, mine]))


def body(crops, teacher_emb, w_first, b_first, w_second, b_second, w_third, b_third, protos):
    batch_index = lax.axis_index("batch")
    proto_index = lax.axis_index("proto")
    batch_size = lax.axis_size("batch")
    proto_size = lax.axis_size("proto")
    share_rows = crops.shape[0]
    group_rows = teacher_emb.shape[0]
    crops_total = group_rows * batch_size
    protos_total = protos.shape[0] * proto_size
    thin = protos.shape[0] // batch_size
    hidden_share = w_first.shape[1]

    all_crops = lax.all_gather(crops, "proto", axis=0, tiled=True)
    w_third_all = lax.all_gather(w_third, "proto", axis=0, tiled=True)
    first_bias = lax.dynamic_slice_in_dim(b_first, proto_index * hidden_share, hidden_share)
    h_first = jax.nn.gelu(
        jnp.dot(all_crops, w_first, preferred_element_type=jnp.float32) + first_bias,
        approximate=False,
    ).astype(jnp.bfloat16)
    partial_value = jnp.dot(h_first, w_second, preferred_element_type=jnp.float32)

    teacher_unit = unit_rows(teacher_emb.astype(jnp.float32))[0].astype(jnp.bfloat16)
    unit_share = lax.dynamic_slice_in_dim(teacher_unit, proto_index * share_rows, share_rows, 0)
    lanes = butterfly(unit_share[None], "batch", in_order)
    all_unit = lax.all_gather(lanes, "proto", axis=1, tiled=True).reshape(crops_total, -1)
    thin_protos = lax.dynamic_slice_in_dim(protos, batch_index * thin, thin, 0)
    thin_logits = scores(thin_protos, all_unit) / teacher_temp
    teacher_top = jnp.max(spread(jnp.max(thin_logits, axis=0), ("batch", "proto")), axis=0)
    thin_weights = jnp.exp(thin_logits - teacher_top[None, :])

    pre_second = sum(exchange_rows(partial_value, "proto"))
    h_second = jax.nn.gelu(pre_second + b_second, approximate=False).astype(jnp.bfloat16)
    bottleneck = jnp.dot(h_second, w_third_all, preferred_element_type=jnp.float32) + b_third
    unit, lengths = unit_rows(bottleneck)
    student_emb = lax.all_gather(unit.astype(jnp.bfloat16), "proto", axis=0, tiled=True)
    logits = scores(student_emb, protos) / student_temp
    local_top = jnp.max(logits, axis=1, keepdims=True)
    shifted = jnp.exp(logits - local_top)
    local_total = jnp.sum(shifted, axis=1, keepdims=True)
    attract = jnp.dot(shifted.astype(jnp.bfloat16), protos, preferred_element_type=jnp.float32)
    attract = jnp.concatenate(
        [attract, jnp.broadcast_to(local_total, (group_rows, 128)), jnp.broadcast_to(local_top, (group_rows, 128))],
        axis=1,
    )
    attract_parts = exchange_rows(attract, "proto")

    row_total = jnp.sum(thin_weights, axis=1)
    for sweep_step in range(ITERS):
        proto_scale = 1.0 / (protos_total * row_total)
        if sweep_step + 1 < ITERS:
            column_part = jnp.sum(thin_weights * proto_scale[:, None], axis=0)
            if sweep_step == 0:
                column_total = jnp.sum(spread(column_part, ("batch", "proto")), axis=0)
            else:
                column_total = butterfly(
                    lax.psum(column_part, "proto"), "batch", lambda mine, other, upper: mine + other
                )
            crop_scale = 1.0 / (crops_total * column_total)
            row_total = jnp.sum(thin_weights * crop_scale[None, :], axis=1)
    all_scale = spread(proto_scale, "batch").reshape(-1)

    own_top = lax.dynamic_slice_in_dim(teacher_top, batch_index * group_rows, group_rows, 0)
    weights_e = jnp.exp(scores(teacher_unit, protos) / teacher_temp - own_top[:, None])
    scaled = weights_e * all_scale[None, :]
    column_part = jnp.sum(scaled, axis=1, keepdims=True)
    repel = jnp.dot(scaled.astype(jnp.bfloat16), protos, preferred_element_type=jnp.float32)
    repel = jnp.concatenate([repel, jnp.broadcast_to(column_part, (group_rows, 128))], axis=1)
    repel_sum = sum(exchange_rows(repel, "proto"))

    width = protos.shape[1]
    tops = [part[:, width + 128 : width + 129] for part in attract_parts]
    row_top = tops[0]
    for top in tops[1:]:
        row_top = jnp.maximum(row_top, top)
    attract_sum = sum(part[:, :width] * jnp.exp(top - row_top) for part, top in zip(attract_parts, tops))
    row_sum = sum(part[:, width : width + 1] * jnp.exp(top - row_top) for part, top in zip(attract_parts, tops))
    emb_grad = (
        attract_sum / row_sum - repel_sum[:, :width] / repel_sum[:, width : width + 1]
    ) / student_temp
    crop_grad = (emb_grad - unit * jnp.sum(unit * emb_grad, axis=1, keepdims=True)) / lengths
    return crop_grad


def solution(mesh):
    in_specs = (
        P(("batch", "proto"), None),
        P("batch", None),
        P(None, "proto"),
        P(),
        P("proto", None),
        P(),
        P("proto", None),
        P(),
        P("proto", None),
    )
    out_specs = P(("batch", "proto"), None)
    return jax.shard_map(body, mesh=mesh, in_specs=in_specs, out_specs=out_specs, check_vma=False)
```

```python
import functools
import math

import jax
import jax.numpy as jnp
from jax import lax
from jax.experimental import pallas as pl
from jax.experimental.pallas import tpu as pltpu
from jax.sharding import PartitionSpec as P

ITERS = 3

student_temp = 0.1
teacher_temp = 0.07
norm_eps = 1e-06
teacher_rate = math.log2(math.e) / teacher_temp
student_rate = math.log2(math.e) / student_temp

VMEM_LIMIT = 48 * 1024 * 1024
BOTH = ("batch", "proto")


def scores(left_rows, right_rows):
    return lax.dot_general(
        left_rows, right_rows, (((1,), (1,)), ((), ())), preferred_element_type=jnp.float32
    )


def unit_rows(values):
    lengths = jnp.sqrt(jnp.sum(values * values, axis=1, keepdims=True) + norm_eps)
    return (values / lengths, lengths)


def whole(memory_space=pltpu.VMEM):
    return pl.BlockSpec(memory_space=memory_space)


def lane_fold(values, combine):
    folded = values[:, :128]
    for start in range(128, values.shape[1], 128):
        folded = combine(folded, values[:, start : start + 128])
    return folded


def params():
    return pltpu.CompilerParams(vmem_limit_bytes=VMEM_LIMIT)


def cost(flops, bytes_accessed, transcendentals=0):
    return pl.CostEstimate(
        flops=int(flops), bytes_accessed=int(bytes_accessed), transcendentals=int(transcendentals)
    )


def teacher_front_kernel(share, proto_ref, emb_ref, protos_ref, unit_ref, block_ref, top_ref):
    step = pl.program_id(0)
    rows = emb_ref.shape[0]

    @pl.when(step == 0)
    def _():
        unit_ref[...] = unit_rows(emb_ref[...].astype(jnp.float32))[0].astype(jnp.bfloat16)
        top_ref[...] = jnp.full(top_ref.shape, -jnp.inf, jnp.float32)

    products = scores(unit_ref[...], protos_ref[...])
    top_ref[:rows, :] = jnp.maximum(top_ref[:rows, :], lane_fold(products, jnp.maximum))

    @pl.when(step == pl.num_programs(0) - 1)
    def _():
        start = pl.multiple_of(proto_ref[0] * share, 16)
        block_ref[:share, :] = unit_ref[pl.ds(start, share), :]
        tops = jnp.max(jnp.transpose(top_ref[...]), axis=0, keepdims=True)
        lanes = lax.broadcasted_iota(jnp.int32, tops.shape, 1)
        tops = jnp.where(lanes < rows, tops, 0.0)
        high = tops.astype(jnp.bfloat16)
        rest = tops - high.astype(jnp.float32)
        middle = rest.astype(jnp.bfloat16)
        low = (rest - middle.astype(jnp.float32)).astype(jnp.bfloat16)
        block_ref[share:, :] = jnp.concatenate(
            [high, middle, low, jnp.zeros((13, tops.shape[1]), jnp.bfloat16)], axis=0
        )


def teacher_front(proto_index, teacher_emb, protos, share, steps):
    rows, width = teacher_emb.shape
    count = protos.shape[0]
    return pl.pallas_call(
        functools.partial(teacher_front_kernel, share),
        grid=(steps,),
        in_specs=[
            whole(pltpu.SMEM),
            whole(),
            pl.BlockSpec((count // steps, width), lambda i: (i, 0)),
        ],
        out_specs=[whole(), whole()],
        out_shape=[
            jax.ShapeDtypeStruct((rows, width), jnp.bfloat16),
            jax.ShapeDtypeStruct((share + 16, width), jnp.bfloat16),
        ],
        scratch_shapes=[pltpu.VMEM((256, 128), jnp.float32)],
        compiler_params=params(),
        cost_estimate=cost(2 * rows * width * count, 2 * width * count),
        name="teacher_front",
    )(proto_index, teacher_emb, protos)


def row_sums(values):
    return jnp.sum(lane_fold(values, jnp.add), axis=1, keepdims=True)


def first_sweep_kernel(chunk, protos_total, protos_ref, units_ref, top_ref, weights_ref, crop_sum_ref):
    crop_sum_ref[...] = jnp.zeros(crop_sum_ref.shape, jnp.float32)

    def sweep(index, carry):
        rows = pl.ds(pl.multiple_of(index * chunk, chunk), chunk)
        products = scores(protos_ref[rows, :], units_ref[...])
        weights = jnp.exp2((products - top_ref[...]) * teacher_rate)
        weights_ref[rows, :] = weights
        proto_scale = 1.0 / (protos_total * row_sums(weights))
        crop_sum_ref[...] += jnp.sum(weights * proto_scale, axis=0, keepdims=True)
        return carry

    lax.fori_loop(0, protos_ref.shape[0] // chunk, sweep, 0)


def first_sweep(thin_protos, units, top, protos_total):
    thin, width = thin_protos.shape
    crops_total = units.shape[0]
    chunk = min(thin, 128)
    return pl.pallas_call(
        functools.partial(first_sweep_kernel, chunk, protos_total),
        in_specs=[whole(), whole(), whole()],
        out_specs=[whole(), whole()],
        out_shape=[
            pltpu.VMEM((thin, crops_total), jnp.float32),
            jax.ShapeDtypeStruct((1, crops_total), jnp.float32),
        ],
        compiler_params=params(),
        cost_estimate=cost(2 * thin * width * crops_total, 2 * width * (thin + crops_total), thin * crops_total),
        name="first_sweep",
    )(thin_protos, units, top)


def crop_scales(parts_ref, crops_total):
    return 1.0 / (crops_total * jnp.sum(parts_ref[...], axis=0, keepdims=True))


def next_sweep_kernel(chunk, protos_total, weights_ref, parts_ref, crop_sum_ref, scale_ref):
    scale_ref[...] = crop_scales(parts_ref, weights_ref.shape[1])
    crop_sum_ref[...] = jnp.zeros(crop_sum_ref.shape, jnp.float32)

    def sweep(index, carry):
        weights = weights_ref[pl.ds(pl.multiple_of(index * chunk, chunk), chunk), :]
        proto_scale = 1.0 / (protos_total * row_sums(weights * scale_ref[...]))
        crop_sum_ref[...] += jnp.sum(weights * proto_scale, axis=0, keepdims=True)
        return carry

    lax.fori_loop(0, weights_ref.shape[0] // chunk, sweep, 0)


def next_sweep(weights, parts, protos_total):
    thin, crops_total = weights.shape
    chunk = min(thin, 64)
    return pl.pallas_call(
        functools.partial(next_sweep_kernel, chunk, protos_total),
        in_specs=[whole(), whole()],
        out_specs=whole(),
        out_shape=jax.ShapeDtypeStruct((1, crops_total), jnp.float32),
        scratch_shapes=[pltpu.VMEM((1, crops_total), jnp.float32)],
        compiler_params=params(),
        cost_estimate=cost(4 * thin * crops_total, 4 * thin * crops_total),
        name="next_sweep",
    )(pltpu.with_memory_space_constraint(weights, pltpu.VMEM), parts)


def last_scales_kernel(chunk, protos_total, weights_ref, parts_ref, proto_scale_ref, scale_ref):
    scale_ref[...] = crop_scales(parts_ref, weights_ref.shape[1])

    def sweep(index, carry):
        rows = pl.ds(pl.multiple_of(index * chunk, chunk), chunk)
        folded = lane_fold(weights_ref[rows, :] * scale_ref[...], jnp.add)
        sums = jnp.sum(jnp.transpose(folded), axis=0, keepdims=True)
        proto_scale_ref[:, rows] = 1.0 / (protos_total * sums)
        return carry

    lax.fori_loop(0, weights_ref.shape[0] // chunk, sweep, 0)


def last_scales(weights, parts, protos_total):
    thin, crops_total = weights.shape
    return pl.pallas_call(
        functools.partial(last_scales_kernel, 128, protos_total),
        in_specs=[whole(), whole()],
        out_specs=whole(),
        out_shape=jax.ShapeDtypeStruct((1, thin), jnp.float32),
        scratch_shapes=[pltpu.VMEM((1, crops_total), jnp.float32)],
        compiler_params=params(),
        cost_estimate=cost(2 * thin * crops_total, 4 * thin * crops_total),
        name="last_scales",
    )(pltpu.with_memory_space_constraint(weights, pltpu.VMEM), parts)


def wide_weights_kernel(unit_ref, protos_ref, top_ref, weights_ref, top_rows_ref):
    step = pl.program_id(0)
    rows = unit_ref.shape[0]
    block = protos_ref.shape[0]

    @pl.when(step == 0)
    def _():
        tops = jnp.transpose(jnp.broadcast_to(top_ref[...], (128, 256)))
        top_rows_ref[...] = tops[:rows, :]

    products = scores(unit_ref[...], protos_ref[...])
    tops = jnp.tile(top_rows_ref[...], (1, block // 128))
    weights_ref[:, pl.ds(pl.multiple_of(step * block, block), block)] = jnp.exp2(
        (products - tops) * teacher_rate
    )


def wide_weights(unit, protos, top, steps):
    rows, width = unit.shape
    count = protos.shape[0]
    return pl.pallas_call(
        wide_weights_kernel,
        grid=(steps,),
        in_specs=[whole(), pl.BlockSpec((count // steps, width), lambda i: (i, 0)), whole()],
        out_specs=whole(),
        out_shape=pltpu.VMEM((rows, count), jnp.float32),
        scratch_shapes=[pltpu.VMEM((rows, 128), jnp.float32)],
        compiler_params=params(),
        cost_estimate=cost(2 * rows * width * count, 2 * width * count, rows * count),
        name="wide_weights",
    )(unit, protos, top)


def repel_kernel(weights_ref, scale_ref, protos_ref, out_ref, sum_ref):
    step = pl.program_id(0)
    block, width = protos_ref.shape

    @pl.when(step == 0)
    def _():
        out_ref[...] = jnp.zeros(out_ref.shape, jnp.float32)
        sum_ref[...] = jnp.zeros(sum_ref.shape, jnp.float32)

    columns = pl.ds(pl.multiple_of(step * block, block), block)
    scaled = weights_ref[:, columns] * scale_ref[:, columns]
    rounded = scaled.astype(jnp.bfloat16)
    out_ref[:, :width] += jnp.dot(rounded, protos_ref[...], preferred_element_type=jnp.float32)
    sum_ref[...] += lane_fold(scaled, jnp.add)

    @pl.when(step == pl.num_programs(0) - 1)
    def _():
        total = jnp.sum(sum_ref[...], axis=1, keepdims=True)
        out_ref[:, width:] = jnp.broadcast_to(total, sum_ref.shape)


def repel(weights, scale, protos, steps):
    rows, count = weights.shape
    width = protos.shape[1]
    return pl.pallas_call(
        repel_kernel,
        grid=(steps,),
        in_specs=[whole(), whole(), pl.BlockSpec((count // steps, width), lambda i: (i, 0))],
        out_specs=whole(),
        out_shape=jax.ShapeDtypeStruct((rows, width + 128), jnp.float32),
        scratch_shapes=[pltpu.VMEM((rows, 128), jnp.float32)],
        compiler_params=params(),
        cost_estimate=cost(2 * rows * width * count, 2 * width * count),
        name="repel",
    )(pltpu.with_memory_space_constraint(weights, pltpu.VMEM), scale, protos)


def attract_kernel(emb_ref, protos_ref, out_ref, total_ref, top_ref):
    step = pl.program_id(0)
    block, width = protos_ref.shape

    @pl.when(step == 0)
    def _():
        out_ref[...] = jnp.zeros(out_ref.shape, jnp.float32)
        total_ref[...] = jnp.zeros(total_ref.shape, jnp.float32)
        top_ref[...] = jnp.full(top_ref.shape, -1e30, jnp.float32)

    products = scores(emb_ref[...], protos_ref[...])
    old_top = top_ref[...]
    block_top = jnp.max(lane_fold(products, jnp.maximum), axis=1, keepdims=True)
    new_top = jnp.maximum(old_top, block_top)
    fade = jnp.exp2((old_top - new_top) * student_rate)
    shifted = jnp.exp2((products - jnp.tile(new_top, (1, block // 128))) * student_rate)
    total_ref[...] = total_ref[...] * fade + lane_fold(shifted, jnp.add)
    top_ref[...] = new_top
    out_ref[:, :width] = out_ref[:, :width] * jnp.tile(fade, (1, width // 128)) + jnp.dot(
        shifted.astype(jnp.bfloat16), protos_ref[...], preferred_element_type=jnp.float32
    )

    @pl.when(step == pl.num_programs(0) - 1)
    def _():
        total = jnp.sum(total_ref[...], axis=1, keepdims=True)
        out_ref[:, width : width + 128] = jnp.broadcast_to(total, total_ref.shape)
        out_ref[:, width + 128 :] = new_top


def attract(emb, protos, steps):
    rows, width = emb.shape
    count = protos.shape[0]
    return pl.pallas_call(
        attract_kernel,
        grid=(steps,),
        in_specs=[whole(), pl.BlockSpec((count // steps, width), lambda i: (i, 0))],
        out_specs=whole(),
        out_shape=jax.ShapeDtypeStruct((rows, width + 256), jnp.float32),
        scratch_shapes=[pltpu.VMEM((rows, 128), jnp.float32), pltpu.VMEM((rows, 128), jnp.float32)],
        compiler_params=params(),
        cost_estimate=cost(4 * rows * width * count, 2 * width * count, rows * count),
        name="attract",
    )(emb, protos)


def exchange_rows(blocks, axis):
    count = lax.axis_size(axis)
    own = lax.axis_index(axis)
    rows = blocks.shape[0] // count
    parts = [lax.dynamic_slice_in_dim(blocks, own * rows, rows, 0)]
    for step in range(1, count):
        target = lax.rem(own + step, count)
        sent = lax.dynamic_slice_in_dim(blocks, target * rows, rows, 0)
        parts.append(lax.ppermute(sent, axis, [(i, (i + step) % count) for i in range(count)]))
    return parts


def spread(values, axes):
    count = lax.axis_size(axes)
    copies = jnp.broadcast_to(values[None], (count,) + values.shape)
    return lax.all_to_all(copies, axes, 0, 0, tiled=True)


def pairwise_gather(values, axis):
    count = lax.axis_size(axis)
    values = values[None, None]
    step = count // 2
    while step:
        other = lax.ppermute(values, axis, [(i, i ^ step) for i in range(count)])
        upper = (lax.axis_index(axis) // step) % 2
        both = jnp.where(
            upper == 0, jnp.concatenate([values, other], 1), jnp.concatenate([other, values], 1)
        )
        values = both.reshape((-1, 1) + values.shape[2:])
        step //= 2
    return values[:, 0]


def body(crops, teacher_emb, w_first, b_first, w_second, b_second, w_third, b_third, protos):
    batch_index = lax.axis_index("batch")
    proto_index = lax.axis_index("proto")
    batch_size = lax.axis_size("batch")
    proto_size = lax.axis_size("proto")
    share_rows = crops.shape[0]
    group_rows = teacher_emb.shape[0]
    crops_total = group_rows * batch_size
    protos_total = protos.shape[0] * proto_size
    thin = protos.shape[0] // batch_size
    hidden_share = w_first.shape[1]
    width = protos.shape[1]
    steps = 8

    own_unit, block = teacher_front(proto_index.reshape(1), teacher_emb, protos, share_rows, steps)
    blocks = pairwise_gather(block, "batch")
    blocks = lax.all_gather(blocks, "proto", axis=1)
    all_unit = blocks[:, :, :share_rows].reshape(crops_total, width)
    pieces = blocks[:, :, share_rows : share_rows + 3, :group_rows].astype(jnp.float32)
    tops = jnp.max(pieces[:, :, 0] + pieces[:, :, 1] + pieces[:, :, 2], axis=1)
    own_top = lax.dynamic_slice_in_dim(tops, batch_index, 1, 0)
    own_top = jnp.pad(own_top, ((0, 0), (0, 256 - group_rows)))
    thin_protos = lax.dynamic_slice_in_dim(protos, batch_index * thin, thin, 0)

    all_crops = lax.all_gather(crops, "proto", axis=0, tiled=True)
    w_third_all = lax.all_gather(w_third, "proto", axis=0, tiled=True)
    first_bias = lax.dynamic_slice_in_dim(b_first, proto_index * hidden_share, hidden_share)
    h_first = jax.nn.gelu(
        jnp.dot(all_crops, w_first, preferred_element_type=jnp.float32) + first_bias,
        approximate=False,
    ).astype(jnp.bfloat16)
    partial_value = jnp.dot(h_first, w_second, preferred_element_type=jnp.float32)
    pre_second = sum(exchange_rows(partial_value, "proto"))
    h_second = jax.nn.gelu(pre_second + b_second, approximate=False).astype(jnp.bfloat16)
    bottleneck = jnp.dot(h_second, w_third_all, preferred_element_type=jnp.float32) + b_third
    unit, lengths = unit_rows(bottleneck)
    student_emb = lax.all_gather(unit.astype(jnp.bfloat16), "proto", axis=0, tiled=True)
    attract_parts = exchange_rows(attract(student_emb, protos, steps), "proto")

    weights, crop_sum = first_sweep(thin_protos, all_unit, tops.reshape(1, crops_total), protos_total)
    for _ in range(ITERS - 2):
        crop_sum = next_sweep(weights, spread(crop_sum, BOTH).reshape(-1, crops_total), protos_total)
    scale = last_scales(weights, spread(crop_sum, BOTH).reshape(-1, crops_total), protos_total)
    all_scale = spread(scale, "batch").reshape(1, -1)

    own_weights = wide_weights(own_unit, protos, own_top, steps)
    repel_sum = sum(exchange_rows(repel(own_weights, all_scale, protos, steps), "proto"))

    tops_in = [part[:, width + 128 : width + 129] for part in attract_parts]
    row_top = functools.reduce(jnp.maximum, tops_in)
    fades = [jnp.exp2((top - row_top) * student_rate) for top in tops_in]
    attract_sum = sum(part[:, :width] * fade for part, fade in zip(attract_parts, fades))
    row_sum = sum(part[:, width : width + 1] * fade for part, fade in zip(attract_parts, fades))
    emb_grad = (
        attract_sum / row_sum - repel_sum[:, :width] / repel_sum[:, width : width + 1]
    ) / student_temp
    crop_grad = (emb_grad - unit * jnp.sum(unit * emb_grad, axis=1, keepdims=True)) / lengths
    return crop_grad


def solution(mesh):
    in_specs = (
        P(("batch", "proto"), None),
        P("batch", None),
        P(None, "proto"),
        P(),
        P("proto", None),
        P(),
        P("proto", None),
        P(),
        P("proto", None),
    )
    out_specs = P(("batch", "proto"), None)
    return jax.shard_map(body, mesh=mesh, in_specs=in_specs, out_specs=out_specs, check_vma=False)
```

```python
import functools
import math

import jax
import jax.numpy as jnp
from jax import lax
from jax.experimental import pallas as pl
from jax.experimental.pallas import tpu as pltpu
from jax.sharding import PartitionSpec as P

ITERS = 3

student_temp = 0.1
teacher_temp = 0.07
norm_eps = 1e-06
teacher_rate = math.log2(math.e) / teacher_temp
student_rate = math.log2(math.e) / student_temp

MIB = 1024 * 1024
BOTH = ("batch", "proto")


def scores(left_rows, right_rows):
    return lax.dot_general(
        left_rows, right_rows, (((1,), (1,)), ((), ())), preferred_element_type=jnp.float32
    )


def unit_rows(values):
    lengths = jnp.sqrt(jnp.sum(values * values, axis=1, keepdims=True) + norm_eps)
    return (values / lengths, lengths)


def whole(memory_space=pltpu.VMEM):
    return pl.BlockSpec(memory_space=memory_space)


def resident(array):
    return pltpu.with_memory_space_constraint(array, pltpu.VMEM)


def lane_fold(values, combine):
    folded = values[:, :128]
    for start in range(128, values.shape[1], 128):
        folded = combine(folded, values[:, start : start + 128])
    return folded


def row_fold(values):
    return jnp.sum(values.reshape(-1, 8, values.shape[1]), axis=0)


def part(index, size):
    return pl.ds(pl.multiple_of(index * size, size), size)


def params(mib):
    return pltpu.CompilerParams(vmem_limit_bytes=mib * MIB)


def cost(flops, bytes_accessed, transcendentals=0):
    return pl.CostEstimate(
        flops=int(flops), bytes_accessed=int(bytes_accessed), transcendentals=int(transcendentals)
    )


def teacher_units_kernel(core_ref, emb_ref, unit_ref, half_ref):
    unit_ref[...] = unit_rows(emb_ref[...].astype(jnp.float32))[0].astype(jnp.bfloat16)
    half = half_ref.shape[0]
    half_ref[...] = unit_ref[part(core_ref[0], half), :]


def teacher_units(core, teacher_emb):
    rows, width = teacher_emb.shape
    return pl.pallas_call(
        teacher_units_kernel,
        in_specs=[whole(pltpu.SMEM), whole()],
        out_specs=[whole(), whole()],
        out_shape=[
            jax.ShapeDtypeStruct((rows, width), jnp.bfloat16),
            jax.ShapeDtypeStruct((rows // 2, width), jnp.bfloat16),
        ],
        compiler_params=params(4),
        cost_estimate=cost(4 * rows * width, 8 * rows * width),
        name="teacher_units",
    )(core, teacher_emb)


def wide_products_kernel(block, unit_ref, protos_ref, products_ref, tops_ref, top_ref):
    rows = unit_ref.shape[0]
    top_ref[...] = jnp.full(top_ref.shape, -jnp.inf, jnp.float32)

    def step(index, carry):
        products = scores(unit_ref[...], protos_ref[part(index, block), :])
        products_ref[:, part(index, block)] = products
        top_ref[:rows, :] = jnp.maximum(top_ref[:rows, :], lane_fold(products, jnp.maximum))
        return carry

    lax.fori_loop(0, protos_ref.shape[0] // block, step, 0, unroll=2)
    tops = jnp.max(jnp.transpose(top_ref[...]), axis=0, keepdims=True)
    tops_ref[...] = jnp.broadcast_to(tops[None], tops_ref.shape)


def wide_products(unit, protos, copies):
    rows, width = unit.shape
    count = protos.shape[0]
    return pl.pallas_call(
        functools.partial(wide_products_kernel, min(count, 1024)),
        in_specs=[whole(), whole()],
        out_specs=[whole(), whole()],
        out_shape=[
            pltpu.VMEM((rows, count), jnp.float32),
            jax.ShapeDtypeStruct((copies, 1, 256), jnp.float32),
        ],
        scratch_shapes=[pltpu.VMEM((256, 128), jnp.float32)],
        compiler_params=params(8),
        cost_estimate=cost(2 * rows * width * count, 2 * width * count + 4 * rows * count),
        name="wide_products",
    )(unit, protos)


def wide_weights_kernel(block, group, batch_ref, products_ref, tops_ref, weights_ref):
    rows = products_ref.shape[0]
    first = batch_ref[0] * group
    top = tops_ref[first]
    for other in range(1, group):
        top = jnp.maximum(top, tops_ref[first + other])
    tops = jnp.transpose(jnp.broadcast_to(top, (128, 256)))[:rows, :]

    def step(index, carry):
        columns = part(index, block)
        weights_ref[:, columns] = jnp.exp2(
            (products_ref[:, columns] - jnp.tile(tops, (1, block // 128))) * teacher_rate
        )
        return carry

    lax.fori_loop(0, products_ref.shape[1] // block, step, 0)


def wide_weights(batch_index, products, tops, proto_size):
    rows, count = products.shape
    return pl.pallas_call(
        functools.partial(wide_weights_kernel, min(count, 1024), proto_size),
        in_specs=[whole(pltpu.SMEM), whole(), whole()],
        out_specs=whole(),
        out_shape=pltpu.VMEM((rows, count), jnp.float32),
        input_output_aliases={1: 0},
        compiler_params=params(8),
        cost_estimate=cost(2 * rows * count, 8 * rows * count, rows * count),
        name="wide_weights",
    )(batch_index, resident(products), tops)


def repel_kernel(block, proto_ref, weights_ref, scale_ref, protos_ref, *rest):
    out_refs, (acc_ref, sum_ref) = rest[:-2], rest[-2:]
    width = protos_ref.shape[1]
    copies = scale_ref.shape[0]
    thin = scale_ref.shape[2]
    acc_ref[...] = jnp.zeros(acc_ref.shape, jnp.float32)
    sum_ref[...] = jnp.zeros(sum_ref.shape, jnp.float32)
    pieces = thin // block

    def step(index, carry):
        columns = part(index, block)
        scale = scale_ref[index // pieces, :, part(lax.rem(index, pieces), block)]
        scaled = weights_ref[:, columns] * scale
        sum_ref[...] += lane_fold(scaled, jnp.add)
        acc_ref[...] += jnp.dot(
            scaled.astype(jnp.bfloat16), protos_ref[columns, :], preferred_element_type=jnp.float32
        )
        return carry

    lax.fori_loop(0, copies * pieces, step, 0, unroll=2)
    total = jnp.sum(sum_ref[...], axis=1, keepdims=True)
    sum_ref[...] = jnp.broadcast_to(total, sum_ref.shape)
    share = out_refs[0].shape[0]
    for flip, out_ref in enumerate(out_refs):
        rows = part(proto_ref[0] ^ flip, share)
        out_ref[:, :width] = acc_ref[rows, :]
        out_ref[:, width:] = sum_ref[rows, :]


def repel(proto_index, weights, scale, protos, proto_size):
    rows, count = weights.shape
    width = protos.shape[1]
    block = min(scale.shape[2], 1024)
    return pl.pallas_call(
        functools.partial(repel_kernel, block),
        in_specs=[whole(pltpu.SMEM), whole(), whole(), whole()],
        out_specs=[whole()] * proto_size,
        out_shape=[jax.ShapeDtypeStruct((rows // proto_size, width + 128), jnp.float32)] * proto_size,
        scratch_shapes=[pltpu.VMEM((rows, width), jnp.float32), pltpu.VMEM((rows, 128), jnp.float32)],
        compiler_params=params(10),
        cost_estimate=cost(2 * rows * width * count, 2 * width * count + 4 * rows * count),
        name="repel",
    )(proto_index, resident(weights), scale, protos)


def attract_kernel(block, emb_ref, protos_ref, *rest):
    out_refs, (products_ref, acc_ref, sum_ref, top_ref) = rest[:-4], rest[-4:]
    width = protos_ref.shape[1]
    steps = protos_ref.shape[0] // block
    acc_ref[...] = jnp.zeros(acc_ref.shape, jnp.float32)
    sum_ref[...] = jnp.zeros(sum_ref.shape, jnp.float32)
    top_ref[...] = jnp.full(top_ref.shape, -jnp.inf, jnp.float32)

    def first(index, carry):
        products = scores(emb_ref[...], protos_ref[part(index, block), :])
        products_ref[:, part(index, block)] = products
        top_ref[...] = jnp.maximum(top_ref[...], lane_fold(products, jnp.maximum))
        return carry

    lax.fori_loop(0, steps, first, 0, unroll=2)
    top = jnp.max(top_ref[...], axis=1, keepdims=True)
    top_ref[...] = jnp.broadcast_to(top, top_ref.shape)

    def second(index, carry):
        columns = part(index, block)
        shifted = jnp.exp2(
            (products_ref[:, columns] - jnp.tile(top_ref[...], (1, block // 128))) * student_rate
        )
        sum_ref[...] += lane_fold(shifted, jnp.add)
        acc_ref[...] += jnp.dot(
            shifted.astype(jnp.bfloat16), protos_ref[columns, :], preferred_element_type=jnp.float32
        )
        return carry

    lax.fori_loop(0, steps, second, 0, unroll=2)
    total = jnp.sum(sum_ref[...], axis=1, keepdims=True)
    sum_ref[...] = jnp.broadcast_to(total, sum_ref.shape)
    share = out_refs[0].shape[0]
    for slot, out_ref in enumerate(out_refs):
        rows = pl.ds(slot * share, share)
        out_ref[:, :width] = acc_ref[rows, :]
        out_ref[:, width : width + 128] = sum_ref[rows, :]
        out_ref[:, width + 128 :] = top_ref[rows, :]


def attract(emb, protos, proto_size):
    rows, width = emb.shape
    count = protos.shape[0]
    return pl.pallas_call(
        functools.partial(attract_kernel, min(count, 1024)),
        in_specs=[whole(), whole()],
        out_specs=[whole()] * proto_size,
        out_shape=[jax.ShapeDtypeStruct((rows // proto_size, width + 256), jnp.float32)] * proto_size,
        scratch_shapes=[
            pltpu.VMEM((rows, count), jnp.float32),
            pltpu.VMEM((rows, width), jnp.float32),
            pltpu.VMEM((rows, 128), jnp.float32),
            pltpu.VMEM((rows, 128), jnp.float32),
        ],
        compiler_params=params(20),
        cost_estimate=cost(4 * rows * width * count, 2 * width * count, rows * count),
        name="attract",
    )(emb, protos)


def row_sums(values):
    return jnp.sum(lane_fold(values, jnp.add), axis=1, keepdims=True)


def give_copies(copies_ref, totals):
    copies_ref[...] = jnp.broadcast_to(totals[None], copies_ref.shape)


def first_sweep_kernel(
    chunk, lanes, protos_total, index_ref, protos_ref, mine_ref, other_ref, top_ref,
    weights_ref, copies_ref, units_ref, scale_ref,
):
    thin, crops_total = weights_ref.shape
    half = mine_ref.shape[0]
    core = index_ref[1]
    units_ref[part(core, half), :] = mine_ref[...]
    units_ref[part(1 - core, half), :] = other_ref[...]
    first_row = index_ref[0] * thin

    def weigh(index, carry):
        rows = part(index, chunk)
        protos = protos_ref[pl.ds(pl.multiple_of(first_row + index * chunk, chunk), chunk), :]
        folded = jnp.zeros((chunk, 128), jnp.float32)
        for start in range(0, crops_total, lanes):
            columns = pl.ds(start, lanes)
            products = scores(protos, units_ref[columns, :])
            weights = jnp.exp2((products - top_ref[:, columns]) * teacher_rate)
            weights_ref[rows, columns] = weights
            folded = folded + lane_fold(weights, jnp.add)
        sums = jnp.sum(folded, axis=1, keepdims=True)
        scale_ref[rows, :] = jnp.broadcast_to(1.0 / (protos_total * sums), (chunk, 128))
        return carry

    lax.fori_loop(0, thin // chunk, weigh, 0)
    small = min(thin, 64)

    def add_up(index, totals):
        rows = part(index, small)
        scaled = weights_ref[rows, :] * jnp.tile(scale_ref[rows, :], (1, crops_total // 128))
        return totals + row_fold(scaled)

    totals = lax.fori_loop(0, thin // small, add_up, jnp.zeros((8, crops_total), jnp.float32))
    give_copies(copies_ref, jnp.sum(totals, axis=0, keepdims=True))


def first_sweep(index, protos, mine, other, top, copies, thin, protos_total):
    width = protos.shape[1]
    crops_total = 2 * mine.shape[0]
    return pl.pallas_call(
        functools.partial(first_sweep_kernel, min(thin, 512), 256, protos_total),
        in_specs=[whole(pltpu.SMEM), whole(), whole(), whole(), whole()],
        out_specs=[whole(), whole()],
        out_shape=[
            pltpu.VMEM((thin, crops_total), jnp.float32),
            jax.ShapeDtypeStruct((copies, 1, crops_total), jnp.float32),
        ],
        scratch_shapes=[
            pltpu.VMEM((crops_total, width), jnp.bfloat16),
            pltpu.VMEM((thin, 128), jnp.float32),
        ],
        compiler_params=params(12 if crops_total <= 2048 else 40),
        cost_estimate=cost(2 * thin * width * crops_total, 4 * thin * crops_total, thin * crops_total),
        name="first_sweep",
    )(index, protos, mine, other, top)


def crop_scales(parts_ref, crops_total):
    return 1.0 / (crops_total * jnp.sum(parts_ref[...], axis=0))


def next_sweep_kernel(chunk, protos_total, weights_ref, parts_ref, copies_ref, scale_ref):
    thin, crops_total = weights_ref.shape
    crop_scale = crop_scales(parts_ref, crops_total)

    def weigh(index):
        sums = row_sums(weights_ref[part(index, chunk), :] * crop_scale)
        return jnp.broadcast_to(1.0 / (protos_total * sums), (chunk, 128))

    def add_up(index, totals):
        scaled = weights_ref[part(index, chunk), :] * jnp.tile(scale_ref[...], (1, crops_total // 128))
        return totals + row_fold(scaled)

    scale_ref[...] = weigh(0)

    def sweep(index, totals):
        totals = add_up(index - 1, totals)
        scale_ref[...] = weigh(index)
        return totals

    steps = thin // chunk
    totals = lax.fori_loop(1, steps, sweep, jnp.zeros((8, crops_total), jnp.float32))
    totals = add_up(steps - 1, totals)
    give_copies(copies_ref, jnp.sum(totals, axis=0, keepdims=True))


def next_sweep(weights, parts, protos_total):
    thin, crops_total = weights.shape
    copies = parts.shape[0]
    return pl.pallas_call(
        functools.partial(next_sweep_kernel, min(thin, 128), protos_total),
        in_specs=[whole(), whole()],
        out_specs=whole(),
        out_shape=jax.ShapeDtypeStruct((copies, 1, crops_total), jnp.float32),
        scratch_shapes=[pltpu.VMEM((min(thin, 128), 128), jnp.float32)],
        compiler_params=params(8 if crops_total <= 2048 else 40),
        cost_estimate=cost(4 * thin * crops_total, 4 * thin * crops_total),
        name="next_sweep",
    )(resident(weights), parts)


def last_scales_kernel(chunk, protos_total, weights_ref, parts_ref, copies_ref, scale_ref):
    thin, crops_total = weights_ref.shape
    crop_scale = crop_scales(parts_ref, crops_total)

    def weigh(index, carry):
        rows = part(index, chunk)
        folded = lane_fold(weights_ref[rows, :] * crop_scale, jnp.add)
        sums = jnp.sum(jnp.transpose(folded), axis=0, keepdims=True)
        scale_ref[:, rows] = 1.0 / (protos_total * sums)
        return carry

    lax.fori_loop(0, thin // chunk, weigh, 0, unroll=2)
    give_copies(copies_ref, scale_ref[...])


def last_scales(weights, parts, copies, protos_total):
    thin, crops_total = weights.shape
    return pl.pallas_call(
        functools.partial(last_scales_kernel, min(thin, 256), protos_total),
        in_specs=[whole(), whole()],
        out_specs=whole(),
        out_shape=jax.ShapeDtypeStruct((copies, 1, thin), jnp.float32),
        scratch_shapes=[pltpu.VMEM((1, thin), jnp.float32)],
        compiler_params=params(8 if crops_total <= 2048 else 40),
        cost_estimate=cost(2 * thin * crops_total, 4 * thin * crops_total),
        name="last_scales",
    )(resident(weights), parts)


def swap(values, axis, flip):
    return lax.ppermute(values, axis, [(i, i ^ flip) for i in range(lax.axis_size(axis))])


def ordered(values, other, axis, flip, dim):
    upper = (lax.axis_index(axis) // flip) % 2
    return jnp.where(
        upper == 0, jnp.concatenate([values, other], dim), jnp.concatenate([other, values], dim)
    )


def gather_batch(values):
    step = lax.axis_size("batch") // 2
    while step:
        values = ordered(values, swap(values, "batch", step), "batch", step, 0)
        step //= 2
    return values


def bit_reversed(values, count):
    bits = count.bit_length() - 1
    split = values.reshape((2,) * bits + values.shape[1:])
    turned = jnp.transpose(split, tuple(reversed(range(bits))) + tuple(range(bits, split.ndim)))
    return turned.reshape(values.shape)


def send_blocks(blocks):
    return [blocks[0]] + [swap(block, "proto", flip) for flip, block in enumerate(blocks) if flip]


def all_to_all(copies, axes):
    return lax.all_to_all(copies, axes, 0, 0, tiled=True)


def body(crops, teacher_emb, w_first, b_first, w_second, b_second, w_third, b_third, protos):
    batch_index = lax.axis_index("batch")
    proto_index = lax.axis_index("proto")
    batch_size = lax.axis_size("batch")
    proto_size = lax.axis_size("proto")
    devices = batch_size * proto_size
    share_rows = crops.shape[0]
    group_rows = teacher_emb.shape[0]
    crops_total = group_rows * batch_size
    protos_total = protos.shape[0] * proto_size
    thin = protos.shape[0] // batch_size
    hidden_share = w_first.shape[1]
    width = protos.shape[1]
    core = proto_index % 2
    protos = resident(protos)

    own_unit, half = teacher_units(core.reshape(1), teacher_emb)
    crops_pair = jnp.concatenate([crops, swap(crops, "proto", 2)])
    mine = gather_batch(half)
    other = swap(mine, "proto", 1)
    products, top_copies = wide_products(own_unit, protos, devices)
    all_tops = all_to_all(top_copies, BOTH)
    tops = jnp.max(all_tops.reshape(batch_size, proto_size, 256)[:, :, :group_rows], axis=1)
    tops = bit_reversed(tops, batch_size).reshape(batch_size, 2, group_rows // 2)
    tops = jnp.transpose(tops, (1, 0, 2)).reshape(1, crops_total)
    own_weights = wide_weights(batch_index.reshape(1), products, all_tops, proto_size)

    all_crops = jnp.concatenate([crops_pair, swap(crops_pair, "proto", 1)])
    w_third_x = ordered(w_third[None], swap(w_third[None], "proto", 2), "proto", 2, 0)
    w_third_all = ordered(w_third_x[:, None], swap(w_third_x[:, None], "proto", 1), "proto", 1, 1)
    w_third_all = w_third_all.reshape(-1, width)
    first_bias = lax.dynamic_slice_in_dim(b_first, proto_index * hidden_share, hidden_share)
    h_first = jax.nn.gelu(
        jnp.dot(all_crops, w_first, preferred_element_type=jnp.float32) + first_bias,
        approximate=False,
    ).astype(jnp.bfloat16)
    partial_value = jnp.dot(h_first, w_second, preferred_element_type=jnp.float32)
    chip_sum = partial_value[: 2 * share_rows] + swap(partial_value[2 * share_rows :], "proto", 1)
    pre_second = chip_sum[:share_rows] + swap(chip_sum[share_rows:], "proto", 2)
    h_second = jax.nn.gelu(pre_second + b_second, approximate=False).astype(jnp.bfloat16)
    bottleneck = jnp.dot(h_second, w_third_all, preferred_element_type=jnp.float32) + b_third
    unit, lengths = unit_rows(bottleneck)
    rounded = unit.astype(jnp.bfloat16)
    emb_pair = jnp.concatenate([rounded, swap(rounded, "proto", 2)])
    student_emb = jnp.concatenate([emb_pair, swap(emb_pair, "proto", 1)])
    slots = attract(student_emb, protos, proto_size)
    attract_parts = send_blocks([slots[0], slots[2], slots[1], slots[3]])

    index = jnp.stack([batch_index, core])
    weights, copies = first_sweep(index, protos, mine, other, tops, devices, thin, protos_total)
    for _ in range(ITERS - 2):
        copies = next_sweep(weights, all_to_all(copies, BOTH), protos_total)
    scale_copies = last_scales(weights, all_to_all(copies, BOTH), batch_size, protos_total)
    all_scale = all_to_all(scale_copies, "batch")
    repel_parts = send_blocks(repel(proto_index.reshape(1), own_weights, all_scale, protos, proto_size))
    repel_sum = sum(repel_parts)

    tops_in = [block[:, width + 128 : width + 129] for block in attract_parts]
    row_top = functools.reduce(jnp.maximum, tops_in)
    fades = [jnp.exp2((top - row_top) * student_rate) for top in tops_in]
    attract_sum = sum(block[:, :width] * fade for block, fade in zip(attract_parts, fades))
    row_sum = sum(block[:, width : width + 1] * fade for block, fade in zip(attract_parts, fades))
    emb_grad = (
        attract_sum / row_sum - repel_sum[:, :width] / repel_sum[:, width : width + 1]
    ) / student_temp
    crop_grad = (emb_grad - unit * jnp.sum(unit * emb_grad, axis=1, keepdims=True)) / lengths
    return crop_grad


def solution(mesh):
    in_specs = (
        P(("batch", "proto"), None),
        P("batch", None),
        P(None, "proto"),
        P(),
        P("proto", None),
        P(),
        P("proto", None),
        P(),
        P("proto", None),
    )
    out_specs = P(("batch", "proto"), None)
    return jax.shard_map(body, mesh=mesh, in_specs=in_specs, out_specs=out_specs, check_vma=False)
```

```python
import functools
import math

import jax
import jax.numpy as jnp
from jax import lax
from jax.experimental import pallas as pl
from jax.experimental.pallas import tpu as pltpu
from jax.sharding import PartitionSpec as P

ITERS = 3

student_temp = 0.1
teacher_temp = 0.07
norm_eps = 1e-06
teacher_rate = math.log2(math.e) / teacher_temp
student_rate = math.log2(math.e) / student_temp

MIB = 1024 * 1024
BOTH = ("batch", "proto")
TILE = 256


def scores(left_rows, right_rows):
    return lax.dot_general(
        left_rows, right_rows, (((1,), (1,)), ((), ())), preferred_element_type=jnp.float32
    )


def unit_rows(values):
    lengths = jnp.sqrt(jnp.sum(values * values, axis=1, keepdims=True) + norm_eps)
    return (values / lengths, lengths)


def gelu(values):
    return 0.5 * values * (1.0 + lax.erf(values * math.sqrt(0.5)))


def whole(memory_space=pltpu.VMEM):
    return pl.BlockSpec(memory_space=memory_space)


def part(index, size):
    return pl.ds(pl.multiple_of(index * size, size), size)


def lane_fold(values, combine):
    folded = values[:, :128]
    for start in range(128, values.shape[1], 128):
        folded = combine(folded, values[:, start : start + 128])
    return folded


def params(mib):
    return pltpu.CompilerParams(vmem_limit_bytes=mib * MIB)


def cost(flops, bytes_accessed, transcendentals=0):
    return pl.CostEstimate(
        flops=int(flops), bytes_accessed=int(bytes_accessed), transcendentals=int(transcendentals)
    )


def fetch(source, target, sems, first_row=0):
    count, rows = target.shape[:2]

    def chunk_copy(index):
        start = pl.multiple_of(first_row + index * rows, rows)
        return pltpu.make_async_copy(source.at[pl.ds(start, rows), :], target.at[index], sems.at[index])

    for index in range(count):
        chunk_copy(index).start()
    return lambda index: chunk_copy(index).wait()


def teacher_units_kernel(core_ref, emb_ref, unit_ref, half_ref):
    unit_ref[...] = unit_rows(emb_ref[...].astype(jnp.float32))[0].astype(jnp.bfloat16)
    half = half_ref.shape[0]
    half_ref[...] = unit_ref[part(core_ref[0], half), :]


def teacher_units(core, teacher_emb):
    rows, width = teacher_emb.shape
    return pl.pallas_call(
        teacher_units_kernel,
        in_specs=[whole(pltpu.SMEM), whole()],
        out_specs=[whole(), whole()],
        out_shape=[
            jax.ShapeDtypeStruct((rows, width), jnp.bfloat16),
            jax.ShapeDtypeStruct((rows // 2, width), jnp.bfloat16),
        ],
        compiler_params=params(4),
        cost_estimate=cost(4 * rows * width, 8 * rows * width),
        name="teacher_units",
    )(core, teacher_emb)


def wide_tops_kernel(unit_ref, protos_hbm, tops_ref, protos_ref, sems, top_ref):
    rows = unit_ref.shape[0]
    steps, block = protos_ref.shape[:2]
    arrived = fetch(protos_hbm, protos_ref, sems)
    top_ref[...] = jnp.full(top_ref.shape, -jnp.inf, jnp.float32)

    def step(index, carry):
        arrived(index)
        top = top_ref[:rows, :]
        for start in range(0, block, TILE):
            products = scores(unit_ref[...], protos_ref[index, start : start + TILE, :])
            top = jnp.maximum(top, lane_fold(products, jnp.maximum))
        top_ref[:rows, :] = top
        return carry

    lax.fori_loop(0, steps, step, 0)
    tops = jnp.max(jnp.transpose(top_ref[...]), axis=0, keepdims=True)
    tops_ref[...] = jnp.broadcast_to(tops[None], tops_ref.shape)


def wide_tops(unit, protos, copies, steps):
    rows, width = unit.shape
    count = protos.shape[0]
    return pl.pallas_call(
        wide_tops_kernel,
        in_specs=[whole(), whole(pl.ANY)],
        out_specs=whole(),
        out_shape=jax.ShapeDtypeStruct((copies, 1, 256), jnp.float32),
        scratch_shapes=[
            pltpu.VMEM((steps, count // steps, width), jnp.bfloat16),
            pltpu.SemaphoreType.DMA((steps,)),
            pltpu.VMEM((256, 128), jnp.float32),
        ],
        compiler_params=params(16),
        cost_estimate=cost(2 * rows * width * count, 2 * width * count),
        name="wide_tops",
    )(unit, protos)


def repel_kernel(group, index_ref, unit_ref, tops_ref, scale_ref, protos_hbm, order_ref, *rest):
    out_refs, (protos_ref, sems, scaled_ref, acc_ref, sum_ref, bias_ref) = rest[:-6], rest[-6:]
    rows, width = unit_ref.shape
    steps, block = protos_ref.shape[:2]
    arrived = fetch(protos_hbm, protos_ref, sems)
    first = index_ref[0] * group
    top = tops_ref[first]
    for other in range(1, group):
        top = jnp.maximum(top, tops_ref[first + other])
    bias_ref[...] = jnp.transpose(jnp.broadcast_to(top, (128, 256)))[:rows, :] * -teacher_rate
    acc_ref[...] = jnp.zeros(acc_ref.shape, jnp.float32)
    sum_ref[...] = jnp.zeros(sum_ref.shape, jnp.float32)

    def step(index, carry):
        arrived(index)
        bias = bias_ref[...]
        total = sum_ref[...]
        for start in range(0, block, TILE):
            products = scores(unit_ref[...], protos_ref[index, start : start + TILE, :])
            for lane in range(0, TILE, 128):
                columns = slice(start + lane, start + lane + 128)
                scaled = jnp.exp2(products[:, lane : lane + 128] * teacher_rate + bias)
                scaled = scaled * scale_ref[index, :, columns]
                total = total + scaled
                scaled_ref[:, columns] = scaled.astype(jnp.bfloat16)
        sum_ref[...] = total
        acc_ref[...] += jnp.dot(scaled_ref[...], protos_ref[index], preferred_element_type=jnp.float32)
        return carry

    lax.fori_loop(0, steps, step, 0)
    total = jnp.sum(sum_ref[...], axis=1, keepdims=True)
    sum_ref[...] = jnp.broadcast_to(total, sum_ref.shape)
    share = out_refs[0].shape[0]
    for flip, out_ref in enumerate(out_refs):
        span = part(index_ref[1] ^ flip, share)
        out_ref[:, :width] = acc_ref[span, :]
        out_ref[:, width:] = sum_ref[span, :]


def repel(index, unit, tops, scale, protos, order, proto_size):
    rows, width = unit.shape
    count = protos.shape[0]
    steps, _, block = scale.shape
    return pl.pallas_call(
        functools.partial(repel_kernel, proto_size),
        in_specs=[whole(pltpu.SMEM), whole(), whole(), whole(), whole(pl.ANY), whole(pl.ANY)],
        out_specs=[whole()] * proto_size,
        out_shape=[jax.ShapeDtypeStruct((rows // proto_size, width + 128), jnp.float32)] * proto_size,
        scratch_shapes=[
            pltpu.VMEM((steps, block, width), jnp.bfloat16),
            pltpu.SemaphoreType.DMA((steps,)),
            pltpu.VMEM((rows, block), jnp.bfloat16),
            pltpu.VMEM((rows, width), jnp.float32),
            pltpu.VMEM((rows, 128), jnp.float32),
            pltpu.VMEM((rows, 128), jnp.float32),
        ],
        compiler_params=params(16),
        cost_estimate=cost(4 * rows * width * count, 2 * width * count, rows * count),
        name="repel",
    )(index, unit, tops, scale, protos, order)


def attract_kernel(first_row, last, emb_ref, state_ref, protos_hbm, *rest):
    out_refs, scratch = rest[:-6], rest[-6:]
    protos_ref, sems, products_ref, acc_ref, sum_ref, top_ref = scratch
    width = emb_ref.shape[1]
    steps, block = protos_ref.shape[:2]
    arrived = fetch(protos_hbm, protos_ref, sems, first_row)
    old_top = state_ref[:, width + 128 :]
    top_ref[...] = old_top

    def first(index, carry):
        arrived(index)
        top = top_ref[...]
        for start in range(0, block, TILE):
            products = scores(emb_ref[...], protos_ref[index, start : start + TILE, :])
            products_ref[index, :, start : start + TILE] = products
            top = jnp.maximum(top, lane_fold(products, jnp.maximum))
        top_ref[...] = top
        return carry

    lax.fori_loop(0, steps, first, 0)
    top = jnp.broadcast_to(jnp.max(top_ref[...], axis=1, keepdims=True), top_ref.shape)
    fade = jnp.exp2((old_top - top) * student_rate)
    top_ref[...] = top
    sum_ref[...] = state_ref[:, width : width + 128] * fade
    acc_ref[...] = state_ref[:, :width] * jnp.tile(fade, (1, width // 128))

    def second(index, carry):
        top = top_ref[...]
        total = sum_ref[...]
        acc = acc_ref[...]
        for start in range(0, block, TILE):
            pieces = []
            for lane in range(start, start + TILE, 128):
                shifted = jnp.exp2((products_ref[index, :, lane : lane + 128] - top) * student_rate)
                total = total + shifted
                pieces.append(shifted.astype(jnp.bfloat16))
            acc = acc + jnp.dot(
                jnp.concatenate(pieces, axis=1),
                protos_ref[index, start : start + TILE, :],
                preferred_element_type=jnp.float32,
            )
        sum_ref[...] = total
        acc_ref[...] = acc
        return carry

    lax.fori_loop(0, steps, second, 0)
    if last:
        total = jnp.sum(sum_ref[...], axis=1, keepdims=True)
        sum_ref[...] = jnp.broadcast_to(total, sum_ref.shape)
    share = out_refs[0].shape[0]
    for slot, out_ref in enumerate(out_refs):
        rows = pl.ds(slot * share, share)
        out_ref[:, :width] = acc_ref[rows, :]
        out_ref[:, width : width + 128] = sum_ref[rows, :]
        out_ref[:, width + 128 :] = top_ref[rows, :]


def attract(emb, state, protos, first_row, count, steps, outputs):
    rows, width = emb.shape
    block = count // steps
    return pl.pallas_call(
        functools.partial(attract_kernel, first_row, outputs > 1),
        in_specs=[whole(), whole(), whole(pl.ANY)],
        out_specs=[whole()] * outputs,
        out_shape=[jax.ShapeDtypeStruct((rows // outputs, width + 256), jnp.float32)] * outputs,
        scratch_shapes=[
            pltpu.VMEM((steps, block, width), jnp.bfloat16),
            pltpu.SemaphoreType.DMA((steps,)),
            pltpu.VMEM((steps, rows, block), jnp.float32),
            pltpu.VMEM((rows, width), jnp.float32),
            pltpu.VMEM((rows, 128), jnp.float32),
            pltpu.VMEM((rows, 128), jnp.float32),
        ],
        compiler_params=params(24),
        cost_estimate=cost(4 * rows * width * count, 2 * width * count, rows * count),
        name="attract",
    )(emb, state, protos)


def local_lanes(core, values, half):
    return jnp.where(
        core == 0, values, jnp.concatenate([values[:, half:], values[:, :half]], axis=1)
    )


def weigh_chunk(protos, mine_ref, other_ref, bias_ref, weights_ref, slot):
    half = mine_ref.shape[0]
    rows = protos.shape[0]
    folds = [None] * (rows // 64)
    for side, units_ref in enumerate((mine_ref, other_ref)):
        for start in range(0, half, TILE):
            products = scores(protos, units_ref[start : start + TILE, :])
            for tile in range(rows // 64):
                for lane in range(0, TILE, 128):
                    column = side * half + start + lane
                    weights = jnp.exp2(
                        products[tile * 64 : tile * 64 + 64, lane : lane + 128] * teacher_rate
                        + bias_ref[:, column : column + 128]
                    )
                    weights_ref[slot, tile * 64 : tile * 64 + 64, column : column + 128] = weights
                    folds[tile] = weights if folds[tile] is None else folds[tile] + weights
    return folds


def sweep_kernel(
    chunk, protos_total, index_ref, protos_hbm, mine_ref, other_ref, base_ref, parts_ref, order_ref,
    copies_ref, protos_ref, sems, bias_ref, weights_ref, scale_ref, totals_ref,
):
    half = mine_ref.shape[0]
    crops_total = 2 * half
    steps = protos_ref.shape[0]
    core = index_ref[1]
    arrived = fetch(protos_hbm, protos_ref, sems, index_ref[0] * steps * chunk)
    inverse = None
    bias = base_ref[...]
    if parts_ref is not None:
        inverse = crops_total * jnp.sum(parts_ref[...], axis=0)
        bias = bias - jnp.log2(inverse)
        inverse = local_lanes(core, inverse, half)
    bias_ref[...] = jnp.broadcast_to(local_lanes(core, bias, half), bias_ref.shape)
    totals_ref[...] = jnp.zeros(totals_ref.shape, jnp.float32)

    def weigh(index, slot):
        arrived(index)
        folds = weigh_chunk(protos_ref[index], mine_ref, other_ref, bias_ref, weights_ref, slot)
        for tile, fold in enumerate(folds):
            sums = jnp.sum(fold, axis=1, keepdims=True)
            scale_ref[slot, tile * 64 : tile * 64 + 64, :] = jnp.broadcast_to(
                1.0 / (protos_total * sums), (64, 128)
            )

    def add_up(slot):
        for lane in range(0, crops_total, 128):
            total = totals_ref[:, lane : lane + 128]
            for row in range(0, chunk, 8):
                total = total + (
                    weights_ref[slot, row : row + 8, lane : lane + 128]
                    * scale_ref[slot, row : row + 8, :]
                )
            totals_ref[:, lane : lane + 128] = total

    weigh(0, 0)

    def sweep(index, carry):
        slot = lax.rem(index, 2)
        weigh(index, slot)
        add_up(1 - slot)
        return carry

    lax.fori_loop(1, steps, sweep, 0)
    add_up((steps - 1) % 2)
    totals = jnp.sum(totals_ref[...], axis=0, keepdims=True)
    if inverse is not None:
        totals = totals * inverse
    totals = local_lanes(core, totals, half)
    copies_ref[...] = jnp.broadcast_to(totals[None], copies_ref.shape)


def first_sweep_kernel(chunk, protos_total, index_ref, protos_hbm, mine_ref, other_ref, base_ref, order_ref, *rest):
    sweep_kernel(chunk, protos_total, index_ref, protos_hbm, mine_ref, other_ref, base_ref, None, order_ref, *rest)


def sweep(index, protos, mine, other, base, parts, order, copies, thin, protos_total):
    width = protos.shape[1]
    half = mine.shape[0]
    crops_total = 2 * half
    chunk = max(thin // 8, 128)
    steps = thin // chunk
    kernel = first_sweep_kernel if parts is None else sweep_kernel
    extra = [] if parts is None else [parts]
    return pl.pallas_call(
        functools.partial(kernel, chunk, protos_total),
        in_specs=[whole(pltpu.SMEM), whole(pl.ANY), whole(), whole(), whole()]
        + [whole()] * len(extra) + [whole(pl.ANY)],
        out_specs=whole(),
        out_shape=jax.ShapeDtypeStruct((copies, 1, crops_total), jnp.float32),
        scratch_shapes=[
            pltpu.VMEM((steps, chunk, width), jnp.bfloat16),
            pltpu.SemaphoreType.DMA((steps,)),
            pltpu.VMEM((64, crops_total), jnp.float32),
            pltpu.VMEM((2, chunk, crops_total), jnp.float32),
            pltpu.VMEM((2, chunk, 128), jnp.float32),
            pltpu.VMEM((8, crops_total), jnp.float32),
        ],
        compiler_params=params(16 if crops_total <= 2048 else 56),
        cost_estimate=cost(2 * thin * width * crops_total, 2 * width * (thin + crops_total), thin * crops_total),
        name="first_sweep" if parts is None else "next_sweep",
    )(index, protos, mine, other, base, *extra, order)


def last_scales_kernel(
    chunk, protos_total, index_ref, protos_hbm, mine_ref, other_ref, base_ref, parts_ref, order_ref,
    copies_ref, protos_ref, sems, bias_ref, scale_ref,
):
    half = mine_ref.shape[0]
    crops_total = 2 * half
    steps = protos_ref.shape[0]
    core = index_ref[1]
    arrived = fetch(protos_hbm, protos_ref, sems, index_ref[0] * steps * chunk)
    bias = base_ref[...] - jnp.log2(crops_total * jnp.sum(parts_ref[...], axis=0))
    bias_ref[...] = jnp.broadcast_to(local_lanes(core, bias, half), bias_ref.shape)

    def step(index, carry):
        arrived(index)
        folds = [None] * (chunk // 64)
        for side, units_ref in enumerate((mine_ref, other_ref)):
            for start in range(0, half, TILE):
                products = scores(protos_ref[index], units_ref[start : start + TILE, :])
                for tile in range(chunk // 64):
                    for lane in range(0, TILE, 128):
                        column = side * half + start + lane
                        weights = jnp.exp2(
                            products[tile * 64 : tile * 64 + 64, lane : lane + 128] * teacher_rate
                            + bias_ref[:, column : column + 128]
                        )
                        folds[tile] = weights if folds[tile] is None else folds[tile] + weights
        folded = jnp.concatenate(folds, axis=0)
        sums = jnp.sum(jnp.transpose(folded), axis=0, keepdims=True)
        scale_ref[:, part(index, chunk)] = 1.0 / (protos_total * sums)
        return carry

    lax.fori_loop(0, steps, step, 0)
    copies_ref[...] = jnp.broadcast_to(scale_ref[...][None], copies_ref.shape)


def last_scales(index, protos, mine, other, base, parts, order, copies, thin, protos_total):
    width = protos.shape[1]
    crops_total = 2 * mine.shape[0]
    chunk = max(thin // 8, 128)
    steps = thin // chunk
    return pl.pallas_call(
        functools.partial(last_scales_kernel, chunk, protos_total),
        in_specs=[whole(pltpu.SMEM), whole(pl.ANY), whole(), whole(), whole(), whole(), whole(pl.ANY)],
        out_specs=whole(),
        out_shape=jax.ShapeDtypeStruct((copies, 1, thin), jnp.float32),
        scratch_shapes=[
            pltpu.VMEM((steps, chunk, width), jnp.bfloat16),
            pltpu.SemaphoreType.DMA((steps,)),
            pltpu.VMEM((64, crops_total), jnp.float32),
            pltpu.VMEM((1, thin), jnp.float32),
        ],
        compiler_params=params(12 if crops_total <= 2048 else 56),
        cost_estimate=cost(2 * thin * width * crops_total, 2 * width * (thin + crops_total), thin * crops_total),
        name="last_scales",
    )(index, protos, mine, other, base, parts, order)


def student_front_kernel(
    index_ref, own_ref, x_ref, pair_ref, bias_ref, first_hbm, second_hbm, keep_ref, give_ref,
    first_ref, second_ref, sems, rows_ref,
):
    first_copy = pltpu.make_async_copy(first_hbm, first_ref, sems.at[0])
    second_copy = pltpu.make_async_copy(second_hbm, second_ref, sems.at[1])
    first_copy.start()
    second_copy.start()
    share = own_ref.shape[0]
    rows_ref[:share, :] = own_ref[...]
    rows_ref[share : 2 * share, :] = x_ref[...]
    rows_ref[2 * share :, :] = pair_ref[...]
    hidden = first_ref.shape[1]
    bias = bias_ref[:, part(index_ref[0], hidden)]
    first_copy.wait()
    h_first = gelu(
        jnp.dot(rows_ref[...], first_ref[...], preferred_element_type=jnp.float32) + bias
    ).astype(jnp.bfloat16)
    second_copy.wait()
    for start in range(0, second_ref.shape[1], 512):
        columns = slice(start, start + 512)
        product = jnp.dot(h_first, second_ref[:, columns], preferred_element_type=jnp.float32)
        keep_ref[:, columns] = product[: 2 * share]
        give_ref[:, columns] = product[2 * share :]


def student_front(index, own, x_rows, pair, bias, first, second):
    share = own.shape[0]
    hidden, units = second.shape
    return pl.pallas_call(
        student_front_kernel,
        in_specs=[whole(pltpu.SMEM), whole(), whole(), whole(), whole(), whole(pl.ANY), whole(pl.ANY)],
        out_specs=[whole(), whole()],
        out_shape=[jax.ShapeDtypeStruct((2 * share, units), jnp.float32)] * 2,
        scratch_shapes=[
            pltpu.VMEM(first.shape, jnp.bfloat16),
            pltpu.VMEM(second.shape, jnp.bfloat16),
            pltpu.SemaphoreType.DMA((2,)),
            pltpu.VMEM((4 * share, own.shape[1]), jnp.bfloat16),
        ],
        compiler_params=params(16),
        cost_estimate=cost(8 * share * hidden * (own.shape[1] + units), 2 * hidden * (own.shape[1] + units)),
        name="student_front",
    )(index, own, x_rows, pair, bias.reshape(1, -1), first, second)


def student_middle_kernel(
    index_ref, keep_ref, core_ref, x_ref, bias_ref, own_ref, partner_ref, pair_ref, last_bias_ref,
    unit_ref, emb_ref, lengths_ref, hidden_ref,
):
    share = x_ref.shape[0]
    block = own_ref.shape[0]
    sums = keep_ref[:share, :] + core_ref[:share, :] + x_ref[...]
    hidden_ref[...] = gelu(sums + bias_ref[...]).astype(jnp.bfloat16)
    index = index_ref[0]
    weights = ((0, own_ref[...]), (2, partner_ref[...]), (1, pair_ref[:block, :]), (3, pair_ref[block:, :]))
    bottleneck = jnp.broadcast_to(last_bias_ref[...], unit_ref.shape)
    for flip, weight in weights:
        bottleneck = bottleneck + jnp.dot(
            hidden_ref[:, part(index ^ flip, block)], weight, preferred_element_type=jnp.float32
        )
    unit, lengths = unit_rows(bottleneck)
    unit_ref[...] = unit
    emb_ref[...] = unit.astype(jnp.bfloat16)
    lengths_ref[...] = jnp.broadcast_to(lengths, lengths_ref.shape)


def student_middle(index, keep, core_rows, x_rows, bias, own, partner, pair, last_bias):
    share, units = x_rows.shape
    width = own.shape[1]
    return pl.pallas_call(
        student_middle_kernel,
        in_specs=[whole(pltpu.SMEM)] + [whole()] * 8,
        out_specs=[whole()] * 3,
        out_shape=[
            jax.ShapeDtypeStruct((share, width), jnp.float32),
            jax.ShapeDtypeStruct((share, width), jnp.bfloat16),
            jax.ShapeDtypeStruct((share, 128), jnp.float32),
        ],
        scratch_shapes=[pltpu.VMEM((share, units), jnp.bfloat16)],
        compiler_params=params(12),
        cost_estimate=cost(2 * share * units * width, 2 * units * width + 16 * share * units),
        name="student_middle",
    )(index, keep, core_rows, x_rows, bias.reshape(1, -1), own, partner, pair, last_bias.reshape(1, -1))


def finish_kernel(unit_ref, lengths_ref, *rest):
    out_ref, blocks = rest[-1], rest[:-1]
    attracts, repels = blocks[: len(blocks) // 2], blocks[len(blocks) // 2 :]
    width = unit_ref.shape[1]
    row_top = functools.reduce(jnp.maximum, [ref[:, width + 128 :] for ref in attracts])
    attract_sum = repel_sum = 0.0
    row_sum = column_sum = 0.0
    for ref in attracts:
        fade = jnp.exp2((ref[:, width + 128 :] - row_top) * student_rate)
        row_sum = row_sum + ref[:, width : width + 128] * fade
        attract_sum = attract_sum + ref[:, :width] * jnp.tile(fade, (1, width // 128))
    for ref in repels:
        column_sum = column_sum + ref[:, width:]
        repel_sum = repel_sum + ref[:, :width]
    emb_grad = (
        attract_sum / jnp.tile(row_sum, (1, width // 128))
        - repel_sum / jnp.tile(column_sum, (1, width // 128))
    ) / student_temp
    unit = unit_ref[...]
    along = jnp.sum(unit * emb_grad, axis=1, keepdims=True)
    out_ref[...] = (emb_grad - unit * along) / jnp.tile(lengths_ref[...], (1, width // 128))


def finish(unit, lengths, attracts, repels):
    return pl.pallas_call(
        finish_kernel,
        in_specs=[whole()] * (2 + len(attracts) + len(repels)),
        out_specs=whole(),
        out_shape=jax.ShapeDtypeStruct(unit.shape, jnp.float32),
        compiler_params=params(8),
        cost_estimate=cost(40 * unit.size, 40 * unit.size),
        name="finish",
    )(unit, lengths, *attracts, *repels)


def swap(values, axis, flip):
    return lax.ppermute(values, axis, [(i, i ^ flip) for i in range(lax.axis_size(axis))])


def gather_batch(values):
    step = lax.axis_size("batch") // 2
    while step:
        other = swap(values, "batch", step)
        upper = (lax.axis_index("batch") // step) % 2
        values = jnp.where(
            upper == 0, jnp.concatenate([values, other]), jnp.concatenate([other, values])
        )
        step //= 2
    return values


def bit_reversed(values, count):
    bits = count.bit_length() - 1
    split = values.reshape((2,) * bits + values.shape[1:])
    turned = jnp.transpose(split, tuple(reversed(range(bits))) + tuple(range(bits, split.ndim)))
    return turned.reshape(values.shape)


def send_blocks(blocks):
    return [blocks[0]] + [swap(block, "proto", flip) for flip, block in enumerate(blocks) if flip]


def all_to_all(copies, axes):
    return lax.all_to_all(copies, axes, 0, 0, tiled=True)


def body(crops, teacher_emb, w_first, b_first, w_second, b_second, w_third, b_third, protos):
    batch_index = lax.axis_index("batch")
    proto_index = lax.axis_index("proto")
    batch_size = lax.axis_size("batch")
    proto_size = lax.axis_size("proto")
    devices = batch_size * proto_size
    share_rows = crops.shape[0]
    group_rows = teacher_emb.shape[0]
    crops_total = group_rows * batch_size
    protos_total = protos.shape[0] * proto_size
    count, width = protos.shape
    thin = count // batch_size
    core = proto_index % 2
    proto_ref = proto_index.reshape(1)
    thin_ref = jnp.stack([batch_index, core])
    wide_ref = jnp.stack([batch_index, proto_index])

    own_unit, half = teacher_units(core.reshape(1), teacher_emb)
    crops_x = swap(crops, "proto", 2)
    mine = gather_batch(half)
    other = swap(mine, "proto", 1)
    all_tops = all_to_all(wide_tops(own_unit, protos, devices, 8), BOTH)
    tops = jnp.max(all_tops.reshape(batch_size, proto_size, 256)[:, :, :group_rows], axis=1)
    tops = bit_reversed(tops, batch_size).reshape(batch_size, 2, group_rows // 2)
    base = jnp.transpose(tops, (1, 0, 2)).reshape(1, crops_total) * -teacher_rate

    crops_pair = swap(jnp.concatenate([crops, crops_x]), "proto", 1)
    keep, give = student_front(proto_ref, crops, crops_x, crops_pair, b_first, w_first, w_second)
    core_rows = swap(give, "proto", 1)
    x_sent = keep[share_rows:] + core_rows[share_rows:]
    x_rows = swap(x_sent, "proto", 2)
    w_third_x = swap(w_third, "proto", 2)
    w_third_pair = swap(jnp.concatenate([w_third, w_third_x]), "proto", 1)
    unit, rounded, lengths = student_middle(
        proto_ref, keep, core_rows, x_rows, b_second, w_third, w_third_x, w_third_pair, b_third
    )
    emb_pair = jnp.concatenate([rounded, swap(rounded, "proto", 2)])
    student_emb = jnp.concatenate([emb_pair, swap(emb_pair, "proto", 1)])
    empty = jnp.concatenate(
        [jnp.zeros((group_rows, width + 128), jnp.float32), jnp.full((group_rows, 128), -1e30, jnp.float32)], axis=1
    )
    (state,) = attract(student_emb, empty, protos, 0, count // 2, 4, 1)
    slots = attract(student_emb, state, protos, count // 2, count // 2, 4, proto_size)
    attract_parts = send_blocks([slots[0], slots[2], slots[1], slots[3]])

    copies = sweep(thin_ref, protos, mine, other, base, None, x_sent, devices, thin, protos_total)
    for _ in range(ITERS - 2):
        copies = sweep(
            thin_ref, protos, mine, other, base, all_to_all(copies, BOTH), rounded, devices, thin, protos_total
        )
    scale_copies = last_scales(
        thin_ref, protos, mine, other, base, all_to_all(copies, BOTH), state, batch_size, thin, protos_total
    )
    all_scale = all_to_all(scale_copies, "batch")
    repels = repel(wide_ref, own_unit, all_tops, all_scale, protos, slots[0], proto_size)
    return finish(unit, lengths, attract_parts, send_blocks(repels))


def solution(mesh):
    in_specs = (
        P(("batch", "proto"), None),
        P("batch", None),
        P(None, "proto"),
        P(),
        P("proto", None),
        P(),
        P("proto", None),
        P(),
        P("proto", None),
    )
    out_specs = P(("batch", "proto"), None)
    return jax.shard_map(body, mesh=mesh, in_specs=in_specs, out_specs=out_specs, check_vma=False)
```

```python
import functools
import math

import jax
import jax.numpy as jnp
from jax import lax
from jax.experimental import pallas as pl
from jax.experimental.pallas import tpu as pltpu
from jax.sharding import PartitionSpec as P

ITERS = 3

student_temp = 0.1
teacher_temp = 0.07
norm_eps = 1e-06
teacher_rate = math.log2(math.e) / teacher_temp
student_rate = math.log2(math.e) / student_temp

MIB = 1024 * 1024
BOTH = ("batch", "proto")
TILE = 256


def scores(left_rows, right_rows):
    return lax.dot_general(
        left_rows, right_rows, (((1,), (1,)), ((), ())), preferred_element_type=jnp.float32
    )


def unit_rows(values):
    lengths = jnp.sqrt(jnp.sum(values * values, axis=1, keepdims=True) + norm_eps)
    return (values / lengths, lengths)


def gelu(values):
    return 0.5 * values * (1.0 + lax.erf(values * math.sqrt(0.5)))


def whole(memory_space=pltpu.VMEM):
    return pl.BlockSpec(memory_space=memory_space)


def part(index, size):
    return pl.ds(pl.multiple_of(index * size, size), size)


def lane_fold(values, combine):
    folded = values[:, :128]
    for start in range(128, values.shape[1], 128):
        folded = combine(folded, values[:, start : start + 128])
    return folded


def params(mib):
    return pltpu.CompilerParams(vmem_limit_bytes=mib * MIB)


def cost(flops, bytes_accessed, transcendentals=0):
    return pl.CostEstimate(
        flops=int(flops), bytes_accessed=int(bytes_accessed), transcendentals=int(transcendentals)
    )


def fetch(source, target, sems, first_row=0):
    count, rows = target.shape[:2]

    def chunk_copy(index):
        start = pl.multiple_of(first_row + index * rows, rows)
        return pltpu.make_async_copy(source.at[pl.ds(start, rows), :], target.at[index], sems.at[index])

    for index in range(count):
        chunk_copy(index).start()
    return lambda index: chunk_copy(index).wait()


def teacher_units_kernel(core_ref, emb_ref, unit_ref, half_ref):
    unit_ref[...] = unit_rows(emb_ref[...].astype(jnp.float32))[0].astype(jnp.bfloat16)
    half = half_ref.shape[1]
    for copy in range(half_ref.shape[0]):
        half_ref[copy] = unit_ref[part(core_ref[0], half), :]


def teacher_units(core, teacher_emb, copies):
    rows, width = teacher_emb.shape
    return pl.pallas_call(
        teacher_units_kernel,
        in_specs=[whole(pltpu.SMEM), whole()],
        out_specs=[whole(), whole()],
        out_shape=[
            jax.ShapeDtypeStruct((rows, width), jnp.bfloat16),
            jax.ShapeDtypeStruct((copies, rows // 2, width), jnp.bfloat16),
        ],
        compiler_params=params(4),
        cost_estimate=cost(4 * rows * width, 8 * rows * width),
        name="teacher_units",
    )(core, teacher_emb)


def wide_tops_kernel(unit_ref, protos_hbm, order_ref, tops_ref, protos_ref, sems, top_ref):
    rows = unit_ref.shape[0]
    steps, block = protos_ref.shape[:2]
    arrived = fetch(protos_hbm, protos_ref, sems)
    top_ref[...] = jnp.full(top_ref.shape, -jnp.inf, jnp.float32)

    def step(index, carry):
        arrived(index)
        top = top_ref[:rows, :]
        for start in range(0, block, TILE):
            products = scores(unit_ref[...], protos_ref[index, start : start + TILE, :])
            top = jnp.maximum(top, lane_fold(products, jnp.maximum))
        top_ref[:rows, :] = top
        return carry

    lax.fori_loop(0, steps, step, 0)
    tops = jnp.max(jnp.transpose(top_ref[...]), axis=0, keepdims=True)
    tops_ref[...] = jnp.broadcast_to(tops[None], tops_ref.shape)


def wide_tops(unit, protos, order, copies, steps):
    rows, width = unit.shape
    count = protos.shape[0]
    return pl.pallas_call(
        wide_tops_kernel,
        in_specs=[whole(), whole(pltpu.HBM), whole(pltpu.HBM)],
        out_specs=whole(),
        out_shape=jax.ShapeDtypeStruct((copies, 1, 256), jnp.float32),
        scratch_shapes=[
            pltpu.VMEM((steps, count // steps, width), jnp.bfloat16),
            pltpu.SemaphoreType.DMA((steps,)),
            pltpu.VMEM((256, 128), jnp.float32),
        ],
        compiler_params=params(16),
        cost_estimate=cost(2 * rows * width * count, 2 * width * count),
        name="wide_tops",
    )(unit, protos, order)


def repel_kernel(group, index_ref, unit_ref, tops_ref, scale_ref, protos_hbm, order_ref, *rest):
    out_refs, (protos_ref, sems, scaled_ref, acc_ref, sum_ref, bias_ref) = rest[:-6], rest[-6:]
    rows, width = unit_ref.shape
    steps, block = protos_ref.shape[:2]
    arrived = fetch(protos_hbm, protos_ref, sems)
    first = index_ref[0] * group
    top = tops_ref[first]
    for other in range(1, group):
        top = jnp.maximum(top, tops_ref[first + other])
    bias_ref[...] = jnp.transpose(jnp.broadcast_to(top, (128, 256)))[:rows, :] * -teacher_rate
    acc_ref[...] = jnp.zeros(acc_ref.shape, jnp.float32)
    sum_ref[...] = jnp.zeros(sum_ref.shape, jnp.float32)

    def step(index, carry):
        arrived(index)
        bias = bias_ref[...]
        total = sum_ref[...]
        for start in range(0, block, TILE):
            products = scores(unit_ref[...], protos_ref[index, start : start + TILE, :])
            for lane in range(0, TILE, 128):
                columns = slice(start + lane, start + lane + 128)
                scaled = jnp.exp2(products[:, lane : lane + 128] * teacher_rate + bias)
                scaled = scaled * scale_ref[index, :, columns]
                total = total + scaled
                scaled_ref[:, columns] = scaled.astype(jnp.bfloat16)
        sum_ref[...] = total
        acc_ref[...] += jnp.dot(scaled_ref[...], protos_ref[index], preferred_element_type=jnp.float32)
        return carry

    lax.fori_loop(0, steps, step, 0)
    total = jnp.sum(sum_ref[...], axis=1, keepdims=True)
    sum_ref[...] = jnp.broadcast_to(total, sum_ref.shape)
    share = out_refs[0].shape[0]
    for flip, out_ref in enumerate(out_refs):
        span = part(index_ref[1] ^ flip, share)
        out_ref[:, :width] = acc_ref[span, :]
        out_ref[:, width:] = sum_ref[span, :]


def repel(index, unit, tops, scale, protos, order, proto_size):
    rows, width = unit.shape
    count = protos.shape[0]
    steps, _, block = scale.shape
    return pl.pallas_call(
        functools.partial(repel_kernel, proto_size),
        in_specs=[whole(pltpu.SMEM), whole(), whole(), whole(), whole(pltpu.HBM), whole(pltpu.HBM)],
        out_specs=[whole()] * proto_size,
        out_shape=[jax.ShapeDtypeStruct((rows // proto_size, width + 128), jnp.float32)] * proto_size,
        scratch_shapes=[
            pltpu.VMEM((steps, block, width), jnp.bfloat16),
            pltpu.SemaphoreType.DMA((steps,)),
            pltpu.VMEM((rows, block), jnp.bfloat16),
            pltpu.VMEM((rows, width), jnp.float32),
            pltpu.VMEM((rows, 128), jnp.float32),
            pltpu.VMEM((rows, 128), jnp.float32),
        ],
        compiler_params=params(16),
        cost_estimate=cost(4 * rows * width * count, 2 * width * count, rows * count),
        name="repel",
    )(index, unit, tops, scale, protos, order)


def attract_kernel(first_row, last, emb_ref, state_ref, protos_hbm, *rest):
    out_refs, scratch = rest[:-6], rest[-6:]
    protos_ref, sems, products_ref, acc_ref, sum_ref, top_ref = scratch
    width = emb_ref.shape[1]
    steps, block = protos_ref.shape[:2]
    arrived = fetch(protos_hbm, protos_ref, sems, first_row)
    old_top = state_ref[:, width + 128 :]
    top_ref[...] = old_top

    def first(index, carry):
        arrived(index)
        top = top_ref[...]
        for start in range(0, block, TILE):
            products = scores(emb_ref[...], protos_ref[index, start : start + TILE, :])
            products_ref[index, :, start : start + TILE] = products
            top = jnp.maximum(top, lane_fold(products, jnp.maximum))
        top_ref[...] = top
        return carry

    lax.fori_loop(0, steps, first, 0)
    top = jnp.broadcast_to(jnp.max(top_ref[...], axis=1, keepdims=True), top_ref.shape)
    fade = jnp.exp2((old_top - top) * student_rate)
    top_ref[...] = top
    sum_ref[...] = state_ref[:, width : width + 128] * fade
    acc_ref[...] = state_ref[:, :width] * jnp.tile(fade, (1, width // 128))

    def second(index, carry):
        top = top_ref[...]
        total = sum_ref[...]
        acc = acc_ref[...]
        for start in range(0, block, TILE):
            pieces = []
            for lane in range(start, start + TILE, 128):
                shifted = jnp.exp2((products_ref[index, :, lane : lane + 128] - top) * student_rate)
                total = total + shifted
                pieces.append(shifted.astype(jnp.bfloat16))
            acc = acc + jnp.dot(
                jnp.concatenate(pieces, axis=1),
                protos_ref[index, start : start + TILE, :],
                preferred_element_type=jnp.float32,
            )
        sum_ref[...] = total
        acc_ref[...] = acc
        return carry

    lax.fori_loop(0, steps, second, 0)
    if last:
        total = jnp.sum(sum_ref[...], axis=1, keepdims=True)
        sum_ref[...] = jnp.broadcast_to(total, sum_ref.shape)
    share = out_refs[0].shape[0]
    for slot, out_ref in enumerate(out_refs):
        rows = pl.ds(slot * share, share)
        out_ref[:, :width] = acc_ref[rows, :]
        out_ref[:, width : width + 128] = sum_ref[rows, :]
        out_ref[:, width + 128 :] = top_ref[rows, :]


def attract(emb, state, protos, first_row, count, steps, outputs):
    rows, width = emb.shape
    block = count // steps
    return pl.pallas_call(
        functools.partial(attract_kernel, first_row, outputs > 1),
        in_specs=[whole(), whole(), whole(pltpu.HBM)],
        out_specs=[whole()] * outputs,
        out_shape=[jax.ShapeDtypeStruct((rows // outputs, width + 256), jnp.float32)] * outputs,
        scratch_shapes=[
            pltpu.VMEM((steps, block, width), jnp.bfloat16),
            pltpu.SemaphoreType.DMA((steps,)),
            pltpu.VMEM((steps, rows, block), jnp.float32),
            pltpu.VMEM((rows, width), jnp.float32),
            pltpu.VMEM((rows, 128), jnp.float32),
            pltpu.VMEM((rows, 128), jnp.float32),
        ],
        compiler_params=params(24),
        cost_estimate=cost(4 * rows * width * count, 2 * width * count, rows * count),
        name="attract",
    )(emb, state, protos)


def three_pieces(values):
    high = values.astype(jnp.bfloat16)
    rest = values - high.astype(jnp.float32)
    middle = rest.astype(jnp.bfloat16)
    low = (rest - middle.astype(jnp.float32)).astype(jnp.bfloat16)
    return jnp.concatenate([high, middle, low, jnp.zeros((13, values.shape[1]), jnp.bfloat16)], axis=0)


def lane_scales(folded, protos_total):
    sums = [
        jnp.sum(jnp.transpose(folded[start : start + 128, :]), axis=0, keepdims=True)
        for start in range(0, folded.shape[0], 128)
    ]
    return 1.0 / (protos_total * jnp.concatenate(sums, axis=1))


def give_copies(copies_ref, totals):
    copies_ref[...] = jnp.broadcast_to(totals[None], copies_ref.shape)


def first_sweep_kernel(
    protos_total, index_ref, protos_hbm, mine_hbm, other_hbm, bias_ref, order_ref,
    copies_ref, weights_hbm, protos_ref, units_ref, weights_ref, fold_ref, totals_ref, sems, out_sems,
):
    tiles, thin, lanes = weights_ref.shape
    half = mine_hbm.shape[0]
    core = index_ref[1]
    copies = (
        pltpu.make_async_copy(protos_hbm.at[part(index_ref[0], thin), :], protos_ref, sems.at[0]),
        pltpu.make_async_copy(mine_hbm, units_ref.at[part(core, half), :], sems.at[1]),
        pltpu.make_async_copy(other_hbm, units_ref.at[part(1 - core, half), :], sems.at[2]),
    )
    for copy in copies:
        copy.start()
    fold_ref[...] = jnp.zeros(fold_ref.shape, jnp.float32)
    for copy in copies:
        copy.wait()

    def tile_out(tile):
        return pltpu.make_async_copy(weights_ref.at[tile], weights_hbm.at[tile], out_sems.at[tile])

    def weigh(tile, carry):
        products = scores(protos_ref[...], units_ref[part(tile, lanes), :])
        bias = bias_ref[:, part(tile, lanes)]
        for row in range(0, thin, 64):
            weights = jnp.exp2(products[row : row + 64, :] * teacher_rate + bias)
            weights_ref[tile, row : row + 64, :] = weights.astype(jnp.bfloat16)
            fold_ref[row : row + 64, :] += lane_fold(weights, jnp.add)
        tile_out(tile).start()
        return carry

    lax.fori_loop(0, tiles, weigh, 0)
    pieces = three_pieces(lane_scales(fold_ref[...], protos_total))

    def add_up(tile, carry):
        sums = jnp.dot(pieces, weights_ref[tile], preferred_element_type=jnp.float32)
        totals_ref[:, part(tile, lanes)] = jnp.sum(sums, axis=0, keepdims=True)
        return carry

    lax.fori_loop(0, tiles, add_up, 0)
    give_copies(copies_ref, totals_ref[...])
    for tile in range(tiles):
        tile_out(tile).wait()


def first_sweep(index, protos, mine, other, base, order, copies, thin, protos_total):
    width = protos.shape[1]
    crops_total = 2 * mine.shape[0]
    tiles = crops_total // TILE
    return pl.pallas_call(
        functools.partial(first_sweep_kernel, protos_total),
        in_specs=[whole(pltpu.SMEM), whole(pltpu.HBM), whole(pltpu.HBM), whole(pltpu.HBM), whole(), whole(pltpu.HBM)],
        out_specs=[whole(), whole(pltpu.HBM)],
        out_shape=[
            jax.ShapeDtypeStruct((copies, 1, crops_total), jnp.float32),
            jax.ShapeDtypeStruct((tiles, thin, TILE), jnp.bfloat16),
        ],
        scratch_shapes=[
            pltpu.VMEM((thin, width), jnp.bfloat16),
            pltpu.VMEM((crops_total, width), jnp.bfloat16),
            pltpu.VMEM((tiles, thin, TILE), jnp.bfloat16),
            pltpu.VMEM((thin, 128), jnp.float32),
            pltpu.VMEM((1, crops_total), jnp.float32),
            pltpu.SemaphoreType.DMA((3,)),
            pltpu.SemaphoreType.DMA((tiles,)),
        ],
        compiler_params=params(24 if crops_total <= 2048 else 50),
        cost_estimate=cost(2 * thin * width * crops_total, 2 * thin * crops_total, thin * crops_total),
        name="first_sweep",
    )(index, protos, mine, other, base, order)


def fetch_rows(weights_hbm, weights_ref, sems):
    steps, _, chunk, _ = weights_ref.shape

    def rows_copy(index):
        return pltpu.make_async_copy(
            weights_hbm.at[:, part(index, chunk), :], weights_ref.at[index], sems.at[index]
        )

    for index in range(steps):
        rows_copy(index).start()
    return lambda index: rows_copy(index).wait()


def scaled_fold(weights_ref, index, scale_ref):
    _, tiles, chunk, lanes = weights_ref.shape
    folds = []
    for row in range(0, chunk, 64):
        fold = None
        for tile in range(tiles):
            weights = weights_ref[index, tile, row : row + 64, :].astype(jnp.float32)
            scaled = lane_fold(weights * scale_ref[:, tile * lanes : (tile + 1) * lanes], jnp.add)
            fold = scaled if fold is None else fold + scaled
        folds.append(fold)
    return jnp.concatenate(folds, axis=0)


def next_sweep_kernel(
    protos_total, weights_hbm, parts_ref, order_ref, copies_ref, weights_ref, scale_ref, pieces_ref, totals_ref, sems,
):
    steps, tiles, chunk, lanes = weights_ref.shape
    arrived = fetch_rows(weights_hbm, weights_ref, sems)
    scale_ref[...] = 1.0 / (tiles * lanes * jnp.sum(parts_ref[...], axis=0))
    totals_ref[...] = jnp.zeros(totals_ref.shape, jnp.float32)

    def weigh(index):
        arrived(index)
        return three_pieces(lane_scales(scaled_fold(weights_ref, index, scale_ref), protos_total))

    def add_up(index):
        pieces = pieces_ref[...]
        for tile in range(tiles):
            columns = slice(tile * lanes, (tile + 1) * lanes)
            totals_ref[:, columns] += jnp.dot(
                pieces, weights_ref[index, tile], preferred_element_type=jnp.float32
            )

    pieces_ref[...] = weigh(0)

    def sweep(index, carry):
        add_up(index - 1)
        pieces_ref[...] = weigh(index)
        return carry

    lax.fori_loop(1, steps, sweep, 0)
    add_up(steps - 1)
    give_copies(copies_ref, jnp.sum(totals_ref[...], axis=0, keepdims=True))


def next_sweep(weights, parts, order, protos_total):
    tiles, thin, lanes = weights.shape
    copies, _, crops_total = parts.shape
    chunk = min(thin, 256)
    return pl.pallas_call(
        functools.partial(next_sweep_kernel, protos_total),
        in_specs=[whole(pltpu.HBM), whole(), whole(pltpu.HBM)],
        out_specs=whole(),
        out_shape=jax.ShapeDtypeStruct((copies, 1, crops_total), jnp.float32),
        scratch_shapes=[
            pltpu.VMEM((thin // chunk, tiles, chunk, lanes), jnp.bfloat16),
            pltpu.VMEM((1, crops_total), jnp.float32),
            pltpu.VMEM((16, chunk), jnp.bfloat16),
            pltpu.VMEM((16, crops_total), jnp.float32),
            pltpu.SemaphoreType.DMA((thin // chunk,)),
        ],
        compiler_params=params(16 if crops_total <= 2048 else 50),
        cost_estimate=cost(8 * thin * crops_total, 2 * thin * crops_total),
        name="next_sweep",
    )(weights, parts, order)


def last_scales_kernel(
    protos_total, weights_hbm, parts_ref, order_ref, copies_ref, weights_ref, scale_ref, out_ref, sems,
):
    steps, tiles, chunk, lanes = weights_ref.shape
    arrived = fetch_rows(weights_hbm, weights_ref, sems)
    scale_ref[...] = 1.0 / (tiles * lanes * jnp.sum(parts_ref[...], axis=0))

    def weigh(index, carry):
        arrived(index)
        out_ref[:, part(index, chunk)] = lane_scales(
            scaled_fold(weights_ref, index, scale_ref), protos_total
        )
        return carry

    lax.fori_loop(0, steps, weigh, 0)
    give_copies(copies_ref, out_ref[...])


def last_scales(weights, parts, order, copies, protos_total):
    tiles, thin, lanes = weights.shape
    crops_total = parts.shape[2]
    chunk = min(thin, 256)
    return pl.pallas_call(
        functools.partial(last_scales_kernel, protos_total),
        in_specs=[whole(pltpu.HBM), whole(), whole(pltpu.HBM)],
        out_specs=whole(),
        out_shape=jax.ShapeDtypeStruct((copies, 1, thin), jnp.float32),
        scratch_shapes=[
            pltpu.VMEM((thin // chunk, tiles, chunk, lanes), jnp.bfloat16),
            pltpu.VMEM((1, crops_total), jnp.float32),
            pltpu.VMEM((1, thin), jnp.float32),
            pltpu.SemaphoreType.DMA((thin // chunk,)),
        ],
        compiler_params=params(16 if crops_total <= 2048 else 50),
        cost_estimate=cost(4 * thin * crops_total, 2 * thin * crops_total),
        name="last_scales",
    )(weights, parts, order)


def student_front_kernel(
    index_ref, bias_ref, own_hbm, x_hbm, core_hbm, last_hbm, first_hbm, second_hbm, keep_ref, give_ref,
    first_ref, second_ref, rows_ref, sems,
):
    share = own_hbm.shape[0]
    copies = [
        pltpu.make_async_copy(source, rows_ref.at[slot * share : (slot + 1) * share, :], sems.at[slot])
        for slot, source in enumerate((own_hbm, x_hbm, core_hbm, last_hbm))
    ]
    copies.append(pltpu.make_async_copy(first_hbm, first_ref, sems.at[4]))
    second_copy = pltpu.make_async_copy(second_hbm, second_ref, sems.at[5])
    for copy in copies:
        copy.start()
    second_copy.start()
    hidden = first_ref.shape[1]
    bias = bias_ref[:, part(index_ref[0], hidden)]
    for copy in copies:
        copy.wait()
    h_first = gelu(
        jnp.dot(rows_ref[...], first_ref[...], preferred_element_type=jnp.float32) + bias
    ).astype(jnp.bfloat16)
    second_copy.wait()
    for start in range(0, second_ref.shape[1], 512):
        columns = slice(start, start + 512)
        product = jnp.dot(h_first, second_ref[:, columns], preferred_element_type=jnp.float32)
        keep_ref[:, columns] = product[: 2 * share]
        give_ref[:, columns] = product[2 * share :]


def student_front(index, bias, rows, first, second):
    share, features = rows[0].shape
    hidden, units = second.shape
    return pl.pallas_call(
        student_front_kernel,
        in_specs=[whole(pltpu.SMEM), whole()] + [whole(pltpu.HBM)] * 6,
        out_specs=[whole(), whole()],
        out_shape=[jax.ShapeDtypeStruct((2 * share, units), jnp.float32)] * 2,
        scratch_shapes=[
            pltpu.VMEM(first.shape, jnp.bfloat16),
            pltpu.VMEM(second.shape, jnp.bfloat16),
            pltpu.VMEM((4 * share, features), jnp.bfloat16),
            pltpu.SemaphoreType.DMA((6,)),
        ],
        compiler_params=params(16),
        cost_estimate=cost(8 * share * hidden * (features + units), 2 * hidden * (features + units)),
        name="student_front",
    )(index, bias.reshape(1, -1), *rows, first, second)


def student_middle_kernel(
    index_ref, keep_ref, core_ref, x_ref, bias_ref, own_ref, partner_ref, other_ref, last_ref, last_bias_ref,
    unit_ref, emb_ref, lengths_ref, hidden_ref,
):
    share = x_ref.shape[0]
    block = own_ref.shape[0]
    sums = keep_ref[:share, :] + core_ref[:share, :] + x_ref[...]
    hidden_ref[...] = gelu(sums + bias_ref[...]).astype(jnp.bfloat16)
    index = index_ref[0]
    weights = ((0, own_ref[...]), (2, partner_ref[...]), (1, other_ref[...]), (3, last_ref[...]))
    bottleneck = jnp.broadcast_to(last_bias_ref[...], unit_ref.shape)
    for flip, weight in weights:
        bottleneck = bottleneck + jnp.dot(
            hidden_ref[:, part(index ^ flip, block)], weight, preferred_element_type=jnp.float32
        )
    unit, lengths = unit_rows(bottleneck)
    unit_ref[...] = unit
    emb_ref[...] = unit.astype(jnp.bfloat16)
    lengths_ref[...] = jnp.broadcast_to(lengths, lengths_ref.shape)


def student_middle(index, keep, core_rows, x_rows, bias, weights, last_bias):
    share, units = x_rows.shape
    width = weights[0].shape[1]
    return pl.pallas_call(
        student_middle_kernel,
        in_specs=[whole(pltpu.SMEM)] + [whole()] * 9,
        out_specs=[whole()] * 3,
        out_shape=[
            jax.ShapeDtypeStruct((share, width), jnp.float32),
            jax.ShapeDtypeStruct((share, width), jnp.bfloat16),
            jax.ShapeDtypeStruct((share, 128), jnp.float32),
        ],
        scratch_shapes=[pltpu.VMEM((share, units), jnp.bfloat16)],
        compiler_params=params(12),
        cost_estimate=cost(2 * share * units * width, 2 * units * width + 16 * share * units),
        name="student_middle",
    )(index, keep, core_rows, x_rows, bias.reshape(1, -1), *weights, last_bias.reshape(1, -1))


def finish_kernel(unit_ref, lengths_ref, *rest):
    out_ref, blocks = rest[-1], rest[:-1]
    attracts, repels = blocks[: len(blocks) // 2], blocks[len(blocks) // 2 :]
    width = unit_ref.shape[1]
    row_top = functools.reduce(jnp.maximum, [ref[:, width + 128 :] for ref in attracts])
    attract_sum = repel_sum = 0.0
    row_sum = column_sum = 0.0
    for ref in attracts:
        fade = jnp.exp2((ref[:, width + 128 :] - row_top) * student_rate)
        row_sum = row_sum + ref[:, width : width + 128] * fade
        attract_sum = attract_sum + ref[:, :width] * jnp.tile(fade, (1, width // 128))
    for ref in repels:
        column_sum = column_sum + ref[:, width:]
        repel_sum = repel_sum + ref[:, :width]
    emb_grad = (
        attract_sum / jnp.tile(row_sum, (1, width // 128))
        - repel_sum / jnp.tile(column_sum, (1, width // 128))
    ) / student_temp
    unit = unit_ref[...]
    along = jnp.sum(unit * emb_grad, axis=1, keepdims=True)
    out_ref[...] = (emb_grad - unit * along) / jnp.tile(lengths_ref[...], (1, width // 128))


def finish(unit, lengths, attracts, repels):
    return pl.pallas_call(
        finish_kernel,
        in_specs=[whole()] * (2 + len(attracts) + len(repels)),
        out_specs=whole(),
        out_shape=jax.ShapeDtypeStruct(unit.shape, jnp.float32),
        compiler_params=params(8),
        cost_estimate=cost(40 * unit.size, 40 * unit.size),
        name="finish",
    )(unit, lengths, *attracts, *repels)


def swap(values, axis, flip):
    return lax.ppermute(values, axis, [(i, i ^ flip) for i in range(lax.axis_size(axis))])


def send_blocks(blocks):
    return [blocks[0]] + [swap(block, "proto", flip) for flip, block in enumerate(blocks) if flip]


def all_to_all(copies, axes):
    return lax.all_to_all(copies, axes, 0, 0, tiled=True)


def body(crops, teacher_emb, w_first, b_first, w_second, b_second, w_third, b_third, protos):
    batch_index = lax.axis_index("batch")
    proto_index = lax.axis_index("proto")
    batch_size = lax.axis_size("batch")
    proto_size = lax.axis_size("proto")
    devices = batch_size * proto_size
    share_rows = crops.shape[0]
    group_rows = teacher_emb.shape[0]
    crops_total = group_rows * batch_size
    protos_total = protos.shape[0] * proto_size
    count, width = protos.shape
    thin = count // batch_size
    core = proto_index % 2
    proto_ref = proto_index.reshape(1)
    thin_ref = jnp.stack([batch_index, core])
    wide_ref = jnp.stack([batch_index, proto_index])

    crops_x = swap(crops, "proto", 2)
    own_unit, halves = teacher_units(core.reshape(1), teacher_emb, batch_size)
    mine = all_to_all(halves, "batch").reshape(crops_total // 2, width)
    other = swap(mine, "proto", 1)
    all_tops = all_to_all(wide_tops(own_unit, protos, crops_x, devices, 8), BOTH)
    tops = jnp.max(all_tops.reshape(batch_size, proto_size, 256)[:, :, :group_rows], axis=1)
    tops = jnp.transpose(tops.reshape(batch_size, 2, group_rows // 2), (1, 0, 2))
    base = tops.reshape(1, crops_total) * -teacher_rate

    rows = [crops, crops_x, swap(crops, "proto", 1), swap(crops_x, "proto", 1)]
    keep, give = student_front(proto_ref, b_first, rows, w_first, w_second)
    core_rows = swap(give, "proto", 1)
    x_sent = keep[share_rows:] + core_rows[share_rows:]
    x_rows = swap(x_sent, "proto", 2)
    third_x = swap(w_third, "proto", 2)
    thirds = [w_third, third_x, swap(w_third, "proto", 1), swap(third_x, "proto", 1)]
    unit, rounded, lengths = student_middle(
        proto_ref, keep, core_rows, x_rows, b_second, thirds, b_third
    )
    emb_pair = jnp.concatenate([rounded, swap(rounded, "proto", 2)])
    student_emb = jnp.concatenate([emb_pair, swap(emb_pair, "proto", 1)])
    empty = jnp.concatenate(
        [jnp.zeros((group_rows, width + 128), jnp.float32), jnp.full((group_rows, 128), -1e30, jnp.float32)], axis=1
    )
    (state,) = attract(student_emb, empty, protos, 0, count // 2, 4, 1)
    slots = attract(student_emb, state, protos, count // 2, count // 2, 4, proto_size)
    attract_parts = send_blocks([slots[0], slots[2], slots[1], slots[3]])

    copies, weights = first_sweep(thin_ref, protos, mine, other, base, x_sent, devices, thin, protos_total)
    for _ in range(ITERS - 2):
        copies = next_sweep(weights, all_to_all(copies, BOTH), rounded, protos_total)
    scale_copies = last_scales(weights, all_to_all(copies, BOTH), state, batch_size, protos_total)
    all_scale = all_to_all(scale_copies, "batch")
    repels = repel(wide_ref, own_unit, all_tops, all_scale, protos, slots[0], proto_size)
    return finish(unit, lengths, attract_parts, send_blocks(repels))


def solution(mesh):
    in_specs = (
        P(("batch", "proto"), None),
        P("batch", None),
        P(None, "proto"),
        P(),
        P("proto", None),
        P(),
        P("proto", None),
        P(),
        P("proto", None),
    )
    out_specs = P(("batch", "proto"), None)
    return jax.shard_map(body, mesh=mesh, in_specs=in_specs, out_specs=out_specs, check_vma=False)
```

```python
import functools
import math

import jax
import jax.numpy as jnp
from jax import lax
from jax.experimental import pallas as pl
from jax.experimental.pallas import tpu as pltpu
from jax.sharding import PartitionSpec as P

ITERS = 3

student_temp = 0.1
teacher_temp = 0.07
norm_eps = 1e-06
teacher_rate = math.log2(math.e) / teacher_temp
student_rate = math.log2(math.e) / student_temp

MIB = 1024 * 1024
BOTH = ("batch", "proto")
TILE = 256


def scores(left_rows, right_rows):
    return lax.dot_general(
        left_rows, right_rows, (((1,), (1,)), ((), ())), preferred_element_type=jnp.float32
    )


def unit_rows(values):
    lengths = jnp.sqrt(jnp.sum(values * values, axis=1, keepdims=True) + norm_eps)
    return (values / lengths, lengths)


def gelu(values):
    return 0.5 * values * (1.0 + lax.erf(values * math.sqrt(0.5)))


def whole(memory_space=pltpu.VMEM):
    return pl.BlockSpec(memory_space=memory_space)


def in_hbm(array):
    return pltpu.with_memory_space_constraint(array, pltpu.HBM)


def part(index, size):
    return pl.ds(pl.multiple_of(index * size, size), size)


def lane_fold(values, combine):
    folded = values[:, :128]
    for start in range(128, values.shape[1], 128):
        folded = combine(folded, values[:, start : start + 128])
    return folded


def params(mib):
    return pltpu.CompilerParams(vmem_limit_bytes=mib * MIB)


def cost(flops, bytes_accessed, transcendentals=0):
    return pl.CostEstimate(
        flops=int(flops), bytes_accessed=int(bytes_accessed), transcendentals=int(transcendentals)
    )


def fetch(source, target, sems, first_row=0):
    count, rows = target.shape[:2]

    def chunk_copy(index):
        start = pl.multiple_of(first_row + index * rows, rows)
        return pltpu.make_async_copy(source.at[pl.ds(start, rows), :], target.at[index], sems.at[index])

    for index in range(count):
        chunk_copy(index).start()
    return lambda index: chunk_copy(index).wait()


def teacher_units_kernel(core_ref, emb_ref, unit_ref, half_ref):
    unit_ref[...] = unit_rows(emb_ref[...].astype(jnp.float32))[0].astype(jnp.bfloat16)
    half = half_ref.shape[0]
    half_ref[...] = unit_ref[part(core_ref[0], half), :]


def teacher_units(core, teacher_emb):
    rows, width = teacher_emb.shape
    return pl.pallas_call(
        teacher_units_kernel,
        in_specs=[whole(pltpu.SMEM), whole()],
        out_specs=[whole(), whole()],
        out_shape=[
            jax.ShapeDtypeStruct((rows, width), jnp.bfloat16),
            jax.ShapeDtypeStruct((rows // 2, width), jnp.bfloat16),
        ],
        compiler_params=params(4),
        cost_estimate=cost(4 * rows * width, 8 * rows * width),
        name="teacher_units",
    )(core, in_hbm(teacher_emb))


def wide_tops_kernel(first_row, last, unit_ref, protos_hbm, before_ref, order_ref, out_ref, protos_ref, sems, top_ref):
    rows = unit_ref.shape[0]
    steps, block = protos_ref.shape[:2]
    arrived = fetch(protos_hbm, protos_ref, sems, first_row)
    top_ref[...] = before_ref[...]

    def step(index, carry):
        arrived(index)
        top = top_ref[:rows, :]
        for start in range(0, block, TILE):
            products = scores(unit_ref[...], protos_ref[index, start : start + TILE, :])
            top = jnp.maximum(top, lane_fold(products, jnp.maximum))
        top_ref[:rows, :] = top
        return carry

    lax.fori_loop(0, steps, step, 0)
    if last:
        tops = jnp.max(jnp.transpose(top_ref[...]), axis=0, keepdims=True)
        out_ref[...] = jnp.broadcast_to(tops[None], out_ref.shape)
    else:
        out_ref[...] = top_ref[...]


def wide_tops(unit, protos, before, order, copies, first_row, count, steps):
    rows, width = unit.shape
    shape = (copies, 1, 256) if copies else before.shape
    return pl.pallas_call(
        functools.partial(wide_tops_kernel, first_row, copies > 0),
        in_specs=[whole(), whole(pl.ANY), whole(), whole(pl.ANY)],
        out_specs=whole(),
        out_shape=jax.ShapeDtypeStruct(shape, jnp.float32),
        scratch_shapes=[
            pltpu.VMEM((steps, count // steps, width), jnp.bfloat16),
            pltpu.SemaphoreType.DMA((steps,)),
            pltpu.VMEM((256, 128), jnp.float32),
        ],
        compiler_params=params(16),
        cost_estimate=cost(2 * rows * width * count, 2 * width * count),
        name="wide_tops",
    )(unit, in_hbm(protos), before, order)


def repel_kernel(group, index_ref, unit_ref, tops_ref, scale_ref, protos_hbm, order_ref, *rest):
    out_refs, (protos_ref, sems, acc_ref, sum_ref, bias_ref) = rest[:-5], rest[-5:]
    rows, width = unit_ref.shape
    steps, block = protos_ref.shape[:2]
    arrived = fetch(protos_hbm, protos_ref, sems)
    first = index_ref[0] * group
    top = tops_ref[first]
    for other in range(1, group):
        top = jnp.maximum(top, tops_ref[first + other])
    bias_ref[...] = jnp.transpose(jnp.broadcast_to(top, (128, 256)))[:rows, :] * -teacher_rate
    acc_ref[...] = jnp.zeros(acc_ref.shape, jnp.float32)
    sum_ref[...] = jnp.zeros(sum_ref.shape, jnp.float32)

    def step(index, carry):
        arrived(index)
        bias = bias_ref[...]
        total = sum_ref[...]
        acc = acc_ref[...]
        for start in range(0, block, TILE):
            protos = protos_ref[index, start : start + TILE, :]
            products = scores(unit_ref[...], protos)
            pieces = []
            for lane in range(0, TILE, 128):
                scaled = jnp.exp2(products[:, lane : lane + 128] * teacher_rate + bias)
                scaled = scaled * scale_ref[index, :, start + lane : start + lane + 128]
                total = total + scaled
                pieces.append(scaled.astype(jnp.bfloat16))
            acc = acc + jnp.dot(
                jnp.concatenate(pieces, axis=1), protos, preferred_element_type=jnp.float32
            )
        sum_ref[...] = total
        acc_ref[...] = acc
        return carry

    lax.fori_loop(0, steps, step, 0)
    total = jnp.sum(sum_ref[...], axis=1, keepdims=True)
    sum_ref[...] = jnp.broadcast_to(total, sum_ref.shape)
    share = out_refs[0].shape[0]
    for flip, out_ref in enumerate(out_refs):
        span = part(index_ref[1] ^ flip, share)
        out_ref[:, :width] = acc_ref[span, :]
        out_ref[:, width:] = sum_ref[span, :]


def repel(index, unit, tops, scale, protos, order, proto_size):
    rows, width = unit.shape
    count = protos.shape[0]
    steps, _, block = scale.shape
    return pl.pallas_call(
        functools.partial(repel_kernel, proto_size),
        in_specs=[whole(pltpu.SMEM), whole(), whole(), whole(), whole(pl.ANY), whole(pl.ANY)],
        out_specs=[whole()] * proto_size,
        out_shape=[jax.ShapeDtypeStruct((rows // proto_size, width + 128), jnp.float32)] * proto_size,
        scratch_shapes=[
            pltpu.VMEM((steps, block, width), jnp.bfloat16),
            pltpu.SemaphoreType.DMA((steps,)),
            pltpu.VMEM((rows, width), jnp.float32),
            pltpu.VMEM((rows, 128), jnp.float32),
            pltpu.VMEM((rows, 128), jnp.float32),
        ],
        compiler_params=params(16),
        cost_estimate=cost(4 * rows * width * count, 2 * width * count, rows * count),
        name="repel",
    )(index, unit, tops, scale, in_hbm(protos), order)


def attract_kernel(first_row, last, emb_ref, state_ref, protos_hbm, *rest):
    out_refs, scratch = rest[:-6], rest[-6:]
    protos_ref, sems, products_ref, acc_ref, sum_ref, top_ref = scratch
    width = emb_ref.shape[1]
    steps, block = protos_ref.shape[:2]
    arrived = fetch(protos_hbm, protos_ref, sems, first_row)
    old_top = state_ref[:, width + 128 :]
    top_ref[...] = old_top

    def first(index, carry):
        arrived(index)
        top = top_ref[...]
        for start in range(0, block, TILE):
            products = scores(emb_ref[...], protos_ref[index, start : start + TILE, :])
            products_ref[index, :, start : start + TILE] = products
            top = jnp.maximum(top, lane_fold(products, jnp.maximum))
        top_ref[...] = top
        return carry

    lax.fori_loop(0, steps, first, 0)
    top = jnp.broadcast_to(jnp.max(top_ref[...], axis=1, keepdims=True), top_ref.shape)
    fade = jnp.exp2((old_top - top) * student_rate)
    top_ref[...] = top
    sum_ref[...] = state_ref[:, width : width + 128] * fade
    acc_ref[...] = state_ref[:, :width] * jnp.tile(fade, (1, width // 128))

    def second(index, carry):
        top = top_ref[...]
        total = sum_ref[...]
        acc = acc_ref[...]
        for start in range(0, block, TILE):
            pieces = []
            for lane in range(start, start + TILE, 128):
                shifted = jnp.exp2((products_ref[index, :, lane : lane + 128] - top) * student_rate)
                total = total + shifted
                pieces.append(shifted.astype(jnp.bfloat16))
            acc = acc + jnp.dot(
                jnp.concatenate(pieces, axis=1),
                protos_ref[index, start : start + TILE, :],
                preferred_element_type=jnp.float32,
            )
        sum_ref[...] = total
        acc_ref[...] = acc
        return carry

    lax.fori_loop(0, steps, second, 0)
    if last:
        total = jnp.sum(sum_ref[...], axis=1, keepdims=True)
        sum_ref[...] = jnp.broadcast_to(total, sum_ref.shape)
    share = out_refs[0].shape[0]
    for slot, out_ref in enumerate(out_refs):
        rows = pl.ds(slot * share, share)
        out_ref[:, :width] = acc_ref[rows, :]
        out_ref[:, width : width + 128] = sum_ref[rows, :]
        out_ref[:, width + 128 :] = top_ref[rows, :]


def attract(emb, state, protos, first_row, count, steps, outputs):
    rows, width = emb.shape
    block = count // steps
    return pl.pallas_call(
        functools.partial(attract_kernel, first_row, outputs > 1),
        in_specs=[whole(), whole(), whole(pl.ANY)],
        out_specs=[whole()] * outputs,
        out_shape=[jax.ShapeDtypeStruct((rows // outputs, width + 256), jnp.float32)] * outputs,
        scratch_shapes=[
            pltpu.VMEM((steps, block, width), jnp.bfloat16),
            pltpu.SemaphoreType.DMA((steps,)),
            pltpu.VMEM((steps, rows, block), jnp.float32),
            pltpu.VMEM((rows, width), jnp.float32),
            pltpu.VMEM((rows, 128), jnp.float32),
            pltpu.VMEM((rows, 128), jnp.float32),
        ],
        compiler_params=params(24),
        cost_estimate=cost(4 * rows * width * count, 2 * width * count, rows * count),
        name="attract",
    )(emb, state, in_hbm(protos))


def three_pieces(values):
    high = values.astype(jnp.bfloat16)
    rest = values - high.astype(jnp.float32)
    middle = rest.astype(jnp.bfloat16)
    low = (rest - middle.astype(jnp.float32)).astype(jnp.bfloat16)
    return jnp.concatenate([high, middle, low, jnp.zeros((13, values.shape[1]), jnp.bfloat16)], axis=0)


def lane_scales(folded, protos_total):
    sums = [
        jnp.sum(jnp.transpose(folded[start : start + 128, :]), axis=0, keepdims=True)
        for start in range(0, folded.shape[0], 128)
    ]
    return 1.0 / (protos_total * jnp.concatenate(sums, axis=1))


def give_copies(copies_ref, totals):
    copies_ref[...] = jnp.broadcast_to(totals[None], copies_ref.shape)


def first_sweep_kernel(
    chunk, protos_total, index_ref, protos_hbm, mine_hbm, other_hbm, bias_ref, order_ref,
    copies_ref, weights_hbm, protos_ref, units_ref, weights_ref, rounded_ref, scale_ref, sems, out_sems,
):
    thin, crops_total = weights_ref.shape
    half = mine_hbm.shape[0]
    core = index_ref[1]
    copies = (
        pltpu.make_async_copy(protos_hbm.at[part(index_ref[0], thin), :], protos_ref, sems.at[0]),
        pltpu.make_async_copy(mine_hbm, units_ref.at[part(core, half), :], sems.at[1]),
        pltpu.make_async_copy(other_hbm, units_ref.at[part(1 - core, half), :], sems.at[2]),
    )
    for copy in copies:
        copy.start()
    for copy in copies:
        copy.wait()

    def chunk_out(index):
        return pltpu.make_async_copy(
            rounded_ref.at[index], weights_hbm.at[part(index, chunk), :], out_sems.at[index]
        )

    def weigh(index, carry):
        rows = part(index, chunk)
        protos = protos_ref[rows, :]
        folded = jnp.zeros((chunk, 128), jnp.float32)
        for start in range(0, crops_total, TILE):
            columns = slice(start, start + TILE)
            products = scores(protos, units_ref[columns, :])
            weights = jnp.exp2(products * teacher_rate + bias_ref[:, columns])
            weights_ref[rows, columns] = weights
            rounded_ref[index, :, columns] = weights.astype(jnp.bfloat16)
            folded = folded + lane_fold(weights, jnp.add)
        sums = jnp.sum(folded, axis=1, keepdims=True)
        scale_ref[rows, :] = jnp.broadcast_to(1.0 / (protos_total * sums), (chunk, 128))
        chunk_out(index).start()
        return carry

    lax.fori_loop(0, thin // chunk, weigh, 0)
    small = min(thin, 64)

    def add_up(index, totals):
        rows = part(index, small)
        scaled = weights_ref[rows, :] * jnp.tile(scale_ref[rows, :], (1, crops_total // 128))
        return totals + jnp.sum(scaled.reshape(-1, 8, crops_total), axis=0)

    totals = lax.fori_loop(0, thin // small, add_up, jnp.zeros((8, crops_total), jnp.float32))
    give_copies(copies_ref, jnp.sum(totals, axis=0, keepdims=True))
    for index in range(thin // chunk):
        chunk_out(index).wait()


def first_sweep(index, protos, mine, other, base, order, copies, thin, protos_total):
    width = protos.shape[1]
    crops_total = 2 * mine.shape[0]
    chunk = min(thin, 512)
    return pl.pallas_call(
        functools.partial(first_sweep_kernel, chunk, protos_total),
        in_specs=[whole(pltpu.SMEM), whole(pl.ANY), whole(pl.ANY), whole(pl.ANY), whole(), whole(pl.ANY)],
        out_specs=[whole(), whole(pl.ANY)],
        out_shape=[
            jax.ShapeDtypeStruct((copies, 1, crops_total), jnp.float32),
            pltpu.HBM((thin, crops_total), jnp.bfloat16),
        ],
        scratch_shapes=[
            pltpu.VMEM((thin, width), jnp.bfloat16),
            pltpu.VMEM((crops_total, width), jnp.bfloat16),
            pltpu.VMEM((thin, crops_total), jnp.float32),
            pltpu.VMEM((thin // chunk, chunk, crops_total), jnp.bfloat16),
            pltpu.VMEM((thin, 128), jnp.float32),
            pltpu.SemaphoreType.DMA((3,)),
            pltpu.SemaphoreType.DMA((thin // chunk,)),
        ],
        compiler_params=params(32 if crops_total <= 2048 else 56),
        cost_estimate=cost(2 * thin * width * crops_total, 2 * thin * crops_total, thin * crops_total),
        name="first_sweep",
    )(index, in_hbm(protos), mine, other, base, order)


def fetch_rows(weights_hbm, weights_ref, sems):
    steps, chunk, _ = weights_ref.shape

    def rows_copy(index):
        return pltpu.make_async_copy(
            weights_hbm.at[part(index, chunk), :], weights_ref.at[index], sems.at[index]
        )

    for index in range(steps):
        rows_copy(index).start()
    return lambda index: rows_copy(index).wait()


def scaled_fold(weights_ref, index, scale_ref):
    _, chunk, crops_total = weights_ref.shape
    folds = []
    for row in range(0, chunk, 64):
        fold = None
        for start in range(0, crops_total, TILE):
            columns = slice(start, start + TILE)
            weights = weights_ref[index, row : row + 64, columns].astype(jnp.float32)
            scaled = lane_fold(weights * scale_ref[:, columns], jnp.add)
            fold = scaled if fold is None else fold + scaled
        folds.append(fold)
    return jnp.concatenate(folds, axis=0)


def next_sweep_kernel(
    protos_total, weights_hbm, parts_ref, order_ref, copies_ref, weights_ref, scale_ref, pieces_ref, totals_ref, sems,
):
    steps, chunk, crops_total = weights_ref.shape
    arrived = fetch_rows(weights_hbm, weights_ref, sems)
    scale_ref[...] = 1.0 / (crops_total * jnp.sum(parts_ref[...], axis=0))
    totals_ref[...] = jnp.zeros(totals_ref.shape, jnp.float32)

    def weigh(index):
        return three_pieces(lane_scales(scaled_fold(weights_ref, index, scale_ref), protos_total))

    def add_up(index):
        return jnp.dot(pieces_ref[...], weights_ref[index], preferred_element_type=jnp.float32)

    arrived(0)
    pieces_ref[...] = weigh(0)

    def sweep(index, carry):
        arrived(index)
        sums = add_up(index - 1)
        pieces = weigh(index)
        totals_ref[...] += sums
        pieces_ref[...] = pieces
        return carry

    lax.fori_loop(1, steps, sweep, 0)
    totals = totals_ref[...] + add_up(steps - 1)
    give_copies(copies_ref, jnp.sum(totals, axis=0, keepdims=True))


def next_sweep(weights, parts, order, protos_total):
    thin, crops_total = weights.shape
    copies = parts.shape[0]
    chunk = min(thin, 256)
    return pl.pallas_call(
        functools.partial(next_sweep_kernel, protos_total),
        in_specs=[whole(pl.ANY), whole(), whole(pl.ANY)],
        out_specs=whole(),
        out_shape=jax.ShapeDtypeStruct((copies, 1, crops_total), jnp.float32),
        scratch_shapes=[
            pltpu.VMEM((thin // chunk, chunk, crops_total), jnp.bfloat16),
            pltpu.VMEM((1, crops_total), jnp.float32),
            pltpu.VMEM((16, chunk), jnp.bfloat16),
            pltpu.VMEM((16, crops_total), jnp.float32),
            pltpu.SemaphoreType.DMA((thin // chunk,)),
        ],
        compiler_params=params(16 if crops_total <= 2048 else 50),
        cost_estimate=cost(8 * thin * crops_total, 2 * thin * crops_total),
        name="next_sweep",
    )(in_hbm(weights), parts, order)


def last_scales_kernel(
    protos_total, weights_hbm, parts_ref, order_ref, copies_ref, weights_ref, scale_ref, out_ref, sems,
):
    steps, chunk, crops_total = weights_ref.shape
    arrived = fetch_rows(weights_hbm, weights_ref, sems)
    scale_ref[...] = 1.0 / (crops_total * jnp.sum(parts_ref[...], axis=0))

    def weigh(index, carry):
        arrived(index)
        out_ref[:, part(index, chunk)] = lane_scales(
            scaled_fold(weights_ref, index, scale_ref), protos_total
        )
        return carry

    lax.fori_loop(0, steps, weigh, 0)
    give_copies(copies_ref, out_ref[...])


def last_scales(weights, parts, order, copies, protos_total):
    thin, crops_total = weights.shape
    chunk = min(thin, 256)
    return pl.pallas_call(
        functools.partial(last_scales_kernel, protos_total),
        in_specs=[whole(pl.ANY), whole(), whole(pl.ANY)],
        out_specs=whole(),
        out_shape=jax.ShapeDtypeStruct((copies, 1, thin), jnp.float32),
        scratch_shapes=[
            pltpu.VMEM((thin // chunk, chunk, crops_total), jnp.bfloat16),
            pltpu.VMEM((1, crops_total), jnp.float32),
            pltpu.VMEM((1, thin), jnp.float32),
            pltpu.SemaphoreType.DMA((thin // chunk,)),
        ],
        compiler_params=params(16 if crops_total <= 2048 else 50),
        cost_estimate=cost(4 * thin * crops_total, 2 * thin * crops_total),
        name="last_scales",
    )(in_hbm(weights), parts, order)


def student_front_kernel(
    index_ref, bias_ref, own_hbm, x_hbm, core_hbm, last_hbm, first_hbm, second_hbm, keep_ref, give_ref,
    first_ref, second_ref, rows_ref, sems,
):
    share = own_hbm.shape[0]
    copies = [
        pltpu.make_async_copy(source, rows_ref.at[slot * share : (slot + 1) * share, :], sems.at[slot])
        for slot, source in enumerate((own_hbm, x_hbm, core_hbm, last_hbm))
    ]
    copies.append(pltpu.make_async_copy(first_hbm, first_ref, sems.at[4]))
    second_copy = pltpu.make_async_copy(second_hbm, second_ref, sems.at[5])
    for copy in copies:
        copy.start()
    second_copy.start()
    hidden = first_ref.shape[1]
    bias = bias_ref[:, part(index_ref[0], hidden)]
    for copy in copies:
        copy.wait()
    h_first = gelu(
        jnp.dot(rows_ref[...], first_ref[...], preferred_element_type=jnp.float32) + bias
    ).astype(jnp.bfloat16)
    second_copy.wait()
    for start in range(0, second_ref.shape[1], 512):
        columns = slice(start, start + 512)
        product = jnp.dot(h_first, second_ref[:, columns], preferred_element_type=jnp.float32)
        keep_ref[:, columns] = product[: 2 * share]
        give_ref[:, columns] = product[2 * share :]


def student_front(index, bias, rows, first, second):
    share, features = rows[0].shape
    hidden, units = second.shape
    return pl.pallas_call(
        student_front_kernel,
        in_specs=[whole(pltpu.SMEM), whole()] + [whole(pl.ANY)] * 6,
        out_specs=[whole(), whole()],
        out_shape=[jax.ShapeDtypeStruct((2 * share, units), jnp.float32)] * 2,
        scratch_shapes=[
            pltpu.VMEM(first.shape, jnp.bfloat16),
            pltpu.VMEM(second.shape, jnp.bfloat16),
            pltpu.VMEM((4 * share, features), jnp.bfloat16),
            pltpu.SemaphoreType.DMA((6,)),
        ],
        compiler_params=params(16),
        cost_estimate=cost(8 * share * hidden * (features + units), 2 * hidden * (features + units)),
        name="student_front",
    )(index, in_hbm(bias.reshape(1, -1)), in_hbm(rows[0]), *rows[1:], in_hbm(first), in_hbm(second))


def student_middle_kernel(
    index_ref, keep_ref, core_ref, x_ref, bias_ref, own_ref, partner_ref, other_ref, last_ref, last_bias_ref,
    unit_ref, emb_ref, lengths_ref, hidden_ref,
):
    share = x_ref.shape[0]
    block = own_ref.shape[0]
    sums = keep_ref[:share, :] + core_ref[:share, :] + x_ref[...]
    hidden_ref[...] = gelu(sums + bias_ref[...]).astype(jnp.bfloat16)
    index = index_ref[0]
    weights = ((0, own_ref[...]), (2, partner_ref[...]), (1, other_ref[...]), (3, last_ref[...]))
    bottleneck = jnp.broadcast_to(last_bias_ref[...], unit_ref.shape)
    for flip, weight in weights:
        bottleneck = bottleneck + jnp.dot(
            hidden_ref[:, part(index ^ flip, block)], weight, preferred_element_type=jnp.float32
        )
    unit, lengths = unit_rows(bottleneck)
    unit_ref[...] = unit
    emb_ref[...] = unit.astype(jnp.bfloat16)
    lengths_ref[...] = jnp.broadcast_to(lengths, lengths_ref.shape)


def student_middle(index, keep, core_rows, x_rows, bias, weights, last_bias):
    share, units = x_rows.shape
    width = weights[0].shape[1]
    return pl.pallas_call(
        student_middle_kernel,
        in_specs=[whole(pltpu.SMEM)] + [whole()] * 9,
        out_specs=[whole()] * 3,
        out_shape=[
            jax.ShapeDtypeStruct((share, width), jnp.float32),
            jax.ShapeDtypeStruct((share, width), jnp.bfloat16),
            jax.ShapeDtypeStruct((share, 128), jnp.float32),
        ],
        scratch_shapes=[pltpu.VMEM((share, units), jnp.bfloat16)],
        compiler_params=params(12),
        cost_estimate=cost(2 * share * units * width, 2 * units * width + 16 * share * units),
        name="student_middle",
    )(index, keep, core_rows, x_rows, in_hbm(bias.reshape(1, -1)), in_hbm(weights[0]), *weights[1:], in_hbm(last_bias.reshape(1, -1)))


def finish_kernel(unit_ref, lengths_ref, *rest):
    out_ref, blocks = rest[-1], rest[:-1]
    attracts, repels = blocks[: len(blocks) // 2], blocks[len(blocks) // 2 :]
    width = unit_ref.shape[1]
    row_top = functools.reduce(jnp.maximum, [ref[:, width + 128 :] for ref in attracts])
    attract_sum = repel_sum = 0.0
    row_sum = column_sum = 0.0
    for ref in attracts:
        fade = jnp.exp2((ref[:, width + 128 :] - row_top) * student_rate)
        row_sum = row_sum + ref[:, width : width + 128] * fade
        attract_sum = attract_sum + ref[:, :width] * jnp.tile(fade, (1, width // 128))
    for ref in repels:
        column_sum = column_sum + ref[:, width:]
        repel_sum = repel_sum + ref[:, :width]
    emb_grad = (
        attract_sum / jnp.tile(row_sum, (1, width // 128))
        - repel_sum / jnp.tile(column_sum, (1, width // 128))
    ) / student_temp
    unit = unit_ref[...]
    along = jnp.sum(unit * emb_grad, axis=1, keepdims=True)
    out_ref[...] = (emb_grad - unit * along) / jnp.tile(lengths_ref[...], (1, width // 128))


def finish(unit, lengths, attracts, repels):
    return pl.pallas_call(
        finish_kernel,
        in_specs=[whole()] * (2 + len(attracts) + len(repels)),
        out_specs=whole(),
        out_shape=jax.ShapeDtypeStruct(unit.shape, jnp.float32),
        compiler_params=params(8),
        cost_estimate=cost(40 * unit.size, 40 * unit.size),
        name="finish",
    )(unit, lengths, *attracts, *repels)


def swap(values, axis, flip):
    return lax.ppermute(values, axis, [(i, i ^ flip) for i in range(lax.axis_size(axis))])


def bit_reversed(values, count):
    bits = count.bit_length() - 1
    split = values.reshape((2,) * bits + values.shape[1:])
    turned = jnp.transpose(split, tuple(reversed(range(bits))) + tuple(range(bits, split.ndim)))
    return turned.reshape(values.shape)


def gather_batch(values):
    step = lax.axis_size("batch") // 2
    stages = [values]
    while step:
        other = swap(values, "batch", step)
        upper = (lax.axis_index("batch") // step) % 2
        values = jnp.where(
            upper == 0, jnp.concatenate([values, other]), jnp.concatenate([other, values])
        )
        stages.append(values)
        step //= 2
    return stages


def send_blocks(blocks):
    return [blocks[0]] + [swap(block, "proto", flip) for flip, block in enumerate(blocks) if flip]


def all_to_all(copies, axes):
    return lax.all_to_all(copies, axes, 0, 0, tiled=True)


def body(crops, teacher_emb, w_first, b_first, w_second, b_second, w_third, b_third, protos):
    batch_index = lax.axis_index("batch")
    proto_index = lax.axis_index("proto")
    batch_size = lax.axis_size("batch")
    proto_size = lax.axis_size("proto")
    devices = batch_size * proto_size
    share_rows = crops.shape[0]
    group_rows = teacher_emb.shape[0]
    crops_total = group_rows * batch_size
    protos_total = protos.shape[0] * proto_size
    count, width = protos.shape
    thin = count // batch_size
    core = proto_index % 2
    proto_ref = proto_index.reshape(1)
    thin_ref = jnp.stack([batch_index, core])
    wide_ref = jnp.stack([batch_index, proto_index])

    own_unit, half = teacher_units(core.reshape(1), teacher_emb)
    stages = gather_batch(half)
    mine = stages[-1]
    other = swap(mine, "proto", 1)
    top = jnp.full((256, 128), -jnp.inf, jnp.float32)
    top = wide_tops(own_unit, protos, top, stages[1], 0, 0, count // 2, 4)
    top_copies = wide_tops(own_unit, protos, top, stages[2], devices, count // 2, count // 2, 4)
    all_tops = all_to_all(top_copies, BOTH)
    tops = jnp.max(all_tops.reshape(batch_size, proto_size, 256)[:, :, :group_rows], axis=1)
    tops = bit_reversed(tops, batch_size).reshape(batch_size, 2, group_rows // 2)
    base = jnp.transpose(tops, (1, 0, 2)).reshape(1, crops_total) * -teacher_rate

    rows = [crops, swap(crops, "proto", 2), swap(crops, "proto", 1), swap(crops, "proto", 3)]
    keep, give = student_front(proto_ref, b_first, rows, w_first, w_second)
    core_rows = swap(give, "proto", 1)
    x_sent = keep[share_rows:] + core_rows[share_rows:]
    x_rows = swap(x_sent, "proto", 2)
    thirds = [w_third, swap(w_third, "proto", 2), swap(w_third, "proto", 1), swap(w_third, "proto", 3)]
    unit, rounded, lengths = student_middle(
        proto_ref, keep, core_rows, x_rows, b_second, thirds, b_third
    )
    emb_pair = jnp.concatenate([rounded, swap(rounded, "proto", 2)])
    student_emb = jnp.concatenate([emb_pair, swap(emb_pair, "proto", 1)])
    empty = jnp.concatenate(
        [jnp.zeros((group_rows, width + 128), jnp.float32), jnp.full((group_rows, 128), -1e30, jnp.float32)], axis=1
    )
    (state,) = attract(student_emb, empty, protos, 0, count // 2, 4, 1)
    slots = attract(student_emb, state, protos, count // 2, count // 2, 4, proto_size)
    attract_parts = send_blocks([slots[0], slots[2], slots[1], slots[3]])

    copies, weights = first_sweep(thin_ref, protos, mine, other, base, x_sent, devices, thin, protos_total)
    for _ in range(ITERS - 2):
        copies = next_sweep(weights, all_to_all(copies, BOTH), rounded, protos_total)
    scale_copies = last_scales(weights, all_to_all(copies, BOTH), state, batch_size, protos_total)
    all_scale = all_to_all(scale_copies, "batch")
    repels = repel(wide_ref, own_unit, all_tops, all_scale, protos, slots[0], proto_size)
    return finish(unit, lengths, attract_parts, send_blocks(repels))


def solution(mesh):
    in_specs = (
        P(("batch", "proto"), None),
        P("batch", None),
        P(None, "proto"),
        P(),
        P("proto", None),
        P(),
        P("proto", None),
        P(),
        P("proto", None),
    )
    out_specs = P(("batch", "proto"), None)
    return jax.shard_map(body, mesh=mesh, in_specs=in_specs, out_specs=out_specs, check_vma=False)
```

```python
import functools
import math

import jax
import jax.numpy as jnp
from jax import lax
from jax.experimental import pallas as pl
from jax.experimental.pallas import tpu as pltpu
from jax.sharding import PartitionSpec as P

ITERS = 3

student_temp = 0.1
teacher_temp = 0.07
norm_eps = 1e-06
teacher_rate = math.log2(math.e) / teacher_temp
student_rate = math.log2(math.e) / student_temp

MIB = 1024 * 1024
BOTH = ("batch", "proto")
TILE = 256
WIDE = 512


def scores(left_rows, right_rows):
    return lax.dot_general(
        left_rows, right_rows, (((1,), (1,)), ((), ())), preferred_element_type=jnp.float32
    )


def unit_rows(values):
    lengths = jnp.sqrt(jnp.sum(values * values, axis=1, keepdims=True) + norm_eps)
    return (values / lengths, lengths)


def gelu(values):
    return 0.5 * values * (1.0 + lax.erf(values * math.sqrt(0.5)))


def whole(memory_space=pltpu.VMEM):
    return pl.BlockSpec(memory_space=memory_space)


def in_hbm(array):
    return pltpu.with_memory_space_constraint(array, pltpu.HBM)


def skipping(kernel, first, count):
    def trimmed(*refs):
        kernel(*refs[:first], *refs[first + count :])

    return trimmed


def part(index, size):
    return pl.ds(pl.multiple_of(index * size, size), size)


def lane_fold(values, combine):
    folded = values[:, :128]
    for start in range(128, values.shape[1], 128):
        folded = combine(folded, values[:, start : start + 128])
    return folded


def params(mib):
    return pltpu.CompilerParams(vmem_limit_bytes=mib * MIB)


def cost(flops, bytes_accessed, transcendentals=0):
    return pl.CostEstimate(
        flops=int(flops), bytes_accessed=int(bytes_accessed), transcendentals=int(transcendentals)
    )


def fetch(source, target, sems, first_row=0):
    count, rows = target.shape[:2]

    def chunk_copy(index):
        start = pl.multiple_of(first_row + index * rows, rows)
        return pltpu.make_async_copy(source.at[pl.ds(start, rows), :], target.at[index], sems.at[index])

    for index in range(count):
        chunk_copy(index).start()
    return lambda index: chunk_copy(index).wait()


def teacher_units_kernel(core_ref, emb_ref, unit_ref, half_ref):
    unit_ref[...] = unit_rows(emb_ref[...].astype(jnp.float32))[0].astype(jnp.bfloat16)
    half = half_ref.shape[0]
    half_ref[...] = unit_ref[part(core_ref[0], half), :]


def teacher_units(core, teacher_emb):
    rows, width = teacher_emb.shape
    return pl.pallas_call(
        teacher_units_kernel,
        in_specs=[whole(pltpu.SMEM), whole()],
        out_specs=[whole(), whole()],
        out_shape=[
            jax.ShapeDtypeStruct((rows, width), jnp.bfloat16),
            jax.ShapeDtypeStruct((rows // 2, width), jnp.bfloat16),
        ],
        compiler_params=params(4),
        cost_estimate=cost(4 * rows * width, 8 * rows * width),
        name="teacher_units",
    )(core, in_hbm(teacher_emb))


def wide_tops_kernel(first_row, last, unit_ref, protos_hbm, before_ref, out_ref, protos_ref, sems, top_ref):
    rows = unit_ref.shape[0]
    steps, block = protos_ref.shape[:2]
    wide = min(WIDE, block)
    arrived = fetch(protos_hbm, protos_ref, sems, first_row)
    top_ref[...] = before_ref[...]

    def step(index, carry):
        arrived(index)
        top = top_ref[:rows, :]
        for start in range(0, block, wide):
            products = scores(unit_ref[...], protos_ref[index, start : start + wide, :])
            top = jnp.maximum(top, lane_fold(products, jnp.maximum))
        top_ref[:rows, :] = top
        return carry

    lax.fori_loop(0, steps, step, 0)
    if last:
        tops = jnp.max(jnp.transpose(top_ref[...]), axis=0, keepdims=True)
        out_ref[...] = jnp.broadcast_to(tops[None], out_ref.shape)
    else:
        out_ref[...] = top_ref[...]


def wide_tops(unit, protos, before, order, copies, first_row, count, steps):
    rows, width = unit.shape
    shape = (copies, 1, 256) if copies else before.shape
    return pl.pallas_call(
        skipping(functools.partial(wide_tops_kernel, first_row, copies > 0), 3, len(order)),
        in_specs=[whole(), whole(pl.ANY), whole()] + [whole(pl.ANY)] * len(order),
        out_specs=whole(),
        out_shape=jax.ShapeDtypeStruct(shape, jnp.float32),
        scratch_shapes=[
            pltpu.VMEM((steps, count // steps, width), jnp.bfloat16),
            pltpu.SemaphoreType.DMA((steps,)),
            pltpu.VMEM((256, 128), jnp.float32),
        ],
        compiler_params=params(16),
        cost_estimate=cost(2 * rows * width * count, 2 * width * count),
        name="wide_tops",
    )(unit, in_hbm(protos), before, *order)


def repel_kernel(group, index_ref, unit_ref, tops_ref, scale_ref, protos_hbm, *rest):
    out_refs, (protos_ref, sems, acc_ref, sum_ref, bias_ref) = rest[:-5], rest[-5:]
    rows, width = unit_ref.shape
    steps, block = protos_ref.shape[:2]
    wide = min(WIDE, block)
    arrived = fetch(protos_hbm, protos_ref, sems)
    first = index_ref[0] * group
    top = tops_ref[first]
    for other in range(1, group):
        top = jnp.maximum(top, tops_ref[first + other])
    bias_ref[...] = jnp.transpose(jnp.broadcast_to(top, (128, 256)))[:rows, :] * -teacher_rate
    acc_ref[...] = jnp.zeros(acc_ref.shape, jnp.float32)
    sum_ref[...] = jnp.zeros(sum_ref.shape, jnp.float32)

    def step(index, carry):
        arrived(index)
        bias = bias_ref[...]
        total = sum_ref[...]
        acc = acc_ref[...]
        for start in range(0, block, wide):
            protos = protos_ref[index, start : start + wide, :]
            products = scores(unit_ref[...], protos)
            pieces = []
            for lane in range(0, wide, 128):
                scaled = jnp.exp2(products[:, lane : lane + 128] * teacher_rate + bias)
                scaled = scaled * scale_ref[index, :, start + lane : start + lane + 128]
                total = total + scaled
                pieces.append(scaled.astype(jnp.bfloat16))
            acc = acc + jnp.dot(
                jnp.concatenate(pieces, axis=1), protos, preferred_element_type=jnp.float32
            )
        sum_ref[...] = total
        acc_ref[...] = acc
        return carry

    lax.fori_loop(0, steps, step, 0)
    total = jnp.sum(sum_ref[...], axis=1, keepdims=True)
    sum_ref[...] = jnp.broadcast_to(total, sum_ref.shape)
    share = out_refs[0].shape[0]
    for flip, out_ref in enumerate(out_refs):
        span = part(index_ref[1] ^ flip, share)
        out_ref[:, :width] = acc_ref[span, :]
        out_ref[:, width:] = sum_ref[span, :]


def repel(index, unit, tops, scale, protos, order, proto_size):
    rows, width = unit.shape
    count = protos.shape[0]
    steps, _, block = scale.shape
    return pl.pallas_call(
        skipping(functools.partial(repel_kernel, proto_size), 5, len(order)),
        in_specs=[whole(pltpu.SMEM), whole(), whole(), whole(), whole(pl.ANY)] + [whole(pl.ANY)] * len(order),
        out_specs=[whole()] * proto_size,
        out_shape=[jax.ShapeDtypeStruct((rows // proto_size, width + 128), jnp.float32)] * proto_size,
        scratch_shapes=[
            pltpu.VMEM((steps, block, width), jnp.bfloat16),
            pltpu.SemaphoreType.DMA((steps,)),
            pltpu.VMEM((rows, width), jnp.float32),
            pltpu.VMEM((rows, 128), jnp.float32),
            pltpu.VMEM((rows, 128), jnp.float32),
        ],
        compiler_params=params(16),
        cost_estimate=cost(4 * rows * width * count, 2 * width * count, rows * count),
        name="repel",
    )(index, unit, tops, scale, in_hbm(protos), *order)


def attract_kernel(first_row, last, emb_ref, state_ref, protos_hbm, *rest):
    out_refs, scratch = rest[:-6], rest[-6:]
    protos_ref, sems, products_ref, acc_ref, sum_ref, top_ref = scratch
    width = emb_ref.shape[1]
    steps, block = protos_ref.shape[:2]
    arrived = fetch(protos_hbm, protos_ref, sems, first_row)
    old_top = state_ref[:, width + 128 :]
    top_ref[...] = old_top

    def first(index, carry):
        arrived(index)
        top = top_ref[...]
        for start in range(0, block, TILE):
            products = scores(emb_ref[...], protos_ref[index, start : start + TILE, :])
            products_ref[index, :, start : start + TILE] = products
            top = jnp.maximum(top, lane_fold(products, jnp.maximum))
        top_ref[...] = top
        return carry

    lax.fori_loop(0, steps, first, 0)
    top = jnp.broadcast_to(jnp.max(top_ref[...], axis=1, keepdims=True), top_ref.shape)
    fade = jnp.exp2((old_top - top) * student_rate)
    top_ref[...] = top
    sum_ref[...] = state_ref[:, width : width + 128] * fade
    acc_ref[...] = state_ref[:, :width] * jnp.tile(fade, (1, width // 128))

    def second(index, carry):
        top = top_ref[...]
        total = sum_ref[...]
        acc = acc_ref[...]
        for start in range(0, block, TILE):
            pieces = []
            for lane in range(start, start + TILE, 128):
                shifted = jnp.exp2((products_ref[index, :, lane : lane + 128] - top) * student_rate)
                total = total + shifted
                pieces.append(shifted.astype(jnp.bfloat16))
            acc = acc + jnp.dot(
                jnp.concatenate(pieces, axis=1),
                protos_ref[index, start : start + TILE, :],
                preferred_element_type=jnp.float32,
            )
        sum_ref[...] = total
        acc_ref[...] = acc
        return carry

    lax.fori_loop(0, steps, second, 0)
    if last:
        total = jnp.sum(sum_ref[...], axis=1, keepdims=True)
        sum_ref[...] = jnp.broadcast_to(total, sum_ref.shape)
    share = out_refs[0].shape[0]
    for slot, out_ref in enumerate(out_refs):
        rows = pl.ds(slot * share, share)
        out_ref[:, :width] = acc_ref[rows, :]
        out_ref[:, width : width + 128] = sum_ref[rows, :]
        out_ref[:, width + 128 :] = top_ref[rows, :]


def attract(emb, state, protos, first_row, count, steps, outputs):
    rows, width = emb.shape
    block = count // steps
    return pl.pallas_call(
        functools.partial(attract_kernel, first_row, outputs > 1),
        in_specs=[whole(), whole(), whole(pl.ANY)],
        out_specs=[whole()] * outputs,
        out_shape=[jax.ShapeDtypeStruct((rows // outputs, width + 256), jnp.float32)] * outputs,
        scratch_shapes=[
            pltpu.VMEM((steps, block, width), jnp.bfloat16),
            pltpu.SemaphoreType.DMA((steps,)),
            pltpu.VMEM((steps, rows, block), jnp.float32),
            pltpu.VMEM((rows, width), jnp.float32),
            pltpu.VMEM((rows, 128), jnp.float32),
            pltpu.VMEM((rows, 128), jnp.float32),
        ],
        compiler_params=params(24),
        cost_estimate=cost(4 * rows * width * count, 2 * width * count, rows * count),
        name="attract",
    )(emb, state, in_hbm(protos))


def three_pieces(values):
    high = values.astype(jnp.bfloat16)
    rest = values - high.astype(jnp.float32)
    middle = rest.astype(jnp.bfloat16)
    low = (rest - middle.astype(jnp.float32)).astype(jnp.bfloat16)
    return jnp.concatenate([high, middle, low, jnp.zeros((13, values.shape[1]), jnp.bfloat16)], axis=0)


def lane_scales(folded, protos_total):
    sums = [
        jnp.sum(jnp.transpose(folded[start : start + 128, :]), axis=0, keepdims=True)
        for start in range(0, folded.shape[0], 128)
    ]
    return 1.0 / (protos_total * jnp.concatenate(sums, axis=1))


def give_copies(copies_ref, totals):
    copies_ref[...] = jnp.broadcast_to(totals[None], copies_ref.shape)


def first_sweep_kernel(
    chunk, protos_total, index_ref, protos_hbm, mine_hbm, other_hbm, bias_ref, copies_ref, weights_hbm, protos_ref, units_ref, weights_ref, rounded_ref, scale_ref, sems, out_sems,
):
    thin, crops_total = weights_ref.shape
    half = mine_hbm.shape[0]
    core = index_ref[1]
    copies = (
        pltpu.make_async_copy(protos_hbm.at[part(index_ref[0], thin), :], protos_ref, sems.at[0]),
        pltpu.make_async_copy(mine_hbm, units_ref.at[part(core, half), :], sems.at[1]),
        pltpu.make_async_copy(other_hbm, units_ref.at[part(1 - core, half), :], sems.at[2]),
    )
    for copy in copies:
        copy.start()
    for copy in copies:
        copy.wait()

    def chunk_out(index):
        return pltpu.make_async_copy(
            rounded_ref.at[index], weights_hbm.at[part(index, chunk), :], out_sems.at[index]
        )

    def weigh(index, carry):
        rows = part(index, chunk)
        protos = protos_ref[rows, :]
        folded = jnp.zeros((chunk, 128), jnp.float32)
        for start in range(0, crops_total, TILE):
            columns = slice(start, start + TILE)
            products = scores(protos, units_ref[columns, :])
            weights = jnp.exp2(products * teacher_rate + bias_ref[:, columns])
            weights_ref[rows, columns] = weights
            rounded_ref[index, :, columns] = weights.astype(jnp.bfloat16)
            folded = folded + lane_fold(weights, jnp.add)
        sums = jnp.sum(folded, axis=1, keepdims=True)
        scale_ref[rows, :] = jnp.broadcast_to(1.0 / (protos_total * sums), (chunk, 128))
        chunk_out(index).start()
        return carry

    lax.fori_loop(0, thin // chunk, weigh, 0)
    small = min(thin, 64)

    def add_up(index, totals):
        rows = part(index, small)
        scaled = weights_ref[rows, :] * jnp.tile(scale_ref[rows, :], (1, crops_total // 128))
        return totals + jnp.sum(scaled.reshape(-1, 8, crops_total), axis=0)

    totals = lax.fori_loop(0, thin // small, add_up, jnp.zeros((8, crops_total), jnp.float32))
    give_copies(copies_ref, jnp.sum(totals, axis=0, keepdims=True))
    for index in range(thin // chunk):
        chunk_out(index).wait()


def first_sweep(index, protos, mine, other, base, order, copies, thin, protos_total):
    width = protos.shape[1]
    crops_total = 2 * mine.shape[0]
    chunk = min(thin, 1024)
    return pl.pallas_call(
        skipping(functools.partial(first_sweep_kernel, chunk, protos_total), 5, len(order)),
        in_specs=[whole(pltpu.SMEM), whole(pl.ANY), whole(pl.ANY), whole(pl.ANY), whole()]
        + [whole(pl.ANY)] * len(order),
        out_specs=[whole(), whole(pl.ANY)],
        out_shape=[
            jax.ShapeDtypeStruct((copies, 1, crops_total), jnp.float32),
            pltpu.HBM((thin, crops_total), jnp.bfloat16),
        ],
        scratch_shapes=[
            pltpu.VMEM((thin, width), jnp.bfloat16),
            pltpu.VMEM((crops_total, width), jnp.bfloat16),
            pltpu.VMEM((thin, crops_total), jnp.float32),
            pltpu.VMEM((thin // chunk, chunk, crops_total), jnp.bfloat16),
            pltpu.VMEM((thin, 128), jnp.float32),
            pltpu.SemaphoreType.DMA((3,)),
            pltpu.SemaphoreType.DMA((thin // chunk,)),
        ],
        compiler_params=params(32 if crops_total <= 2048 else 56),
        cost_estimate=cost(2 * thin * width * crops_total, 2 * thin * crops_total, thin * crops_total),
        name="first_sweep",
    )(index, in_hbm(protos), mine, other, base, *order)


def fetch_rows(weights_hbm, weights_ref, sems):
    steps, chunk, _ = weights_ref.shape

    def rows_copy(index):
        return pltpu.make_async_copy(
            weights_hbm.at[part(index, chunk), :], weights_ref.at[index], sems.at[index]
        )

    for index in range(steps):
        rows_copy(index).start()
    return lambda index: rows_copy(index).wait()


def scaled_fold(weights_ref, index, scale_ref):
    _, chunk, crops_total = weights_ref.shape
    folds = []
    for row in range(0, chunk, 64):
        fold = None
        for start in range(0, crops_total, TILE):
            columns = slice(start, start + TILE)
            weights = weights_ref[index, row : row + 64, columns].astype(jnp.float32)
            scaled = lane_fold(weights * scale_ref[:, columns], jnp.add)
            fold = scaled if fold is None else fold + scaled
        folds.append(fold)
    return jnp.concatenate(folds, axis=0)


def next_sweep_kernel(
    protos_total, weights_hbm, parts_ref, copies_ref, weights_ref, scale_ref, pieces_ref, totals_ref, sems,
):
    steps, chunk, crops_total = weights_ref.shape
    arrived = fetch_rows(weights_hbm, weights_ref, sems)
    scale_ref[...] = 1.0 / (crops_total * jnp.sum(parts_ref[...], axis=0))
    totals_ref[...] = jnp.zeros(totals_ref.shape, jnp.float32)

    def weigh(index):
        return three_pieces(lane_scales(scaled_fold(weights_ref, index, scale_ref), protos_total))

    def add_up(index):
        return jnp.dot(pieces_ref[...], weights_ref[index], preferred_element_type=jnp.float32)

    arrived(0)
    pieces_ref[...] = weigh(0)

    def sweep(index, carry):
        arrived(index)
        sums = add_up(index - 1)
        pieces = weigh(index)
        totals_ref[...] += sums
        pieces_ref[...] = pieces
        return carry

    lax.fori_loop(1, steps, sweep, 0)
    totals = totals_ref[...] + add_up(steps - 1)
    give_copies(copies_ref, jnp.sum(totals, axis=0, keepdims=True))


def next_sweep(weights, parts, order, protos_total):
    thin, crops_total = weights.shape
    copies = parts.shape[0]
    chunk = min(thin, 256)
    return pl.pallas_call(
        skipping(functools.partial(next_sweep_kernel, protos_total), 2, len(order)),
        in_specs=[whole(pl.ANY), whole()] + [whole(pl.ANY)] * len(order),
        out_specs=whole(),
        out_shape=jax.ShapeDtypeStruct((copies, 1, crops_total), jnp.float32),
        scratch_shapes=[
            pltpu.VMEM((thin // chunk, chunk, crops_total), jnp.bfloat16),
            pltpu.VMEM((1, crops_total), jnp.float32),
            pltpu.VMEM((16, chunk), jnp.bfloat16),
            pltpu.VMEM((16, crops_total), jnp.float32),
            pltpu.SemaphoreType.DMA((thin // chunk,)),
        ],
        compiler_params=params(16 if crops_total <= 2048 else 50),
        cost_estimate=cost(8 * thin * crops_total, 2 * thin * crops_total),
        name="next_sweep",
    )(in_hbm(weights), parts, *order)


def last_scales_kernel(
    protos_total, weights_hbm, parts_ref, copies_ref, weights_ref, scale_ref, out_ref, sems,
):
    steps, chunk, crops_total = weights_ref.shape
    arrived = fetch_rows(weights_hbm, weights_ref, sems)
    scale_ref[...] = 1.0 / (crops_total * jnp.sum(parts_ref[...], axis=0))

    def weigh(index, carry):
        arrived(index)
        out_ref[:, part(index, chunk)] = lane_scales(
            scaled_fold(weights_ref, index, scale_ref), protos_total
        )
        return carry

    lax.fori_loop(0, steps, weigh, 0)
    give_copies(copies_ref, out_ref[...])


def last_scales(weights, parts, order, copies, protos_total):
    thin, crops_total = weights.shape
    chunk = min(thin, 256)
    return pl.pallas_call(
        skipping(functools.partial(last_scales_kernel, protos_total), 2, len(order)),
        in_specs=[whole(pl.ANY), whole()] + [whole(pl.ANY)] * len(order),
        out_specs=whole(),
        out_shape=jax.ShapeDtypeStruct((copies, 1, thin), jnp.float32),
        scratch_shapes=[
            pltpu.VMEM((thin // chunk, chunk, crops_total), jnp.bfloat16),
            pltpu.VMEM((1, crops_total), jnp.float32),
            pltpu.VMEM((1, thin), jnp.float32),
            pltpu.SemaphoreType.DMA((thin // chunk,)),
        ],
        compiler_params=params(16 if crops_total <= 2048 else 50),
        cost_estimate=cost(4 * thin * crops_total, 2 * thin * crops_total),
        name="last_scales",
    )(in_hbm(weights), parts, *order)


def student_front_kernel(
    index_ref, bias_ref, own_hbm, x_hbm, core_hbm, last_hbm, first_hbm, second_hbm, keep_ref, give_ref,
    first_ref, second_ref, rows_ref, sems,
):
    share = own_hbm.shape[0]
    copies = [
        pltpu.make_async_copy(source, rows_ref.at[slot * share : (slot + 1) * share, :], sems.at[slot])
        for slot, source in enumerate((own_hbm, x_hbm, core_hbm, last_hbm))
    ]
    copies.append(pltpu.make_async_copy(first_hbm, first_ref, sems.at[4]))
    second_copy = pltpu.make_async_copy(second_hbm, second_ref, sems.at[5])
    for copy in copies:
        copy.start()
    second_copy.start()
    hidden = first_ref.shape[1]
    bias = bias_ref[:, part(index_ref[0], hidden)]
    for copy in copies:
        copy.wait()
    h_first = gelu(
        jnp.dot(rows_ref[...], first_ref[...], preferred_element_type=jnp.float32) + bias
    ).astype(jnp.bfloat16)
    second_copy.wait()
    for start in range(0, second_ref.shape[1], 512):
        columns = slice(start, start + 512)
        product = jnp.dot(h_first, second_ref[:, columns], preferred_element_type=jnp.float32)
        keep_ref[:, columns] = product[: 2 * share]
        give_ref[:, columns] = product[2 * share :]


def student_front(index, bias, rows, first, second, order):
    share, features = rows[0].shape
    hidden, units = second.shape
    return pl.pallas_call(
        skipping(student_front_kernel, 8, len(order)),
        in_specs=[whole(pltpu.SMEM), whole()] + [whole(pl.ANY)] * (6 + len(order)),
        out_specs=[whole(), whole()],
        out_shape=[jax.ShapeDtypeStruct((2 * share, units), jnp.float32)] * 2,
        scratch_shapes=[
            pltpu.VMEM(first.shape, jnp.bfloat16),
            pltpu.VMEM(second.shape, jnp.bfloat16),
            pltpu.VMEM((4 * share, features), jnp.bfloat16),
            pltpu.SemaphoreType.DMA((6,)),
        ],
        compiler_params=params(16),
        cost_estimate=cost(8 * share * hidden * (features + units), 2 * hidden * (features + units)),
        name="student_front",
    )(index, in_hbm(bias.reshape(1, -1)), in_hbm(rows[0]), *rows[1:], in_hbm(first), in_hbm(second), *order)


def student_middle_kernel(
    index_ref, keep_ref, core_ref, x_ref, bias_ref, own_ref, partner_ref, other_ref, last_ref, last_bias_ref,
    unit_ref, emb_ref, lengths_ref, hidden_ref,
):
    share = x_ref.shape[0]
    block = own_ref.shape[0]
    sums = keep_ref[:share, :] + core_ref[:share, :] + x_ref[...]
    hidden_ref[...] = gelu(sums + bias_ref[...]).astype(jnp.bfloat16)
    index = index_ref[0]
    weights = ((0, own_ref[...]), (2, partner_ref[...]), (1, other_ref[...]), (3, last_ref[...]))
    bottleneck = jnp.broadcast_to(last_bias_ref[...], unit_ref.shape)
    for flip, weight in weights:
        bottleneck = bottleneck + jnp.dot(
            hidden_ref[:, part(index ^ flip, block)], weight, preferred_element_type=jnp.float32
        )
    unit, lengths = unit_rows(bottleneck)
    unit_ref[...] = unit
    emb_ref[...] = unit.astype(jnp.bfloat16)
    lengths_ref[...] = jnp.broadcast_to(lengths, lengths_ref.shape)


def student_middle(index, keep, core_rows, x_rows, bias, weights, last_bias):
    share, units = x_rows.shape
    width = weights[0].shape[1]
    return pl.pallas_call(
        student_middle_kernel,
        in_specs=[whole(pltpu.SMEM)] + [whole()] * 9,
        out_specs=[whole()] * 3,
        out_shape=[
            jax.ShapeDtypeStruct((share, width), jnp.float32),
            jax.ShapeDtypeStruct((share, width), jnp.bfloat16),
            jax.ShapeDtypeStruct((share, 128), jnp.float32),
        ],
        scratch_shapes=[pltpu.VMEM((share, units), jnp.bfloat16)],
        compiler_params=params(12),
        cost_estimate=cost(2 * share * units * width, 2 * units * width + 16 * share * units),
        name="student_middle",
    )(index, keep, core_rows, x_rows, in_hbm(bias.reshape(1, -1)), in_hbm(weights[0]), *weights[1:], in_hbm(last_bias.reshape(1, -1)))


def finish_kernel(unit_ref, lengths_ref, *rest):
    out_ref, blocks = rest[-1], rest[:-1]
    attracts, repels = blocks[: len(blocks) // 2], blocks[len(blocks) // 2 :]
    width = unit_ref.shape[1]
    row_top = functools.reduce(jnp.maximum, [ref[:, width + 128 :] for ref in attracts])
    attract_sum = repel_sum = 0.0
    row_sum = column_sum = 0.0
    for ref in attracts:
        fade = jnp.exp2((ref[:, width + 128 :] - row_top) * student_rate)
        row_sum = row_sum + ref[:, width : width + 128] * fade
        attract_sum = attract_sum + ref[:, :width] * jnp.tile(fade, (1, width // 128))
    for ref in repels:
        column_sum = column_sum + ref[:, width:]
        repel_sum = repel_sum + ref[:, :width]
    emb_grad = (
        attract_sum / jnp.tile(row_sum, (1, width // 128))
        - repel_sum / jnp.tile(column_sum, (1, width // 128))
    ) / student_temp
    unit = unit_ref[...]
    along = jnp.sum(unit * emb_grad, axis=1, keepdims=True)
    out_ref[...] = (emb_grad - unit * along) / jnp.tile(lengths_ref[...], (1, width // 128))


def finish(unit, lengths, attracts, repels):
    return pl.pallas_call(
        finish_kernel,
        in_specs=[whole()] * (2 + len(attracts) + len(repels)),
        out_specs=whole(),
        out_shape=jax.ShapeDtypeStruct(unit.shape, jnp.float32),
        compiler_params=params(8),
        cost_estimate=cost(40 * unit.size, 40 * unit.size),
        name="finish",
    )(unit, lengths, *attracts, *repels)


def swap(values, axis, flip):
    return lax.ppermute(values, axis, [(i, i ^ flip) for i in range(lax.axis_size(axis))])


def bit_reversed(values, count):
    bits = count.bit_length() - 1
    split = values.reshape((2,) * bits + values.shape[1:])
    turned = jnp.transpose(split, tuple(reversed(range(bits))) + tuple(range(bits, split.ndim)))
    return turned.reshape(values.shape)


def gather_batch(values):
    step = lax.axis_size("batch") // 2
    stages = [values]
    while step:
        other = swap(values, "batch", step)
        upper = (lax.axis_index("batch") // step) % 2
        values = jnp.where(
            upper == 0, jnp.concatenate([values, other]), jnp.concatenate([other, values])
        )
        stages.append(values)
        step //= 2
    return stages


def send_blocks(blocks):
    return [blocks[0]] + [swap(block, "proto", flip) for flip, block in enumerate(blocks) if flip]


def all_to_all(copies, axes):
    return lax.all_to_all(copies, axes, 0, 0, tiled=True)


def body(crops, teacher_emb, w_first, b_first, w_second, b_second, w_third, b_third, protos):
    batch_index = lax.axis_index("batch")
    proto_index = lax.axis_index("proto")
    batch_size = lax.axis_size("batch")
    proto_size = lax.axis_size("proto")
    devices = batch_size * proto_size
    share_rows = crops.shape[0]
    group_rows = teacher_emb.shape[0]
    crops_total = group_rows * batch_size
    protos_total = protos.shape[0] * proto_size
    count, width = protos.shape
    thin = count // batch_size
    core = proto_index % 2
    proto_ref = proto_index.reshape(1)
    thin_ref = jnp.stack([batch_index, core])
    wide_ref = jnp.stack([batch_index, proto_index])

    own_unit, half = teacher_units(core.reshape(1), teacher_emb)
    stages = gather_batch(half)
    mine = stages[-1]
    other = swap(mine, "proto", 1)
    top = jnp.full((256, 128), -jnp.inf, jnp.float32)
    top = wide_tops(own_unit, protos, top, (stages[1],), 0, 0, count // 2, 4)
    top_copies = wide_tops(own_unit, protos, top, (stages[2],), devices, count // 2, count // 2, 4)
    all_tops = all_to_all(top_copies, BOTH)
    tops = jnp.max(all_tops.reshape(batch_size, proto_size, 256)[:, :, :group_rows], axis=1)
    tops = bit_reversed(tops, batch_size).reshape(batch_size, 2, group_rows // 2)
    base = jnp.transpose(tops, (1, 0, 2)).reshape(1, crops_total) * -teacher_rate

    crops_x = swap(crops, "proto", 2)
    rows = [crops, crops_x, swap(crops, "proto", 1), swap(crops_x, "proto", 1)]
    third_x = swap(w_third, "proto", 2)
    thirds = [w_third, third_x, swap(w_third, "proto", 1), swap(third_x, "proto", 1)]
    keep, give = student_front(proto_ref, b_first, rows, w_first, w_second, (top,))
    core_rows = swap(give, "proto", 1)
    x_sent = keep[share_rows:] + core_rows[share_rows:]
    x_rows = swap(x_sent, "proto", 2)
    unit, rounded, lengths = student_middle(
        proto_ref, keep, core_rows, x_rows, b_second, thirds, b_third
    )
    emb_pair = jnp.concatenate([rounded, swap(rounded, "proto", 2)])
    student_emb = jnp.concatenate([emb_pair, swap(emb_pair, "proto", 1)])
    empty = jnp.concatenate(
        [jnp.zeros((group_rows, width + 128), jnp.float32), jnp.full((group_rows, 128), -1e30, jnp.float32)], axis=1
    )
    (state,) = attract(student_emb, empty, protos, 0, count // 2, 4, 1)
    slots = attract(student_emb, state, protos, count // 2, count // 2, 4, proto_size)
    attract_parts = send_blocks([slots[0], slots[2], slots[1], slots[3]])

    copies, weights = first_sweep(thin_ref, protos, mine, other, base, (x_sent, *thirds[2:]), devices, thin, protos_total)
    for _ in range(ITERS - 2):
        copies = next_sweep(weights, all_to_all(copies, BOTH), (rounded,), protos_total)
    scale_copies = last_scales(weights, all_to_all(copies, BOTH), (state,), batch_size, protos_total)
    all_scale = all_to_all(scale_copies, "batch")
    repels = repel(wide_ref, own_unit, all_tops, all_scale, protos, (slots[0],), proto_size)
    return finish(unit, lengths, attract_parts, send_blocks(repels))


def solution(mesh):
    in_specs = (
        P(("batch", "proto"), None),
        P("batch", None),
        P(None, "proto"),
        P(),
        P("proto", None),
        P(),
        P("proto", None),
        P(),
        P("proto", None),
    )
    out_specs = P(("batch", "proto"), None)
    return jax.shard_map(body, mesh=mesh, in_specs=in_specs, out_specs=out_specs, check_vma=False)
```

```python
import functools
import math

import jax
import jax.numpy as jnp
from jax import lax
from jax.experimental import pallas as pl
from jax.experimental.pallas import tpu as pltpu
from jax.sharding import PartitionSpec as P

ITERS = 3

student_temp = 0.1
teacher_temp = 0.07
norm_eps = 1e-06
teacher_rate = math.log2(math.e) / teacher_temp
student_rate = math.log2(math.e) / student_temp

MIB = 1024 * 1024
BOTH = ("batch", "proto")
TILE = 256
WIDE = 512


def scores(left_rows, right_rows):
    return lax.dot_general(
        left_rows, right_rows, (((1,), (1,)), ((), ())), preferred_element_type=jnp.float32
    )


def unit_rows(values):
    lengths = jnp.sqrt(jnp.sum(values * values, axis=1, keepdims=True) + norm_eps)
    return (values / lengths, lengths)


def gelu(values):
    return 0.5 * values * (1.0 + lax.erf(values * math.sqrt(0.5)))


def whole(memory_space=pltpu.VMEM):
    return pl.BlockSpec(memory_space=memory_space)


def in_hbm(array):
    return pltpu.with_memory_space_constraint(array, pltpu.HBM)


def skipping(kernel, first, count):
    def trimmed(*refs):
        kernel(*refs[:first], *refs[first + count :])

    return trimmed


def part(index, size):
    return pl.ds(pl.multiple_of(index * size, size), size)


def lane_fold(values, combine):
    folded = values[:, :128]
    for start in range(128, values.shape[1], 128):
        folded = combine(folded, values[:, start : start + 128])
    return folded


def params(mib):
    return pltpu.CompilerParams(vmem_limit_bytes=mib * MIB)


def cost(flops, bytes_accessed, transcendentals=0):
    return pl.CostEstimate(
        flops=int(flops), bytes_accessed=int(bytes_accessed), transcendentals=int(transcendentals)
    )


def fetch(source, target, sems, first_row=0):
    count, rows = target.shape[:2]

    def chunk_copy(index):
        start = pl.multiple_of(first_row + index * rows, rows)
        return pltpu.make_async_copy(source.at[pl.ds(start, rows), :], target.at[index], sems.at[index])

    for index in range(count):
        chunk_copy(index).start()
    return lambda index: chunk_copy(index).wait()


def teacher_units_kernel(core_ref, emb_ref, unit_ref, half_ref):
    unit_ref[...] = unit_rows(emb_ref[...].astype(jnp.float32))[0].astype(jnp.bfloat16)
    half = half_ref.shape[0]
    half_ref[...] = unit_ref[part(core_ref[0], half), :]


def teacher_units(core, teacher_emb):
    rows, width = teacher_emb.shape
    return pl.pallas_call(
        teacher_units_kernel,
        in_specs=[whole(pltpu.SMEM), whole()],
        out_specs=[whole(), whole()],
        out_shape=[
            jax.ShapeDtypeStruct((rows, width), jnp.bfloat16),
            jax.ShapeDtypeStruct((rows // 2, width), jnp.bfloat16),
        ],
        compiler_params=params(4),
        cost_estimate=cost(4 * rows * width, 8 * rows * width),
        name="teacher_units",
    )(core, in_hbm(teacher_emb))


def wide_tops_kernel(first_row, unit_ref, protos_hbm, before_ref, out_ref, protos_ref, sems, top_ref):
    rows = unit_ref.shape[0]
    steps, block = protos_ref.shape[:2]
    wide = min(WIDE, block)
    arrived = fetch(protos_hbm, protos_ref, sems, first_row)
    top_ref[...] = before_ref[...]

    def step(index, carry):
        arrived(index)
        top = top_ref[:rows, :]
        for start in range(0, block, wide):
            products = scores(unit_ref[...], protos_ref[index, start : start + wide, :])
            top = jnp.maximum(top, lane_fold(products, jnp.maximum))
        top_ref[:rows, :] = top
        return carry

    lax.fori_loop(0, steps, step, 0)
    out_ref[...] = top_ref[...]


def wide_tops(unit, protos, before, order, first_row, count, steps):
    rows, width = unit.shape
    return pl.pallas_call(
        skipping(functools.partial(wide_tops_kernel, first_row), 3, len(order)),
        in_specs=[whole(), whole(pl.ANY), whole()] + [whole(pl.ANY)] * len(order),
        out_specs=whole(),
        out_shape=jax.ShapeDtypeStruct(before.shape, jnp.float32),
        scratch_shapes=[
            pltpu.VMEM((steps, count // steps, width), jnp.bfloat16),
            pltpu.SemaphoreType.DMA((steps,)),
            pltpu.VMEM((256, 128), jnp.float32),
        ],
        compiler_params=params(16),
        cost_estimate=cost(2 * rows * width * count, 2 * width * count),
        name="wide_tops",
    )(unit, in_hbm(protos), before, *order)


def spread_tops_kernel(top_ref, out_ref):
    tops = jnp.max(jnp.transpose(top_ref[...]), axis=0, keepdims=True)
    out_ref[...] = jnp.broadcast_to(tops[None], out_ref.shape)


def spread_tops(top, order, copies):
    return pl.pallas_call(
        skipping(spread_tops_kernel, 1, len(order)),
        in_specs=[whole()] + [whole(pl.ANY)] * len(order),
        out_specs=whole(),
        out_shape=jax.ShapeDtypeStruct((copies, 1, 256), jnp.float32),
        compiler_params=params(4),
        cost_estimate=cost(top.size, 8 * top.size),
        name="spread_tops",
    )(top, *order)


def repel_kernel(group, index_ref, unit_ref, tops_ref, scale_ref, protos_hbm, *rest):
    out_refs, (protos_ref, sems, acc_ref, sum_ref, bias_ref) = rest[:-5], rest[-5:]
    rows, width = unit_ref.shape
    steps, block = protos_ref.shape[:2]
    wide = min(WIDE, block)
    arrived = fetch(protos_hbm, protos_ref, sems)
    first = index_ref[0] * group
    top = tops_ref[first]
    for other in range(1, group):
        top = jnp.maximum(top, tops_ref[first + other])
    bias_ref[...] = jnp.transpose(jnp.broadcast_to(top, (128, 256)))[:rows, :] * -teacher_rate
    acc_ref[...] = jnp.zeros(acc_ref.shape, jnp.float32)
    sum_ref[...] = jnp.zeros(sum_ref.shape, jnp.float32)

    def step(index, carry):
        arrived(index)
        bias = bias_ref[...]
        total = sum_ref[...]
        acc = acc_ref[...]
        for start in range(0, block, wide):
            protos = protos_ref[index, start : start + wide, :]
            products = scores(unit_ref[...], protos)
            pieces = []
            for lane in range(0, wide, 128):
                scaled = jnp.exp2(products[:, lane : lane + 128] * teacher_rate + bias)
                scaled = scaled * scale_ref[index, :, start + lane : start + lane + 128]
                total = total + scaled
                pieces.append(scaled.astype(jnp.bfloat16))
            acc = acc + jnp.dot(
                jnp.concatenate(pieces, axis=1), protos, preferred_element_type=jnp.float32
            )
        sum_ref[...] = total
        acc_ref[...] = acc
        return carry

    lax.fori_loop(0, steps, step, 0)
    total = jnp.sum(sum_ref[...], axis=1, keepdims=True)
    sum_ref[...] = jnp.broadcast_to(total, sum_ref.shape)
    share = out_refs[0].shape[0]
    for flip, out_ref in enumerate(out_refs):
        span = part(index_ref[1] ^ flip, share)
        out_ref[:, :width] = acc_ref[span, :]
        out_ref[:, width:] = sum_ref[span, :]


def repel(index, unit, tops, scale, protos, order, proto_size):
    rows, width = unit.shape
    count = protos.shape[0]
    steps, _, block = scale.shape
    return pl.pallas_call(
        skipping(functools.partial(repel_kernel, proto_size), 5, len(order)),
        in_specs=[whole(pltpu.SMEM), whole(), whole(), whole(), whole(pl.ANY)] + [whole(pl.ANY)] * len(order),
        out_specs=[whole()] * proto_size,
        out_shape=[jax.ShapeDtypeStruct((rows // proto_size, width + 128), jnp.float32)] * proto_size,
        scratch_shapes=[
            pltpu.VMEM((steps, block, width), jnp.bfloat16),
            pltpu.SemaphoreType.DMA((steps,)),
            pltpu.VMEM((rows, width), jnp.float32),
            pltpu.VMEM((rows, 128), jnp.float32),
            pltpu.VMEM((rows, 128), jnp.float32),
        ],
        compiler_params=params(16),
        cost_estimate=cost(4 * rows * width * count, 2 * width * count, rows * count),
        name="repel",
    )(index, unit, tops, scale, in_hbm(protos), *order)


def attract_kernel(first_row, last, emb_ref, state_ref, protos_hbm, *rest):
    out_refs, scratch = rest[:-6], rest[-6:]
    protos_ref, sems, products_ref, acc_ref, sum_ref, top_ref = scratch
    width = emb_ref.shape[1]
    steps, block = protos_ref.shape[:2]
    arrived = fetch(protos_hbm, protos_ref, sems, first_row)
    old_top = state_ref[:, width + 128 :]
    top_ref[...] = old_top

    def first(index, carry):
        arrived(index)
        top = top_ref[...]
        for start in range(0, block, TILE):
            products = scores(emb_ref[...], protos_ref[index, start : start + TILE, :])
            products_ref[index, :, start : start + TILE] = products
            top = jnp.maximum(top, lane_fold(products, jnp.maximum))
        top_ref[...] = top
        return carry

    lax.fori_loop(0, steps, first, 0)
    top = jnp.broadcast_to(jnp.max(top_ref[...], axis=1, keepdims=True), top_ref.shape)
    fade = jnp.exp2((old_top - top) * student_rate)
    top_ref[...] = top
    sum_ref[...] = state_ref[:, width : width + 128] * fade
    acc_ref[...] = state_ref[:, :width] * jnp.tile(fade, (1, width // 128))

    def second(index, carry):
        top = top_ref[...]
        total = sum_ref[...]
        acc = acc_ref[...]
        for start in range(0, block, TILE):
            pieces = []
            for lane in range(start, start + TILE, 128):
                shifted = jnp.exp2((products_ref[index, :, lane : lane + 128] - top) * student_rate)
                total = total + shifted
                pieces.append(shifted.astype(jnp.bfloat16))
            acc = acc + jnp.dot(
                jnp.concatenate(pieces, axis=1),
                protos_ref[index, start : start + TILE, :],
                preferred_element_type=jnp.float32,
            )
        sum_ref[...] = total
        acc_ref[...] = acc
        return carry

    lax.fori_loop(0, steps, second, 0)
    if last:
        total = jnp.sum(sum_ref[...], axis=1, keepdims=True)
        sum_ref[...] = jnp.broadcast_to(total, sum_ref.shape)
    share = out_refs[0].shape[0]
    for slot, out_ref in enumerate(out_refs):
        rows = pl.ds(slot * share, share)
        out_ref[:, :width] = acc_ref[rows, :]
        out_ref[:, width : width + 128] = sum_ref[rows, :]
        out_ref[:, width + 128 :] = top_ref[rows, :]


def attract(emb, state, protos, first_row, count, steps, outputs):
    rows, width = emb.shape
    block = count // steps
    return pl.pallas_call(
        functools.partial(attract_kernel, first_row, outputs > 1),
        in_specs=[whole(), whole(), whole(pl.ANY)],
        out_specs=[whole()] * outputs,
        out_shape=[jax.ShapeDtypeStruct((rows // outputs, width + 256), jnp.float32)] * outputs,
        scratch_shapes=[
            pltpu.VMEM((steps, block, width), jnp.bfloat16),
            pltpu.SemaphoreType.DMA((steps,)),
            pltpu.VMEM((steps, rows, block), jnp.float32),
            pltpu.VMEM((rows, width), jnp.float32),
            pltpu.VMEM((rows, 128), jnp.float32),
            pltpu.VMEM((rows, 128), jnp.float32),
        ],
        compiler_params=params(24),
        cost_estimate=cost(4 * rows * width * count, 2 * width * count, rows * count),
        name="attract",
    )(emb, state, in_hbm(protos))


def three_pieces(values):
    high = values.astype(jnp.bfloat16)
    rest = values - high.astype(jnp.float32)
    middle = rest.astype(jnp.bfloat16)
    low = (rest - middle.astype(jnp.float32)).astype(jnp.bfloat16)
    return jnp.concatenate([high, middle, low, jnp.zeros((13, values.shape[1]), jnp.bfloat16)], axis=0)


def lane_scales(folded, protos_total):
    sums = [
        jnp.sum(jnp.transpose(folded[start : start + 128, :]), axis=0, keepdims=True)
        for start in range(0, folded.shape[0], 128)
    ]
    return 1.0 / (protos_total * jnp.concatenate(sums, axis=1))


def give_sums(copies_ref, totals):
    rows = [totals[:, start : start + 128] for start in range(0, totals.shape[1], 128)]
    spare = copies_ref.shape[1] - len(rows)
    if spare:
        rows.append(jnp.zeros((spare, 128), jnp.float32))
    packed = jnp.concatenate(rows, axis=0).astype(jnp.bfloat16)
    copies_ref[...] = jnp.broadcast_to(packed[None], copies_ref.shape)


def take_scales(parts_ref, scale_ref):
    crops_total = scale_ref.shape[1]
    sums = jnp.sum(parts_ref[...].astype(jnp.float32), axis=0)
    for row in range(crops_total // 128):
        scale_ref[:, row * 128 : row * 128 + 128] = 1.0 / (crops_total * sums[row : row + 1, :])


def sums_shape(copies, crops_total):
    return (copies, -(-crops_total // 2048) * 16, 128)


def first_sweep_kernel(
    chunk, protos_total, index_ref, protos_hbm, mine_hbm, other_hbm, bias_ref, copies_ref, weights_hbm, protos_ref, units_ref, weights_ref, rounded_ref, scale_ref, sems, out_sems,
):
    thin, crops_total = weights_ref.shape
    half = mine_hbm.shape[0]
    core = index_ref[1]
    copies = (
        pltpu.make_async_copy(protos_hbm.at[part(index_ref[0], thin), :], protos_ref, sems.at[0]),
        pltpu.make_async_copy(mine_hbm, units_ref.at[part(core, half), :], sems.at[1]),
        pltpu.make_async_copy(other_hbm, units_ref.at[part(1 - core, half), :], sems.at[2]),
    )
    for copy in copies:
        copy.start()
    for copy in copies:
        copy.wait()

    def chunk_out(index):
        return pltpu.make_async_copy(
            rounded_ref.at[index], weights_hbm.at[part(index, chunk), :], out_sems.at[index]
        )

    def weigh(index, carry):
        rows = part(index, chunk)
        protos = protos_ref[rows, :]
        folded = jnp.zeros((chunk, 128), jnp.float32)
        for start in range(0, crops_total, TILE):
            columns = slice(start, start + TILE)
            products = scores(protos, units_ref[columns, :])
            weights = jnp.exp2(products * teacher_rate + bias_ref[:, columns])
            weights_ref[rows, columns] = weights
            rounded_ref[index, :, columns] = weights.astype(jnp.bfloat16)
            folded = folded + lane_fold(weights, jnp.add)
        sums = jnp.sum(folded, axis=1, keepdims=True)
        scale_ref[rows, :] = jnp.broadcast_to(1.0 / (protos_total * sums), (chunk, 128))
        chunk_out(index).start()
        return carry

    lax.fori_loop(0, thin // chunk, weigh, 0)
    small = min(thin, 64)

    def add_up(index, totals):
        rows = part(index, small)
        scaled = weights_ref[rows, :] * jnp.tile(scale_ref[rows, :], (1, crops_total // 128))
        return totals + jnp.sum(scaled.reshape(-1, 8, crops_total), axis=0)

    totals = lax.fori_loop(0, thin // small, add_up, jnp.zeros((8, crops_total), jnp.float32))
    give_sums(copies_ref, jnp.sum(totals, axis=0, keepdims=True))
    for index in range(thin // chunk):
        chunk_out(index).wait()


def first_sweep(index, protos, mine, other, base, order, copies, thin, protos_total):
    width = protos.shape[1]
    crops_total = 2 * mine.shape[0]
    chunk = min(thin, 1024)
    return pl.pallas_call(
        skipping(functools.partial(first_sweep_kernel, chunk, protos_total), 5, len(order)),
        in_specs=[whole(pltpu.SMEM), whole(pl.ANY), whole(pl.ANY), whole(pl.ANY), whole()]
        + [whole(pl.ANY)] * len(order),
        out_specs=[whole(), whole(pl.ANY)],
        out_shape=[
            jax.ShapeDtypeStruct(sums_shape(copies, crops_total), jnp.bfloat16),
            pltpu.HBM((thin, crops_total), jnp.bfloat16),
        ],
        scratch_shapes=[
            pltpu.VMEM((thin, width), jnp.bfloat16),
            pltpu.VMEM((crops_total, width), jnp.bfloat16),
            pltpu.VMEM((thin, crops_total), jnp.float32),
            pltpu.VMEM((thin // chunk, chunk, crops_total), jnp.bfloat16),
            pltpu.VMEM((thin, 128), jnp.float32),
            pltpu.SemaphoreType.DMA((3,)),
            pltpu.SemaphoreType.DMA((thin // chunk,)),
        ],
        compiler_params=params(32 if crops_total <= 2048 else 56),
        cost_estimate=cost(2 * thin * width * crops_total, 2 * thin * crops_total, thin * crops_total),
        name="first_sweep",
    )(index, in_hbm(protos), mine, other, base, *order)


def fetch_rows(weights_hbm, weights_ref, sems):
    steps, chunk, _ = weights_ref.shape

    def rows_copy(index):
        return pltpu.make_async_copy(
            weights_hbm.at[part(index, chunk), :], weights_ref.at[index], sems.at[index]
        )

    for index in range(steps):
        rows_copy(index).start()
    return lambda index: rows_copy(index).wait()


def scaled_fold(weights_ref, index, scale_ref):
    _, chunk, crops_total = weights_ref.shape
    folds = []
    for row in range(0, chunk, 64):
        fold = None
        for start in range(0, crops_total, TILE):
            columns = slice(start, start + TILE)
            weights = weights_ref[index, row : row + 64, columns].astype(jnp.float32)
            scaled = lane_fold(weights * scale_ref[:, columns], jnp.add)
            fold = scaled if fold is None else fold + scaled
        folds.append(fold)
    return jnp.concatenate(folds, axis=0)


def next_sweep_kernel(
    protos_total, weights_hbm, parts_ref, copies_ref, weights_ref, scale_ref, pieces_ref, totals_ref, sems,
):
    steps, chunk, crops_total = weights_ref.shape
    arrived = fetch_rows(weights_hbm, weights_ref, sems)
    take_scales(parts_ref, scale_ref)
    totals_ref[...] = jnp.zeros(totals_ref.shape, jnp.float32)

    def weigh(index):
        return three_pieces(lane_scales(scaled_fold(weights_ref, index, scale_ref), protos_total))

    def add_up(index):
        return jnp.dot(pieces_ref[...], weights_ref[index], preferred_element_type=jnp.float32)

    arrived(0)
    pieces_ref[...] = weigh(0)

    def sweep(index, carry):
        arrived(index)
        sums = add_up(index - 1)
        pieces = weigh(index)
        totals_ref[...] += sums
        pieces_ref[...] = pieces
        return carry

    lax.fori_loop(1, steps, sweep, 0)
    totals = totals_ref[...] + add_up(steps - 1)
    give_sums(copies_ref, jnp.sum(totals, axis=0, keepdims=True))


def next_sweep(weights, parts, order, protos_total):
    thin, crops_total = weights.shape
    copies = parts.shape[0]
    chunk = min(thin, 256)
    return pl.pallas_call(
        skipping(functools.partial(next_sweep_kernel, protos_total), 2, len(order)),
        in_specs=[whole(pl.ANY), whole()] + [whole(pl.ANY)] * len(order),
        out_specs=whole(),
        out_shape=jax.ShapeDtypeStruct(sums_shape(copies, crops_total), jnp.bfloat16),
        scratch_shapes=[
            pltpu.VMEM((thin // chunk, chunk, crops_total), jnp.bfloat16),
            pltpu.VMEM((1, crops_total), jnp.float32),
            pltpu.VMEM((16, chunk), jnp.bfloat16),
            pltpu.VMEM((16, crops_total), jnp.float32),
            pltpu.SemaphoreType.DMA((thin // chunk,)),
        ],
        compiler_params=params(16 if crops_total <= 2048 else 50),
        cost_estimate=cost(8 * thin * crops_total, 2 * thin * crops_total),
        name="next_sweep",
    )(in_hbm(weights), parts, *order)


def last_scales_kernel(
    protos_total, weights_hbm, parts_ref, copies_ref, weights_ref, scale_ref, out_ref, sems,
):
    steps, chunk, crops_total = weights_ref.shape
    arrived = fetch_rows(weights_hbm, weights_ref, sems)
    take_scales(parts_ref, scale_ref)

    def weigh(index, carry):
        arrived(index)
        out_ref[:, part(index, chunk)] = lane_scales(
            scaled_fold(weights_ref, index, scale_ref), protos_total
        )
        return carry

    lax.fori_loop(0, steps, weigh, 0)
    copies_ref[...] = jnp.broadcast_to(out_ref[...][None], copies_ref.shape)


def last_scales(weights, parts, order, copies, protos_total):
    thin, crops_total = weights.shape
    chunk = min(thin, 256)
    return pl.pallas_call(
        skipping(functools.partial(last_scales_kernel, protos_total), 2, len(order)),
        in_specs=[whole(pl.ANY), whole()] + [whole(pl.ANY)] * len(order),
        out_specs=whole(),
        out_shape=jax.ShapeDtypeStruct((copies, 1, thin), jnp.float32),
        scratch_shapes=[
            pltpu.VMEM((thin // chunk, chunk, crops_total), jnp.bfloat16),
            pltpu.VMEM((1, crops_total), jnp.float32),
            pltpu.VMEM((1, thin), jnp.float32),
            pltpu.SemaphoreType.DMA((thin // chunk,)),
        ],
        compiler_params=params(16 if crops_total <= 2048 else 50),
        cost_estimate=cost(4 * thin * crops_total, 2 * thin * crops_total),
        name="last_scales",
    )(in_hbm(weights), parts, *order)


def student_front_kernel(
    index_ref, bias_ref, own_hbm, x_hbm, core_hbm, last_hbm, first_hbm, second_hbm, keep_ref, give_ref,
    first_ref, second_ref, rows_ref, sems,
):
    share = own_hbm.shape[0]
    copies = [
        pltpu.make_async_copy(source, rows_ref.at[slot * share : (slot + 1) * share, :], sems.at[slot])
        for slot, source in enumerate((own_hbm, x_hbm, core_hbm, last_hbm))
    ]
    copies.append(pltpu.make_async_copy(first_hbm, first_ref, sems.at[4]))
    second_copy = pltpu.make_async_copy(second_hbm, second_ref, sems.at[5])
    for copy in copies:
        copy.start()
    second_copy.start()
    hidden = first_ref.shape[1]
    bias = bias_ref[:, part(index_ref[0], hidden)]
    for copy in copies:
        copy.wait()
    h_first = gelu(
        jnp.dot(rows_ref[...], first_ref[...], preferred_element_type=jnp.float32) + bias
    ).astype(jnp.bfloat16)
    second_copy.wait()
    for start in range(0, second_ref.shape[1], 512):
        columns = slice(start, start + 512)
        product = jnp.dot(h_first, second_ref[:, columns], preferred_element_type=jnp.float32)
        keep_ref[:, columns] = product[: 2 * share]
        give_ref[:, columns] = product[2 * share :]


def student_front(index, bias, rows, first, second, order):
    share, features = rows[0].shape
    hidden, units = second.shape
    return pl.pallas_call(
        skipping(student_front_kernel, 8, len(order)),
        in_specs=[whole(pltpu.SMEM), whole()] + [whole(pl.ANY)] * (6 + len(order)),
        out_specs=[whole(), whole()],
        out_shape=[jax.ShapeDtypeStruct((2 * share, units), jnp.float32)] * 2,
        scratch_shapes=[
            pltpu.VMEM(first.shape, jnp.bfloat16),
            pltpu.VMEM(second.shape, jnp.bfloat16),
            pltpu.VMEM((4 * share, features), jnp.bfloat16),
            pltpu.SemaphoreType.DMA((6,)),
        ],
        compiler_params=params(16),
        cost_estimate=cost(8 * share * hidden * (features + units), 2 * hidden * (features + units)),
        name="student_front",
    )(index, in_hbm(bias.reshape(1, -1)), in_hbm(rows[0]), *rows[1:], in_hbm(first), in_hbm(second), *order)


def student_middle_kernel(
    index_ref, keep_ref, core_ref, x_ref, bias_ref, own_ref, partner_ref, other_ref, last_ref, last_bias_ref,
    unit_ref, emb_ref, lengths_ref, hidden_ref,
):
    share = x_ref.shape[0]
    block = own_ref.shape[0]
    sums = keep_ref[:share, :] + core_ref[:share, :] + x_ref[...]
    hidden_ref[...] = gelu(sums + bias_ref[...]).astype(jnp.bfloat16)
    index = index_ref[0]
    weights = ((0, own_ref[...]), (2, partner_ref[...]), (1, other_ref[...]), (3, last_ref[...]))
    bottleneck = jnp.broadcast_to(last_bias_ref[...], unit_ref.shape)
    for flip, weight in weights:
        bottleneck = bottleneck + jnp.dot(
            hidden_ref[:, part(index ^ flip, block)], weight, preferred_element_type=jnp.float32
        )
    unit, lengths = unit_rows(bottleneck)
    unit_ref[...] = unit
    emb_ref[...] = unit.astype(jnp.bfloat16)
    lengths_ref[...] = jnp.broadcast_to(lengths, lengths_ref.shape)


def student_middle(index, keep, core_rows, x_rows, bias, weights, last_bias):
    share, units = x_rows.shape
    width = weights[0].shape[1]
    return pl.pallas_call(
        student_middle_kernel,
        in_specs=[whole(pltpu.SMEM)] + [whole()] * 9,
        out_specs=[whole()] * 3,
        out_shape=[
            jax.ShapeDtypeStruct((share, width), jnp.float32),
            jax.ShapeDtypeStruct((share, width), jnp.bfloat16),
            jax.ShapeDtypeStruct((share, 128), jnp.float32),
        ],
        scratch_shapes=[pltpu.VMEM((share, units), jnp.bfloat16)],
        compiler_params=params(12),
        cost_estimate=cost(2 * share * units * width, 2 * units * width + 16 * share * units),
        name="student_middle",
    )(index, keep, core_rows, x_rows, in_hbm(bias.reshape(1, -1)), in_hbm(weights[0]), *weights[1:], in_hbm(last_bias.reshape(1, -1)))


def finish_kernel(unit_ref, lengths_ref, *rest):
    out_ref, blocks = rest[-1], rest[:-1]
    attracts, repels = blocks[: len(blocks) // 2], blocks[len(blocks) // 2 :]
    width = unit_ref.shape[1]
    row_top = functools.reduce(jnp.maximum, [ref[:, width + 128 :] for ref in attracts])
    attract_sum = repel_sum = 0.0
    row_sum = column_sum = 0.0
    for ref in attracts:
        fade = jnp.exp2((ref[:, width + 128 :] - row_top) * student_rate)
        row_sum = row_sum + ref[:, width : width + 128] * fade
        attract_sum = attract_sum + ref[:, :width] * jnp.tile(fade, (1, width // 128))
    for ref in repels:
        column_sum = column_sum + ref[:, width:]
        repel_sum = repel_sum + ref[:, :width]
    emb_grad = (
        attract_sum / jnp.tile(row_sum, (1, width // 128))
        - repel_sum / jnp.tile(column_sum, (1, width // 128))
    ) / student_temp
    unit = unit_ref[...]
    along = jnp.sum(unit * emb_grad, axis=1, keepdims=True)
    out_ref[...] = (emb_grad - unit * along) / jnp.tile(lengths_ref[...], (1, width // 128))


def finish(unit, lengths, attracts, repels):
    return pl.pallas_call(
        finish_kernel,
        in_specs=[whole()] * (2 + len(attracts) + len(repels)),
        out_specs=whole(),
        out_shape=jax.ShapeDtypeStruct(unit.shape, jnp.float32),
        compiler_params=params(8),
        cost_estimate=cost(40 * unit.size, 40 * unit.size),
        name="finish",
    )(unit, lengths, *attracts, *repels)


def swap(values, axis, flip):
    return lax.ppermute(values, axis, [(i, i ^ flip) for i in range(lax.axis_size(axis))])


def bit_reversed(values, count):
    bits = count.bit_length() - 1
    split = values.reshape((2,) * bits + values.shape[1:])
    turned = jnp.transpose(split, tuple(reversed(range(bits))) + tuple(range(bits, split.ndim)))
    return turned.reshape(values.shape)


def gather_batch(values):
    step = lax.axis_size("batch") // 2
    stages = [values]
    while step:
        other = swap(values, "batch", step)
        upper = (lax.axis_index("batch") // step) % 2
        values = jnp.where(
            upper == 0, jnp.concatenate([values, other]), jnp.concatenate([other, values])
        )
        stages.append(values)
        step //= 2
    return stages


def send_blocks(blocks):
    return [blocks[0]] + [swap(block, "proto", flip) for flip, block in enumerate(blocks) if flip]


def all_to_all(copies, axes):
    return lax.all_to_all(copies, axes, 0, 0, tiled=True)


def body(crops, teacher_emb, w_first, b_first, w_second, b_second, w_third, b_third, protos):
    batch_index = lax.axis_index("batch")
    proto_index = lax.axis_index("proto")
    batch_size = lax.axis_size("batch")
    proto_size = lax.axis_size("proto")
    devices = batch_size * proto_size
    share_rows = crops.shape[0]
    group_rows = teacher_emb.shape[0]
    crops_total = group_rows * batch_size
    protos_total = protos.shape[0] * proto_size
    count, width = protos.shape
    thin = count // batch_size
    core = proto_index % 2
    proto_ref = proto_index.reshape(1)
    thin_ref = jnp.stack([batch_index, core])
    wide_ref = jnp.stack([batch_index, proto_index])

    own_unit, half = teacher_units(core.reshape(1), teacher_emb)
    stages = gather_batch(half)
    mine = stages[-1]
    other = swap(mine, "proto", 1)
    top = jnp.full((256, 128), -jnp.inf, jnp.float32)
    top = wide_tops(own_unit, protos, top, (), 0, count // 2, 4)

    crops_x = swap(crops, "proto", 2)
    rows = [crops, crops_x, swap(crops, "proto", 1), swap(crops_x, "proto", 1)]
    third_x = swap(w_third, "proto", 2)
    thirds = [w_third, third_x, swap(w_third, "proto", 1), swap(third_x, "proto", 1)]
    keep, give = student_front(proto_ref, b_first, rows, w_first, w_second, (top, stages[1]))
    top = wide_tops(own_unit, protos, top, (stages[2], give), count // 2, count // 2, 4)
    all_tops = all_to_all(spread_tops(top, (mine,), devices), BOTH)
    tops = jnp.max(all_tops.reshape(batch_size, proto_size, 256)[:, :, :group_rows], axis=1)
    tops = bit_reversed(tops, batch_size).reshape(batch_size, 2, group_rows // 2)
    base = jnp.transpose(tops, (1, 0, 2)).reshape(1, crops_total) * -teacher_rate

    core_rows = swap(give, "proto", 1)
    x_sent = keep[share_rows:] + core_rows[share_rows:]
    x_rows = swap(x_sent, "proto", 2)
    unit, rounded, lengths = student_middle(
        proto_ref, keep, core_rows, x_rows, b_second, thirds, b_third
    )
    emb_pair = jnp.concatenate([rounded, swap(rounded, "proto", 2)])
    student_emb = jnp.concatenate([emb_pair, swap(emb_pair, "proto", 1)])
    empty = jnp.concatenate(
        [jnp.zeros((group_rows, width + 128), jnp.float32), jnp.full((group_rows, 128), -1e30, jnp.float32)], axis=1
    )
    (state,) = attract(student_emb, empty, protos, 0, count // 2, 4, 1)
    slots = attract(student_emb, state, protos, count // 2, count // 2, 4, proto_size)
    attract_parts = send_blocks([slots[0], slots[2], slots[1], slots[3]])

    copies, weights = first_sweep(thin_ref, protos, mine, other, base, (x_sent, *thirds[2:]), devices, thin, protos_total)
    for _ in range(ITERS - 2):
        copies = next_sweep(weights, all_to_all(copies, BOTH), (rounded,), protos_total)
    scale_copies = last_scales(weights, all_to_all(copies, BOTH), (state,), batch_size, protos_total)
    all_scale = all_to_all(scale_copies, "batch")
    repels = repel(wide_ref, own_unit, all_tops, all_scale, protos, (slots[0],), proto_size)
    return finish(unit, lengths, attract_parts, send_blocks(repels))


def solution(mesh):
    in_specs = (
        P(("batch", "proto"), None),
        P("batch", None),
        P(None, "proto"),
        P(),
        P("proto", None),
        P(),
        P("proto", None),
        P(),
        P("proto", None),
    )
    out_specs = P(("batch", "proto"), None)
    return jax.shard_map(body, mesh=mesh, in_specs=in_specs, out_specs=out_specs, check_vma=False)
```

```python
import functools
import math

import jax
import jax.numpy as jnp
from jax import lax
from jax.experimental import pallas as pl
from jax.experimental.pallas import tpu as pltpu
from jax.sharding import PartitionSpec as P

ITERS = 3

student_temp = 0.1
teacher_temp = 0.07
norm_eps = 1e-06
teacher_rate = math.log2(math.e) / teacher_temp
student_rate = math.log2(math.e) / student_temp

MIB = 1024 * 1024
BOTH = ("batch", "proto")
TILE = 256
WIDE = 512


def scores(left_rows, right_rows):
    return lax.dot_general(
        left_rows, right_rows, (((1,), (1,)), ((), ())), preferred_element_type=jnp.float32
    )


def unit_rows(values):
    lengths = jnp.sqrt(jnp.sum(values * values, axis=1, keepdims=True) + norm_eps)
    return (values / lengths, lengths)


def gelu(values):
    return 0.5 * values * (1.0 + lax.erf(values * math.sqrt(0.5)))


def whole(memory_space=pltpu.VMEM):
    return pl.BlockSpec(memory_space=memory_space)


def in_hbm(array):
    return pltpu.with_memory_space_constraint(array, pltpu.HBM)


def skipping(kernel, first, count):
    def trimmed(*refs):
        kernel(*refs[:first], *refs[first + count :])

    return trimmed


def part(index, size):
    return pl.ds(pl.multiple_of(index * size, size), size)


def lane_fold(values, combine):
    folded = values[:, :128]
    for start in range(128, values.shape[1], 128):
        folded = combine(folded, values[:, start : start + 128])
    return folded


def params(mib):
    return pltpu.CompilerParams(vmem_limit_bytes=mib * MIB)


def cost(flops, bytes_accessed, transcendentals=0):
    return pl.CostEstimate(
        flops=int(flops), bytes_accessed=int(bytes_accessed), transcendentals=int(transcendentals)
    )


def fetch(source, target, sems, first_row=0):
    count, rows = target.shape[:2]

    def chunk_copy(index):
        start = pl.multiple_of(first_row + index * rows, rows)
        return pltpu.make_async_copy(source.at[pl.ds(start, rows), :], target.at[index], sems.at[index])

    for index in range(count):
        chunk_copy(index).start()
    return lambda index: chunk_copy(index).wait()


def teacher_units_kernel(core_ref, emb_ref, unit_ref, half_ref):
    unit_ref[...] = unit_rows(emb_ref[...].astype(jnp.float32))[0].astype(jnp.bfloat16)
    half = half_ref.shape[0]
    half_ref[...] = unit_ref[part(core_ref[0], half), :]


def teacher_units(core, teacher_emb):
    rows, width = teacher_emb.shape
    return pl.pallas_call(
        teacher_units_kernel,
        in_specs=[whole(pltpu.SMEM), whole()],
        out_specs=[whole(), whole()],
        out_shape=[
            jax.ShapeDtypeStruct((rows, width), jnp.bfloat16),
            jax.ShapeDtypeStruct((rows // 2, width), jnp.bfloat16),
        ],
        compiler_params=params(4),
        cost_estimate=cost(4 * rows * width, 8 * rows * width),
        name="teacher_units",
    )(core, in_hbm(teacher_emb))


def front_kernel(
    index_ref, unit_ref, bias_ref, own_hbm, x_hbm, core_hbm, last_hbm, first_hbm, second_hbm, protos_hbm,
    tops_ref, keep_ref, give_ref, first_ref, second_ref, rows_ref, protos_ref, top_ref, sems, chunk_sems,
):
    rows = unit_ref.shape[0]
    steps, block = protos_ref.shape[:2]
    wide = min(WIDE, block)
    share = own_hbm.shape[0]
    arrived = fetch(protos_hbm, protos_ref, chunk_sems)
    copies = [
        pltpu.make_async_copy(source, rows_ref.at[slot * share : (slot + 1) * share, :], sems.at[slot])
        for slot, source in enumerate((own_hbm, x_hbm, core_hbm, last_hbm))
    ]
    copies.append(pltpu.make_async_copy(first_hbm, first_ref, sems.at[4]))
    copies.append(pltpu.make_async_copy(second_hbm, second_ref, sems.at[5]))
    for copy in copies:
        copy.start()
    top_ref[...] = jnp.full(top_ref.shape, -jnp.inf, jnp.float32)

    def step(index, carry):
        arrived(index)
        top = top_ref[:rows, :]
        for start in range(0, block, wide):
            products = scores(unit_ref[...], protos_ref[index, start : start + wide, :])
            top = jnp.maximum(top, lane_fold(products, jnp.maximum))
        top_ref[:rows, :] = top
        return carry

    lax.fori_loop(0, steps, step, 0)
    tops = jnp.max(jnp.transpose(top_ref[...]), axis=0, keepdims=True)
    tops_ref[...] = jnp.broadcast_to(tops[None], tops_ref.shape)
    for copy in copies:
        copy.wait()
    hidden = first_ref.shape[1]
    bias = bias_ref[:, part(index_ref[0], hidden)]
    h_first = gelu(
        jnp.dot(rows_ref[...], first_ref[...], preferred_element_type=jnp.float32) + bias
    ).astype(jnp.bfloat16)
    for start in range(0, second_ref.shape[1], 512):
        columns = slice(start, start + 512)
        product = jnp.dot(h_first, second_ref[:, columns], preferred_element_type=jnp.float32)
        keep_ref[:, columns] = product[: 2 * share]
        give_ref[:, columns] = product[2 * share :]


def front(index, unit, bias, rows, first, second, protos, order, copies, steps):
    share, features = rows[0].shape
    hidden, units = second.shape
    count, width = protos.shape
    return pl.pallas_call(
        skipping(front_kernel, 10, len(order)),
        in_specs=[whole(pltpu.SMEM), whole(), whole()] + [whole(pl.ANY)] * (7 + len(order)),
        out_specs=[whole()] * 3,
        out_shape=[jax.ShapeDtypeStruct((copies, 1, 256), jnp.float32)]
        + [jax.ShapeDtypeStruct((2 * share, units), jnp.float32)] * 2,
        scratch_shapes=[
            pltpu.VMEM(first.shape, jnp.bfloat16),
            pltpu.VMEM(second.shape, jnp.bfloat16),
            pltpu.VMEM((4 * share, features), jnp.bfloat16),
            pltpu.VMEM((steps, count // steps, width), jnp.bfloat16),
            pltpu.VMEM((256, 128), jnp.float32),
            pltpu.SemaphoreType.DMA((6,)),
            pltpu.SemaphoreType.DMA((steps,)),
        ],
        compiler_params=params(26),
        cost_estimate=cost(
            2 * unit.size * count + 8 * share * hidden * (features + units), 2 * width * count
        ),
        name="front",
    )(
        index, unit, in_hbm(bias.reshape(1, -1)), in_hbm(rows[0]), *rows[1:],
        in_hbm(first), in_hbm(second), in_hbm(protos), *order,
    )


def wide_weights_kernel(group, index_ref, unit_ref, tops_ref, protos_hbm, weights_hbm, protos_ref, weights_ref, bias_ref, sems, out_sems):
    rows = unit_ref.shape[0]
    steps, block = protos_ref.shape[:2]
    arrived = fetch(protos_hbm, protos_ref, sems)
    first = index_ref[0] * group
    top = tops_ref[first]
    for other in range(1, group):
        top = jnp.maximum(top, tops_ref[first + other])
    bias_ref[...] = jnp.transpose(jnp.broadcast_to(top, (128, 256)))[:rows, :] * -teacher_rate

    def chunk_out(index):
        return pltpu.make_async_copy(weights_ref.at[index], weights_hbm.at[index], out_sems.at[index])

    def step(index, carry):
        arrived(index)
        bias = bias_ref[...]
        for start in range(0, block, TILE):
            products = scores(unit_ref[...], protos_ref[index, start : start + TILE, :])
            for lane in range(0, TILE, 128):
                weights = jnp.exp2(products[:, lane : lane + 128] * teacher_rate + bias)
                weights_ref[index, :, start + lane : start + lane + 128] = weights.astype(jnp.bfloat16)
        chunk_out(index).start()
        return carry

    lax.fori_loop(0, steps, step, 0)
    for index in range(steps):
        chunk_out(index).wait()


def wide_weights(index, unit, tops, protos, order, proto_size, steps):
    rows, width = unit.shape
    count = protos.shape[0]
    block = count // steps
    return pl.pallas_call(
        skipping(functools.partial(wide_weights_kernel, proto_size), 4, len(order)),
        in_specs=[whole(pltpu.SMEM), whole(), whole(), whole(pl.ANY)] + [whole(pl.ANY)] * len(order),
        out_specs=whole(pl.ANY),
        out_shape=pltpu.HBM((steps, rows, block), jnp.bfloat16),
        scratch_shapes=[
            pltpu.VMEM((steps, block, width), jnp.bfloat16),
            pltpu.VMEM((steps, rows, block), jnp.bfloat16),
            pltpu.VMEM((rows, 128), jnp.float32),
            pltpu.SemaphoreType.DMA((steps,)),
            pltpu.SemaphoreType.DMA((steps,)),
        ],
        compiler_params=params(22),
        cost_estimate=cost(2 * rows * width * count, 2 * (width + rows) * count, rows * count),
        name="wide_weights",
    )(index, unit, tops, in_hbm(protos), *order)


def repel_kernel(index_ref, scale_ref, weights_hbm, protos_hbm, *rest):
    out_refs, (protos_ref, weights_ref, acc_ref, sum_ref, sems, weight_sems) = rest[:-6], rest[-6:]
    steps, block, width = protos_ref.shape

    def weights_copy(index):
        return pltpu.make_async_copy(weights_hbm.at[index], weights_ref.at[index], weight_sems.at[index])

    def protos_copy(index):
        return pltpu.make_async_copy(protos_hbm.at[part(index, block), :], protos_ref.at[index], sems.at[index])

    for index in range(steps):
        weights_copy(index).start()
        protos_copy(index).start()
    acc_ref[...] = jnp.zeros(acc_ref.shape, jnp.float32)
    sum_ref[...] = jnp.zeros(sum_ref.shape, jnp.float32)
    pieces = scale_ref.shape[2] // block

    def step(index, carry):
        weights_copy(index).wait()
        protos_copy(index).wait()
        total = sum_ref[...]
        acc = acc_ref[...]
        scale = scale_ref[index // pieces, :, part(lax.rem(index, pieces), block)]
        for start in range(0, block, TILE):
            rounded = []
            for lane in range(start, start + TILE, 128):
                columns = slice(lane, lane + 128)
                scaled = weights_ref[index, :, columns].astype(jnp.float32) * scale[:, columns]
                total = total + scaled
                rounded.append(scaled.astype(jnp.bfloat16))
            acc = acc + jnp.dot(
                jnp.concatenate(rounded, axis=1),
                protos_ref[index, start : start + TILE, :],
                preferred_element_type=jnp.float32,
            )
        sum_ref[...] = total
        acc_ref[...] = acc
        return carry

    lax.fori_loop(0, steps, step, 0)
    total = jnp.sum(sum_ref[...], axis=1, keepdims=True)
    sum_ref[...] = jnp.broadcast_to(total, sum_ref.shape)
    share = out_refs[0].shape[0]
    for flip, out_ref in enumerate(out_refs):
        span = part(index_ref[1] ^ flip, share)
        out_ref[:, :width] = acc_ref[span, :]
        out_ref[:, width:] = sum_ref[span, :]


def repel(index, scale, weights, protos, order, proto_size):
    steps, rows, block = weights.shape
    count, width = protos.shape
    return pl.pallas_call(
        skipping(repel_kernel, 4, len(order)),
        in_specs=[whole(pltpu.SMEM), whole(), whole(pl.ANY), whole(pl.ANY)] + [whole(pl.ANY)] * len(order),
        out_specs=[whole()] * proto_size,
        out_shape=[jax.ShapeDtypeStruct((rows // proto_size, width + 128), jnp.float32)] * proto_size,
        scratch_shapes=[
            pltpu.VMEM((steps, block, width), jnp.bfloat16),
            pltpu.VMEM((steps, rows, block), jnp.bfloat16),
            pltpu.VMEM((rows, width), jnp.float32),
            pltpu.VMEM((rows, 128), jnp.float32),
            pltpu.SemaphoreType.DMA((steps,)),
            pltpu.SemaphoreType.DMA((steps,)),
        ],
        compiler_params=params(24),
        cost_estimate=cost(2 * rows * width * count, 2 * (width + rows) * count),
        name="repel",
    )(index, scale, in_hbm(weights), in_hbm(protos), *order)


def attract_kernel(first_row, last, emb_ref, state_ref, protos_hbm, *rest):
    out_refs, scratch = rest[:-6], rest[-6:]
    protos_ref, sems, products_ref, acc_ref, sum_ref, top_ref = scratch
    width = emb_ref.shape[1]
    steps, block = protos_ref.shape[:2]
    arrived = fetch(protos_hbm, protos_ref, sems, first_row)
    old_top = state_ref[:, width + 128 :]
    top_ref[...] = old_top

    def first(index, carry):
        arrived(index)
        top = top_ref[...]
        for start in range(0, block, TILE):
            products = scores(emb_ref[...], protos_ref[index, start : start + TILE, :])
            products_ref[index, :, start : start + TILE] = products
            top = jnp.maximum(top, lane_fold(products, jnp.maximum))
        top_ref[...] = top
        return carry

    lax.fori_loop(0, steps, first, 0)
    top = jnp.broadcast_to(jnp.max(top_ref[...], axis=1, keepdims=True), top_ref.shape)
    fade = jnp.exp2((old_top - top) * student_rate)
    top_ref[...] = top
    sum_ref[...] = state_ref[:, width : width + 128] * fade
    acc_ref[...] = state_ref[:, :width] * jnp.tile(fade, (1, width // 128))

    def second(index, carry):
        top = top_ref[...]
        total = sum_ref[...]
        acc = acc_ref[...]
        for start in range(0, block, TILE):
            pieces = []
            for lane in range(start, start + TILE, 128):
                shifted = jnp.exp2((products_ref[index, :, lane : lane + 128] - top) * student_rate)
                total = total + shifted
                pieces.append(shifted.astype(jnp.bfloat16))
            acc = acc + jnp.dot(
                jnp.concatenate(pieces, axis=1),
                protos_ref[index, start : start + TILE, :],
                preferred_element_type=jnp.float32,
            )
        sum_ref[...] = total
        acc_ref[...] = acc
        return carry

    lax.fori_loop(0, steps, second, 0)
    if last:
        total = jnp.sum(sum_ref[...], axis=1, keepdims=True)
        sum_ref[...] = jnp.broadcast_to(total, sum_ref.shape)
    share = out_refs[0].shape[0]
    for slot, out_ref in enumerate(out_refs):
        rows = pl.ds(slot * share, share)
        out_ref[:, :width] = acc_ref[rows, :]
        out_ref[:, width : width + 128] = sum_ref[rows, :]
        out_ref[:, width + 128 :] = top_ref[rows, :]


def attract(emb, state, protos, first_row, count, steps, outputs):
    rows, width = emb.shape
    block = count // steps
    return pl.pallas_call(
        functools.partial(attract_kernel, first_row, outputs > 1),
        in_specs=[whole(), whole(), whole(pl.ANY)],
        out_specs=[whole()] * outputs,
        out_shape=[jax.ShapeDtypeStruct((rows // outputs, width + 256), jnp.float32)] * outputs,
        scratch_shapes=[
            pltpu.VMEM((steps, block, width), jnp.bfloat16),
            pltpu.SemaphoreType.DMA((steps,)),
            pltpu.VMEM((steps, rows, block), jnp.float32),
            pltpu.VMEM((rows, width), jnp.float32),
            pltpu.VMEM((rows, 128), jnp.float32),
            pltpu.VMEM((rows, 128), jnp.float32),
        ],
        compiler_params=params(24),
        cost_estimate=cost(4 * rows * width * count, 2 * width * count, rows * count),
        name="attract",
    )(emb, state, in_hbm(protos))


def three_pieces(values):
    high = values.astype(jnp.bfloat16)
    rest = values - high.astype(jnp.float32)
    middle = rest.astype(jnp.bfloat16)
    low = (rest - middle.astype(jnp.float32)).astype(jnp.bfloat16)
    return jnp.concatenate([high, middle, low, jnp.zeros((13, values.shape[1]), jnp.bfloat16)], axis=0)


def lane_scales(folded, protos_total):
    sums = [
        jnp.sum(jnp.transpose(folded[start : start + 128, :]), axis=0, keepdims=True)
        for start in range(0, folded.shape[0], 128)
    ]
    return 1.0 / (protos_total * jnp.concatenate(sums, axis=1))


def give_sums(copies_ref, totals):
    rows = [totals[:, start : start + 128] for start in range(0, totals.shape[1], 128)]
    spare = copies_ref.shape[1] - len(rows)
    if spare:
        rows.append(jnp.zeros((spare, 128), jnp.float32))
    packed = jnp.concatenate(rows, axis=0).astype(jnp.bfloat16)
    copies_ref[...] = jnp.broadcast_to(packed[None], copies_ref.shape)


def take_scales(parts_ref, scale_ref):
    crops_total = scale_ref.shape[1]
    sums = jnp.sum(parts_ref[...].astype(jnp.float32), axis=0)
    for row in range(crops_total // 128):
        scale_ref[:, row * 128 : row * 128 + 128] = 1.0 / (crops_total * sums[row : row + 1, :])


def sums_shape(copies, crops_total):
    return (copies, -(-crops_total // 2048) * 16, 128)


def first_sweep_kernel(
    chunk, protos_total, index_ref, protos_hbm, mine_hbm, other_hbm, bias_ref, copies_ref, weights_hbm, protos_ref, units_ref, weights_ref, rounded_ref, scale_ref, sems, out_sems,
):
    thin, crops_total = weights_ref.shape
    half = mine_hbm.shape[0]
    core = index_ref[1]
    copies = (
        pltpu.make_async_copy(protos_hbm.at[part(index_ref[0], thin), :], protos_ref, sems.at[0]),
        pltpu.make_async_copy(mine_hbm, units_ref.at[part(core, half), :], sems.at[1]),
        pltpu.make_async_copy(other_hbm, units_ref.at[part(1 - core, half), :], sems.at[2]),
    )
    for copy in copies:
        copy.start()
    for copy in copies:
        copy.wait()

    def chunk_out(index):
        return pltpu.make_async_copy(
            rounded_ref.at[index], weights_hbm.at[part(index, chunk), :], out_sems.at[index]
        )

    def weigh(index, carry):
        rows = part(index, chunk)
        protos = protos_ref[rows, :]
        folded = jnp.zeros((chunk, 128), jnp.float32)
        for start in range(0, crops_total, TILE):
            columns = slice(start, start + TILE)
            products = scores(protos, units_ref[columns, :])
            weights = jnp.exp2(products * teacher_rate + bias_ref[:, columns])
            weights_ref[rows, columns] = weights
            rounded_ref[index, :, columns] = weights.astype(jnp.bfloat16)
            folded = folded + lane_fold(weights, jnp.add)
        sums = jnp.sum(folded, axis=1, keepdims=True)
        scale_ref[rows, :] = jnp.broadcast_to(1.0 / (protos_total * sums), (chunk, 128))
        chunk_out(index).start()
        return carry

    lax.fori_loop(0, thin // chunk, weigh, 0)
    small = min(thin, 64)

    def add_up(index, totals):
        rows = part(index, small)
        scaled = weights_ref[rows, :] * jnp.tile(scale_ref[rows, :], (1, crops_total // 128))
        return totals + jnp.sum(scaled.reshape(-1, 8, crops_total), axis=0)

    totals = lax.fori_loop(0, thin // small, add_up, jnp.zeros((8, crops_total), jnp.float32))
    give_sums(copies_ref, jnp.sum(totals, axis=0, keepdims=True))
    for index in range(thin // chunk):
        chunk_out(index).wait()


def first_sweep(index, protos, mine, other, base, order, copies, thin, protos_total):
    width = protos.shape[1]
    crops_total = 2 * mine.shape[0]
    chunk = min(thin, 1024)
    return pl.pallas_call(
        skipping(functools.partial(first_sweep_kernel, chunk, protos_total), 5, len(order)),
        in_specs=[whole(pltpu.SMEM), whole(pl.ANY), whole(pl.ANY), whole(pl.ANY), whole()]
        + [whole(pl.ANY)] * len(order),
        out_specs=[whole(), whole(pl.ANY)],
        out_shape=[
            jax.ShapeDtypeStruct(sums_shape(copies, crops_total), jnp.bfloat16),
            pltpu.HBM((thin, crops_total), jnp.bfloat16),
        ],
        scratch_shapes=[
            pltpu.VMEM((thin, width), jnp.bfloat16),
            pltpu.VMEM((crops_total, width), jnp.bfloat16),
            pltpu.VMEM((thin, crops_total), jnp.float32),
            pltpu.VMEM((thin // chunk, chunk, crops_total), jnp.bfloat16),
            pltpu.VMEM((thin, 128), jnp.float32),
            pltpu.SemaphoreType.DMA((3,)),
            pltpu.SemaphoreType.DMA((thin // chunk,)),
        ],
        compiler_params=params(32 if crops_total <= 2048 else 56),
        cost_estimate=cost(2 * thin * width * crops_total, 2 * thin * crops_total, thin * crops_total),
        name="first_sweep",
    )(index, in_hbm(protos), mine, other, base, *order)


def fetch_rows(weights_hbm, weights_ref, sems):
    steps, chunk, _ = weights_ref.shape

    def rows_copy(index):
        return pltpu.make_async_copy(
            weights_hbm.at[part(index, chunk), :], weights_ref.at[index], sems.at[index]
        )

    for index in range(steps):
        rows_copy(index).start()
    return lambda index: rows_copy(index).wait()


def scaled_fold(weights_ref, index, scale_ref):
    _, chunk, crops_total = weights_ref.shape
    folds = []
    for row in range(0, chunk, 64):
        fold = None
        for start in range(0, crops_total, TILE):
            columns = slice(start, start + TILE)
            weights = weights_ref[index, row : row + 64, columns].astype(jnp.float32)
            scaled = lane_fold(weights * scale_ref[:, columns], jnp.add)
            fold = scaled if fold is None else fold + scaled
        folds.append(fold)
    return jnp.concatenate(folds, axis=0)


def next_sweep_kernel(
    protos_total, weights_hbm, parts_ref, copies_ref, weights_ref, scale_ref, pieces_ref, totals_ref, sems,
):
    steps, chunk, crops_total = weights_ref.shape
    arrived = fetch_rows(weights_hbm, weights_ref, sems)
    take_scales(parts_ref, scale_ref)
    totals_ref[...] = jnp.zeros(totals_ref.shape, jnp.float32)

    def weigh(index):
        return three_pieces(lane_scales(scaled_fold(weights_ref, index, scale_ref), protos_total))

    def add_up(index):
        return jnp.dot(pieces_ref[...], weights_ref[index], preferred_element_type=jnp.float32)

    arrived(0)
    pieces_ref[...] = weigh(0)

    def sweep(index, carry):
        arrived(index)
        sums = add_up(index - 1)
        pieces = weigh(index)
        totals_ref[...] += sums
        pieces_ref[...] = pieces
        return carry

    lax.fori_loop(1, steps, sweep, 0)
    totals = totals_ref[...] + add_up(steps - 1)
    give_sums(copies_ref, jnp.sum(totals, axis=0, keepdims=True))


def next_sweep(weights, parts, order, protos_total):
    thin, crops_total = weights.shape
    copies = parts.shape[0]
    chunk = min(thin, 256)
    return pl.pallas_call(
        skipping(functools.partial(next_sweep_kernel, protos_total), 2, len(order)),
        in_specs=[whole(pl.ANY), whole()] + [whole(pl.ANY)] * len(order),
        out_specs=whole(),
        out_shape=jax.ShapeDtypeStruct(sums_shape(copies, crops_total), jnp.bfloat16),
        scratch_shapes=[
            pltpu.VMEM((thin // chunk, chunk, crops_total), jnp.bfloat16),
            pltpu.VMEM((1, crops_total), jnp.float32),
            pltpu.VMEM((16, chunk), jnp.bfloat16),
            pltpu.VMEM((16, crops_total), jnp.float32),
            pltpu.SemaphoreType.DMA((thin // chunk,)),
        ],
        compiler_params=params(16 if crops_total <= 2048 else 50),
        cost_estimate=cost(8 * thin * crops_total, 2 * thin * crops_total),
        name="next_sweep",
    )(in_hbm(weights), parts, *order)


def last_scales_kernel(
    protos_total, weights_hbm, parts_ref, copies_ref, weights_ref, scale_ref, out_ref, sems,
):
    steps, chunk, crops_total = weights_ref.shape
    arrived = fetch_rows(weights_hbm, weights_ref, sems)
    take_scales(parts_ref, scale_ref)

    def weigh(index, carry):
        arrived(index)
        out_ref[:, part(index, chunk)] = lane_scales(
            scaled_fold(weights_ref, index, scale_ref), protos_total
        )
        return carry

    lax.fori_loop(0, steps, weigh, 0)
    copies_ref[...] = jnp.broadcast_to(out_ref[...][None], copies_ref.shape)


def last_scales(weights, parts, order, copies, protos_total):
    thin, crops_total = weights.shape
    chunk = min(thin, 256)
    return pl.pallas_call(
        skipping(functools.partial(last_scales_kernel, protos_total), 2, len(order)),
        in_specs=[whole(pl.ANY), whole()] + [whole(pl.ANY)] * len(order),
        out_specs=whole(),
        out_shape=jax.ShapeDtypeStruct((copies, 1, thin), jnp.float32),
        scratch_shapes=[
            pltpu.VMEM((thin // chunk, chunk, crops_total), jnp.bfloat16),
            pltpu.VMEM((1, crops_total), jnp.float32),
            pltpu.VMEM((1, thin), jnp.float32),
            pltpu.SemaphoreType.DMA((thin // chunk,)),
        ],
        compiler_params=params(16 if crops_total <= 2048 else 50),
        cost_estimate=cost(4 * thin * crops_total, 2 * thin * crops_total),
        name="last_scales",
    )(in_hbm(weights), parts, *order)


def student_middle_kernel(
    index_ref, keep_ref, core_ref, x_ref, bias_ref, own_ref, partner_ref, other_ref, last_ref, last_bias_ref,
    unit_ref, emb_ref, lengths_ref, hidden_ref,
):
    share = x_ref.shape[0]
    block = own_ref.shape[0]
    sums = keep_ref[:share, :] + core_ref[:share, :] + x_ref[...]
    hidden_ref[...] = gelu(sums + bias_ref[...]).astype(jnp.bfloat16)
    index = index_ref[0]
    weights = ((0, own_ref[...]), (2, partner_ref[...]), (1, other_ref[...]), (3, last_ref[...]))
    bottleneck = jnp.broadcast_to(last_bias_ref[...], unit_ref.shape)
    for flip, weight in weights:
        bottleneck = bottleneck + jnp.dot(
            hidden_ref[:, part(index ^ flip, block)], weight, preferred_element_type=jnp.float32
        )
    unit, lengths = unit_rows(bottleneck)
    unit_ref[...] = unit
    emb_ref[...] = unit.astype(jnp.bfloat16)
    lengths_ref[...] = jnp.broadcast_to(lengths, lengths_ref.shape)


def student_middle(index, keep, core_rows, x_rows, bias, weights, last_bias):
    share, units = x_rows.shape
    width = weights[0].shape[1]
    return pl.pallas_call(
        student_middle_kernel,
        in_specs=[whole(pltpu.SMEM)] + [whole()] * 9,
        out_specs=[whole()] * 3,
        out_shape=[
            jax.ShapeDtypeStruct((share, width), jnp.float32),
            jax.ShapeDtypeStruct((share, width), jnp.bfloat16),
            jax.ShapeDtypeStruct((share, 128), jnp.float32),
        ],
        scratch_shapes=[pltpu.VMEM((share, units), jnp.bfloat16)],
        compiler_params=params(12),
        cost_estimate=cost(2 * share * units * width, 2 * units * width + 16 * share * units),
        name="student_middle",
    )(index, keep, core_rows, x_rows, in_hbm(bias.reshape(1, -1)), in_hbm(weights[0]), *weights[1:], in_hbm(last_bias.reshape(1, -1)))


def finish_kernel(unit_ref, lengths_ref, *rest):
    out_ref, blocks = rest[-1], rest[:-1]
    attracts, repels = blocks[: len(blocks) // 2], blocks[len(blocks) // 2 :]
    width = unit_ref.shape[1]
    row_top = functools.reduce(jnp.maximum, [ref[:, width + 128 :] for ref in attracts])
    attract_sum = repel_sum = 0.0
    row_sum = column_sum = 0.0
    for ref in attracts:
        fade = jnp.exp2((ref[:, width + 128 :] - row_top) * student_rate)
        row_sum = row_sum + ref[:, width : width + 128] * fade
        attract_sum = attract_sum + ref[:, :width] * jnp.tile(fade, (1, width // 128))
    for ref in repels:
        column_sum = column_sum + ref[:, width:]
        repel_sum = repel_sum + ref[:, :width]
    emb_grad = (
        attract_sum / jnp.tile(row_sum, (1, width // 128))
        - repel_sum / jnp.tile(column_sum, (1, width // 128))
    ) / student_temp
    unit = unit_ref[...]
    along = jnp.sum(unit * emb_grad, axis=1, keepdims=True)
    out_ref[...] = (emb_grad - unit * along) / jnp.tile(lengths_ref[...], (1, width // 128))


def finish(unit, lengths, attracts, repels):
    return pl.pallas_call(
        finish_kernel,
        in_specs=[whole()] * (2 + len(attracts) + len(repels)),
        out_specs=whole(),
        out_shape=jax.ShapeDtypeStruct(unit.shape, jnp.float32),
        compiler_params=params(8),
        cost_estimate=cost(40 * unit.size, 40 * unit.size),
        name="finish",
    )(unit, lengths, *attracts, *repels)


def swap(values, axis, flip):
    return lax.ppermute(values, axis, [(i, i ^ flip) for i in range(lax.axis_size(axis))])


def bit_reversed(values, count):
    bits = count.bit_length() - 1
    split = values.reshape((2,) * bits + values.shape[1:])
    turned = jnp.transpose(split, tuple(reversed(range(bits))) + tuple(range(bits, split.ndim)))
    return turned.reshape(values.shape)


def gather_batch(values):
    step = lax.axis_size("batch") // 2
    stages = [values]
    while step:
        other = swap(values, "batch", step)
        upper = (lax.axis_index("batch") // step) % 2
        values = jnp.where(
            upper == 0, jnp.concatenate([values, other]), jnp.concatenate([other, values])
        )
        stages.append(values)
        step //= 2
    return stages


def send_blocks(blocks):
    return [blocks[0]] + [swap(block, "proto", flip) for flip, block in enumerate(blocks) if flip]


def all_to_all(copies, axes):
    return lax.all_to_all(copies, axes, 0, 0, tiled=True)


def body(crops, teacher_emb, w_first, b_first, w_second, b_second, w_third, b_third, protos):
    batch_index = lax.axis_index("batch")
    proto_index = lax.axis_index("proto")
    batch_size = lax.axis_size("batch")
    proto_size = lax.axis_size("proto")
    devices = batch_size * proto_size
    share_rows = crops.shape[0]
    group_rows = teacher_emb.shape[0]
    crops_total = group_rows * batch_size
    protos_total = protos.shape[0] * proto_size
    count, width = protos.shape
    thin = count // batch_size
    core = proto_index % 2
    proto_ref = proto_index.reshape(1)
    thin_ref = jnp.stack([batch_index, core])
    wide_ref = jnp.stack([batch_index, proto_index])

    own_unit, half = teacher_units(core.reshape(1), teacher_emb)
    stages = gather_batch(half)
    mine = stages[-1]
    other = swap(mine, "proto", 1)

    crops_x = swap(crops, "proto", 2)
    rows = [crops, crops_x, swap(crops, "proto", 1), swap(crops_x, "proto", 1)]
    third_x = swap(w_third, "proto", 2)
    thirds = [w_third, third_x, swap(w_third, "proto", 1), swap(third_x, "proto", 1)]
    top_copies, keep, give = front(
        proto_ref, own_unit, b_first, rows, w_first, w_second, protos, (stages[2],), devices, 8
    )
    all_tops = all_to_all(top_copies, BOTH)
    tops = jnp.max(all_tops.reshape(batch_size, proto_size, 256)[:, :, :group_rows], axis=1)
    tops = bit_reversed(tops, batch_size).reshape(batch_size, 2, group_rows // 2)
    base = jnp.transpose(tops, (1, 0, 2)).reshape(1, crops_total) * -teacher_rate

    core_rows = swap(give, "proto", 1)
    x_sent = keep[share_rows:] + core_rows[share_rows:]
    x_rows = swap(x_sent, "proto", 2)
    unit, rounded, lengths = student_middle(
        proto_ref, keep, core_rows, x_rows, b_second, thirds, b_third
    )
    emb_pair = jnp.concatenate([rounded, swap(rounded, "proto", 2)])
    student_emb = jnp.concatenate([emb_pair, swap(emb_pair, "proto", 1)])
    empty = jnp.concatenate(
        [jnp.zeros((group_rows, width + 128), jnp.float32), jnp.full((group_rows, 128), -1e30, jnp.float32)], axis=1
    )
    (state,) = attract(student_emb, empty, protos, 0, count // 2, 4, 1)
    slots = attract(student_emb, state, protos, count // 2, count // 2, 4, proto_size)
    attract_parts = send_blocks([slots[0], slots[2], slots[1], slots[3]])

    copies, weights = first_sweep(thin_ref, protos, mine, other, base, (x_sent, *thirds[2:]), devices, thin, protos_total)
    own_weights = wide_weights(wide_ref, own_unit, all_tops, protos, (rounded,), proto_size, max(8, batch_size))
    for _ in range(ITERS - 2):
        copies = next_sweep(weights, all_to_all(copies, BOTH), (own_weights,), protos_total)
    scale_copies = last_scales(weights, all_to_all(copies, BOTH), (state,), batch_size, protos_total)
    all_scale = all_to_all(scale_copies, "batch")
    repels = repel(wide_ref, all_scale, own_weights, protos, (slots[0],), proto_size)
    return finish(unit, lengths, attract_parts, send_blocks(repels))


def solution(mesh):
    in_specs = (
        P(("batch", "proto"), None),
        P("batch", None),
        P(None, "proto"),
        P(),
        P("proto", None),
        P(),
        P("proto", None),
        P(),
        P("proto", None),
    )
    out_specs = P(("batch", "proto"), None)
    return jax.shard_map(body, mesh=mesh, in_specs=in_specs, out_specs=out_specs, check_vma=False)
```

```python
import functools
import math

import jax
import jax.numpy as jnp
from jax import lax
from jax.experimental import pallas as pl
from jax.experimental.pallas import tpu as pltpu
from jax.sharding import PartitionSpec as P

ITERS = 3

student_temp = 0.1
teacher_temp = 0.07
norm_eps = 1e-06
teacher_rate = math.log2(math.e) / teacher_temp
student_rate = math.log2(math.e) / student_temp

MIB = 1024 * 1024
BOTH = ("batch", "proto")
TILE = 256
WIDE = 512


def scores(left_rows, right_rows):
    return lax.dot_general(
        left_rows, right_rows, (((1,), (1,)), ((), ())), preferred_element_type=jnp.float32
    )


def unit_rows(values):
    lengths = jnp.sqrt(jnp.sum(values * values, axis=1, keepdims=True) + norm_eps)
    return (values / lengths, lengths)


def gelu(values):
    return 0.5 * values * (1.0 + lax.erf(values * math.sqrt(0.5)))


def whole(memory_space=pltpu.VMEM):
    return pl.BlockSpec(memory_space=memory_space)


def in_hbm(array):
    return pltpu.with_memory_space_constraint(array, pltpu.HBM)


def skipping(kernel, first, count):
    def trimmed(*refs):
        kernel(*refs[:first], *refs[first + count :])

    return trimmed


def part(index, size):
    return pl.ds(pl.multiple_of(index * size, size), size)


def lane_fold(values, combine):
    folded = values[:, :128]
    for start in range(128, values.shape[1], 128):
        folded = combine(folded, values[:, start : start + 128])
    return folded


def params(mib):
    return pltpu.CompilerParams(vmem_limit_bytes=mib * MIB)


def cost(flops, bytes_accessed, transcendentals=0):
    return pl.CostEstimate(
        flops=int(flops), bytes_accessed=int(bytes_accessed), transcendentals=int(transcendentals)
    )


def fetch(source, target, sems, first_row=0):
    count, rows = target.shape[:2]

    def chunk_copy(index):
        start = pl.multiple_of(first_row + index * rows, rows)
        return pltpu.make_async_copy(source.at[pl.ds(start, rows), :], target.at[index], sems.at[index])

    for index in range(count):
        chunk_copy(index).start()
    return lambda index: chunk_copy(index).wait()


def teacher_units_kernel(core_ref, emb_ref, unit_ref, half_ref):
    unit_ref[...] = unit_rows(emb_ref[...].astype(jnp.float32))[0].astype(jnp.bfloat16)
    half = half_ref.shape[0]
    half_ref[...] = unit_ref[part(core_ref[0], half), :]


def teacher_units(core, teacher_emb):
    rows, width = teacher_emb.shape
    return pl.pallas_call(
        teacher_units_kernel,
        in_specs=[whole(pltpu.SMEM), whole()],
        out_specs=[whole(), whole()],
        out_shape=[
            jax.ShapeDtypeStruct((rows, width), jnp.bfloat16),
            jax.ShapeDtypeStruct((rows // 2, width), jnp.bfloat16),
        ],
        compiler_params=params(4),
        cost_estimate=cost(4 * rows * width, 8 * rows * width),
        name="teacher_units",
    )(core, in_hbm(teacher_emb))


def front_kernel(
    index_ref, unit_ref, bias_ref, own_hbm, x_hbm, core_hbm, last_hbm, first_hbm, second_hbm, protos_hbm,
    tops_ref, keep_ref, give_ref, first_ref, second_ref, rows_ref, protos_ref, top_ref, sems, chunk_sems,
):
    rows = unit_ref.shape[0]
    steps, block = protos_ref.shape[:2]
    wide = min(WIDE, block)
    share = own_hbm.shape[0]
    arrived = fetch(protos_hbm, protos_ref, chunk_sems)
    copies = [
        pltpu.make_async_copy(source, rows_ref.at[slot * share : (slot + 1) * share, :], sems.at[slot])
        for slot, source in enumerate((own_hbm, x_hbm, core_hbm, last_hbm))
    ]
    copies.append(pltpu.make_async_copy(first_hbm, first_ref, sems.at[4]))
    copies.append(pltpu.make_async_copy(second_hbm, second_ref, sems.at[5]))
    for copy in copies:
        copy.start()
    top_ref[...] = jnp.full(top_ref.shape, -jnp.inf, jnp.float32)

    def step(index, carry):
        arrived(index)
        top = top_ref[:rows, :]
        for start in range(0, block, wide):
            products = scores(unit_ref[...], protos_ref[index, start : start + wide, :])
            top = jnp.maximum(top, lane_fold(products, jnp.maximum))
        top_ref[:rows, :] = top
        return carry

    lax.fori_loop(0, steps, step, 0)
    tops = jnp.max(jnp.transpose(top_ref[...]), axis=0, keepdims=True)
    tops_ref[...] = jnp.broadcast_to(tops[None], tops_ref.shape)
    for copy in copies:
        copy.wait()
    hidden = first_ref.shape[1]
    bias = bias_ref[:, part(index_ref[0], hidden)]
    h_first = gelu(
        jnp.dot(rows_ref[...], first_ref[...], preferred_element_type=jnp.float32) + bias
    ).astype(jnp.bfloat16)
    for start in range(0, second_ref.shape[1], 512):
        columns = slice(start, start + 512)
        product = jnp.dot(h_first, second_ref[:, columns], preferred_element_type=jnp.float32)
        keep_ref[:, columns] = product[: 2 * share]
        give_ref[:, columns] = product[2 * share :]


def front(index, unit, bias, rows, first, second, protos, order, copies, steps):
    share, features = rows[0].shape
    hidden, units = second.shape
    count, width = protos.shape
    return pl.pallas_call(
        skipping(front_kernel, 10, len(order)),
        in_specs=[whole(pltpu.SMEM), whole(), whole()] + [whole(pl.ANY)] * (7 + len(order)),
        out_specs=[whole()] * 3,
        out_shape=[jax.ShapeDtypeStruct((copies, 1, 256), jnp.float32)]
        + [jax.ShapeDtypeStruct((2 * share, units), jnp.float32)] * 2,
        scratch_shapes=[
            pltpu.VMEM(first.shape, jnp.bfloat16),
            pltpu.VMEM(second.shape, jnp.bfloat16),
            pltpu.VMEM((4 * share, features), jnp.bfloat16),
            pltpu.VMEM((steps, count // steps, width), jnp.bfloat16),
            pltpu.VMEM((256, 128), jnp.float32),
            pltpu.SemaphoreType.DMA((6,)),
            pltpu.SemaphoreType.DMA((steps,)),
        ],
        compiler_params=params(26),
        cost_estimate=cost(
            2 * unit.size * count + 8 * share * hidden * (features + units), 2 * width * count
        ),
        name="front",
    )(
        index, unit, in_hbm(bias.reshape(1, -1)), in_hbm(rows[0]), *rows[1:],
        in_hbm(first), in_hbm(second), in_hbm(protos), *order,
    )


def repel_kernel(group, index_ref, unit_ref, tops_ref, scale_ref, protos_hbm, *rest):
    out_refs, (protos_ref, sems, acc_ref, sum_ref, bias_ref) = rest[:-5], rest[-5:]
    rows, width = unit_ref.shape
    steps, block = protos_ref.shape[:2]
    wide = min(WIDE, block)
    arrived = fetch(protos_hbm, protos_ref, sems)
    first = index_ref[0] * group
    top = tops_ref[first]
    for other in range(1, group):
        top = jnp.maximum(top, tops_ref[first + other])
    bias_ref[...] = jnp.transpose(jnp.broadcast_to(top, (128, 256)))[:rows, :] * -teacher_rate
    acc_ref[...] = jnp.zeros(acc_ref.shape, jnp.float32)
    sum_ref[...] = jnp.zeros(sum_ref.shape, jnp.float32)

    def step(index, carry):
        arrived(index)
        bias = bias_ref[...]
        total = sum_ref[...]
        acc = acc_ref[...]
        for start in range(0, block, wide):
            protos = protos_ref[index, start : start + wide, :]
            products = scores(unit_ref[...], protos)
            pieces = []
            for lane in range(0, wide, 128):
                scaled = jnp.exp2(products[:, lane : lane + 128] * teacher_rate + bias)
                scaled = scaled * scale_ref[index, :, start + lane : start + lane + 128]
                total = total + scaled
                pieces.append(scaled.astype(jnp.bfloat16))
            acc = acc + jnp.dot(
                jnp.concatenate(pieces, axis=1), protos, preferred_element_type=jnp.float32
            )
        sum_ref[...] = total
        acc_ref[...] = acc
        return carry

    lax.fori_loop(0, steps, step, 0)
    total = jnp.sum(sum_ref[...], axis=1, keepdims=True)
    sum_ref[...] = jnp.broadcast_to(total, sum_ref.shape)
    share = out_refs[0].shape[0]
    for flip, out_ref in enumerate(out_refs):
        span = part(index_ref[1] ^ flip, share)
        out_ref[:, :width] = acc_ref[span, :]
        out_ref[:, width:] = sum_ref[span, :]


def repel(index, unit, tops, scale, protos, order, proto_size):
    rows, width = unit.shape
    count = protos.shape[0]
    steps, _, block = scale.shape
    return pl.pallas_call(
        skipping(functools.partial(repel_kernel, proto_size), 5, len(order)),
        in_specs=[whole(pltpu.SMEM), whole(), whole(), whole(), whole(pl.ANY)] + [whole(pl.ANY)] * len(order),
        out_specs=[whole()] * proto_size,
        out_shape=[jax.ShapeDtypeStruct((rows // proto_size, width + 128), jnp.float32)] * proto_size,
        scratch_shapes=[
            pltpu.VMEM((steps, block, width), jnp.bfloat16),
            pltpu.SemaphoreType.DMA((steps,)),
            pltpu.VMEM((rows, width), jnp.float32),
            pltpu.VMEM((rows, 128), jnp.float32),
            pltpu.VMEM((rows, 128), jnp.float32),
        ],
        compiler_params=params(16),
        cost_estimate=cost(4 * rows * width * count, 2 * width * count, rows * count),
        name="repel",
    )(index, unit, tops, scale, in_hbm(protos), *order)


def attract_kernel(first_row, last, emb_ref, state_ref, protos_hbm, *rest):
    out_refs, scratch = rest[:-6], rest[-6:]
    protos_ref, sems, products_ref, acc_ref, sum_ref, top_ref = scratch
    width = emb_ref.shape[1]
    steps, block = protos_ref.shape[:2]
    arrived = fetch(protos_hbm, protos_ref, sems, first_row)
    old_top = state_ref[:, width + 128 :]
    top_ref[...] = old_top

    def first(index, carry):
        arrived(index)
        top = top_ref[...]
        for start in range(0, block, TILE):
            products = scores(emb_ref[...], protos_ref[index, start : start + TILE, :])
            products_ref[index, :, start : start + TILE] = products
            top = jnp.maximum(top, lane_fold(products, jnp.maximum))
        top_ref[...] = top
        return carry

    lax.fori_loop(0, steps, first, 0)
    top = jnp.broadcast_to(jnp.max(top_ref[...], axis=1, keepdims=True), top_ref.shape)
    fade = jnp.exp2((old_top - top) * student_rate)
    top_ref[...] = top
    sum_ref[...] = state_ref[:, width : width + 128] * fade
    acc_ref[...] = state_ref[:, :width] * jnp.tile(fade, (1, width // 128))

    def second(index, carry):
        top = top_ref[...]
        total = sum_ref[...]
        acc = acc_ref[...]
        for start in range(0, block, TILE):
            pieces = []
            for lane in range(start, start + TILE, 128):
                shifted = jnp.exp2((products_ref[index, :, lane : lane + 128] - top) * student_rate)
                total = total + shifted
                pieces.append(shifted.astype(jnp.bfloat16))
            acc = acc + jnp.dot(
                jnp.concatenate(pieces, axis=1),
                protos_ref[index, start : start + TILE, :],
                preferred_element_type=jnp.float32,
            )
        sum_ref[...] = total
        acc_ref[...] = acc
        return carry

    lax.fori_loop(0, steps, second, 0)
    if last:
        total = jnp.sum(sum_ref[...], axis=1, keepdims=True)
        sum_ref[...] = jnp.broadcast_to(total, sum_ref.shape)
    share = out_refs[0].shape[0]
    for slot, out_ref in enumerate(out_refs):
        rows = pl.ds(slot * share, share)
        out_ref[:, :width] = acc_ref[rows, :]
        out_ref[:, width : width + 128] = sum_ref[rows, :]
        out_ref[:, width + 128 :] = top_ref[rows, :]


def attract(emb, state, protos, first_row, count, steps, outputs):
    rows, width = emb.shape
    block = count // steps
    return pl.pallas_call(
        functools.partial(attract_kernel, first_row, outputs > 1),
        in_specs=[whole(), whole(), whole(pl.ANY)],
        out_specs=[whole()] * outputs,
        out_shape=[jax.ShapeDtypeStruct((rows // outputs, width + 256), jnp.float32)] * outputs,
        scratch_shapes=[
            pltpu.VMEM((steps, block, width), jnp.bfloat16),
            pltpu.SemaphoreType.DMA((steps,)),
            pltpu.VMEM((steps, rows, block), jnp.float32),
            pltpu.VMEM((rows, width), jnp.float32),
            pltpu.VMEM((rows, 128), jnp.float32),
            pltpu.VMEM((rows, 128), jnp.float32),
        ],
        compiler_params=params(24),
        cost_estimate=cost(4 * rows * width * count, 2 * width * count, rows * count),
        name="attract",
    )(emb, state, in_hbm(protos))


def three_pieces(values):
    high = values.astype(jnp.bfloat16)
    rest = values - high.astype(jnp.float32)
    middle = rest.astype(jnp.bfloat16)
    low = (rest - middle.astype(jnp.float32)).astype(jnp.bfloat16)
    return jnp.concatenate([high, middle, low, jnp.zeros((13, values.shape[1]), jnp.bfloat16)], axis=0)


def lane_scales(folded, protos_total):
    sums = [
        jnp.sum(jnp.transpose(folded[start : start + 128, :]), axis=0, keepdims=True)
        for start in range(0, folded.shape[0], 128)
    ]
    return 1.0 / (protos_total * jnp.concatenate(sums, axis=1))


def give_sums(copies_ref, totals):
    rows = [totals[:, start : start + 128] for start in range(0, totals.shape[1], 128)]
    spare = copies_ref.shape[1] - len(rows)
    if spare:
        rows.append(jnp.zeros((spare, 128), jnp.float32))
    packed = jnp.concatenate(rows, axis=0).astype(jnp.bfloat16)
    copies_ref[...] = jnp.broadcast_to(packed[None], copies_ref.shape)


def take_scales(parts_ref, scale_ref):
    crops_total = scale_ref.shape[1]
    sums = jnp.sum(parts_ref[...].astype(jnp.float32), axis=0)
    for row in range(crops_total // 128):
        scale_ref[:, row * 128 : row * 128 + 128] = 1.0 / (crops_total * sums[row : row + 1, :])


def sums_shape(copies, crops_total):
    return (copies, -(-crops_total // 2048) * 16, 128)


def first_sweep_kernel(
    protos_total, index_ref, protos_hbm, mine_hbm, other_hbm, bias_ref, copies_ref, weights_hbm,
    protos_ref, units_ref, weights_ref, rounded_ref, scale_ref, totals_ref, sems, out_sems,
):
    steps, chunk, crops_total = rounded_ref.shape
    thin = steps * chunk
    half = mine_hbm.shape[0]
    core = index_ref[1]
    copies = (
        pltpu.make_async_copy(mine_hbm, units_ref.at[part(core, half), :], sems.at[1]),
        pltpu.make_async_copy(other_hbm, units_ref.at[part(1 - core, half), :], sems.at[2]),
        pltpu.make_async_copy(protos_hbm.at[part(index_ref[0], thin), :], protos_ref, sems.at[0]),
    )
    for copy in copies:
        copy.start()
    totals_ref[...] = jnp.zeros(totals_ref.shape, jnp.float32)
    for copy in copies:
        copy.wait()

    def chunk_out(index):
        return pltpu.make_async_copy(
            rounded_ref.at[index], weights_hbm.at[part(index, chunk), :], out_sems.at[index]
        )

    def weigh(index, slot):
        protos = protos_ref[part(index, chunk), :]
        folded = jnp.zeros((chunk, 128), jnp.float32)
        for start in range(0, crops_total, TILE):
            columns = slice(start, start + TILE)
            products = scores(protos, units_ref[columns, :])
            weights = jnp.exp2(products * teacher_rate + bias_ref[:, columns])
            weights_ref[slot, :, columns] = weights
            rounded_ref[index, :, columns] = weights.astype(jnp.bfloat16)
            folded = folded + lane_fold(weights, jnp.add)
        sums = jnp.sum(folded, axis=1, keepdims=True)
        scale_ref[slot] = jnp.broadcast_to(1.0 / (protos_total * sums), (chunk, 128))
        chunk_out(index).start()

    def add_up(slot):
        for lane in range(0, crops_total, 128):
            total = totals_ref[:, lane : lane + 128]
            for row in range(0, chunk, 64):
                scaled = weights_ref[slot, row : row + 64, lane : lane + 128] * scale_ref[slot, row : row + 64, :]
                total = total + jnp.sum(scaled.reshape(-1, 8, 128), axis=0)
            totals_ref[:, lane : lane + 128] = total

    weigh(0, 0)

    def sweep(index, carry):
        slot = lax.rem(index, 2)
        weigh(index, slot)
        add_up(1 - slot)
        return carry

    lax.fori_loop(1, steps, sweep, 0)
    add_up((steps - 1) % 2)
    give_sums(copies_ref, jnp.sum(totals_ref[...], axis=0, keepdims=True))
    for index in range(steps):
        chunk_out(index).wait()


def first_sweep(index, protos, mine, other, base, order, copies, thin, protos_total):
    width = protos.shape[1]
    crops_total = 2 * mine.shape[0]
    chunk = min(thin, 512) if crops_total <= 2048 else 128
    steps = thin // chunk
    return pl.pallas_call(
        skipping(functools.partial(first_sweep_kernel, protos_total), 5, len(order)),
        in_specs=[whole(pltpu.SMEM), whole(pl.ANY), whole(pl.ANY), whole(pl.ANY), whole()]
        + [whole(pl.ANY)] * len(order),
        out_specs=[whole(), whole(pl.ANY)],
        out_shape=[
            jax.ShapeDtypeStruct(sums_shape(copies, crops_total), jnp.bfloat16),
            pltpu.HBM((thin, crops_total), jnp.bfloat16),
        ],
        scratch_shapes=[
            pltpu.VMEM((thin, width), jnp.bfloat16),
            pltpu.VMEM((crops_total, width), jnp.bfloat16),
            pltpu.VMEM((2, chunk, crops_total), jnp.float32),
            pltpu.VMEM((steps, chunk, crops_total), jnp.bfloat16),
            pltpu.VMEM((2, chunk, 128), jnp.float32),
            pltpu.VMEM((8, crops_total), jnp.float32),
            pltpu.SemaphoreType.DMA((3,)),
            pltpu.SemaphoreType.DMA((steps,)),
        ],
        compiler_params=params(32 if crops_total <= 2048 else 56),
        cost_estimate=cost(2 * thin * width * crops_total, 2 * thin * crops_total, thin * crops_total),
        name="first_sweep",
    )(index, in_hbm(protos), mine, other, base, *order)


def fetch_rows(weights_hbm, weights_ref, sems):
    steps, chunk, _ = weights_ref.shape

    def rows_copy(index):
        return pltpu.make_async_copy(
            weights_hbm.at[part(index, chunk), :], weights_ref.at[index], sems.at[index]
        )

    for index in range(steps):
        rows_copy(index).start()
    return lambda index: rows_copy(index).wait()


def scaled_fold(weights_ref, index, scale_ref):
    _, chunk, crops_total = weights_ref.shape
    folds = []
    for row in range(0, chunk, 64):
        fold = None
        for start in range(0, crops_total, TILE):
            columns = slice(start, start + TILE)
            weights = weights_ref[index, row : row + 64, columns].astype(jnp.float32)
            scaled = lane_fold(weights * scale_ref[:, columns], jnp.add)
            fold = scaled if fold is None else fold + scaled
        folds.append(fold)
    return jnp.concatenate(folds, axis=0)


def next_sweep_kernel(
    protos_total, weights_hbm, parts_ref, copies_ref, weights_ref, scale_ref, pieces_ref, totals_ref, sems,
):
    steps, chunk, crops_total = weights_ref.shape
    arrived = fetch_rows(weights_hbm, weights_ref, sems)
    take_scales(parts_ref, scale_ref)
    totals_ref[...] = jnp.zeros(totals_ref.shape, jnp.float32)

    def weigh(index):
        return three_pieces(lane_scales(scaled_fold(weights_ref, index, scale_ref), protos_total))

    def add_up(index):
        return jnp.dot(pieces_ref[...], weights_ref[index], preferred_element_type=jnp.float32)

    arrived(0)
    pieces_ref[...] = weigh(0)

    def sweep(index, carry):
        arrived(index)
        sums = add_up(index - 1)
        pieces = weigh(index)
        totals_ref[...] += sums
        pieces_ref[...] = pieces
        return carry

    lax.fori_loop(1, steps, sweep, 0)
    totals = totals_ref[...] + add_up(steps - 1)
    give_sums(copies_ref, jnp.sum(totals, axis=0, keepdims=True))


def next_sweep(weights, parts, order, protos_total):
    thin, crops_total = weights.shape
    copies = parts.shape[0]
    chunk = min(thin, 256)
    return pl.pallas_call(
        skipping(functools.partial(next_sweep_kernel, protos_total), 2, len(order)),
        in_specs=[whole(pl.ANY), whole()] + [whole(pl.ANY)] * len(order),
        out_specs=whole(),
        out_shape=jax.ShapeDtypeStruct(sums_shape(copies, crops_total), jnp.bfloat16),
        scratch_shapes=[
            pltpu.VMEM((thin // chunk, chunk, crops_total), jnp.bfloat16),
            pltpu.VMEM((1, crops_total), jnp.float32),
            pltpu.VMEM((16, chunk), jnp.bfloat16),
            pltpu.VMEM((16, crops_total), jnp.float32),
            pltpu.SemaphoreType.DMA((thin // chunk,)),
        ],
        compiler_params=params(16 if crops_total <= 2048 else 50),
        cost_estimate=cost(8 * thin * crops_total, 2 * thin * crops_total),
        name="next_sweep",
    )(in_hbm(weights), parts, *order)


def last_scales_kernel(
    protos_total, weights_hbm, parts_ref, copies_ref, weights_ref, scale_ref, out_ref, sems,
):
    steps, chunk, crops_total = weights_ref.shape
    arrived = fetch_rows(weights_hbm, weights_ref, sems)
    take_scales(parts_ref, scale_ref)

    def weigh(index, carry):
        arrived(index)
        out_ref[:, part(index, chunk)] = lane_scales(
            scaled_fold(weights_ref, index, scale_ref), protos_total
        )
        return carry

    lax.fori_loop(0, steps, weigh, 0)
    copies_ref[...] = jnp.broadcast_to(out_ref[...][None], copies_ref.shape)


def last_scales(weights, parts, order, copies, protos_total):
    thin, crops_total = weights.shape
    chunk = min(thin, 256)
    return pl.pallas_call(
        skipping(functools.partial(last_scales_kernel, protos_total), 2, len(order)),
        in_specs=[whole(pl.ANY), whole()] + [whole(pl.ANY)] * len(order),
        out_specs=whole(),
        out_shape=jax.ShapeDtypeStruct((copies, 1, thin), jnp.float32),
        scratch_shapes=[
            pltpu.VMEM((thin // chunk, chunk, crops_total), jnp.bfloat16),
            pltpu.VMEM((1, crops_total), jnp.float32),
            pltpu.VMEM((1, thin), jnp.float32),
            pltpu.SemaphoreType.DMA((thin // chunk,)),
        ],
        compiler_params=params(16 if crops_total <= 2048 else 50),
        cost_estimate=cost(4 * thin * crops_total, 2 * thin * crops_total),
        name="last_scales",
    )(in_hbm(weights), parts, *order)


def student_middle_kernel(
    index_ref, keep_ref, core_ref, x_ref, bias_ref, own_ref, partner_ref, other_ref, last_ref, last_bias_ref,
    unit_ref, emb_ref, lengths_ref, hidden_ref,
):
    share = x_ref.shape[0]
    block = own_ref.shape[0]
    sums = keep_ref[:share, :] + core_ref[:share, :] + x_ref[...]
    hidden_ref[...] = gelu(sums + bias_ref[...]).astype(jnp.bfloat16)
    index = index_ref[0]
    weights = ((0, own_ref[...]), (2, partner_ref[...]), (1, other_ref[...]), (3, last_ref[...]))
    bottleneck = jnp.broadcast_to(last_bias_ref[...], unit_ref.shape)
    for flip, weight in weights:
        bottleneck = bottleneck + jnp.dot(
            hidden_ref[:, part(index ^ flip, block)], weight, preferred_element_type=jnp.float32
        )
    unit, lengths = unit_rows(bottleneck)
    unit_ref[...] = unit
    emb_ref[...] = unit.astype(jnp.bfloat16)
    lengths_ref[...] = jnp.broadcast_to(lengths, lengths_ref.shape)


def student_middle(index, keep, core_rows, x_rows, bias, weights, last_bias):
    share, units = x_rows.shape
    width = weights[0].shape[1]
    return pl.pallas_call(
        student_middle_kernel,
        in_specs=[whole(pltpu.SMEM)] + [whole()] * 9,
        out_specs=[whole()] * 3,
        out_shape=[
            jax.ShapeDtypeStruct((share, width), jnp.float32),
            jax.ShapeDtypeStruct((share, width), jnp.bfloat16),
            jax.ShapeDtypeStruct((share, 128), jnp.float32),
        ],
        scratch_shapes=[pltpu.VMEM((share, units), jnp.bfloat16)],
        compiler_params=params(12),
        cost_estimate=cost(2 * share * units * width, 2 * units * width + 16 * share * units),
        name="student_middle",
    )(index, keep, core_rows, x_rows, in_hbm(bias.reshape(1, -1)), in_hbm(weights[0]), *weights[1:], in_hbm(last_bias.reshape(1, -1)))


def finish_kernel(unit_ref, lengths_ref, *rest):
    out_ref, blocks = rest[-1], rest[:-1]
    attracts, repels = blocks[: len(blocks) // 2], blocks[len(blocks) // 2 :]
    width = unit_ref.shape[1]
    row_top = functools.reduce(jnp.maximum, [ref[:, width + 128 :] for ref in attracts])
    attract_sum = repel_sum = 0.0
    row_sum = column_sum = 0.0
    for ref in attracts:
        fade = jnp.exp2((ref[:, width + 128 :] - row_top) * student_rate)
        row_sum = row_sum + ref[:, width : width + 128] * fade
        attract_sum = attract_sum + ref[:, :width] * jnp.tile(fade, (1, width // 128))
    for ref in repels:
        column_sum = column_sum + ref[:, width:]
        repel_sum = repel_sum + ref[:, :width]
    emb_grad = (
        attract_sum / jnp.tile(row_sum, (1, width // 128))
        - repel_sum / jnp.tile(column_sum, (1, width // 128))
    ) / student_temp
    unit = unit_ref[...]
    along = jnp.sum(unit * emb_grad, axis=1, keepdims=True)
    out_ref[...] = (emb_grad - unit * along) / jnp.tile(lengths_ref[...], (1, width // 128))


def finish(unit, lengths, attracts, repels):
    return pl.pallas_call(
        finish_kernel,
        in_specs=[whole()] * (2 + len(attracts) + len(repels)),
        out_specs=whole(),
        out_shape=jax.ShapeDtypeStruct(unit.shape, jnp.float32),
        compiler_params=params(8),
        cost_estimate=cost(40 * unit.size, 40 * unit.size),
        name="finish",
    )(unit, lengths, *attracts, *repels)


def swap(values, axis, flip):
    return lax.ppermute(values, axis, [(i, i ^ flip) for i in range(lax.axis_size(axis))])


def bit_reversed(values, count):
    bits = count.bit_length() - 1
    split = values.reshape((2,) * bits + values.shape[1:])
    turned = jnp.transpose(split, tuple(reversed(range(bits))) + tuple(range(bits, split.ndim)))
    return turned.reshape(values.shape)


def gather_batch(values):
    step = lax.axis_size("batch") // 2
    stages = [values]
    while step:
        other = swap(values, "batch", step)
        upper = (lax.axis_index("batch") // step) % 2
        values = jnp.where(
            upper == 0, jnp.concatenate([values, other]), jnp.concatenate([other, values])
        )
        stages.append(values)
        step //= 2
    return stages


def send_blocks(blocks):
    return [blocks[0]] + [swap(block, "proto", flip) for flip, block in enumerate(blocks) if flip]


def all_to_all(copies, axes):
    return lax.all_to_all(copies, axes, 0, 0, tiled=True)


def body(crops, teacher_emb, w_first, b_first, w_second, b_second, w_third, b_third, protos):
    batch_index = lax.axis_index("batch")
    proto_index = lax.axis_index("proto")
    batch_size = lax.axis_size("batch")
    proto_size = lax.axis_size("proto")
    devices = batch_size * proto_size
    share_rows = crops.shape[0]
    group_rows = teacher_emb.shape[0]
    crops_total = group_rows * batch_size
    protos_total = protos.shape[0] * proto_size
    count, width = protos.shape
    thin = count // batch_size
    core = proto_index % 2
    proto_ref = proto_index.reshape(1)
    thin_ref = jnp.stack([batch_index, core])
    wide_ref = jnp.stack([batch_index, proto_index])

    own_unit, half = teacher_units(core.reshape(1), teacher_emb)
    stages = gather_batch(half)
    mine = stages[-1]
    other = swap(mine, "proto", 1)

    crops_x = swap(crops, "proto", 2)
    rows = [crops, crops_x, swap(crops, "proto", 1), swap(crops_x, "proto", 1)]
    thirds = [w_third, swap(w_third, "proto", 2), swap(w_third, "proto", 1), swap(w_third, "proto", 3)]
    top_copies, keep, give = front(
        proto_ref, own_unit, b_first, rows, w_first, w_second, protos, (stages[2],), devices, 8
    )
    all_tops = all_to_all(top_copies, BOTH)
    tops = jnp.max(all_tops.reshape(batch_size, proto_size, 256)[:, :, :group_rows], axis=1)
    tops = bit_reversed(tops, batch_size).reshape(batch_size, 2, group_rows // 2)
    base = jnp.transpose(tops, (1, 0, 2)).reshape(1, crops_total) * -teacher_rate

    core_rows = swap(give, "proto", 1)
    x_sent = keep[share_rows:] + core_rows[share_rows:]
    x_rows = swap(x_sent, "proto", 2)
    unit, rounded, lengths = student_middle(
        proto_ref, keep, core_rows, x_rows, b_second, thirds, b_third
    )
    emb_pair = jnp.concatenate([rounded, swap(rounded, "proto", 2)])
    student_emb = jnp.concatenate([emb_pair, swap(emb_pair, "proto", 1)])
    empty = jnp.concatenate(
        [jnp.zeros((group_rows, width + 128), jnp.float32), jnp.full((group_rows, 128), -1e30, jnp.float32)], axis=1
    )
    (state,) = attract(student_emb, empty, protos, 0, count // 2, 4, 1)
    slots = attract(student_emb, state, protos, count // 2, count // 2, 4, proto_size)
    attract_parts = send_blocks([slots[0], slots[2], slots[1], slots[3]])

    copies, weights = first_sweep(thin_ref, protos, mine, other, base, (x_sent, *thirds[1:]), devices, thin, protos_total)
    for _ in range(ITERS - 2):
        copies = next_sweep(weights, all_to_all(copies, BOTH), (rounded,), protos_total)
    scale_copies = last_scales(weights, all_to_all(copies, BOTH), (state,), batch_size, protos_total)
    all_scale = all_to_all(scale_copies, "batch")
    repels = repel(wide_ref, own_unit, all_tops, all_scale, protos, (slots[0],), proto_size)
    return finish(unit, lengths, attract_parts, send_blocks(repels))


def solution(mesh):
    in_specs = (
        P(("batch", "proto"), None),
        P("batch", None),
        P(None, "proto"),
        P(),
        P("proto", None),
        P(),
        P("proto", None),
        P(),
        P("proto", None),
    )
    out_specs = P(("batch", "proto"), None)
    return jax.shard_map(body, mesh=mesh, in_specs=in_specs, out_specs=out_specs, check_vma=False)
```

```python
import functools
import math

import jax
import jax.numpy as jnp
from jax import lax
from jax.experimental import pallas as pl
from jax.experimental.pallas import tpu as pltpu
from jax.sharding import PartitionSpec as P

ITERS = 3

student_temp = 0.1
teacher_temp = 0.07
norm_eps = 1e-06
teacher_rate = math.log2(math.e) / teacher_temp
student_rate = math.log2(math.e) / student_temp

MIB = 1024 * 1024
BOTH = ("batch", "proto")
TILE = 256
WIDE = 512


def scores(left_rows, right_rows):
    return lax.dot_general(
        left_rows, right_rows, (((1,), (1,)), ((), ())), preferred_element_type=jnp.float32
    )


def unit_rows(values):
    lengths = jnp.sqrt(jnp.sum(values * values, axis=1, keepdims=True) + norm_eps)
    return (values / lengths, lengths)


def gelu(values):
    return 0.5 * values * (1.0 + lax.erf(values * math.sqrt(0.5)))


def whole(memory_space=pltpu.VMEM):
    return pl.BlockSpec(memory_space=memory_space)


def in_hbm(array):
    return pltpu.with_memory_space_constraint(array, pltpu.HBM)


def skipping(kernel, first, count):
    def trimmed(*refs):
        kernel(*refs[:first], *refs[first + count :])

    return trimmed


def part(index, size):
    return pl.ds(pl.multiple_of(index * size, size), size)


def lane_fold(values, combine):
    folded = values[:, :128]
    for start in range(128, values.shape[1], 128):
        folded = combine(folded, values[:, start : start + 128])
    return folded


def params(mib):
    return pltpu.CompilerParams(vmem_limit_bytes=mib * MIB)


def cost(flops, bytes_accessed, transcendentals=0):
    return pl.CostEstimate(
        flops=int(flops), bytes_accessed=int(bytes_accessed), transcendentals=int(transcendentals)
    )


def fetch(source, target, sems, first_row=0):
    count, rows = target.shape[:2]

    def chunk_copy(index):
        start = pl.multiple_of(first_row + index * rows, rows)
        return pltpu.make_async_copy(source.at[pl.ds(start, rows), :], target.at[index], sems.at[index])

    for index in range(count):
        chunk_copy(index).start()
    return lambda index: chunk_copy(index).wait()


def teacher_units_kernel(core_ref, emb_ref, unit_ref, half_ref):
    unit_ref[...] = unit_rows(emb_ref[...].astype(jnp.float32))[0].astype(jnp.bfloat16)
    half = half_ref.shape[0]
    half_ref[...] = unit_ref[part(core_ref[0], half), :]


def teacher_units(core, teacher_emb):
    rows, width = teacher_emb.shape
    return pl.pallas_call(
        teacher_units_kernel,
        in_specs=[whole(pltpu.SMEM), whole()],
        out_specs=[whole(), whole()],
        out_shape=[
            jax.ShapeDtypeStruct((rows, width), jnp.bfloat16),
            jax.ShapeDtypeStruct((rows // 2, width), jnp.bfloat16),
        ],
        compiler_params=params(4),
        cost_estimate=cost(4 * rows * width, 8 * rows * width),
        name="teacher_units",
    )(core, in_hbm(teacher_emb))


def front_kernel(
    index_ref, unit_ref, bias_ref, own_hbm, x_hbm, core_hbm, last_hbm, first_hbm, second_hbm, protos_hbm,
    tops_ref, keep_ref, give_ref, first_ref, second_ref, rows_ref, protos_ref, top_ref, sems, chunk_sems,
):
    rows = unit_ref.shape[0]
    steps, block = protos_ref.shape[:2]
    wide = min(WIDE, block)
    share = own_hbm.shape[0]
    arrived = fetch(protos_hbm, protos_ref, chunk_sems)
    copies = [
        pltpu.make_async_copy(source, rows_ref.at[slot * share : (slot + 1) * share, :], sems.at[slot])
        for slot, source in enumerate((own_hbm, x_hbm, core_hbm, last_hbm))
    ]
    copies.append(pltpu.make_async_copy(first_hbm, first_ref, sems.at[4]))
    copies.append(pltpu.make_async_copy(second_hbm, second_ref, sems.at[5]))
    for copy in copies:
        copy.start()
    top_ref[...] = jnp.full(top_ref.shape, -jnp.inf, jnp.float32)

    def step(index, carry):
        arrived(index)
        top = top_ref[:rows, :]
        for start in range(0, block, wide):
            products = scores(unit_ref[...], protos_ref[index, start : start + wide, :])
            top = jnp.maximum(top, lane_fold(products, jnp.maximum))
        top_ref[:rows, :] = top
        return carry

    lax.fori_loop(0, steps, step, 0)
    tops = jnp.max(jnp.transpose(top_ref[...]), axis=0, keepdims=True)
    tops_ref[...] = jnp.broadcast_to(tops[None], tops_ref.shape)
    for copy in copies:
        copy.wait()
    hidden = first_ref.shape[1]
    bias = bias_ref[:, part(index_ref[0], hidden)]
    h_first = gelu(
        jnp.dot(rows_ref[...], first_ref[...], preferred_element_type=jnp.float32) + bias
    ).astype(jnp.bfloat16)
    for start in range(0, second_ref.shape[1], 512):
        columns = slice(start, start + 512)
        product = jnp.dot(h_first, second_ref[:, columns], preferred_element_type=jnp.float32)
        keep_ref[:, columns] = product[: 2 * share]
        give_ref[:, columns] = product[2 * share :]


def front(index, unit, bias, rows, first, second, protos, order, copies, steps):
    share, features = rows[0].shape
    hidden, units = second.shape
    count, width = protos.shape
    return pl.pallas_call(
        skipping(front_kernel, 10, len(order)),
        in_specs=[whole(pltpu.SMEM), whole(), whole()] + [whole(pl.ANY)] * (7 + len(order)),
        out_specs=[whole()] * 3,
        out_shape=[jax.ShapeDtypeStruct((copies, 1, 256), jnp.float32)]
        + [jax.ShapeDtypeStruct((2 * share, units), jnp.float32)] * 2,
        scratch_shapes=[
            pltpu.VMEM(first.shape, jnp.bfloat16),
            pltpu.VMEM(second.shape, jnp.bfloat16),
            pltpu.VMEM((4 * share, features), jnp.bfloat16),
            pltpu.VMEM((steps, count // steps, width), jnp.bfloat16),
            pltpu.VMEM((256, 128), jnp.float32),
            pltpu.SemaphoreType.DMA((6,)),
            pltpu.SemaphoreType.DMA((steps,)),
        ],
        compiler_params=params(26),
        cost_estimate=cost(
            2 * unit.size * count + 8 * share * hidden * (features + units), 2 * width * count
        ),
        name="front",
    )(
        index, unit, in_hbm(bias.reshape(1, -1)), in_hbm(rows[0]), *rows[1:],
        in_hbm(first), in_hbm(second), in_hbm(protos), *order,
    )


def repel_kernel(group, index_ref, unit_ref, tops_ref, scale_ref, protos_hbm, *rest):
    out_refs, (protos_ref, sems, acc_ref, sum_ref, bias_ref) = rest[:-5], rest[-5:]
    rows, width = unit_ref.shape
    steps, block = protos_ref.shape[:2]
    wide = min(WIDE, block)
    arrived = fetch(protos_hbm, protos_ref, sems)
    first = index_ref[0] * group
    top = tops_ref[first]
    for other in range(1, group):
        top = jnp.maximum(top, tops_ref[first + other])
    bias_ref[...] = jnp.transpose(jnp.broadcast_to(top, (128, 256)))[:rows, :] * -teacher_rate
    acc_ref[...] = jnp.zeros(acc_ref.shape, jnp.float32)
    sum_ref[...] = jnp.zeros(sum_ref.shape, jnp.float32)

    def step(index, carry):
        arrived(index)
        bias = bias_ref[...]
        total = sum_ref[...]
        acc = acc_ref[...]
        for start in range(0, block, wide):
            protos = protos_ref[index, start : start + wide, :]
            products = scores(unit_ref[...], protos)
            pieces = []
            for lane in range(0, wide, 128):
                scaled = jnp.exp2(products[:, lane : lane + 128] * teacher_rate + bias)
                scaled = scaled * scale_ref[index, :, start + lane : start + lane + 128]
                total = total + scaled
                pieces.append(scaled.astype(jnp.bfloat16))
            acc = acc + jnp.dot(
                jnp.concatenate(pieces, axis=1), protos, preferred_element_type=jnp.float32
            )
        sum_ref[...] = total
        acc_ref[...] = acc
        return carry

    lax.fori_loop(0, steps, step, 0)
    total = jnp.sum(sum_ref[...], axis=1, keepdims=True)
    lanes = lax.broadcasted_iota(jnp.int32, sum_ref.shape, 1)
    sum_ref[...] = jnp.broadcast_to(total, sum_ref.shape)
    share = out_refs[0].shape[0]
    lanes = lanes[:share, :]
    for flip, out_ref in enumerate(out_refs):
        span = part(index_ref[1] ^ flip, share)
        total = sum_ref[span, :]
        out_ref[:, :width] = acc_ref[span, :].astype(out_ref.dtype)
        if flip == 0:
            out_ref[:, width:] = jnp.where(lanes == 0, total, 0.0)
        else:
            high = total.astype(jnp.bfloat16).astype(jnp.float32)
            middle = (total - high).astype(jnp.bfloat16).astype(jnp.float32)
            pieces = jnp.where(lanes == 0, high, jnp.where(lanes == 1, middle, total - high - middle))
            out_ref[:, width:] = jnp.where(lanes < 3, pieces, 0.0).astype(jnp.bfloat16)


def repel(index, unit, tops, scale, protos, order, proto_size):
    rows, width = unit.shape
    count = protos.shape[0]
    steps, _, block = scale.shape
    return pl.pallas_call(
        skipping(functools.partial(repel_kernel, proto_size), 5, len(order)),
        in_specs=[whole(pltpu.SMEM), whole(), whole(), whole(), whole(pl.ANY)] + [whole(pl.ANY)] * len(order),
        out_specs=[whole()] * proto_size,
        out_shape=[
            jax.ShapeDtypeStruct((rows // proto_size, width + 128), jnp.bfloat16 if flip else jnp.float32)
            for flip in range(proto_size)
        ],
        scratch_shapes=[
            pltpu.VMEM((steps, block, width), jnp.bfloat16),
            pltpu.SemaphoreType.DMA((steps,)),
            pltpu.VMEM((rows, width), jnp.float32),
            pltpu.VMEM((rows, 128), jnp.float32),
            pltpu.VMEM((rows, 128), jnp.float32),
        ],
        compiler_params=params(16),
        cost_estimate=cost(4 * rows * width * count, 2 * width * count, rows * count),
        name="repel",
    )(index, unit, tops, scale, in_hbm(protos), *order)


def attract_kernel(first_row, last, emb_ref, state_ref, protos_hbm, *rest):
    out_refs, scratch = rest[:-6], rest[-6:]
    protos_ref, sems, products_ref, acc_ref, sum_ref, top_ref = scratch
    width = emb_ref.shape[1]
    steps, block = protos_ref.shape[:2]
    arrived = fetch(protos_hbm, protos_ref, sems, first_row)
    old_top = state_ref[:, width + 128 :]
    top_ref[...] = old_top

    def first(index, carry):
        arrived(index)
        top = top_ref[...]
        for start in range(0, block, TILE):
            products = scores(emb_ref[...], protos_ref[index, start : start + TILE, :])
            products_ref[index, :, start : start + TILE] = products
            top = jnp.maximum(top, lane_fold(products, jnp.maximum))
        top_ref[...] = top
        return carry

    lax.fori_loop(0, steps, first, 0)
    top = jnp.broadcast_to(jnp.max(top_ref[...], axis=1, keepdims=True), top_ref.shape)
    fade = jnp.exp2((old_top - top) * student_rate)
    top_ref[...] = top
    sum_ref[...] = state_ref[:, width : width + 128] * fade
    acc_ref[...] = state_ref[:, :width] * jnp.tile(fade, (1, width // 128))

    def second(index, carry):
        top = top_ref[...]
        total = sum_ref[...]
        acc = acc_ref[...]
        for start in range(0, block, TILE):
            pieces = []
            for lane in range(start, start + TILE, 128):
                shifted = jnp.exp2((products_ref[index, :, lane : lane + 128] - top) * student_rate)
                total = total + shifted
                pieces.append(shifted.astype(jnp.bfloat16))
            acc = acc + jnp.dot(
                jnp.concatenate(pieces, axis=1),
                protos_ref[index, start : start + TILE, :],
                preferred_element_type=jnp.float32,
            )
        sum_ref[...] = total
        acc_ref[...] = acc
        return carry

    lax.fori_loop(0, steps, second, 0)
    if last:
        total = jnp.sum(sum_ref[...], axis=1, keepdims=True)
        sum_ref[...] = jnp.broadcast_to(total, sum_ref.shape)
    share = out_refs[0].shape[0]
    for slot, out_ref in enumerate(out_refs):
        rows = pl.ds(slot * share, share)
        out_ref[:, :width] = acc_ref[rows, :]
        out_ref[:, width : width + 128] = sum_ref[rows, :]
        out_ref[:, width + 128 :] = top_ref[rows, :]


def attract(emb, state, protos, first_row, count, steps, outputs):
    rows, width = emb.shape
    block = count // steps
    return pl.pallas_call(
        functools.partial(attract_kernel, first_row, outputs > 1),
        in_specs=[whole(), whole(), whole(pl.ANY)],
        out_specs=[whole()] * outputs,
        out_shape=[jax.ShapeDtypeStruct((rows // outputs, width + 256), jnp.float32)] * outputs,
        scratch_shapes=[
            pltpu.VMEM((steps, block, width), jnp.bfloat16),
            pltpu.SemaphoreType.DMA((steps,)),
            pltpu.VMEM((steps, rows, block), jnp.float32),
            pltpu.VMEM((rows, width), jnp.float32),
            pltpu.VMEM((rows, 128), jnp.float32),
            pltpu.VMEM((rows, 128), jnp.float32),
        ],
        compiler_params=params(24),
        cost_estimate=cost(4 * rows * width * count, 2 * width * count, rows * count),
        name="attract",
    )(emb, state, in_hbm(protos))


def three_pieces(values):
    high = values.astype(jnp.bfloat16)
    rest = values - high.astype(jnp.float32)
    middle = rest.astype(jnp.bfloat16)
    low = (rest - middle.astype(jnp.float32)).astype(jnp.bfloat16)
    return jnp.concatenate([high, middle, low, jnp.zeros((13, values.shape[1]), jnp.bfloat16)], axis=0)


def lane_scales(folded, protos_total):
    sums = [
        jnp.sum(jnp.transpose(folded[start : start + 128, :]), axis=0, keepdims=True)
        for start in range(0, folded.shape[0], 128)
    ]
    return 1.0 / (protos_total * jnp.concatenate(sums, axis=1))


def give_sums(copies_ref, totals):
    rows = [totals[:, start : start + 128] for start in range(0, totals.shape[1], 128)]
    spare = copies_ref.shape[1] - len(rows)
    if spare:
        rows.append(jnp.zeros((spare, 128), jnp.float32))
    packed = jnp.concatenate(rows, axis=0).astype(jnp.bfloat16)
    copies_ref[...] = jnp.broadcast_to(packed[None], copies_ref.shape)


def take_scales(parts_ref, scale_ref):
    crops_total = scale_ref.shape[1]
    sums = jnp.sum(parts_ref[...].astype(jnp.float32), axis=0)
    for row in range(crops_total // 128):
        scale_ref[:, row * 128 : row * 128 + 128] = 1.0 / (crops_total * sums[row : row + 1, :])


def sums_shape(copies, crops_total):
    return (copies, -(-crops_total // 2048) * 16, 128)


def first_sweep_kernel(
    chunk, protos_total, index_ref, protos_hbm, mine_hbm, other_hbm, bias_ref, copies_ref, weights_hbm, protos_ref, units_ref, weights_ref, rounded_ref, scale_ref, sems, out_sems,
):
    thin, crops_total = weights_ref.shape
    half = mine_hbm.shape[0]
    core = index_ref[1]
    copies = (
        pltpu.make_async_copy(protos_hbm.at[part(index_ref[0], thin), :], protos_ref, sems.at[0]),
        pltpu.make_async_copy(mine_hbm, units_ref.at[part(core, half), :], sems.at[1]),
        pltpu.make_async_copy(other_hbm, units_ref.at[part(1 - core, half), :], sems.at[2]),
    )
    for copy in copies:
        copy.start()
    for copy in copies:
        copy.wait()

    def chunk_out(index):
        return pltpu.make_async_copy(
            rounded_ref.at[index], weights_hbm.at[part(index, chunk), :], out_sems.at[index]
        )

    def weigh(index, carry):
        rows = part(index, chunk)
        protos = protos_ref[rows, :]
        folded = jnp.zeros((chunk, 128), jnp.float32)
        for start in range(0, crops_total, TILE):
            columns = slice(start, start + TILE)
            products = scores(protos, units_ref[columns, :])
            weights = jnp.exp2(products * teacher_rate + bias_ref[:, columns])
            weights_ref[rows, columns] = weights
            rounded_ref[index, :, columns] = weights.astype(jnp.bfloat16)
            folded = folded + lane_fold(weights, jnp.add)
        sums = jnp.sum(folded, axis=1, keepdims=True)
        scale_ref[rows, :] = jnp.broadcast_to(1.0 / (protos_total * sums), (chunk, 128))
        chunk_out(index).start()
        return carry

    lax.fori_loop(0, thin // chunk, weigh, 0)
    small = min(thin, 64)

    def add_up(index, totals):
        rows = part(index, small)
        scaled = weights_ref[rows, :] * jnp.tile(scale_ref[rows, :], (1, crops_total // 128))
        return totals + jnp.sum(scaled.reshape(-1, 8, crops_total), axis=0)

    totals = lax.fori_loop(0, thin // small, add_up, jnp.zeros((8, crops_total), jnp.float32))
    give_sums(copies_ref, jnp.sum(totals, axis=0, keepdims=True))
    for index in range(thin // chunk):
        chunk_out(index).wait()


def first_sweep(index, protos, mine, other, base, order, copies, thin, protos_total):
    width = protos.shape[1]
    crops_total = 2 * mine.shape[0]
    chunk = min(thin, 1024)
    return pl.pallas_call(
        skipping(functools.partial(first_sweep_kernel, chunk, protos_total), 5, len(order)),
        in_specs=[whole(pltpu.SMEM), whole(pl.ANY), whole(pl.ANY), whole(pl.ANY), whole()]
        + [whole(pl.ANY)] * len(order),
        out_specs=[whole(), whole(pl.ANY)],
        out_shape=[
            jax.ShapeDtypeStruct(sums_shape(copies, crops_total), jnp.bfloat16),
            pltpu.HBM((thin, crops_total), jnp.bfloat16),
        ],
        scratch_shapes=[
            pltpu.VMEM((thin, width), jnp.bfloat16),
            pltpu.VMEM((crops_total, width), jnp.bfloat16),
            pltpu.VMEM((thin, crops_total), jnp.float32),
            pltpu.VMEM((thin // chunk, chunk, crops_total), jnp.bfloat16),
            pltpu.VMEM((thin, 128), jnp.float32),
            pltpu.SemaphoreType.DMA((3,)),
            pltpu.SemaphoreType.DMA((thin // chunk,)),
        ],
        compiler_params=params(32 if crops_total <= 2048 else 56),
        cost_estimate=cost(2 * thin * width * crops_total, 2 * thin * crops_total, thin * crops_total),
        name="first_sweep",
    )(index, in_hbm(protos), mine, other, base, *order)


def fetch_rows(weights_hbm, weights_ref, sems):
    steps, chunk, _ = weights_ref.shape

    def rows_copy(index):
        return pltpu.make_async_copy(
            weights_hbm.at[part(index, chunk), :], weights_ref.at[index], sems.at[index]
        )

    for index in range(steps):
        rows_copy(index).start()
    return lambda index: rows_copy(index).wait()


def scaled_fold(weights_ref, index, scale_ref):
    _, chunk, crops_total = weights_ref.shape
    folds = []
    for row in range(0, chunk, 64):
        fold = None
        for start in range(0, crops_total, TILE):
            columns = slice(start, start + TILE)
            weights = weights_ref[index, row : row + 64, columns].astype(jnp.float32)
            scaled = lane_fold(weights * scale_ref[:, columns], jnp.add)
            fold = scaled if fold is None else fold + scaled
        folds.append(fold)
    return jnp.concatenate(folds, axis=0)


def next_sweep_kernel(
    protos_total, weights_hbm, parts_ref, copies_ref, weights_ref, scale_ref, pieces_ref, totals_ref, sems,
):
    steps, chunk, crops_total = weights_ref.shape
    arrived = fetch_rows(weights_hbm, weights_ref, sems)
    take_scales(parts_ref, scale_ref)
    totals_ref[...] = jnp.zeros(totals_ref.shape, jnp.float32)

    def weigh(index):
        return three_pieces(lane_scales(scaled_fold(weights_ref, index, scale_ref), protos_total))

    def add_up(index):
        return jnp.dot(pieces_ref[...], weights_ref[index], preferred_element_type=jnp.float32)

    arrived(0)
    pieces_ref[...] = weigh(0)

    def sweep(index, carry):
        arrived(index)
        sums = add_up(index - 1)
        pieces = weigh(index)
        totals_ref[...] += sums
        pieces_ref[...] = pieces
        return carry

    lax.fori_loop(1, steps, sweep, 0)
    totals = totals_ref[...] + add_up(steps - 1)
    give_sums(copies_ref, jnp.sum(totals, axis=0, keepdims=True))


def next_sweep(weights, parts, order, protos_total):
    thin, crops_total = weights.shape
    copies = parts.shape[0]
    chunk = min(thin, 256)
    return pl.pallas_call(
        skipping(functools.partial(next_sweep_kernel, protos_total), 2, len(order)),
        in_specs=[whole(pl.ANY), whole()] + [whole(pl.ANY)] * len(order),
        out_specs=whole(),
        out_shape=jax.ShapeDtypeStruct(sums_shape(copies, crops_total), jnp.bfloat16),
        scratch_shapes=[
            pltpu.VMEM((thin // chunk, chunk, crops_total), jnp.bfloat16),
            pltpu.VMEM((1, crops_total), jnp.float32),
            pltpu.VMEM((16, chunk), jnp.bfloat16),
            pltpu.VMEM((16, crops_total), jnp.float32),
            pltpu.SemaphoreType.DMA((thin // chunk,)),
        ],
        compiler_params=params(16 if crops_total <= 2048 else 50),
        cost_estimate=cost(8 * thin * crops_total, 2 * thin * crops_total),
        name="next_sweep",
    )(in_hbm(weights), parts, *order)


def last_scales_kernel(
    protos_total, weights_hbm, parts_ref, copies_ref, weights_ref, scale_ref, out_ref, sems,
):
    steps, chunk, crops_total = weights_ref.shape
    arrived = fetch_rows(weights_hbm, weights_ref, sems)
    take_scales(parts_ref, scale_ref)

    def weigh(index, carry):
        arrived(index)
        out_ref[:, part(index, chunk)] = lane_scales(
            scaled_fold(weights_ref, index, scale_ref), protos_total
        )
        return carry

    lax.fori_loop(0, steps, weigh, 0)
    copies_ref[...] = jnp.broadcast_to(out_ref[...][None], copies_ref.shape)


def last_scales(weights, parts, order, copies, protos_total):
    thin, crops_total = weights.shape
    chunk = min(thin, 256)
    return pl.pallas_call(
        skipping(functools.partial(last_scales_kernel, protos_total), 2, len(order)),
        in_specs=[whole(pl.ANY), whole()] + [whole(pl.ANY)] * len(order),
        out_specs=whole(),
        out_shape=jax.ShapeDtypeStruct((copies, 1, thin), jnp.float32),
        scratch_shapes=[
            pltpu.VMEM((thin // chunk, chunk, crops_total), jnp.bfloat16),
            pltpu.VMEM((1, crops_total), jnp.float32),
            pltpu.VMEM((1, thin), jnp.float32),
            pltpu.SemaphoreType.DMA((thin // chunk,)),
        ],
        compiler_params=params(16 if crops_total <= 2048 else 50),
        cost_estimate=cost(4 * thin * crops_total, 2 * thin * crops_total),
        name="last_scales",
    )(in_hbm(weights), parts, *order)


def student_middle_kernel(
    index_ref, keep_ref, core_ref, x_ref, bias_ref, own_ref, partner_ref, other_ref, last_ref, last_bias_ref,
    unit_ref, emb_ref, lengths_ref, hidden_ref,
):
    share = x_ref.shape[0]
    block = own_ref.shape[0]
    sums = keep_ref[:share, :] + core_ref[:share, :] + x_ref[...]
    hidden_ref[...] = gelu(sums + bias_ref[...]).astype(jnp.bfloat16)
    index = index_ref[0]
    weights = ((0, own_ref[...]), (2, partner_ref[...]), (1, other_ref[...]), (3, last_ref[...]))
    bottleneck = jnp.broadcast_to(last_bias_ref[...], unit_ref.shape)
    for flip, weight in weights:
        bottleneck = bottleneck + jnp.dot(
            hidden_ref[:, part(index ^ flip, block)], weight, preferred_element_type=jnp.float32
        )
    unit, lengths = unit_rows(bottleneck)
    unit_ref[...] = unit
    emb_ref[...] = unit.astype(jnp.bfloat16)
    lengths_ref[...] = jnp.broadcast_to(lengths, lengths_ref.shape)


def student_middle(index, keep, core_rows, x_rows, bias, weights, last_bias):
    share, units = x_rows.shape
    width = weights[0].shape[1]
    return pl.pallas_call(
        student_middle_kernel,
        in_specs=[whole(pltpu.SMEM)] + [whole()] * 9,
        out_specs=[whole()] * 3,
        out_shape=[
            jax.ShapeDtypeStruct((share, width), jnp.float32),
            jax.ShapeDtypeStruct((share, width), jnp.bfloat16),
            jax.ShapeDtypeStruct((share, 128), jnp.float32),
        ],
        scratch_shapes=[pltpu.VMEM((share, units), jnp.bfloat16)],
        compiler_params=params(12),
        cost_estimate=cost(2 * share * units * width, 2 * units * width + 16 * share * units),
        name="student_middle",
    )(index, keep, core_rows, x_rows, in_hbm(bias.reshape(1, -1)), in_hbm(weights[0]), *weights[1:], in_hbm(last_bias.reshape(1, -1)))


def finish_kernel(unit_ref, lengths_ref, *rest):
    out_ref, blocks = rest[-1], rest[:-1]
    attracts, repels = blocks[: len(blocks) // 2], blocks[len(blocks) // 2 :]
    width = unit_ref.shape[1]
    row_top = functools.reduce(jnp.maximum, [ref[:, width + 128 :] for ref in attracts])
    attract_sum = repel_sum = 0.0
    row_sum = column_sum = 0.0
    for ref in attracts:
        fade = jnp.exp2((ref[:, width + 128 :] - row_top) * student_rate)
        row_sum = row_sum + ref[:, width : width + 128] * fade
        attract_sum = attract_sum + ref[:, :width] * jnp.tile(fade, (1, width // 128))
    for ref in repels:
        column_sum = column_sum + jnp.sum(ref[:, width:].astype(jnp.float32), axis=1, keepdims=True)
        repel_sum = repel_sum + ref[:, :width].astype(jnp.float32)
    emb_grad = (
        attract_sum / jnp.tile(row_sum, (1, width // 128))
        - repel_sum / column_sum
    ) / student_temp
    unit = unit_ref[...]
    along = jnp.sum(unit * emb_grad, axis=1, keepdims=True)
    out_ref[...] = (emb_grad - unit * along) / jnp.tile(lengths_ref[...], (1, width // 128))


def finish(unit, lengths, attracts, repels):
    return pl.pallas_call(
        finish_kernel,
        in_specs=[whole()] * (2 + len(attracts) + len(repels)),
        out_specs=whole(),
        out_shape=jax.ShapeDtypeStruct(unit.shape, jnp.float32),
        compiler_params=params(8),
        cost_estimate=cost(40 * unit.size, 40 * unit.size),
        name="finish",
    )(unit, lengths, *attracts, *repels)


def swap(values, axis, flip):
    return lax.ppermute(values, axis, [(i, i ^ flip) for i in range(lax.axis_size(axis))])


def bit_reversed(values, count):
    bits = count.bit_length() - 1
    split = values.reshape((2,) * bits + values.shape[1:])
    turned = jnp.transpose(split, tuple(reversed(range(bits))) + tuple(range(bits, split.ndim)))
    return turned.reshape(values.shape)


def gather_batch(values):
    step = lax.axis_size("batch") // 2
    stages = [values]
    while step:
        other = swap(values, "batch", step)
        upper = (lax.axis_index("batch") // step) % 2
        values = jnp.where(
            upper == 0, jnp.concatenate([values, other]), jnp.concatenate([other, values])
        )
        stages.append(values)
        step //= 2
    return stages


def send_blocks(blocks):
    return [blocks[0]] + [swap(block, "proto", flip) for flip, block in enumerate(blocks) if flip]


def all_to_all(copies, axes):
    return lax.all_to_all(copies, axes, 0, 0, tiled=True)


def body(crops, teacher_emb, w_first, b_first, w_second, b_second, w_third, b_third, protos):
    batch_index = lax.axis_index("batch")
    proto_index = lax.axis_index("proto")
    batch_size = lax.axis_size("batch")
    proto_size = lax.axis_size("proto")
    devices = batch_size * proto_size
    share_rows = crops.shape[0]
    group_rows = teacher_emb.shape[0]
    crops_total = group_rows * batch_size
    protos_total = protos.shape[0] * proto_size
    count, width = protos.shape
    thin = count // batch_size
    core = proto_index % 2
    proto_ref = proto_index.reshape(1)
    thin_ref = jnp.stack([batch_index, core])
    wide_ref = jnp.stack([batch_index, proto_index])

    own_unit, half = teacher_units(core.reshape(1), teacher_emb)
    stages = gather_batch(half)
    mine = stages[-1]
    other = swap(mine, "proto", 1)

    crops_x = swap(crops, "proto", 2)
    rows = [crops, crops_x, swap(crops, "proto", 1), swap(crops_x, "proto", 1)]
    third_x = swap(w_third, "proto", 2)
    thirds = [w_third, third_x, swap(w_third, "proto", 1), swap(third_x, "proto", 1)]
    top_copies, keep, give = front(
        proto_ref, own_unit, b_first, rows, w_first, w_second, protos, (stages[2], third_x), devices, 8
    )
    all_tops = all_to_all(top_copies, BOTH)
    tops = jnp.max(all_tops.reshape(batch_size, proto_size, 256)[:, :, :group_rows], axis=1)
    tops = bit_reversed(tops, batch_size).reshape(batch_size, 2, group_rows // 2)
    base = jnp.transpose(tops, (1, 0, 2)).reshape(1, crops_total) * -teacher_rate

    core_rows = swap(give, "proto", 1)
    x_sent = keep[share_rows:] + core_rows[share_rows:]
    x_rows = swap(x_sent, "proto", 2)
    unit, rounded, lengths = student_middle(
        proto_ref, keep, core_rows, x_rows, b_second, thirds, b_third
    )
    student_emb = jnp.concatenate([rounded] + [swap(rounded, "proto", flip) for flip in range(1, proto_size)])
    empty = jnp.concatenate(
        [jnp.zeros((group_rows, width + 128), jnp.float32), jnp.full((group_rows, 128), -1e30, jnp.float32)], axis=1
    )
    (state,) = attract(student_emb, empty, protos, 0, count // 2, 4, 1)
    slots = attract(student_emb, state, protos, count // 2, count // 2, 4, proto_size)
    attract_parts = send_blocks(slots)

    copies, weights = first_sweep(thin_ref, protos, mine, other, base, (x_sent, *thirds[2:]), devices, thin, protos_total)
    for _ in range(ITERS - 2):
        copies = next_sweep(weights, all_to_all(copies, BOTH), (rounded,), protos_total)
    scale_copies = last_scales(weights, all_to_all(copies, BOTH), (state,), batch_size, protos_total)
    all_scale = all_to_all(scale_copies, "batch")
    repels = repel(wide_ref, own_unit, all_tops, all_scale, protos, (slots[0],), proto_size)
    return finish(unit, lengths, attract_parts, send_blocks(repels))


def solution(mesh):
    in_specs = (
        P(("batch", "proto"), None),
        P("batch", None),
        P(None, "proto"),
        P(),
        P("proto", None),
        P(),
        P("proto", None),
        P(),
        P("proto", None),
    )
    out_specs = P(("batch", "proto"), None)
    return jax.shard_map(body, mesh=mesh, in_specs=in_specs, out_specs=out_specs, check_vma=False)
```

```python
import functools
import math

import jax
import jax.numpy as jnp
from jax import lax
from jax.experimental import pallas as pl
from jax.experimental.pallas import tpu as pltpu
from jax.sharding import PartitionSpec as P

ITERS = 3

student_temp = 0.1
teacher_temp = 0.07
norm_eps = 1e-06
teacher_rate = math.log2(math.e) / teacher_temp
student_rate = math.log2(math.e) / student_temp

MIB = 1024 * 1024
BOTH = ("batch", "proto")
TILE = 256
WIDE = 512


def scores(left_rows, right_rows):
    return lax.dot_general(
        left_rows, right_rows, (((1,), (1,)), ((), ())), preferred_element_type=jnp.float32
    )


def unit_rows(values):
    lengths = jnp.sqrt(jnp.sum(values * values, axis=1, keepdims=True) + norm_eps)
    return (values / lengths, lengths)


def gelu(values):
    return 0.5 * values * (1.0 + lax.erf(values * math.sqrt(0.5)))


def whole(memory_space=pltpu.VMEM):
    return pl.BlockSpec(memory_space=memory_space)


def in_hbm(array):
    return pltpu.with_memory_space_constraint(array, pltpu.HBM)


def skipping(kernel, first, count):
    def trimmed(*refs):
        kernel(*refs[:first], *refs[first + count :])

    return trimmed


def part(index, size):
    return pl.ds(pl.multiple_of(index * size, size), size)


def lane_fold(values, combine):
    folded = values[:, :128]
    for start in range(128, values.shape[1], 128):
        folded = combine(folded, values[:, start : start + 128])
    return folded


def params(mib):
    return pltpu.CompilerParams(vmem_limit_bytes=mib * MIB)


def cost(flops, bytes_accessed, transcendentals=0):
    return pl.CostEstimate(
        flops=int(flops), bytes_accessed=int(bytes_accessed), transcendentals=int(transcendentals)
    )


def fetch(source, target, sems, first_row=0):
    count, rows = target.shape[:2]

    def chunk_copy(index):
        start = pl.multiple_of(first_row + index * rows, rows)
        return pltpu.make_async_copy(source.at[pl.ds(start, rows), :], target.at[index], sems.at[index])

    for index in range(count):
        chunk_copy(index).start()
    return lambda index: chunk_copy(index).wait()


def teacher_units_kernel(core_ref, emb_ref, unit_ref, half_ref):
    unit_ref[...] = unit_rows(emb_ref[...].astype(jnp.float32))[0].astype(jnp.bfloat16)
    half = half_ref.shape[0]
    half_ref[...] = unit_ref[part(core_ref[0], half), :]


def teacher_units(core, teacher_emb):
    rows, width = teacher_emb.shape
    return pl.pallas_call(
        teacher_units_kernel,
        in_specs=[whole(pltpu.SMEM), whole()],
        out_specs=[whole(), whole()],
        out_shape=[
            jax.ShapeDtypeStruct((rows, width), jnp.bfloat16),
            jax.ShapeDtypeStruct((rows // 2, width), jnp.bfloat16),
        ],
        compiler_params=params(4),
        cost_estimate=cost(4 * rows * width, 8 * rows * width),
        name="teacher_units",
    )(core, in_hbm(teacher_emb))


def wide_tops_kernel(unit_ref, protos_hbm, tops_ref, protos_ref, sems, top_ref):
    rows = unit_ref.shape[0]
    steps, block = protos_ref.shape[:2]
    wide = min(WIDE, block)
    arrived = fetch(protos_hbm, protos_ref, sems)
    top_ref[...] = jnp.full(top_ref.shape, -jnp.inf, jnp.float32)

    def step(index, carry):
        arrived(index)
        top = top_ref[:rows, :]
        for start in range(0, block, wide):
            products = scores(unit_ref[...], protos_ref[index, start : start + wide, :])
            top = jnp.maximum(top, lane_fold(products, jnp.maximum))
        top_ref[:rows, :] = top
        return carry

    lax.fori_loop(0, steps, step, 0)
    tops = jnp.max(jnp.transpose(top_ref[...]), axis=0, keepdims=True)
    tops_ref[...] = jnp.broadcast_to(tops[None], tops_ref.shape)


def wide_tops(unit, protos, order, copies, steps):
    rows, width = unit.shape
    count = protos.shape[0]
    return pl.pallas_call(
        skipping(wide_tops_kernel, 2, len(order)),
        in_specs=[whole(), whole(pl.ANY)] + [whole(pl.ANY)] * len(order),
        out_specs=whole(),
        out_shape=jax.ShapeDtypeStruct((copies, 1, 256), jnp.float32),
        scratch_shapes=[
            pltpu.VMEM((steps, count // steps, width), jnp.bfloat16),
            pltpu.SemaphoreType.DMA((steps,)),
            pltpu.VMEM((256, 128), jnp.float32),
        ],
        compiler_params=params(16),
        cost_estimate=cost(2 * rows * width * count, 2 * width * count),
        name="wide_tops",
    )(unit, in_hbm(protos), *order)


def repel_kernel(group, index_ref, unit_ref, tops_ref, scale_ref, protos_hbm, *rest):
    out_refs, (protos_ref, sems, acc_ref, sum_ref, bias_ref) = rest[:-5], rest[-5:]
    rows, width = unit_ref.shape
    steps, block = protos_ref.shape[:2]
    wide = min(WIDE, block)
    arrived = fetch(protos_hbm, protos_ref, sems)
    first = index_ref[0] * group
    top = tops_ref[first]
    for other in range(1, group):
        top = jnp.maximum(top, tops_ref[first + other])
    bias_ref[...] = jnp.transpose(jnp.broadcast_to(top, (128, 256)))[:rows, :] * -teacher_rate
    acc_ref[...] = jnp.zeros(acc_ref.shape, jnp.float32)
    sum_ref[...] = jnp.zeros(sum_ref.shape, jnp.float32)

    def step(index, carry):
        arrived(index)
        bias = bias_ref[...]
        total = sum_ref[...]
        acc = acc_ref[...]
        for start in range(0, block, wide):
            protos = protos_ref[index, start : start + wide, :]
            products = scores(unit_ref[...], protos)
            pieces = []
            for lane in range(0, wide, 128):
                scaled = jnp.exp2(products[:, lane : lane + 128] * teacher_rate + bias)
                scaled = scaled * scale_ref[index, :, start + lane : start + lane + 128]
                total = total + scaled
                pieces.append(scaled.astype(jnp.bfloat16))
            acc = acc + jnp.dot(
                jnp.concatenate(pieces, axis=1), protos, preferred_element_type=jnp.float32
            )
        sum_ref[...] = total
        acc_ref[...] = acc
        return carry

    lax.fori_loop(0, steps, step, 0)
    total = jnp.sum(sum_ref[...], axis=1, keepdims=True)
    lanes = lax.broadcasted_iota(jnp.int32, sum_ref.shape, 1)
    sum_ref[...] = jnp.broadcast_to(total, sum_ref.shape)
    share = out_refs[0].shape[0]
    lanes = lanes[:share, :]
    for flip, out_ref in enumerate(out_refs):
        span = part(index_ref[1] ^ flip, share)
        total = sum_ref[span, :]
        out_ref[:, :width] = acc_ref[span, :].astype(out_ref.dtype)
        if flip == 0:
            out_ref[:, width:] = jnp.where(lanes == 0, total, 0.0)
        else:
            high = total.astype(jnp.bfloat16).astype(jnp.float32)
            middle = (total - high).astype(jnp.bfloat16).astype(jnp.float32)
            pieces = jnp.where(lanes == 0, high, jnp.where(lanes == 1, middle, total - high - middle))
            out_ref[:, width:] = jnp.where(lanes < 3, pieces, 0.0).astype(jnp.bfloat16)


def repel(index, unit, tops, scale, protos, order, proto_size):
    rows, width = unit.shape
    count = protos.shape[0]
    steps, _, block = scale.shape
    return pl.pallas_call(
        skipping(functools.partial(repel_kernel, proto_size), 5, len(order)),
        in_specs=[whole(pltpu.SMEM), whole(), whole(), whole(), whole(pl.ANY)] + [whole(pl.ANY)] * len(order),
        out_specs=[whole()] * proto_size,
        out_shape=[
            jax.ShapeDtypeStruct((rows // proto_size, width + 128), jnp.bfloat16 if flip else jnp.float32)
            for flip in range(proto_size)
        ],
        scratch_shapes=[
            pltpu.VMEM((steps, block, width), jnp.bfloat16),
            pltpu.SemaphoreType.DMA((steps,)),
            pltpu.VMEM((rows, width), jnp.float32),
            pltpu.VMEM((rows, 128), jnp.float32),
            pltpu.VMEM((rows, 128), jnp.float32),
        ],
        compiler_params=params(16),
        cost_estimate=cost(4 * rows * width * count, 2 * width * count, rows * count),
        name="repel",
    )(index, unit, tops, scale, in_hbm(protos), *order)


def attract_kernel(first_row, last, emb_ref, state_ref, protos_hbm, *rest):
    out_refs, scratch = rest[:-6], rest[-6:]
    protos_ref, sems, products_ref, acc_ref, sum_ref, top_ref = scratch
    width = emb_ref.shape[1]
    steps, block = protos_ref.shape[:2]
    arrived = fetch(protos_hbm, protos_ref, sems, first_row)
    old_top = state_ref[:, width + 128 :]
    top_ref[...] = old_top

    def first(index, carry):
        arrived(index)
        top = top_ref[...]
        for start in range(0, block, TILE):
            products = scores(emb_ref[...], protos_ref[index, start : start + TILE, :])
            products_ref[index, :, start : start + TILE] = products
            top = jnp.maximum(top, lane_fold(products, jnp.maximum))
        top_ref[...] = top
        return carry

    lax.fori_loop(0, steps, first, 0)
    top = jnp.broadcast_to(jnp.max(top_ref[...], axis=1, keepdims=True), top_ref.shape)
    fade = jnp.exp2((old_top - top) * student_rate)
    top_ref[...] = top
    sum_ref[...] = state_ref[:, width : width + 128] * fade
    acc_ref[...] = state_ref[:, :width] * jnp.tile(fade, (1, width // 128))

    def second(index, carry):
        top = top_ref[...]
        total = sum_ref[...]
        acc = acc_ref[...]
        for start in range(0, block, TILE):
            pieces = []
            for lane in range(start, start + TILE, 128):
                shifted = jnp.exp2((products_ref[index, :, lane : lane + 128] - top) * student_rate)
                total = total + shifted
                pieces.append(shifted.astype(jnp.bfloat16))
            acc = acc + jnp.dot(
                jnp.concatenate(pieces, axis=1),
                protos_ref[index, start : start + TILE, :],
                preferred_element_type=jnp.float32,
            )
        sum_ref[...] = total
        acc_ref[...] = acc
        return carry

    lax.fori_loop(0, steps, second, 0)
    if last:
        total = jnp.sum(sum_ref[...], axis=1, keepdims=True)
        sum_ref[...] = jnp.broadcast_to(total, sum_ref.shape)
    share = out_refs[0].shape[0]
    for slot, out_ref in enumerate(out_refs):
        rows = pl.ds(slot * share, share)
        out_ref[:, :width] = acc_ref[rows, :]
        out_ref[:, width : width + 128] = sum_ref[rows, :]
        out_ref[:, width + 128 :] = top_ref[rows, :]


def attract(emb, state, protos, first_row, count, steps, outputs):
    rows, width = emb.shape
    block = count // steps
    return pl.pallas_call(
        functools.partial(attract_kernel, first_row, outputs > 1),
        in_specs=[whole(), whole(), whole(pl.ANY)],
        out_specs=[whole()] * outputs,
        out_shape=[jax.ShapeDtypeStruct((rows // outputs, width + 256), jnp.float32)] * outputs,
        scratch_shapes=[
            pltpu.VMEM((steps, block, width), jnp.bfloat16),
            pltpu.SemaphoreType.DMA((steps,)),
            pltpu.VMEM((steps, rows, block), jnp.float32),
            pltpu.VMEM((rows, width), jnp.float32),
            pltpu.VMEM((rows, 128), jnp.float32),
            pltpu.VMEM((rows, 128), jnp.float32),
        ],
        compiler_params=params(24),
        cost_estimate=cost(4 * rows * width * count, 2 * width * count, rows * count),
        name="attract",
    )(emb, state, in_hbm(protos))


def three_pieces(values):
    high = values.astype(jnp.bfloat16)
    rest = values - high.astype(jnp.float32)
    middle = rest.astype(jnp.bfloat16)
    low = (rest - middle.astype(jnp.float32)).astype(jnp.bfloat16)
    return jnp.concatenate([high, middle, low, jnp.zeros((13, values.shape[1]), jnp.bfloat16)], axis=0)


def lane_scales(folded, protos_total):
    sums = [
        jnp.sum(jnp.transpose(folded[start : start + 128, :]), axis=0, keepdims=True)
        for start in range(0, folded.shape[0], 128)
    ]
    return 1.0 / (protos_total * jnp.concatenate(sums, axis=1))


def give_sums(copies_ref, totals):
    rows = [totals[:, start : start + 128] for start in range(0, totals.shape[1], 128)]
    spare = copies_ref.shape[1] - len(rows)
    if spare:
        rows.append(jnp.zeros((spare, 128), jnp.float32))
    packed = jnp.concatenate(rows, axis=0).astype(jnp.bfloat16)
    copies_ref[...] = jnp.broadcast_to(packed[None], copies_ref.shape)


def take_scales(parts_ref, scale_ref):
    crops_total = scale_ref.shape[1]
    sums = jnp.sum(parts_ref[...].astype(jnp.float32), axis=0)
    for row in range(crops_total // 128):
        scale_ref[:, row * 128 : row * 128 + 128] = 1.0 / (crops_total * sums[row : row + 1, :])


def sums_shape(copies, crops_total):
    return (copies, -(-crops_total // 2048) * 16, 128)


def first_sweep_kernel(
    chunk, protos_total, index_ref, protos_hbm, mine_hbm, other_hbm, bias_ref, copies_ref, weights_hbm, protos_ref, units_ref, weights_ref, rounded_ref, scale_ref, sems, out_sems,
):
    thin, crops_total = weights_ref.shape
    half = mine_hbm.shape[0]
    core = index_ref[1]
    copies = (
        pltpu.make_async_copy(protos_hbm.at[part(index_ref[0], thin), :], protos_ref, sems.at[0]),
        pltpu.make_async_copy(mine_hbm, units_ref.at[part(core, half), :], sems.at[1]),
        pltpu.make_async_copy(other_hbm, units_ref.at[part(1 - core, half), :], sems.at[2]),
    )
    for copy in copies:
        copy.start()
    for copy in copies:
        copy.wait()

    def chunk_out(index):
        return pltpu.make_async_copy(
            rounded_ref.at[index], weights_hbm.at[part(index, chunk), :], out_sems.at[index]
        )

    def weigh(index, carry):
        rows = part(index, chunk)
        protos = protos_ref[rows, :]
        folded = jnp.zeros((chunk, 128), jnp.float32)
        for start in range(0, crops_total, TILE):
            columns = slice(start, start + TILE)
            products = scores(protos, units_ref[columns, :])
            weights = jnp.exp2(products * teacher_rate + bias_ref[:, columns])
            weights_ref[rows, columns] = weights
            rounded_ref[index, :, columns] = weights.astype(jnp.bfloat16)
            folded = folded + lane_fold(weights, jnp.add)
        sums = jnp.sum(folded, axis=1, keepdims=True)
        scale_ref[rows, :] = jnp.broadcast_to(1.0 / (protos_total * sums), (chunk, 128))
        chunk_out(index).start()
        return carry

    lax.fori_loop(0, thin // chunk, weigh, 0)
    small = min(thin, 64)

    def add_up(index, totals):
        rows = part(index, small)
        scaled = weights_ref[rows, :] * jnp.tile(scale_ref[rows, :], (1, crops_total // 128))
        return totals + jnp.sum(scaled.reshape(-1, 8, crops_total), axis=0)

    totals = lax.fori_loop(0, thin // small, add_up, jnp.zeros((8, crops_total), jnp.float32))
    give_sums(copies_ref, jnp.sum(totals, axis=0, keepdims=True))
    for index in range(thin // chunk):
        chunk_out(index).wait()


def first_sweep(index, protos, mine, other, base, order, copies, thin, protos_total):
    width = protos.shape[1]
    crops_total = 2 * mine.shape[0]
    chunk = min(thin, 1024)
    return pl.pallas_call(
        skipping(functools.partial(first_sweep_kernel, chunk, protos_total), 5, len(order)),
        in_specs=[whole(pltpu.SMEM), whole(pl.ANY), whole(pl.ANY), whole(pl.ANY), whole()]
        + [whole(pl.ANY)] * len(order),
        out_specs=[whole(), whole(pl.ANY)],
        out_shape=[
            jax.ShapeDtypeStruct(sums_shape(copies, crops_total), jnp.bfloat16),
            pltpu.HBM((thin, crops_total), jnp.bfloat16),
        ],
        scratch_shapes=[
            pltpu.VMEM((thin, width), jnp.bfloat16),
            pltpu.VMEM((crops_total, width), jnp.bfloat16),
            pltpu.VMEM((thin, crops_total), jnp.float32),
            pltpu.VMEM((thin // chunk, chunk, crops_total), jnp.bfloat16),
            pltpu.VMEM((thin, 128), jnp.float32),
            pltpu.SemaphoreType.DMA((3,)),
            pltpu.SemaphoreType.DMA((thin // chunk,)),
        ],
        compiler_params=params(32 if crops_total <= 2048 else 56),
        cost_estimate=cost(2 * thin * width * crops_total, 2 * thin * crops_total, thin * crops_total),
        name="first_sweep",
    )(index, in_hbm(protos), mine, other, base, *order)


def fetch_rows(weights_hbm, weights_ref, sems):
    steps, chunk, _ = weights_ref.shape

    def rows_copy(index):
        return pltpu.make_async_copy(
            weights_hbm.at[part(index, chunk), :], weights_ref.at[index], sems.at[index]
        )

    for index in range(steps):
        rows_copy(index).start()
    return lambda index: rows_copy(index).wait()


def scaled_fold(weights_ref, index, scale_ref):
    _, chunk, crops_total = weights_ref.shape
    folds = []
    for row in range(0, chunk, 64):
        fold = None
        for start in range(0, crops_total, TILE):
            columns = slice(start, start + TILE)
            weights = weights_ref[index, row : row + 64, columns].astype(jnp.float32)
            scaled = lane_fold(weights * scale_ref[:, columns], jnp.add)
            fold = scaled if fold is None else fold + scaled
        folds.append(fold)
    return jnp.concatenate(folds, axis=0)


def next_sweep_kernel(
    protos_total, weights_hbm, parts_ref, copies_ref, weights_ref, scale_ref, pieces_ref, totals_ref, sems,
):
    steps, chunk, crops_total = weights_ref.shape
    arrived = fetch_rows(weights_hbm, weights_ref, sems)
    take_scales(parts_ref, scale_ref)
    totals_ref[...] = jnp.zeros(totals_ref.shape, jnp.float32)

    def weigh(index):
        return three_pieces(lane_scales(scaled_fold(weights_ref, index, scale_ref), protos_total))

    def add_up(index):
        return jnp.dot(pieces_ref[...], weights_ref[index], preferred_element_type=jnp.float32)

    arrived(0)
    pieces_ref[...] = weigh(0)

    def sweep(index, carry):
        arrived(index)
        sums = add_up(index - 1)
        pieces = weigh(index)
        totals_ref[...] += sums
        pieces_ref[...] = pieces
        return carry

    lax.fori_loop(1, steps, sweep, 0)
    totals = totals_ref[...] + add_up(steps - 1)
    give_sums(copies_ref, jnp.sum(totals, axis=0, keepdims=True))


def next_sweep(weights, parts, order, protos_total):
    thin, crops_total = weights.shape
    copies = parts.shape[0]
    chunk = min(thin, 256)
    return pl.pallas_call(
        skipping(functools.partial(next_sweep_kernel, protos_total), 2, len(order)),
        in_specs=[whole(pl.ANY), whole()] + [whole(pl.ANY)] * len(order),
        out_specs=whole(),
        out_shape=jax.ShapeDtypeStruct(sums_shape(copies, crops_total), jnp.bfloat16),
        scratch_shapes=[
            pltpu.VMEM((thin // chunk, chunk, crops_total), jnp.bfloat16),
            pltpu.VMEM((1, crops_total), jnp.float32),
            pltpu.VMEM((16, chunk), jnp.bfloat16),
            pltpu.VMEM((16, crops_total), jnp.float32),
            pltpu.SemaphoreType.DMA((thin // chunk,)),
        ],
        compiler_params=params(16 if crops_total <= 2048 else 50),
        cost_estimate=cost(8 * thin * crops_total, 2 * thin * crops_total),
        name="next_sweep",
    )(in_hbm(weights), parts, *order)


def last_scales_kernel(
    protos_total, weights_hbm, parts_ref, copies_ref, weights_ref, scale_ref, out_ref, sems,
):
    steps, chunk, crops_total = weights_ref.shape
    arrived = fetch_rows(weights_hbm, weights_ref, sems)
    take_scales(parts_ref, scale_ref)

    def weigh(index, carry):
        arrived(index)
        out_ref[:, part(index, chunk)] = lane_scales(
            scaled_fold(weights_ref, index, scale_ref), protos_total
        )
        return carry

    lax.fori_loop(0, steps, weigh, 0)
    copies_ref[...] = jnp.broadcast_to(out_ref[...][None], copies_ref.shape)


def last_scales(weights, parts, order, copies, protos_total):
    thin, crops_total = weights.shape
    chunk = min(thin, 256)
    return pl.pallas_call(
        skipping(functools.partial(last_scales_kernel, protos_total), 2, len(order)),
        in_specs=[whole(pl.ANY), whole()] + [whole(pl.ANY)] * len(order),
        out_specs=whole(),
        out_shape=jax.ShapeDtypeStruct((copies, 1, thin), jnp.float32),
        scratch_shapes=[
            pltpu.VMEM((thin // chunk, chunk, crops_total), jnp.bfloat16),
            pltpu.VMEM((1, crops_total), jnp.float32),
            pltpu.VMEM((1, thin), jnp.float32),
            pltpu.SemaphoreType.DMA((thin // chunk,)),
        ],
        compiler_params=params(16 if crops_total <= 2048 else 50),
        cost_estimate=cost(4 * thin * crops_total, 2 * thin * crops_total),
        name="last_scales",
    )(in_hbm(weights), parts, *order)


def student_front_kernel(
    index_ref, bias_ref, own_hbm, x_hbm, core_hbm, last_hbm, first_hbm, second_hbm, keep_ref, give_ref,
    first_ref, second_ref, rows_ref, sems,
):
    share = own_hbm.shape[0]
    copies = [
        pltpu.make_async_copy(source, rows_ref.at[slot * share : (slot + 1) * share, :], sems.at[slot])
        for slot, source in enumerate((own_hbm, x_hbm, core_hbm, last_hbm))
    ]
    copies.append(pltpu.make_async_copy(first_hbm, first_ref, sems.at[4]))
    second_copy = pltpu.make_async_copy(second_hbm, second_ref, sems.at[5])
    for copy in copies:
        copy.start()
    second_copy.start()
    hidden = first_ref.shape[1]
    bias = bias_ref[:, part(index_ref[0], hidden)]
    for copy in copies:
        copy.wait()
    h_first = gelu(
        jnp.dot(rows_ref[...], first_ref[...], preferred_element_type=jnp.float32) + bias
    ).astype(jnp.bfloat16)
    second_copy.wait()
    for start in range(0, second_ref.shape[1], 512):
        columns = slice(start, start + 512)
        product = jnp.dot(h_first, second_ref[:, columns], preferred_element_type=jnp.float32)
        keep_ref[:, columns] = product[: 2 * share]
        give_ref[:, columns] = product[2 * share :]


def student_front(index, bias, rows, first, second, order):
    share, features = rows[0].shape
    hidden, units = second.shape
    return pl.pallas_call(
        skipping(student_front_kernel, 8, len(order)),
        in_specs=[whole(pltpu.SMEM), whole()] + [whole(pl.ANY)] * (6 + len(order)),
        out_specs=[whole(), whole()],
        out_shape=[jax.ShapeDtypeStruct((2 * share, units), jnp.float32)] * 2,
        scratch_shapes=[
            pltpu.VMEM(first.shape, jnp.bfloat16),
            pltpu.VMEM(second.shape, jnp.bfloat16),
            pltpu.VMEM((4 * share, features), jnp.bfloat16),
            pltpu.SemaphoreType.DMA((6,)),
        ],
        compiler_params=params(16),
        cost_estimate=cost(8 * share * hidden * (features + units), 2 * hidden * (features + units)),
        name="student_front",
    )(index, in_hbm(bias.reshape(1, -1)), in_hbm(rows[0]), *rows[1:], in_hbm(first), in_hbm(second), *order)


def student_middle_kernel(
    index_ref, keep_ref, core_ref, x_ref, bias_ref, own_ref, partner_ref, other_ref, last_ref, last_bias_ref,
    unit_ref, emb_ref, lengths_ref, hidden_ref,
):
    share = x_ref.shape[0]
    block = own_ref.shape[0]
    sums = keep_ref[:share, :] + core_ref[:share, :] + x_ref[...]
    hidden_ref[...] = gelu(sums + bias_ref[...]).astype(jnp.bfloat16)
    index = index_ref[0]
    weights = ((0, own_ref[...]), (2, partner_ref[...]), (1, other_ref[...]), (3, last_ref[...]))
    bottleneck = jnp.broadcast_to(last_bias_ref[...], unit_ref.shape)
    for flip, weight in weights:
        bottleneck = bottleneck + jnp.dot(
            hidden_ref[:, part(index ^ flip, block)], weight, preferred_element_type=jnp.float32
        )
    unit, lengths = unit_rows(bottleneck)
    unit_ref[...] = unit
    emb_ref[...] = unit.astype(jnp.bfloat16)
    lengths_ref[...] = jnp.broadcast_to(lengths, lengths_ref.shape)


def student_middle(index, keep, core_rows, x_rows, bias, weights, last_bias):
    share, units = x_rows.shape
    width = weights[0].shape[1]
    return pl.pallas_call(
        student_middle_kernel,
        in_specs=[whole(pltpu.SMEM)] + [whole()] * 9,
        out_specs=[whole()] * 3,
        out_shape=[
            jax.ShapeDtypeStruct((share, width), jnp.float32),
            jax.ShapeDtypeStruct((share, width), jnp.bfloat16),
            jax.ShapeDtypeStruct((share, 128), jnp.float32),
        ],
        scratch_shapes=[pltpu.VMEM((share, units), jnp.bfloat16)],
        compiler_params=params(12),
        cost_estimate=cost(2 * share * units * width, 2 * units * width + 16 * share * units),
        name="student_middle",
    )(index, keep, core_rows, x_rows, in_hbm(bias.reshape(1, -1)), in_hbm(weights[0]), *weights[1:], in_hbm(last_bias.reshape(1, -1)))


def finish_kernel(unit_ref, lengths_ref, *rest):
    out_ref, blocks = rest[-1], rest[:-1]
    attracts, repels = blocks[: len(blocks) // 2], blocks[len(blocks) // 2 :]
    width = unit_ref.shape[1]
    row_top = functools.reduce(jnp.maximum, [ref[:, width + 128 :] for ref in attracts])
    attract_sum = repel_sum = 0.0
    row_sum = column_sum = 0.0
    for ref in attracts:
        fade = jnp.exp2((ref[:, width + 128 :] - row_top) * student_rate)
        row_sum = row_sum + ref[:, width : width + 128] * fade
        attract_sum = attract_sum + ref[:, :width] * jnp.tile(fade, (1, width // 128))
    for ref in repels:
        column_sum = column_sum + jnp.sum(ref[:, width:].astype(jnp.float32), axis=1, keepdims=True)
        repel_sum = repel_sum + ref[:, :width].astype(jnp.float32)
    emb_grad = (
        attract_sum / jnp.tile(row_sum, (1, width // 128))
        - repel_sum / column_sum
    ) / student_temp
    unit = unit_ref[...]
    along = jnp.sum(unit * emb_grad, axis=1, keepdims=True)
    out_ref[...] = (emb_grad - unit * along) / jnp.tile(lengths_ref[...], (1, width // 128))


def finish(unit, lengths, attracts, repels):
    return pl.pallas_call(
        finish_kernel,
        in_specs=[whole()] * (2 + len(attracts) + len(repels)),
        out_specs=whole(),
        out_shape=jax.ShapeDtypeStruct(unit.shape, jnp.float32),
        compiler_params=params(8),
        cost_estimate=cost(40 * unit.size, 40 * unit.size),
        name="finish",
    )(unit, lengths, *attracts, *repels)


def swap(values, axis, flip):
    return lax.ppermute(values, axis, [(i, i ^ flip) for i in range(lax.axis_size(axis))])


def bit_reversed(values, count):
    bits = count.bit_length() - 1
    split = values.reshape((2,) * bits + values.shape[1:])
    turned = jnp.transpose(split, tuple(reversed(range(bits))) + tuple(range(bits, split.ndim)))
    return turned.reshape(values.shape)


def gather_batch(values):
    step = lax.axis_size("batch") // 2
    stages = [values]
    while step:
        other = swap(values, "batch", step)
        upper = (lax.axis_index("batch") // step) % 2
        values = jnp.where(
            upper == 0, jnp.concatenate([values, other]), jnp.concatenate([other, values])
        )
        stages.append(values)
        step //= 2
    return stages


def send_blocks(blocks):
    return [blocks[0]] + [swap(block, "proto", flip) for flip, block in enumerate(blocks) if flip]


def all_to_all(copies, axes):
    return lax.all_to_all(copies, axes, 0, 0, tiled=True)


def body(crops, teacher_emb, w_first, b_first, w_second, b_second, w_third, b_third, protos):
    batch_index = lax.axis_index("batch")
    proto_index = lax.axis_index("proto")
    batch_size = lax.axis_size("batch")
    proto_size = lax.axis_size("proto")
    devices = batch_size * proto_size
    share_rows = crops.shape[0]
    group_rows = teacher_emb.shape[0]
    crops_total = group_rows * batch_size
    protos_total = protos.shape[0] * proto_size
    count, width = protos.shape
    thin = count // batch_size
    core = proto_index % 2
    proto_ref = proto_index.reshape(1)
    thin_ref = jnp.stack([batch_index, core])
    wide_ref = jnp.stack([batch_index, proto_index])

    own_unit, half = teacher_units(core.reshape(1), teacher_emb)
    stages = gather_batch(half)
    mine = stages[-1]
    other = swap(mine, "proto", 1)

    crops_x = swap(crops, "proto", 2)
    rows = [crops, crops_x, swap(crops, "proto", 1), swap(crops_x, "proto", 1)]
    third_x = swap(w_third, "proto", 2)
    thirds = [w_third, third_x, swap(w_third, "proto", 1), swap(third_x, "proto", 1)]
    top_copies = wide_tops(own_unit, protos, (stages[1],), devices, 8)
    keep, give = student_front(proto_ref, b_first, rows, w_first, w_second, (stages[2], third_x))
    all_tops = all_to_all(top_copies, BOTH)
    tops = jnp.max(all_tops.reshape(batch_size, proto_size, 256)[:, :, :group_rows], axis=1)
    tops = bit_reversed(tops, batch_size).reshape(batch_size, 2, group_rows // 2)
    base = jnp.transpose(tops, (1, 0, 2)).reshape(1, crops_total) * -teacher_rate

    core_rows = swap(give, "proto", 1)
    x_sent = keep[share_rows:] + core_rows[share_rows:]
    x_rows = swap(x_sent, "proto", 2)
    unit, rounded, lengths = student_middle(
        proto_ref, keep, core_rows, x_rows, b_second, thirds, b_third
    )
    student_emb = jnp.concatenate([rounded] + [swap(rounded, "proto", flip) for flip in range(1, proto_size)])
    empty = jnp.concatenate(
        [jnp.zeros((group_rows, width + 128), jnp.float32), jnp.full((group_rows, 128), -1e30, jnp.float32)], axis=1
    )
    (state,) = attract(student_emb, empty, protos, 0, count // 2, 4, 1)
    slots = attract(student_emb, state, protos, count // 2, count // 2, 4, proto_size)
    attract_parts = send_blocks(slots)

    copies, weights = first_sweep(thin_ref, protos, mine, other, base, (x_sent, *thirds[2:]), devices, thin, protos_total)
    for _ in range(ITERS - 2):
        copies = next_sweep(weights, all_to_all(copies, BOTH), (rounded,), protos_total)
    scale_copies = last_scales(weights, all_to_all(copies, BOTH), (state,), batch_size, protos_total)
    all_scale = all_to_all(scale_copies, "batch")
    repels = repel(wide_ref, own_unit, all_tops, all_scale, protos, (slots[0],), proto_size)
    return finish(unit, lengths, attract_parts, send_blocks(repels))


def solution(mesh):
    in_specs = (
        P(("batch", "proto"), None),
        P("batch", None),
        P(None, "proto"),
        P(),
        P("proto", None),
        P(),
        P("proto", None),
        P(),
        P("proto", None),
    )
    out_specs = P(("batch", "proto"), None)
    return jax.shard_map(body, mesh=mesh, in_specs=in_specs, out_specs=out_specs, check_vma=False)
```

```python
import functools
import math

import jax
import jax.numpy as jnp
from jax import lax
from jax.experimental import pallas as pl
from jax.experimental.pallas import tpu as pltpu
from jax.sharding import PartitionSpec as P

ITERS = 3

student_temp = 0.1
teacher_temp = 0.07
norm_eps = 1e-06
teacher_rate = math.log2(math.e) / teacher_temp
student_rate = math.log2(math.e) / student_temp

MIB = 1024 * 1024
BOTH = ("batch", "proto")
TILE = 256
WIDE = 512


def scores(left_rows, right_rows):
    return lax.dot_general(
        left_rows, right_rows, (((1,), (1,)), ((), ())), preferred_element_type=jnp.float32
    )


def unit_rows(values):
    lengths = jnp.sqrt(jnp.sum(values * values, axis=1, keepdims=True) + norm_eps)
    return (values / lengths, lengths)


def gelu(values):
    return 0.5 * values * (1.0 + lax.erf(values * math.sqrt(0.5)))


def whole(memory_space=pltpu.VMEM):
    return pl.BlockSpec(memory_space=memory_space)


def in_hbm(array):
    return pltpu.with_memory_space_constraint(array, pltpu.HBM)


def skipping(kernel, first, count):
    def trimmed(*refs):
        kernel(*refs[:first], *refs[first + count :])

    return trimmed


def part(index, size):
    return pl.ds(pl.multiple_of(index * size, size), size)


def lane_fold(values, combine):
    folded = values[:, :128]
    for start in range(128, values.shape[1], 128):
        folded = combine(folded, values[:, start : start + 128])
    return folded


def params(mib):
    return pltpu.CompilerParams(vmem_limit_bytes=mib * MIB)


def cost(flops, bytes_accessed, transcendentals=0):
    return pl.CostEstimate(
        flops=int(flops), bytes_accessed=int(bytes_accessed), transcendentals=int(transcendentals)
    )


def fetch(source, target, sems, first_row=0):
    count, rows = target.shape[:2]

    def chunk_copy(index):
        start = pl.multiple_of(first_row + index * rows, rows)
        return pltpu.make_async_copy(source.at[pl.ds(start, rows), :], target.at[index], sems.at[index])

    for index in range(count):
        chunk_copy(index).start()
    return lambda index: chunk_copy(index).wait()


def teacher_units_kernel(core_ref, emb_ref, unit_ref, half_ref):
    unit_ref[...] = unit_rows(emb_ref[...].astype(jnp.float32))[0].astype(jnp.bfloat16)
    half = half_ref.shape[0]
    half_ref[...] = unit_ref[part(core_ref[0], half), :]


def teacher_units(core, teacher_emb):
    rows, width = teacher_emb.shape
    return pl.pallas_call(
        teacher_units_kernel,
        in_specs=[whole(pltpu.SMEM), whole()],
        out_specs=[whole(), whole()],
        out_shape=[
            jax.ShapeDtypeStruct((rows, width), jnp.bfloat16),
            jax.ShapeDtypeStruct((rows // 2, width), jnp.bfloat16),
        ],
        compiler_params=params(4),
        cost_estimate=cost(4 * rows * width, 8 * rows * width),
        name="teacher_units",
    )(core, in_hbm(teacher_emb))


def front_kernel(
    index_ref, unit_ref, bias_ref, own_hbm, x_hbm, core_hbm, last_hbm, first_hbm, second_hbm, protos_hbm,
    top_ref, keep_ref, give_ref, turned_hbm, first_ref, second_ref, rows_ref, protos_ref, turned_ref, sems,
    chunk_sems, out_sems,
):
    rows = unit_ref.shape[0]
    steps, block = protos_ref.shape[:2]
    wide = min(WIDE, block)
    share = own_hbm.shape[0]
    arrived = fetch(protos_hbm, protos_ref, chunk_sems)
    copies = [
        pltpu.make_async_copy(source, rows_ref.at[slot * share : (slot + 1) * share, :], sems.at[slot])
        for slot, source in enumerate((own_hbm, x_hbm, core_hbm, last_hbm))
    ]
    copies.append(pltpu.make_async_copy(first_hbm, first_ref, sems.at[4]))
    copies.append(pltpu.make_async_copy(second_hbm, second_ref, sems.at[5]))
    for copy in copies:
        copy.start()
    top_ref[...] = jnp.full(top_ref.shape, -jnp.inf, jnp.float32)

    def chunk_out(index):
        return pltpu.make_async_copy(turned_ref.at[index], turned_hbm.at[index], out_sems.at[index])

    def step(index, carry):
        arrived(index)
        top = top_ref[:rows, :]
        for start in range(0, block, wide):
            turned = jnp.transpose(protos_ref[index, start : start + wide, :])
            turned_ref[index, :, start : start + wide] = turned
            products = jnp.dot(unit_ref[...], turned, preferred_element_type=jnp.float32)
            top = jnp.maximum(top, lane_fold(products, jnp.maximum))
        top_ref[:rows, :] = top
        chunk_out(index).start()
        return carry

    lax.fori_loop(0, steps, step, 0)
    for copy in copies:
        copy.wait()
    hidden = first_ref.shape[1]
    bias = bias_ref[:, part(index_ref[0], hidden)]
    h_first = gelu(
        jnp.dot(rows_ref[...], first_ref[...], preferred_element_type=jnp.float32) + bias
    ).astype(jnp.bfloat16)
    for start in range(0, second_ref.shape[1], 512):
        columns = slice(start, start + 512)
        product = jnp.dot(h_first, second_ref[:, columns], preferred_element_type=jnp.float32)
        keep_ref[:, columns] = product[: 2 * share]
        give_ref[:, columns] = product[2 * share :]
    for index in range(steps):
        chunk_out(index).wait()


def front(index, unit, bias, rows, first, second, protos, order, steps):
    share, features = rows[0].shape
    hidden, units = second.shape
    count, width = protos.shape
    return pl.pallas_call(
        skipping(front_kernel, 10, len(order)),
        in_specs=[whole(pltpu.SMEM), whole(), whole()] + [whole(pl.ANY)] * (7 + len(order)),
        out_specs=[whole()] * 3 + [whole(pl.ANY)],
        out_shape=[jax.ShapeDtypeStruct((256, 128), jnp.float32)]
        + [jax.ShapeDtypeStruct((2 * share, units), jnp.float32)] * 2
        + [pltpu.HBM((steps, width, count // steps), jnp.bfloat16)],
        scratch_shapes=[
            pltpu.VMEM(first.shape, jnp.bfloat16),
            pltpu.VMEM(second.shape, jnp.bfloat16),
            pltpu.VMEM((4 * share, features), jnp.bfloat16),
            pltpu.VMEM((steps, count // steps, width), jnp.bfloat16),
            pltpu.VMEM((steps, width, count // steps), jnp.bfloat16),
            pltpu.SemaphoreType.DMA((6,)),
            pltpu.SemaphoreType.DMA((steps,)),
            pltpu.SemaphoreType.DMA((steps,)),
        ],
        compiler_params=params(34),
        cost_estimate=cost(
            2 * unit.size * count + 8 * share * hidden * (features + units), 2 * width * count
        ),
        name="front",
    )(
        index, unit, in_hbm(bias.reshape(1, -1)), in_hbm(rows[0]), *rows[1:],
        in_hbm(first), in_hbm(second), in_hbm(protos), *order,
    )


def fetch_turned(source, target, sems, first_block=0):
    count, _, columns = target.shape
    pieces = source.shape[2] // columns

    def chunk_copy(index):
        place = source.at[first_block + index // pieces]
        if pieces > 1:
            place = place.at[:, part(lax.rem(index, pieces), columns)]
        return pltpu.make_async_copy(place, target.at[index], sems.at[index])

    for index in range(count):
        chunk_copy(index).start()
    return lambda index: chunk_copy(index).wait()


def spread_tops_kernel(top_ref, out_ref):
    tops = jnp.max(jnp.transpose(top_ref[...]), axis=0, keepdims=True)
    out_ref[...] = jnp.broadcast_to(tops[None], out_ref.shape)


def spread_tops(top, order, copies):
    return pl.pallas_call(
        skipping(spread_tops_kernel, 1, len(order)),
        in_specs=[whole()] + [whole(pl.ANY)] * len(order),
        out_specs=whole(),
        out_shape=jax.ShapeDtypeStruct((copies, 1, 256), jnp.float32),
        compiler_params=params(4),
        cost_estimate=cost(top.size, 8 * top.size),
        name="spread_tops",
    )(top, *order)


def repel_kernel(group, index_ref, unit_ref, tops_ref, scale_ref, protos_hbm, turned_hbm, *rest):
    out_refs, (protos_ref, turned_ref, sems, turned_sems, acc_ref, sum_ref, bias_ref) = rest[:-7], rest[-7:]
    rows, width = unit_ref.shape
    steps, block = protos_ref.shape[:2]
    wide = min(WIDE, block)
    turned_arrived = fetch_turned(turned_hbm, turned_ref, turned_sems)
    arrived = fetch(protos_hbm, protos_ref, sems)
    first = index_ref[0] * group
    top = tops_ref[first]
    for other in range(1, group):
        top = jnp.maximum(top, tops_ref[first + other])
    bias_ref[...] = jnp.transpose(jnp.broadcast_to(top, (128, 256)))[:rows, :] * -teacher_rate
    acc_ref[...] = jnp.zeros(acc_ref.shape, jnp.float32)
    sum_ref[...] = jnp.zeros(sum_ref.shape, jnp.float32)

    def step(index, carry):
        turned_arrived(index)
        arrived(index)
        bias = bias_ref[...]
        total = sum_ref[...]
        acc = acc_ref[...]
        for start in range(0, block, wide):
            protos = protos_ref[index, start : start + wide, :]
            turned = turned_ref[index, :, start : start + wide]
            products = jnp.dot(unit_ref[...], turned, preferred_element_type=jnp.float32)
            pieces = []
            for lane in range(0, wide, 128):
                scaled = jnp.exp2(products[:, lane : lane + 128] * teacher_rate + bias)
                scaled = scaled * scale_ref[index, :, start + lane : start + lane + 128]
                total = total + scaled
                pieces.append(scaled.astype(jnp.bfloat16))
            acc = acc + jnp.dot(
                jnp.concatenate(pieces, axis=1), protos, preferred_element_type=jnp.float32
            )
        sum_ref[...] = total
        acc_ref[...] = acc
        return carry

    lax.fori_loop(0, steps, step, 0)
    total = jnp.sum(sum_ref[...], axis=1, keepdims=True)
    lanes = lax.broadcasted_iota(jnp.int32, sum_ref.shape, 1)
    sum_ref[...] = jnp.broadcast_to(total, sum_ref.shape)
    share = out_refs[0].shape[0]
    lanes = lanes[:share, :]
    for flip, out_ref in enumerate(out_refs):
        span = part(index_ref[1] ^ flip, share)
        total = sum_ref[span, :]
        out_ref[:, :width] = acc_ref[span, :].astype(out_ref.dtype)
        if flip == 0:
            out_ref[:, width:] = jnp.where(lanes == 0, total, 0.0)
        else:
            high = total.astype(jnp.bfloat16).astype(jnp.float32)
            middle = (total - high).astype(jnp.bfloat16).astype(jnp.float32)
            pieces = jnp.where(lanes == 0, high, jnp.where(lanes == 1, middle, total - high - middle))
            out_ref[:, width:] = jnp.where(lanes < 3, pieces, 0.0).astype(jnp.bfloat16)


def repel(index, unit, tops, scale, protos, turned, order, proto_size):
    rows, width = unit.shape
    count = protos.shape[0]
    steps, _, block = scale.shape
    return pl.pallas_call(
        skipping(functools.partial(repel_kernel, proto_size), 6, len(order)),
        in_specs=[whole(pltpu.SMEM), whole(), whole(), whole(), whole(pl.ANY), whole(pl.ANY)] + [whole(pl.ANY)] * len(order),
        out_specs=[whole()] * proto_size,
        out_shape=[
            jax.ShapeDtypeStruct((rows // proto_size, width + 128), jnp.bfloat16 if flip else jnp.float32)
            for flip in range(proto_size)
        ],
        scratch_shapes=[
            pltpu.VMEM((steps, block, width), jnp.bfloat16),
            pltpu.VMEM((steps, width, block), jnp.bfloat16),
            pltpu.SemaphoreType.DMA((steps,)),
            pltpu.SemaphoreType.DMA((steps,)),
            pltpu.VMEM((rows, width), jnp.float32),
            pltpu.VMEM((rows, 128), jnp.float32),
            pltpu.VMEM((rows, 128), jnp.float32),
        ],
        compiler_params=params(26),
        cost_estimate=cost(4 * rows * width * count, 2 * width * count, rows * count),
        name="repel",
    )(index, unit, tops, scale, in_hbm(protos), in_hbm(turned), *order)


def attract_kernel(first_row, last, emb_ref, state_ref, protos_hbm, turned_hbm, *rest):
    out_refs, scratch = rest[:-8], rest[-8:]
    protos_ref, turned_ref, sems, turned_sems, products_ref, acc_ref, sum_ref, top_ref = scratch
    width = emb_ref.shape[1]
    steps, block = protos_ref.shape[:2]
    turned_arrived = fetch_turned(turned_hbm, turned_ref, turned_sems, first_row // block)
    arrived = fetch(protos_hbm, protos_ref, sems, first_row)
    old_top = state_ref[:, width + 128 :]
    top_ref[...] = old_top

    def first(index, carry):
        turned_arrived(index)
        top = top_ref[...]
        for start in range(0, block, TILE):
            turned = turned_ref[index, :, start : start + TILE]
            products = jnp.dot(emb_ref[...], turned, preferred_element_type=jnp.float32)
            products_ref[index, :, start : start + TILE] = products
            top = jnp.maximum(top, lane_fold(products, jnp.maximum))
        top_ref[...] = top
        return carry

    lax.fori_loop(0, steps, first, 0)
    top = jnp.broadcast_to(jnp.max(top_ref[...], axis=1, keepdims=True), top_ref.shape)
    fade = jnp.exp2((old_top - top) * student_rate)
    top_ref[...] = top
    sum_ref[...] = state_ref[:, width : width + 128] * fade
    acc_ref[...] = state_ref[:, :width] * jnp.tile(fade, (1, width // 128))

    def second(index, carry):
        arrived(index)
        top = top_ref[...]
        total = sum_ref[...]
        acc = acc_ref[...]
        for start in range(0, block, TILE):
            pieces = []
            for lane in range(start, start + TILE, 128):
                shifted = jnp.exp2((products_ref[index, :, lane : lane + 128] - top) * student_rate)
                total = total + shifted
                pieces.append(shifted.astype(jnp.bfloat16))
            acc = acc + jnp.dot(
                jnp.concatenate(pieces, axis=1),
                protos_ref[index, start : start + TILE, :],
                preferred_element_type=jnp.float32,
            )
        sum_ref[...] = total
        acc_ref[...] = acc
        return carry

    lax.fori_loop(0, steps, second, 0)
    if last:
        total = jnp.sum(sum_ref[...], axis=1, keepdims=True)
        sum_ref[...] = jnp.broadcast_to(total, sum_ref.shape)
    share = out_refs[0].shape[0]
    for slot, out_ref in enumerate(out_refs):
        rows = pl.ds(slot * share, share)
        out_ref[:, :width] = acc_ref[rows, :]
        out_ref[:, width : width + 128] = sum_ref[rows, :]
        out_ref[:, width + 128 :] = top_ref[rows, :]


def attract(emb, state, protos, turned, first_row, count, steps, outputs):
    rows, width = emb.shape
    block = count // steps
    return pl.pallas_call(
        functools.partial(attract_kernel, first_row, outputs > 1),
        in_specs=[whole(), whole(), whole(pl.ANY), whole(pl.ANY)],
        out_specs=[whole()] * outputs,
        out_shape=[jax.ShapeDtypeStruct((rows // outputs, width + 256), jnp.float32)] * outputs,
        scratch_shapes=[
            pltpu.VMEM((steps, block, width), jnp.bfloat16),
            pltpu.VMEM((steps, width, block), jnp.bfloat16),
            pltpu.SemaphoreType.DMA((steps,)),
            pltpu.SemaphoreType.DMA((steps,)),
            pltpu.VMEM((steps, rows, block), jnp.float32),
            pltpu.VMEM((rows, width), jnp.float32),
            pltpu.VMEM((rows, 128), jnp.float32),
            pltpu.VMEM((rows, 128), jnp.float32),
        ],
        compiler_params=params(30),
        cost_estimate=cost(4 * rows * width * count, 2 * width * count, rows * count),
        name="attract",
    )(emb, state, in_hbm(protos), in_hbm(turned))


def three_pieces(values):
    high = values.astype(jnp.bfloat16)
    rest = values - high.astype(jnp.float32)
    middle = rest.astype(jnp.bfloat16)
    low = (rest - middle.astype(jnp.float32)).astype(jnp.bfloat16)
    return jnp.concatenate([high, middle, low, jnp.zeros((13, values.shape[1]), jnp.bfloat16)], axis=0)


def lane_scales(folded, protos_total):
    sums = [
        jnp.sum(jnp.transpose(folded[start : start + 128, :]), axis=0, keepdims=True)
        for start in range(0, folded.shape[0], 128)
    ]
    return 1.0 / (protos_total * jnp.concatenate(sums, axis=1))


def give_sums(copies_ref, totals):
    rows = [totals[:, start : start + 128] for start in range(0, totals.shape[1], 128)]
    spare = copies_ref.shape[1] - len(rows)
    if spare:
        rows.append(jnp.zeros((spare, 128), jnp.float32))
    packed = jnp.concatenate(rows, axis=0).astype(jnp.bfloat16)
    copies_ref[...] = jnp.broadcast_to(packed[None], copies_ref.shape)


def take_scales(parts_ref, scale_ref):
    crops_total = scale_ref.shape[1]
    sums = jnp.sum(parts_ref[...].astype(jnp.float32), axis=0)
    for row in range(crops_total // 128):
        scale_ref[:, row * 128 : row * 128 + 128] = 1.0 / (crops_total * sums[row : row + 1, :])


def sums_shape(copies, crops_total):
    return (copies, -(-crops_total // 2048) * 16, 128)


def first_sweep_kernel(
    chunk, protos_total, index_ref, protos_hbm, mine_hbm, other_hbm, bias_ref, copies_ref, weights_hbm, protos_ref, units_ref, weights_ref, rounded_ref, scale_ref, sems, chunk_sems, out_sems,
):
    thin, crops_total = weights_ref.shape
    half = mine_hbm.shape[0]
    core = index_ref[1]
    copies = (
        pltpu.make_async_copy(mine_hbm, units_ref.at[part(core, half), :], sems.at[0]),
        pltpu.make_async_copy(other_hbm, units_ref.at[part(1 - core, half), :], sems.at[1]),
    )
    for copy in copies:
        copy.start()
    arrived = fetch(protos_hbm, protos_ref, chunk_sems, index_ref[0] * thin)
    for copy in copies:
        copy.wait()

    def chunk_out(index):
        return pltpu.make_async_copy(
            rounded_ref.at[index], weights_hbm.at[part(index, chunk), :], out_sems.at[index]
        )

    def weigh(index, carry):
        rows = part(index, chunk)
        arrived(index)
        protos = protos_ref[index]
        folded = jnp.zeros((chunk, 128), jnp.float32)
        for start in range(0, crops_total, TILE):
            columns = slice(start, start + TILE)
            products = scores(protos, units_ref[columns, :])
            weights = jnp.exp2(products * teacher_rate + bias_ref[:, columns])
            weights_ref[rows, columns] = weights
            rounded_ref[index, :, columns] = weights.astype(jnp.bfloat16)
            folded = folded + lane_fold(weights, jnp.add)
        sums = jnp.sum(folded, axis=1, keepdims=True)
        scale_ref[rows, :] = jnp.broadcast_to(1.0 / (protos_total * sums), (chunk, 128))
        chunk_out(index).start()
        return carry

    lax.fori_loop(0, thin // chunk, weigh, 0)
    small = min(thin, 64)

    def add_up(index, totals):
        rows = part(index, small)
        scaled = weights_ref[rows, :] * jnp.tile(scale_ref[rows, :], (1, crops_total // 128))
        return totals + jnp.sum(scaled.reshape(-1, 8, crops_total), axis=0)

    totals = lax.fori_loop(0, thin // small, add_up, jnp.zeros((8, crops_total), jnp.float32))
    give_sums(copies_ref, jnp.sum(totals, axis=0, keepdims=True))
    for index in range(thin // chunk):
        chunk_out(index).wait()


def first_sweep(index, protos, mine, other, base, order, copies, thin, protos_total):
    width = protos.shape[1]
    crops_total = 2 * mine.shape[0]
    chunk = min(thin, 1024)
    return pl.pallas_call(
        skipping(functools.partial(first_sweep_kernel, chunk, protos_total), 5, len(order)),
        in_specs=[whole(pltpu.SMEM), whole(pl.ANY), whole(pl.ANY), whole(pl.ANY), whole()]
        + [whole(pl.ANY)] * len(order),
        out_specs=[whole(), whole(pl.ANY)],
        out_shape=[
            jax.ShapeDtypeStruct(sums_shape(copies, crops_total), jnp.bfloat16),
            pltpu.HBM((thin, crops_total), jnp.bfloat16),
        ],
        scratch_shapes=[
            pltpu.VMEM((thin // chunk, chunk, width), jnp.bfloat16),
            pltpu.VMEM((crops_total, width), jnp.bfloat16),
            pltpu.VMEM((thin, crops_total), jnp.float32),
            pltpu.VMEM((thin // chunk, chunk, crops_total), jnp.bfloat16),
            pltpu.VMEM((thin, 128), jnp.float32),
            pltpu.SemaphoreType.DMA((2,)),
            pltpu.SemaphoreType.DMA((thin // chunk,)),
            pltpu.SemaphoreType.DMA((thin // chunk,)),
        ],
        compiler_params=params(32 if crops_total <= 2048 else 56),
        cost_estimate=cost(2 * thin * width * crops_total, 2 * thin * crops_total, thin * crops_total),
        name="first_sweep",
    )(index, in_hbm(protos), mine, other, base, *order)


def fetch_rows(weights_hbm, weights_ref, sems):
    steps, chunk, _ = weights_ref.shape

    def rows_copy(index):
        return pltpu.make_async_copy(
            weights_hbm.at[part(index, chunk), :], weights_ref.at[index], sems.at[index]
        )

    for index in range(steps):
        rows_copy(index).start()
    return lambda index: rows_copy(index).wait()


def scaled_fold(weights_ref, index, scale_ref):
    _, chunk, crops_total = weights_ref.shape
    folds = []
    for row in range(0, chunk, 64):
        fold = None
        for start in range(0, crops_total, TILE):
            columns = slice(start, start + TILE)
            weights = weights_ref[index, row : row + 64, columns].astype(jnp.float32)
            scaled = lane_fold(weights * scale_ref[:, columns], jnp.add)
            fold = scaled if fold is None else fold + scaled
        folds.append(fold)
    return jnp.concatenate(folds, axis=0)


def next_sweep_kernel(
    protos_total, weights_hbm, parts_ref, copies_ref, weights_ref, scale_ref, pieces_ref, totals_ref, sems,
):
    steps, chunk, crops_total = weights_ref.shape
    arrived = fetch_rows(weights_hbm, weights_ref, sems)
    take_scales(parts_ref, scale_ref)
    totals_ref[...] = jnp.zeros(totals_ref.shape, jnp.float32)

    def weigh(index):
        return three_pieces(lane_scales(scaled_fold(weights_ref, index, scale_ref), protos_total))

    def add_up(index):
        return jnp.dot(pieces_ref[...], weights_ref[index], preferred_element_type=jnp.float32)

    arrived(0)
    pieces_ref[...] = weigh(0)

    def sweep(index, carry):
        arrived(index)
        sums = add_up(index - 1)
        pieces = weigh(index)
        totals_ref[...] += sums
        pieces_ref[...] = pieces
        return carry

    lax.fori_loop(1, steps, sweep, 0)
    totals = totals_ref[...] + add_up(steps - 1)
    give_sums(copies_ref, jnp.sum(totals, axis=0, keepdims=True))


def next_sweep(weights, parts, order, protos_total):
    thin, crops_total = weights.shape
    copies = parts.shape[0]
    chunk = min(thin, 256)
    return pl.pallas_call(
        skipping(functools.partial(next_sweep_kernel, protos_total), 2, len(order)),
        in_specs=[whole(pl.ANY), whole()] + [whole(pl.ANY)] * len(order),
        out_specs=whole(),
        out_shape=jax.ShapeDtypeStruct(sums_shape(copies, crops_total), jnp.bfloat16),
        scratch_shapes=[
            pltpu.VMEM((thin // chunk, chunk, crops_total), jnp.bfloat16),
            pltpu.VMEM((1, crops_total), jnp.float32),
            pltpu.VMEM((16, chunk), jnp.bfloat16),
            pltpu.VMEM((16, crops_total), jnp.float32),
            pltpu.SemaphoreType.DMA((thin // chunk,)),
        ],
        compiler_params=params(16 if crops_total <= 2048 else 50),
        cost_estimate=cost(8 * thin * crops_total, 2 * thin * crops_total),
        name="next_sweep",
    )(in_hbm(weights), parts, *order)


def last_scales_kernel(
    protos_total, weights_hbm, parts_ref, copies_ref, weights_ref, scale_ref, out_ref, sems,
):
    steps, chunk, crops_total = weights_ref.shape
    arrived = fetch_rows(weights_hbm, weights_ref, sems)
    take_scales(parts_ref, scale_ref)

    def weigh(index, carry):
        arrived(index)
        out_ref[:, part(index, chunk)] = lane_scales(
            scaled_fold(weights_ref, index, scale_ref), protos_total
        )
        return carry

    lax.fori_loop(0, steps, weigh, 0)
    copies_ref[...] = jnp.broadcast_to(out_ref[...][None], copies_ref.shape)


def last_scales(weights, parts, order, copies, protos_total):
    thin, crops_total = weights.shape
    chunk = min(thin, 256)
    return pl.pallas_call(
        skipping(functools.partial(last_scales_kernel, protos_total), 2, len(order)),
        in_specs=[whole(pl.ANY), whole()] + [whole(pl.ANY)] * len(order),
        out_specs=whole(),
        out_shape=jax.ShapeDtypeStruct((copies, 1, thin), jnp.float32),
        scratch_shapes=[
            pltpu.VMEM((thin // chunk, chunk, crops_total), jnp.bfloat16),
            pltpu.VMEM((1, crops_total), jnp.float32),
            pltpu.VMEM((1, thin), jnp.float32),
            pltpu.SemaphoreType.DMA((thin // chunk,)),
        ],
        compiler_params=params(16 if crops_total <= 2048 else 50),
        cost_estimate=cost(4 * thin * crops_total, 2 * thin * crops_total),
        name="last_scales",
    )(in_hbm(weights), parts, *order)


def student_middle_kernel(
    index_ref, keep_ref, core_ref, x_ref, bias_ref, own_ref, partner_ref, other_ref, last_ref, last_bias_ref,
    unit_ref, emb_ref, lengths_ref, hidden_ref,
):
    share = x_ref.shape[0]
    block = own_ref.shape[0]
    sums = keep_ref[:share, :] + core_ref[:share, :] + x_ref[...]
    hidden_ref[...] = gelu(sums + bias_ref[...]).astype(jnp.bfloat16)
    index = index_ref[0]
    weights = ((0, own_ref[...]), (2, partner_ref[...]), (1, other_ref[...]), (3, last_ref[...]))
    bottleneck = jnp.broadcast_to(last_bias_ref[...], unit_ref.shape)
    for flip, weight in weights:
        bottleneck = bottleneck + jnp.dot(
            hidden_ref[:, part(index ^ flip, block)], weight, preferred_element_type=jnp.float32
        )
    unit, lengths = unit_rows(bottleneck)
    unit_ref[...] = unit
    emb_ref[...] = unit.astype(jnp.bfloat16)
    lengths_ref[...] = jnp.broadcast_to(lengths, lengths_ref.shape)


def student_middle(index, keep, core_rows, x_rows, bias, weights, last_bias):
    share, units = x_rows.shape
    width = weights[0].shape[1]
    return pl.pallas_call(
        student_middle_kernel,
        in_specs=[whole(pltpu.SMEM)] + [whole()] * 9,
        out_specs=[whole()] * 3,
        out_shape=[
            jax.ShapeDtypeStruct((share, width), jnp.float32),
            jax.ShapeDtypeStruct((share, width), jnp.bfloat16),
            jax.ShapeDtypeStruct((share, 128), jnp.float32),
        ],
        scratch_shapes=[pltpu.VMEM((share, units), jnp.bfloat16)],
        compiler_params=params(12),
        cost_estimate=cost(2 * share * units * width, 2 * units * width + 16 * share * units),
        name="student_middle",
    )(index, keep, core_rows, x_rows, in_hbm(bias.reshape(1, -1)), in_hbm(weights[0]), *weights[1:], in_hbm(last_bias.reshape(1, -1)))


def finish_kernel(unit_ref, lengths_ref, *rest):
    out_ref, blocks = rest[-1], rest[:-1]
    attracts, repels = blocks[: len(blocks) // 2], blocks[len(blocks) // 2 :]
    width = unit_ref.shape[1]
    row_top = functools.reduce(jnp.maximum, [ref[:, width + 128 :] for ref in attracts])
    attract_sum = repel_sum = 0.0
    row_sum = column_sum = 0.0
    for ref in attracts:
        fade = jnp.exp2((ref[:, width + 128 :] - row_top) * student_rate)
        row_sum = row_sum + ref[:, width : width + 128] * fade
        attract_sum = attract_sum + ref[:, :width] * jnp.tile(fade, (1, width // 128))
    for ref in repels:
        column_sum = column_sum + jnp.sum(ref[:, width:].astype(jnp.float32), axis=1, keepdims=True)
        repel_sum = repel_sum + ref[:, :width].astype(jnp.float32)
    emb_grad = (
        attract_sum / jnp.tile(row_sum, (1, width // 128))
        - repel_sum / column_sum
    ) / student_temp
    unit = unit_ref[...]
    along = jnp.sum(unit * emb_grad, axis=1, keepdims=True)
    out_ref[...] = (emb_grad - unit * along) / jnp.tile(lengths_ref[...], (1, width // 128))


def finish(unit, lengths, attracts, repels):
    return pl.pallas_call(
        finish_kernel,
        in_specs=[whole()] * (2 + len(attracts) + len(repels)),
        out_specs=whole(),
        out_shape=jax.ShapeDtypeStruct(unit.shape, jnp.float32),
        compiler_params=params(8),
        cost_estimate=cost(40 * unit.size, 40 * unit.size),
        name="finish",
    )(unit, lengths, *attracts, *repels)


def swap(values, axis, flip):
    return lax.ppermute(values, axis, [(i, i ^ flip) for i in range(lax.axis_size(axis))])


def bit_reversed(values, count):
    bits = count.bit_length() - 1
    split = values.reshape((2,) * bits + values.shape[1:])
    turned = jnp.transpose(split, tuple(reversed(range(bits))) + tuple(range(bits, split.ndim)))
    return turned.reshape(values.shape)


def gather_batch(values):
    step = lax.axis_size("batch") // 2
    stages = [values]
    while step:
        other = swap(values, "batch", step)
        upper = (lax.axis_index("batch") // step) % 2
        values = jnp.where(
            upper == 0, jnp.concatenate([values, other]), jnp.concatenate([other, values])
        )
        stages.append(values)
        step //= 2
    return stages


def send_blocks(blocks):
    return [blocks[0]] + [swap(block, "proto", flip) for flip, block in enumerate(blocks) if flip]


def all_to_all(copies, axes):
    return lax.all_to_all(copies, axes, 0, 0, tiled=True)


def body(crops, teacher_emb, w_first, b_first, w_second, b_second, w_third, b_third, protos):
    batch_index = lax.axis_index("batch")
    proto_index = lax.axis_index("proto")
    batch_size = lax.axis_size("batch")
    proto_size = lax.axis_size("proto")
    devices = batch_size * proto_size
    share_rows = crops.shape[0]
    group_rows = teacher_emb.shape[0]
    crops_total = group_rows * batch_size
    protos_total = protos.shape[0] * proto_size
    count, width = protos.shape
    thin = count // batch_size
    core = proto_index % 2
    proto_ref = proto_index.reshape(1)
    thin_ref = jnp.stack([batch_index, core])
    wide_ref = jnp.stack([batch_index, proto_index])

    own_unit, half = teacher_units(core.reshape(1), teacher_emb)
    stages = gather_batch(half)
    mine = stages[-1]
    other = swap(mine, "proto", 1)

    crops_x = swap(crops, "proto", 2)
    rows = [crops, crops_x, swap(crops, "proto", 1), swap(crops_x, "proto", 1)]
    third_x = swap(w_third, "proto", 2)
    thirds = [w_third, third_x, swap(w_third, "proto", 1), swap(third_x, "proto", 1)]
    top, keep, give, turned = front(
        proto_ref, own_unit, b_first, rows, w_first, w_second, protos, (stages[2],), 8
    )
    all_tops = all_to_all(spread_tops(top, (third_x,), devices), BOTH)
    tops = jnp.max(all_tops.reshape(batch_size, proto_size, 256)[:, :, :group_rows], axis=1)
    tops = bit_reversed(tops, batch_size).reshape(batch_size, 2, group_rows // 2)
    base = jnp.transpose(tops, (1, 0, 2)).reshape(1, crops_total) * -teacher_rate

    core_rows = swap(give, "proto", 1)
    x_sent = keep[share_rows:] + core_rows[share_rows:]
    x_rows = swap(x_sent, "proto", 2)
    unit, rounded, lengths = student_middle(
        proto_ref, keep, core_rows, x_rows, b_second, thirds, b_third
    )
    student_emb = jnp.concatenate([rounded] + [swap(rounded, "proto", flip) for flip in range(1, proto_size)])
    empty = jnp.concatenate(
        [jnp.zeros((group_rows, width + 128), jnp.float32), jnp.full((group_rows, 128), -1e30, jnp.float32)], axis=1
    )
    (state,) = attract(student_emb, empty, protos, turned, 0, count // 2, 4, 1)
    slots = attract(student_emb, state, protos, turned, count // 2, count // 2, 4, proto_size)
    attract_parts = send_blocks(slots)

    copies, weights = first_sweep(thin_ref, protos, mine, other, base, (x_sent, *thirds[2:]), devices, thin, protos_total)
    for _ in range(ITERS - 2):
        copies = next_sweep(weights, all_to_all(copies, BOTH), (rounded,), protos_total)
    scale_copies = last_scales(weights, all_to_all(copies, BOTH), (state,), batch_size, protos_total)
    all_scale = all_to_all(scale_copies, "batch")
    repels = repel(wide_ref, own_unit, all_tops, all_scale, protos, turned, (slots[0],), proto_size)
    return finish(unit, lengths, attract_parts, send_blocks(repels))


def solution(mesh):
    in_specs = (
        P(("batch", "proto"), None),
        P("batch", None),
        P(None, "proto"),
        P(),
        P("proto", None),
        P(),
        P("proto", None),
        P(),
        P("proto", None),
    )
    out_specs = P(("batch", "proto"), None)
    return jax.shard_map(body, mesh=mesh, in_specs=in_specs, out_specs=out_specs, check_vma=False)
```

```python
import functools
import math

import jax
import jax.numpy as jnp
from jax import lax
from jax.experimental import pallas as pl
from jax.experimental.pallas import tpu as pltpu
from jax.sharding import PartitionSpec as P

ITERS = 3

student_temp = 0.1
teacher_temp = 0.07
norm_eps = 1e-06
teacher_rate = math.log2(math.e) / teacher_temp
student_rate = math.log2(math.e) / student_temp

MIB = 1024 * 1024
BOTH = ("batch", "proto")
TILE = 256
WIDE = 512


def scores(left_rows, right_rows):
    return lax.dot_general(
        left_rows, right_rows, (((1,), (1,)), ((), ())), preferred_element_type=jnp.float32
    )


def unit_rows(values):
    lengths = jnp.sqrt(jnp.sum(values * values, axis=1, keepdims=True) + norm_eps)
    return (values / lengths, lengths)


def gelu(values):
    return 0.5 * values * (1.0 + lax.erf(values * math.sqrt(0.5)))


def whole(memory_space=pltpu.VMEM):
    return pl.BlockSpec(memory_space=memory_space)


def in_hbm(array):
    return pltpu.with_memory_space_constraint(array, pltpu.HBM)


def skipping(kernel, first, count):
    def trimmed(*refs):
        kernel(*refs[:first], *refs[first + count :])

    return trimmed


def part(index, size):
    return pl.ds(pl.multiple_of(index * size, size), size)


def lane_fold(values, combine):
    folded = values[:, :128]
    for start in range(128, values.shape[1], 128):
        folded = combine(folded, values[:, start : start + 128])
    return folded


def params(mib):
    return pltpu.CompilerParams(vmem_limit_bytes=mib * MIB)


def cost(flops, bytes_accessed, transcendentals=0):
    return pl.CostEstimate(
        flops=int(flops), bytes_accessed=int(bytes_accessed), transcendentals=int(transcendentals)
    )


def fetch(source, target, sems, first_row=0):
    count, rows = target.shape[:2]

    def chunk_copy(index):
        start = pl.multiple_of(first_row + index * rows, rows)
        return pltpu.make_async_copy(source.at[pl.ds(start, rows), :], target.at[index], sems.at[index])

    for index in range(count):
        chunk_copy(index).start()
    return lambda index: chunk_copy(index).wait()


def teacher_units_kernel(core_ref, emb_ref, unit_ref, half_ref):
    unit_ref[...] = unit_rows(emb_ref[...].astype(jnp.float32))[0].astype(jnp.bfloat16)
    half = half_ref.shape[0]
    half_ref[...] = unit_ref[part(core_ref[0], half), :]


def teacher_units(core, teacher_emb):
    rows, width = teacher_emb.shape
    return pl.pallas_call(
        teacher_units_kernel,
        in_specs=[whole(pltpu.SMEM), whole()],
        out_specs=[whole(), whole()],
        out_shape=[
            jax.ShapeDtypeStruct((rows, width), jnp.bfloat16),
            jax.ShapeDtypeStruct((rows // 2, width), jnp.bfloat16),
        ],
        compiler_params=params(4),
        cost_estimate=cost(4 * rows * width, 8 * rows * width),
        name="teacher_units",
    )(core, in_hbm(teacher_emb))


def wide_tops_kernel(unit_ref, protos_hbm, tops_ref, protos_ref, sems, top_ref):
    rows = unit_ref.shape[0]
    steps, block = protos_ref.shape[:2]
    wide = min(WIDE, block)
    arrived = fetch(protos_hbm, protos_ref, sems)
    top_ref[...] = jnp.full(top_ref.shape, -jnp.inf, jnp.float32)

    def step(index, carry):
        arrived(index)
        top = top_ref[:rows, :]
        for start in range(0, block, wide):
            products = scores(unit_ref[...], protos_ref[index, start : start + wide, :])
            top = jnp.maximum(top, lane_fold(products, jnp.maximum))
        top_ref[:rows, :] = top
        return carry

    lax.fori_loop(0, steps, step, 0)
    tops = jnp.max(jnp.transpose(top_ref[...]), axis=0, keepdims=True)
    tops_ref[...] = jnp.broadcast_to(tops[None], tops_ref.shape)


def wide_tops(unit, protos, order, copies, steps):
    rows, width = unit.shape
    count = protos.shape[0]
    return pl.pallas_call(
        skipping(wide_tops_kernel, 2, len(order)),
        in_specs=[whole(), whole(pl.ANY)] + [whole(pl.ANY)] * len(order),
        out_specs=whole(),
        out_shape=jax.ShapeDtypeStruct((copies, 1, 256), jnp.float32),
        scratch_shapes=[
            pltpu.VMEM((steps, count // steps, width), jnp.bfloat16),
            pltpu.SemaphoreType.DMA((steps,)),
            pltpu.VMEM((256, 128), jnp.float32),
        ],
        compiler_params=params(16),
        cost_estimate=cost(2 * rows * width * count, 2 * width * count),
        name="wide_tops",
    )(unit, in_hbm(protos), *order)


def repel_kernel(group, index_ref, unit_ref, tops_ref, scale_ref, protos_hbm, *rest):
    out_refs, (protos_ref, sems, acc_ref, sum_ref, bias_ref) = rest[:-5], rest[-5:]
    rows, width = unit_ref.shape
    steps, block = protos_ref.shape[:2]
    wide = min(WIDE, block)
    arrived = fetch(protos_hbm, protos_ref, sems)
    first = index_ref[0] * group
    top = tops_ref[first]
    for other in range(1, group):
        top = jnp.maximum(top, tops_ref[first + other])
    bias_ref[...] = jnp.transpose(jnp.broadcast_to(top, (128, 256)))[:rows, :] * -teacher_rate
    acc_ref[...] = jnp.zeros(acc_ref.shape, jnp.float32)
    sum_ref[...] = jnp.zeros(sum_ref.shape, jnp.float32)

    def step(index, carry):
        arrived(index)
        bias = bias_ref[...]
        total = sum_ref[...]
        acc = acc_ref[...]
        for start in range(0, block, wide):
            protos = protos_ref[index, start : start + wide, :]
            products = scores(unit_ref[...], protos)
            pieces = []
            for lane in range(0, wide, 128):
                scaled = jnp.exp2(products[:, lane : lane + 128] * teacher_rate + bias)
                scaled = scaled * scale_ref[index, :, start + lane : start + lane + 128]
                total = total + scaled
                pieces.append(scaled.astype(jnp.bfloat16))
            acc = acc + jnp.dot(
                jnp.concatenate(pieces, axis=1), protos, preferred_element_type=jnp.float32
            )
        sum_ref[...] = total
        acc_ref[...] = acc
        return carry

    lax.fori_loop(0, steps, step, 0)
    total = jnp.sum(sum_ref[...], axis=1, keepdims=True)
    lanes = lax.broadcasted_iota(jnp.int32, sum_ref.shape, 1)
    sum_ref[...] = jnp.broadcast_to(total, sum_ref.shape)
    share = out_refs[0].shape[0]
    lanes = lanes[:share, :]
    for flip, out_ref in enumerate(out_refs):
        span = part(index_ref[1] ^ flip, share)
        total = sum_ref[span, :]
        out_ref[:, :width] = acc_ref[span, :].astype(out_ref.dtype)
        if flip == 0:
            out_ref[:, width:] = jnp.where(lanes == 0, total, 0.0)
        else:
            high = total.astype(jnp.bfloat16).astype(jnp.float32)
            middle = (total - high).astype(jnp.bfloat16).astype(jnp.float32)
            pieces = jnp.where(lanes == 0, high, jnp.where(lanes == 1, middle, total - high - middle))
            out_ref[:, width:] = jnp.where(lanes < 3, pieces, 0.0).astype(jnp.bfloat16)


def repel(index, unit, tops, scale, protos, order, proto_size):
    rows, width = unit.shape
    count = protos.shape[0]
    steps, _, block = scale.shape
    return pl.pallas_call(
        skipping(functools.partial(repel_kernel, proto_size), 5, len(order)),
        in_specs=[whole(pltpu.SMEM), whole(), whole(), whole(), whole(pl.ANY)] + [whole(pl.ANY)] * len(order),
        out_specs=[whole()] * proto_size,
        out_shape=[
            jax.ShapeDtypeStruct((rows // proto_size, width + 128), jnp.bfloat16 if flip else jnp.float32)
            for flip in range(proto_size)
        ],
        scratch_shapes=[
            pltpu.VMEM((steps, block, width), jnp.bfloat16),
            pltpu.SemaphoreType.DMA((steps,)),
            pltpu.VMEM((rows, width), jnp.float32),
            pltpu.VMEM((rows, 128), jnp.float32),
            pltpu.VMEM((rows, 128), jnp.float32),
        ],
        compiler_params=params(16),
        cost_estimate=cost(4 * rows * width * count, 2 * width * count, rows * count),
        name="repel",
    )(index, unit, tops, scale, in_hbm(protos), *order)


def attract_kernel(first_row, last, emb_ref, state_ref, protos_hbm, *rest):
    out_refs, scratch = rest[:-6], rest[-6:]
    protos_ref, sems, products_ref, acc_ref, sum_ref, top_ref = scratch
    width = emb_ref.shape[1]
    steps, block = protos_ref.shape[:2]
    arrived = fetch(protos_hbm, protos_ref, sems, first_row)
    old_top = state_ref[:, width + 128 :]
    top_ref[...] = old_top

    def first(index, carry):
        arrived(index)
        top = top_ref[...]
        for start in range(0, block, TILE):
            products = scores(emb_ref[...], protos_ref[index, start : start + TILE, :])
            products_ref[index, :, start : start + TILE] = products
            top = jnp.maximum(top, lane_fold(products, jnp.maximum))
        top_ref[...] = top
        return carry

    lax.fori_loop(0, steps, first, 0)
    top = jnp.broadcast_to(jnp.max(top_ref[...], axis=1, keepdims=True), top_ref.shape)
    fade = jnp.exp2((old_top - top) * student_rate)
    top_ref[...] = top
    sum_ref[...] = state_ref[:, width : width + 128] * fade
    acc_ref[...] = state_ref[:, :width] * jnp.tile(fade, (1, width // 128))

    def second(index, carry):
        top = top_ref[...]
        total = sum_ref[...]
        acc = acc_ref[...]
        for start in range(0, block, TILE):
            pieces = []
            for lane in range(start, start + TILE, 128):
                shifted = jnp.exp2((products_ref[index, :, lane : lane + 128] - top) * student_rate)
                total = total + shifted
                pieces.append(shifted.astype(jnp.bfloat16))
            acc = acc + jnp.dot(
                jnp.concatenate(pieces, axis=1),
                protos_ref[index, start : start + TILE, :],
                preferred_element_type=jnp.float32,
            )
        sum_ref[...] = total
        acc_ref[...] = acc
        return carry

    lax.fori_loop(0, steps, second, 0)
    if last:
        total = jnp.sum(sum_ref[...], axis=1, keepdims=True)
        sum_ref[...] = jnp.broadcast_to(total, sum_ref.shape)
    share = out_refs[0].shape[0]
    for slot, out_ref in enumerate(out_refs):
        rows = pl.ds(slot * share, share)
        out_ref[:, :width] = acc_ref[rows, :]
        out_ref[:, width : width + 128] = sum_ref[rows, :]
        out_ref[:, width + 128 :] = top_ref[rows, :]


def attract(emb, state, protos, first_row, count, steps, outputs):
    rows, width = emb.shape
    block = count // steps
    return pl.pallas_call(
        functools.partial(attract_kernel, first_row, outputs > 1),
        in_specs=[whole(), whole(), whole(pl.ANY)],
        out_specs=[whole()] * outputs,
        out_shape=[jax.ShapeDtypeStruct((rows // outputs, width + 256), jnp.float32)] * outputs,
        scratch_shapes=[
            pltpu.VMEM((steps, block, width), jnp.bfloat16),
            pltpu.SemaphoreType.DMA((steps,)),
            pltpu.VMEM((steps, rows, block), jnp.float32),
            pltpu.VMEM((rows, width), jnp.float32),
            pltpu.VMEM((rows, 128), jnp.float32),
            pltpu.VMEM((rows, 128), jnp.float32),
        ],
        compiler_params=params(24),
        cost_estimate=cost(4 * rows * width * count, 2 * width * count, rows * count),
        name="attract",
    )(emb, state, in_hbm(protos))


def three_pieces(values):
    high = values.astype(jnp.bfloat16)
    rest = values - high.astype(jnp.float32)
    middle = rest.astype(jnp.bfloat16)
    low = (rest - middle.astype(jnp.float32)).astype(jnp.bfloat16)
    return jnp.concatenate([high, middle, low, jnp.zeros((13, values.shape[1]), jnp.bfloat16)], axis=0)


def lane_scales(folded, protos_total):
    sums = [
        jnp.sum(jnp.transpose(folded[start : start + 128, :]), axis=0, keepdims=True)
        for start in range(0, folded.shape[0], 128)
    ]
    return 1.0 / (protos_total * jnp.concatenate(sums, axis=1))


def give_sums(copies_ref, totals):
    rows = [totals[:, start : start + 128] for start in range(0, totals.shape[1], 128)]
    spare = copies_ref.shape[1] - len(rows)
    if spare:
        rows.append(jnp.zeros((spare, 128), jnp.float32))
    packed = jnp.concatenate(rows, axis=0).astype(jnp.bfloat16)
    copies_ref[...] = jnp.broadcast_to(packed[None], copies_ref.shape)


def take_scales(parts_ref, scale_ref):
    crops_total = scale_ref.shape[1]
    sums = jnp.sum(parts_ref[...].astype(jnp.float32), axis=0)
    for row in range(crops_total // 128):
        scale_ref[:, row * 128 : row * 128 + 128] = 1.0 / (crops_total * sums[row : row + 1, :])


def sums_shape(copies, crops_total):
    return (copies, -(-crops_total // 2048) * 16, 128)


def first_sweep_kernel(
    chunk, protos_total, index_ref, protos_hbm, mine_hbm, other_hbm, bias_ref, copies_ref, weights_hbm, protos_ref, units_ref, weights_ref, rounded_ref, scale_ref, sems, out_sems,
):
    thin, crops_total = weights_ref.shape
    half = mine_hbm.shape[0]
    core = index_ref[1]
    copies = (
        pltpu.make_async_copy(protos_hbm.at[part(index_ref[0], thin), :], protos_ref, sems.at[0]),
        pltpu.make_async_copy(mine_hbm, units_ref.at[part(core, half), :], sems.at[1]),
        pltpu.make_async_copy(other_hbm, units_ref.at[part(1 - core, half), :], sems.at[2]),
    )
    for copy in copies:
        copy.start()
    for copy in copies:
        copy.wait()

    def chunk_out(index):
        return pltpu.make_async_copy(
            rounded_ref.at[index], weights_hbm.at[part(index, chunk), :], out_sems.at[index]
        )

    def weigh(index, carry):
        rows = part(index, chunk)
        protos = protos_ref[rows, :]
        folded = jnp.zeros((chunk, 128), jnp.float32)
        for start in range(0, crops_total, TILE):
            columns = slice(start, start + TILE)
            products = scores(protos, units_ref[columns, :])
            weights = jnp.exp2(products * teacher_rate + bias_ref[:, columns])
            weights_ref[rows, columns] = weights
            rounded_ref[index, :, columns] = weights.astype(jnp.bfloat16)
            folded = folded + lane_fold(weights, jnp.add)
        sums = jnp.sum(folded, axis=1, keepdims=True)
        scale_ref[rows, :] = jnp.broadcast_to(1.0 / (protos_total * sums), (chunk, 128))
        chunk_out(index).start()
        return carry

    lax.fori_loop(0, thin // chunk, weigh, 0)
    small = min(thin, 64)

    def add_up(index, totals):
        rows = part(index, small)
        scaled = weights_ref[rows, :] * jnp.tile(scale_ref[rows, :], (1, crops_total // 128))
        return totals + jnp.sum(scaled.reshape(-1, 8, crops_total), axis=0)

    totals = lax.fori_loop(0, thin // small, add_up, jnp.zeros((8, crops_total), jnp.float32))
    give_sums(copies_ref, jnp.sum(totals, axis=0, keepdims=True))
    for index in range(thin // chunk):
        chunk_out(index).wait()


def first_sweep(index, protos, mine, other, base, order, copies, thin, protos_total):
    width = protos.shape[1]
    crops_total = 2 * mine.shape[0]
    chunk = min(thin, 1024)
    return pl.pallas_call(
        skipping(functools.partial(first_sweep_kernel, chunk, protos_total), 5, len(order)),
        in_specs=[whole(pltpu.SMEM), whole(pl.ANY), whole(pl.ANY), whole(pl.ANY), whole()]
        + [whole(pl.ANY)] * len(order),
        out_specs=[whole(), whole(pl.ANY)],
        out_shape=[
            jax.ShapeDtypeStruct(sums_shape(copies, crops_total), jnp.bfloat16),
            pltpu.HBM((thin, crops_total), jnp.bfloat16),
        ],
        scratch_shapes=[
            pltpu.VMEM((thin, width), jnp.bfloat16),
            pltpu.VMEM((crops_total, width), jnp.bfloat16),
            pltpu.VMEM((thin, crops_total), jnp.float32),
            pltpu.VMEM((thin // chunk, chunk, crops_total), jnp.bfloat16),
            pltpu.VMEM((thin, 128), jnp.float32),
            pltpu.SemaphoreType.DMA((3,)),
            pltpu.SemaphoreType.DMA((thin // chunk,)),
        ],
        compiler_params=params(32 if crops_total <= 2048 else 56),
        cost_estimate=cost(2 * thin * width * crops_total, 2 * thin * crops_total, thin * crops_total),
        name="first_sweep",
    )(index, in_hbm(protos), mine, other, base, *order)


def fetch_rows(weights_hbm, weights_ref, sems):
    steps, chunk, _ = weights_ref.shape

    def rows_copy(index):
        return pltpu.make_async_copy(
            weights_hbm.at[part(index, chunk), :], weights_ref.at[index], sems.at[index]
        )

    for index in range(steps):
        rows_copy(index).start()
    return lambda index: rows_copy(index).wait()


def scaled_fold(weights_ref, index, scale_ref):
    _, chunk, crops_total = weights_ref.shape
    folds = []
    for row in range(0, chunk, 64):
        fold = None
        for start in range(0, crops_total, TILE):
            columns = slice(start, start + TILE)
            weights = weights_ref[index, row : row + 64, columns].astype(jnp.float32)
            scaled = lane_fold(weights * scale_ref[:, columns], jnp.add)
            fold = scaled if fold is None else fold + scaled
        folds.append(fold)
    return jnp.concatenate(folds, axis=0)


def next_sweep_kernel(
    protos_total, weights_hbm, parts_ref, copies_ref, weights_ref, scale_ref, pieces_ref, totals_ref, sems,
):
    steps, chunk, crops_total = weights_ref.shape
    arrived = fetch_rows(weights_hbm, weights_ref, sems)
    take_scales(parts_ref, scale_ref)
    totals_ref[...] = jnp.zeros(totals_ref.shape, jnp.float32)

    def weigh(index):
        return three_pieces(lane_scales(scaled_fold(weights_ref, index, scale_ref), protos_total))

    def add_up(index):
        return jnp.dot(pieces_ref[...], weights_ref[index], preferred_element_type=jnp.float32)

    arrived(0)
    pieces_ref[...] = weigh(0)

    def sweep(index, carry):
        arrived(index)
        sums = add_up(index - 1)
        pieces = weigh(index)
        totals_ref[...] += sums
        pieces_ref[...] = pieces
        return carry

    lax.fori_loop(1, steps, sweep, 0)
    totals = totals_ref[...] + add_up(steps - 1)
    give_sums(copies_ref, jnp.sum(totals, axis=0, keepdims=True))


def next_sweep(weights, parts, order, protos_total):
    thin, crops_total = weights.shape
    copies = parts.shape[0]
    chunk = min(thin, 256)
    return pl.pallas_call(
        skipping(functools.partial(next_sweep_kernel, protos_total), 2, len(order)),
        in_specs=[whole(pl.ANY), whole()] + [whole(pl.ANY)] * len(order),
        out_specs=whole(),
        out_shape=jax.ShapeDtypeStruct(sums_shape(copies, crops_total), jnp.bfloat16),
        scratch_shapes=[
            pltpu.VMEM((thin // chunk, chunk, crops_total), jnp.bfloat16),
            pltpu.VMEM((1, crops_total), jnp.float32),
            pltpu.VMEM((16, chunk), jnp.bfloat16),
            pltpu.VMEM((16, crops_total), jnp.float32),
            pltpu.SemaphoreType.DMA((thin // chunk,)),
        ],
        compiler_params=params(16 if crops_total <= 2048 else 50),
        cost_estimate=cost(8 * thin * crops_total, 2 * thin * crops_total),
        name="next_sweep",
    )(in_hbm(weights), parts, *order)


def last_scales_kernel(
    protos_total, weights_hbm, parts_ref, copies_ref, weights_ref, scale_ref, out_ref, sems,
):
    steps, chunk, crops_total = weights_ref.shape
    arrived = fetch_rows(weights_hbm, weights_ref, sems)
    take_scales(parts_ref, scale_ref)

    def weigh(index, carry):
        arrived(index)
        out_ref[:, part(index, chunk)] = lane_scales(
            scaled_fold(weights_ref, index, scale_ref), protos_total
        )
        return carry

    lax.fori_loop(0, steps, weigh, 0)
    copies_ref[...] = jnp.broadcast_to(out_ref[...][None], copies_ref.shape)


def last_scales(weights, parts, order, copies, protos_total):
    thin, crops_total = weights.shape
    chunk = min(thin, 256)
    return pl.pallas_call(
        skipping(functools.partial(last_scales_kernel, protos_total), 2, len(order)),
        in_specs=[whole(pl.ANY), whole()] + [whole(pl.ANY)] * len(order),
        out_specs=whole(),
        out_shape=jax.ShapeDtypeStruct((copies, 1, thin), jnp.float32),
        scratch_shapes=[
            pltpu.VMEM((thin // chunk, chunk, crops_total), jnp.bfloat16),
            pltpu.VMEM((1, crops_total), jnp.float32),
            pltpu.VMEM((1, thin), jnp.float32),
            pltpu.SemaphoreType.DMA((thin // chunk,)),
        ],
        compiler_params=params(16 if crops_total <= 2048 else 50),
        cost_estimate=cost(4 * thin * crops_total, 2 * thin * crops_total),
        name="last_scales",
    )(in_hbm(weights), parts, *order)


def student_front_kernel(
    index_ref, bias_ref, own_hbm, x_hbm, core_hbm, last_hbm, first_hbm, second_hbm, keep_ref, give_ref,
    first_ref, second_ref, rows_ref, sems,
):
    share = own_hbm.shape[0]
    copies = [
        pltpu.make_async_copy(source, rows_ref.at[slot * share : (slot + 1) * share, :], sems.at[slot])
        for slot, source in enumerate((own_hbm, x_hbm, core_hbm, last_hbm))
    ]
    copies.append(pltpu.make_async_copy(first_hbm, first_ref, sems.at[4]))
    second_copy = pltpu.make_async_copy(second_hbm, second_ref, sems.at[5])
    for copy in copies:
        copy.start()
    second_copy.start()
    hidden = first_ref.shape[1]
    bias = bias_ref[:, part(index_ref[0], hidden)]
    for copy in copies:
        copy.wait()
    h_first = gelu(
        jnp.dot(rows_ref[...], first_ref[...], preferred_element_type=jnp.float32) + bias
    ).astype(jnp.bfloat16)
    second_copy.wait()
    for start in range(0, second_ref.shape[1], 512):
        columns = slice(start, start + 512)
        product = jnp.dot(h_first, second_ref[:, columns], preferred_element_type=jnp.float32)
        keep_ref[:, columns] = product[: 2 * share]
        give_ref[:, columns] = product[2 * share :]


def student_front(index, bias, rows, first, second, order):
    share, features = rows[0].shape
    hidden, units = second.shape
    return pl.pallas_call(
        skipping(student_front_kernel, 8, len(order)),
        in_specs=[whole(pltpu.SMEM), whole()] + [whole(pl.ANY)] * (6 + len(order)),
        out_specs=[whole(), whole()],
        out_shape=[jax.ShapeDtypeStruct((2 * share, units), jnp.float32)] * 2,
        scratch_shapes=[
            pltpu.VMEM(first.shape, jnp.bfloat16),
            pltpu.VMEM(second.shape, jnp.bfloat16),
            pltpu.VMEM((4 * share, features), jnp.bfloat16),
            pltpu.SemaphoreType.DMA((6,)),
        ],
        compiler_params=params(16),
        cost_estimate=cost(8 * share * hidden * (features + units), 2 * hidden * (features + units)),
        name="student_front",
    )(index, in_hbm(bias.reshape(1, -1)), in_hbm(rows[0]), *rows[1:], in_hbm(first), in_hbm(second), *order)


def student_middle_kernel(
    index_ref, keep_ref, core_ref, x_ref, bias_ref, own_ref, partner_ref, other_ref, last_ref, last_bias_ref,
    unit_ref, emb_ref, lengths_ref, hidden_ref,
):
    share = x_ref.shape[0]
    block = own_ref.shape[0]
    sums = keep_ref[:share, :] + core_ref[:share, :] + x_ref[...]
    hidden_ref[...] = gelu(sums + bias_ref[...]).astype(jnp.bfloat16)
    index = index_ref[0]
    weights = ((0, own_ref[...]), (2, partner_ref[...]), (1, other_ref[...]), (3, last_ref[...]))
    bottleneck = jnp.broadcast_to(last_bias_ref[...], unit_ref.shape)
    for flip, weight in weights:
        bottleneck = bottleneck + jnp.dot(
            hidden_ref[:, part(index ^ flip, block)], weight, preferred_element_type=jnp.float32
        )
    unit, lengths = unit_rows(bottleneck)
    unit_ref[...] = unit
    emb_ref[...] = unit.astype(jnp.bfloat16)
    lengths_ref[...] = jnp.broadcast_to(lengths, lengths_ref.shape)


def student_middle(index, keep, core_rows, x_rows, bias, weights, last_bias):
    share, units = x_rows.shape
    width = weights[0].shape[1]
    return pl.pallas_call(
        student_middle_kernel,
        in_specs=[whole(pltpu.SMEM)] + [whole()] * 9,
        out_specs=[whole()] * 3,
        out_shape=[
            jax.ShapeDtypeStruct((share, width), jnp.float32),
            jax.ShapeDtypeStruct((share, width), jnp.bfloat16),
            jax.ShapeDtypeStruct((share, 128), jnp.float32),
        ],
        scratch_shapes=[pltpu.VMEM((share, units), jnp.bfloat16)],
        compiler_params=params(12),
        cost_estimate=cost(2 * share * units * width, 2 * units * width + 16 * share * units),
        name="student_middle",
    )(index, keep, core_rows, x_rows, in_hbm(bias.reshape(1, -1)), in_hbm(weights[0]), *weights[1:], in_hbm(last_bias.reshape(1, -1)))


def finish_kernel(unit_ref, lengths_ref, *rest):
    out_ref, blocks = rest[-1], rest[:-1]
    attracts, repels = blocks[: len(blocks) // 2], blocks[len(blocks) // 2 :]
    width = unit_ref.shape[1]
    row_top = functools.reduce(jnp.maximum, [ref[:, width + 128 :] for ref in attracts])
    attract_sum = repel_sum = 0.0
    row_sum = column_sum = 0.0
    for ref in attracts:
        fade = jnp.exp2((ref[:, width + 128 :] - row_top) * student_rate)
        row_sum = row_sum + ref[:, width : width + 128] * fade
        attract_sum = attract_sum + ref[:, :width] * jnp.tile(fade, (1, width // 128))
    for ref in repels:
        column_sum = column_sum + jnp.sum(ref[:, width:].astype(jnp.float32), axis=1, keepdims=True)
        repel_sum = repel_sum + ref[:, :width].astype(jnp.float32)
    emb_grad = (
        attract_sum / jnp.tile(row_sum, (1, width // 128))
        - repel_sum / column_sum
    ) / student_temp
    unit = unit_ref[...]
    along = jnp.sum(unit * emb_grad, axis=1, keepdims=True)
    out_ref[...] = (emb_grad - unit * along) / jnp.tile(lengths_ref[...], (1, width // 128))


def finish(unit, lengths, attracts, repels):
    return pl.pallas_call(
        finish_kernel,
        in_specs=[whole()] * (2 + len(attracts) + len(repels)),
        out_specs=whole(),
        out_shape=jax.ShapeDtypeStruct(unit.shape, jnp.float32),
        compiler_params=params(8),
        cost_estimate=cost(40 * unit.size, 40 * unit.size),
        name="finish",
    )(unit, lengths, *attracts, *repels)


def swap(values, axis, flip):
    return lax.ppermute(values, axis, [(i, i ^ flip) for i in range(lax.axis_size(axis))])


def bit_reversed(values, count):
    bits = count.bit_length() - 1
    split = values.reshape((2,) * bits + values.shape[1:])
    turned = jnp.transpose(split, tuple(reversed(range(bits))) + tuple(range(bits, split.ndim)))
    return turned.reshape(values.shape)


def gather_batch(values):
    step = lax.axis_size("batch") // 2
    stages = [values]
    while step:
        other = swap(values, "batch", step)
        upper = (lax.axis_index("batch") // step) % 2
        values = jnp.where(
            upper == 0, jnp.concatenate([values, other]), jnp.concatenate([other, values])
        )
        stages.append(values)
        step //= 2
    return stages


def send_blocks(blocks):
    return [blocks[0]] + [swap(block, "proto", flip) for flip, block in enumerate(blocks) if flip]


def all_to_all(copies, axes):
    return lax.all_to_all(copies, axes, 0, 0, tiled=True)


def body(crops, teacher_emb, w_first, b_first, w_second, b_second, w_third, b_third, protos):
    batch_index = lax.axis_index("batch")
    proto_index = lax.axis_index("proto")
    batch_size = lax.axis_size("batch")
    proto_size = lax.axis_size("proto")
    devices = batch_size * proto_size
    share_rows = crops.shape[0]
    group_rows = teacher_emb.shape[0]
    crops_total = group_rows * batch_size
    protos_total = protos.shape[0] * proto_size
    count, width = protos.shape
    thin = count // batch_size
    core = proto_index % 2
    proto_ref = proto_index.reshape(1)
    thin_ref = jnp.stack([batch_index, core])
    wide_ref = jnp.stack([batch_index, proto_index])

    own_unit, half = teacher_units(core.reshape(1), teacher_emb)
    stages = gather_batch(half)
    mine = stages[-1]
    other = swap(mine, "proto", 1)

    crops_x = swap(crops, "proto", 2)
    rows = [crops, crops_x, swap(crops, "proto", 1), swap(crops_x, "proto", 1)]
    third_x = swap(w_third, "proto", 2)
    thirds = [w_third, third_x, swap(w_third, "proto", 1), swap(third_x, "proto", 1)]
    top_copies = wide_tops(own_unit, protos, (stages[1],), devices, 8)
    keep, give = student_front(proto_ref, b_first, rows, w_first, w_second, (stages[2], third_x, top_copies))
    all_tops = all_to_all(top_copies, BOTH)
    tops = jnp.max(all_tops.reshape(batch_size, proto_size, 256)[:, :, :group_rows], axis=1)
    tops = bit_reversed(tops, batch_size).reshape(batch_size, 2, group_rows // 2)
    base = jnp.transpose(tops, (1, 0, 2)).reshape(1, crops_total) * -teacher_rate

    core_rows = swap(give, "proto", 1)
    x_sent = keep[share_rows:] + core_rows[share_rows:]
    x_rows = swap(x_sent, "proto", 2)
    unit, rounded, lengths = student_middle(
        proto_ref, keep, core_rows, x_rows, b_second, thirds, b_third
    )
    student_emb = jnp.concatenate([rounded] + [swap(rounded, "proto", flip) for flip in range(1, proto_size)])
    empty = jnp.concatenate(
        [jnp.zeros((group_rows, width + 128), jnp.float32), jnp.full((group_rows, 128), -1e30, jnp.float32)], axis=1
    )
    (state,) = attract(student_emb, empty, protos, 0, count // 2, 4, 1)
    slots = attract(student_emb, state, protos, count // 2, count // 2, 4, proto_size)
    attract_parts = send_blocks(slots)

    copies, weights = first_sweep(thin_ref, protos, mine, other, base, (x_sent, *thirds[2:]), devices, thin, protos_total)
    for _ in range(ITERS - 2):
        copies = next_sweep(weights, all_to_all(copies, BOTH), (rounded,), protos_total)
    scale_copies = last_scales(weights, all_to_all(copies, BOTH), (state,), batch_size, protos_total)
    all_scale = all_to_all(scale_copies, "batch")
    repels = repel(wide_ref, own_unit, all_tops, all_scale, protos, (slots[0],), proto_size)
    return finish(unit, lengths, attract_parts, send_blocks(repels))


def solution(mesh):
    in_specs = (
        P(("batch", "proto"), None),
        P("batch", None),
        P(None, "proto"),
        P(),
        P("proto", None),
        P(),
        P("proto", None),
        P(),
        P("proto", None),
    )
    out_specs = P(("batch", "proto"), None)
    return jax.shard_map(body, mesh=mesh, in_specs=in_specs, out_specs=out_specs, check_vma=False)
```

```python
import functools
import math

import jax
import jax.numpy as jnp
from jax import lax
from jax.experimental import pallas as pl
from jax.experimental.pallas import tpu as pltpu
from jax.sharding import PartitionSpec as P

ITERS = 3

student_temp = 0.1
teacher_temp = 0.07
norm_eps = 1e-06
teacher_rate = math.log2(math.e) / teacher_temp
student_rate = math.log2(math.e) / student_temp

MIB = 1024 * 1024
BOTH = ("batch", "proto")
TILE = 256
WIDE = 512


def scores(left_rows, right_rows):
    return lax.dot_general(
        left_rows, right_rows, (((1,), (1,)), ((), ())), preferred_element_type=jnp.float32
    )


def unit_rows(values):
    lengths = jnp.sqrt(jnp.sum(values * values, axis=1, keepdims=True) + norm_eps)
    return (values / lengths, lengths)


def gelu(values):
    return 0.5 * values * (1.0 + lax.erf(values * math.sqrt(0.5)))


def whole(memory_space=pltpu.VMEM):
    return pl.BlockSpec(memory_space=memory_space)


def in_hbm(array):
    return pltpu.with_memory_space_constraint(array, pltpu.HBM)


def skipping(kernel, first, count):
    def trimmed(*refs):
        kernel(*refs[:first], *refs[first + count :])

    return trimmed


def part(index, size):
    return pl.ds(pl.multiple_of(index * size, size), size)


def lane_fold(values, combine):
    folded = values[:, :128]
    for start in range(128, values.shape[1], 128):
        folded = combine(folded, values[:, start : start + 128])
    return folded


def params(mib):
    return pltpu.CompilerParams(vmem_limit_bytes=mib * MIB)


def cost(flops, bytes_accessed, transcendentals=0):
    return pl.CostEstimate(
        flops=int(flops), bytes_accessed=int(bytes_accessed), transcendentals=int(transcendentals)
    )


def fetch(source, target, sems, first_row=0):
    count, rows = target.shape[:2]

    def chunk_copy(index):
        start = pl.multiple_of(first_row + index * rows, rows)
        return pltpu.make_async_copy(source.at[pl.ds(start, rows), :], target.at[index], sems.at[index])

    for index in range(count):
        chunk_copy(index).start()
    return lambda index: chunk_copy(index).wait()


def teacher_units_kernel(core_ref, emb_ref, unit_ref, half_ref):
    unit_ref[...] = unit_rows(emb_ref[...].astype(jnp.float32))[0].astype(jnp.bfloat16)
    half = half_ref.shape[0]
    half_ref[...] = unit_ref[part(core_ref[0], half), :]


def teacher_units(core, teacher_emb):
    rows, width = teacher_emb.shape
    return pl.pallas_call(
        teacher_units_kernel,
        in_specs=[whole(pltpu.SMEM), whole()],
        out_specs=[whole(), whole()],
        out_shape=[
            jax.ShapeDtypeStruct((rows, width), jnp.bfloat16),
            jax.ShapeDtypeStruct((rows // 2, width), jnp.bfloat16),
        ],
        compiler_params=params(4),
        cost_estimate=cost(4 * rows * width, 8 * rows * width),
        name="teacher_units",
    )(core, in_hbm(teacher_emb))


def wide_tops_kernel(unit_ref, protos_hbm, tops_ref, protos_ref, sems, top_ref):
    rows = unit_ref.shape[0]
    steps, block = protos_ref.shape[:2]
    wide = min(WIDE, block)
    arrived = fetch(protos_hbm, protos_ref, sems)
    top_ref[...] = jnp.full(top_ref.shape, -jnp.inf, jnp.float32)

    def step(index, carry):
        arrived(index)
        top = top_ref[:rows, :]
        for start in range(0, block, wide):
            products = scores(unit_ref[...], protos_ref[index, start : start + wide, :])
            top = jnp.maximum(top, lane_fold(products, jnp.maximum))
        top_ref[:rows, :] = top
        return carry

    lax.fori_loop(0, steps, step, 0)
    tops = jnp.max(jnp.transpose(top_ref[...]), axis=0, keepdims=True)
    tops_ref[...] = jnp.broadcast_to(tops[None], tops_ref.shape)


def wide_tops(unit, protos, order, copies, steps):
    rows, width = unit.shape
    count = protos.shape[0]
    return pl.pallas_call(
        skipping(wide_tops_kernel, 2, len(order)),
        in_specs=[whole(), whole(pl.ANY)] + [whole(pl.ANY)] * len(order),
        out_specs=whole(),
        out_shape=jax.ShapeDtypeStruct((copies, 1, 256), jnp.float32),
        scratch_shapes=[
            pltpu.VMEM((steps, count // steps, width), jnp.bfloat16),
            pltpu.SemaphoreType.DMA((steps,)),
            pltpu.VMEM((256, 128), jnp.float32),
        ],
        compiler_params=params(16),
        cost_estimate=cost(2 * rows * width * count, 2 * width * count),
        name="wide_tops",
    )(unit, in_hbm(protos), *order)


def repel_kernel(group, index_ref, unit_ref, tops_ref, scale_ref, protos_hbm, *rest):
    out_refs, (protos_ref, sems, acc_ref, sum_ref, bias_ref) = rest[:-5], rest[-5:]
    rows, width = unit_ref.shape
    steps, block = protos_ref.shape[:2]
    wide = min(WIDE, block)
    arrived = fetch(protos_hbm, protos_ref, sems)
    first = index_ref[0] * group
    top = tops_ref[first]
    for other in range(1, group):
        top = jnp.maximum(top, tops_ref[first + other])
    bias_ref[...] = jnp.transpose(jnp.broadcast_to(top, (128, 256)))[:rows, :] * -teacher_rate
    acc_ref[...] = jnp.zeros(acc_ref.shape, jnp.float32)
    sum_ref[...] = jnp.zeros(sum_ref.shape, jnp.float32)

    def step(index, carry):
        arrived(index)
        bias = bias_ref[...]
        total = sum_ref[...]
        acc = acc_ref[...]
        for start in range(0, block, wide):
            protos = protos_ref[index, start : start + wide, :]
            products = scores(unit_ref[...], protos)
            pieces = []
            for lane in range(0, wide, 128):
                scaled = jnp.exp2(products[:, lane : lane + 128] * teacher_rate + bias)
                scaled = scaled * scale_ref[index, :, start + lane : start + lane + 128]
                total = total + scaled
                pieces.append(scaled.astype(jnp.bfloat16))
            acc = acc + jnp.dot(
                jnp.concatenate(pieces, axis=1), protos, preferred_element_type=jnp.float32
            )
        sum_ref[...] = total
        acc_ref[...] = acc
        return carry

    lax.fori_loop(0, steps, step, 0)
    total = jnp.sum(sum_ref[...], axis=1, keepdims=True)
    lanes = lax.broadcasted_iota(jnp.int32, sum_ref.shape, 1)
    sum_ref[...] = jnp.broadcast_to(total, sum_ref.shape)
    share = out_refs[0].shape[0]
    lanes = lanes[:share, :]
    for flip, out_ref in enumerate(out_refs):
        span = part(index_ref[1] ^ flip, share)
        total = sum_ref[span, :]
        out_ref[:, :width] = acc_ref[span, :].astype(out_ref.dtype)
        if flip == 0:
            out_ref[:, width:] = jnp.where(lanes == 0, total, 0.0)
        else:
            high = total.astype(jnp.bfloat16).astype(jnp.float32)
            middle = (total - high).astype(jnp.bfloat16).astype(jnp.float32)
            pieces = jnp.where(lanes == 0, high, jnp.where(lanes == 1, middle, total - high - middle))
            out_ref[:, width:] = jnp.where(lanes < 3, pieces, 0.0).astype(jnp.bfloat16)


def repel(index, unit, tops, scale, protos, order, proto_size):
    rows, width = unit.shape
    count = protos.shape[0]
    steps, _, block = scale.shape
    return pl.pallas_call(
        skipping(functools.partial(repel_kernel, proto_size), 5, len(order)),
        in_specs=[whole(pltpu.SMEM), whole(), whole(), whole(), whole(pl.ANY)] + [whole(pl.ANY)] * len(order),
        out_specs=[whole()] * proto_size,
        out_shape=[
            jax.ShapeDtypeStruct((rows // proto_size, width + 128), jnp.bfloat16 if flip else jnp.float32)
            for flip in range(proto_size)
        ],
        scratch_shapes=[
            pltpu.VMEM((steps, block, width), jnp.bfloat16),
            pltpu.SemaphoreType.DMA((steps,)),
            pltpu.VMEM((rows, width), jnp.float32),
            pltpu.VMEM((rows, 128), jnp.float32),
            pltpu.VMEM((rows, 128), jnp.float32),
        ],
        compiler_params=params(16),
        cost_estimate=cost(4 * rows * width * count, 2 * width * count, rows * count),
        name="repel",
    )(index, unit, tops, scale, in_hbm(protos), *order)


def attract_kernel(first_row, last, emb_ref, state_ref, protos_hbm, *rest):
    out_refs, scratch = rest[:-6], rest[-6:]
    protos_ref, sems, products_ref, acc_ref, sum_ref, top_ref = scratch
    width = emb_ref.shape[1]
    steps, block = protos_ref.shape[:2]
    arrived = fetch(protos_hbm, protos_ref, sems, first_row)
    old_top = state_ref[:, width + 128 :]
    top_ref[...] = old_top

    def first(index, carry):
        arrived(index)
        top = top_ref[...]
        for start in range(0, block, TILE):
            products = scores(emb_ref[...], protos_ref[index, start : start + TILE, :])
            products_ref[index, :, start : start + TILE] = products
            top = jnp.maximum(top, lane_fold(products, jnp.maximum))
        top_ref[...] = top
        return carry

    lax.fori_loop(0, steps, first, 0)
    top = jnp.broadcast_to(jnp.max(top_ref[...], axis=1, keepdims=True), top_ref.shape)
    fade = jnp.exp2((old_top - top) * student_rate)
    top_ref[...] = top
    sum_ref[...] = state_ref[:, width : width + 128] * fade
    acc_ref[...] = state_ref[:, :width] * jnp.tile(fade, (1, width // 128))

    def second(index, carry):
        top = top_ref[...]
        total = sum_ref[...]
        acc = acc_ref[...]
        for start in range(0, block, TILE):
            pieces = []
            for lane in range(start, start + TILE, 128):
                shifted = jnp.exp2((products_ref[index, :, lane : lane + 128] - top) * student_rate)
                total = total + shifted
                pieces.append(shifted.astype(jnp.bfloat16))
            acc = acc + jnp.dot(
                jnp.concatenate(pieces, axis=1),
                protos_ref[index, start : start + TILE, :],
                preferred_element_type=jnp.float32,
            )
        sum_ref[...] = total
        acc_ref[...] = acc
        return carry

    lax.fori_loop(0, steps, second, 0)
    if last:
        total = jnp.sum(sum_ref[...], axis=1, keepdims=True)
        sum_ref[...] = jnp.broadcast_to(total, sum_ref.shape)
    share = out_refs[0].shape[0]
    for slot, out_ref in enumerate(out_refs):
        rows = pl.ds(slot * share, share)
        out_ref[:, :width] = acc_ref[rows, :]
        out_ref[:, width : width + 128] = sum_ref[rows, :]
        out_ref[:, width + 128 :] = top_ref[rows, :]


def attract(emb, state, protos, first_row, count, steps, outputs):
    rows, width = emb.shape
    block = count // steps
    return pl.pallas_call(
        functools.partial(attract_kernel, first_row, outputs > 1),
        in_specs=[whole(), whole(), whole(pl.ANY)],
        out_specs=[whole()] * outputs,
        out_shape=[jax.ShapeDtypeStruct((rows // outputs, width + 256), jnp.float32)] * outputs,
        scratch_shapes=[
            pltpu.VMEM((steps, block, width), jnp.bfloat16),
            pltpu.SemaphoreType.DMA((steps,)),
            pltpu.VMEM((steps, rows, block), jnp.float32),
            pltpu.VMEM((rows, width), jnp.float32),
            pltpu.VMEM((rows, 128), jnp.float32),
            pltpu.VMEM((rows, 128), jnp.float32),
        ],
        compiler_params=params(24),
        cost_estimate=cost(4 * rows * width * count, 2 * width * count, rows * count),
        name="attract",
    )(emb, state, in_hbm(protos))


def three_pieces(values):
    high = values.astype(jnp.bfloat16)
    rest = values - high.astype(jnp.float32)
    middle = rest.astype(jnp.bfloat16)
    low = (rest - middle.astype(jnp.float32)).astype(jnp.bfloat16)
    return jnp.concatenate([high, middle, low, jnp.zeros((13, values.shape[1]), jnp.bfloat16)], axis=0)


def lane_scales(folded, protos_total):
    sums = [
        jnp.sum(jnp.transpose(folded[start : start + 128, :]), axis=0, keepdims=True)
        for start in range(0, folded.shape[0], 128)
    ]
    return 1.0 / (protos_total * jnp.concatenate(sums, axis=1))


def give_sums(copies_ref, totals):
    rows = [totals[:, start : start + 128] for start in range(0, totals.shape[1], 128)]
    spare = copies_ref.shape[1] - len(rows)
    if spare:
        rows.append(jnp.zeros((spare, 128), jnp.float32))
    packed = jnp.concatenate(rows, axis=0).astype(jnp.bfloat16)
    copies_ref[...] = jnp.broadcast_to(packed[None], copies_ref.shape)


def take_scales(parts_ref, scale_ref):
    crops_total = scale_ref.shape[1]
    sums = jnp.sum(parts_ref[...].astype(jnp.float32), axis=0)
    for row in range(crops_total // 128):
        scale_ref[:, row * 128 : row * 128 + 128] = 1.0 / (crops_total * sums[row : row + 1, :])


def sums_shape(copies, crops_total):
    return (copies, -(-crops_total // 2048) * 16, 128)


def first_sweep_kernel(
    chunk, protos_total, index_ref, protos_hbm, mine_hbm, other_hbm, bias_ref, copies_ref, weights_hbm, protos_ref, units_ref, weights_ref, rounded_ref, scale_ref, sems, out_sems,
):
    thin, crops_total = weights_ref.shape
    half = mine_hbm.shape[0]
    core = index_ref[1]
    copies = (
        pltpu.make_async_copy(protos_hbm.at[part(index_ref[0], thin), :], protos_ref, sems.at[0]),
        pltpu.make_async_copy(mine_hbm, units_ref.at[part(core, half), :], sems.at[1]),
        pltpu.make_async_copy(other_hbm, units_ref.at[part(1 - core, half), :], sems.at[2]),
    )
    for copy in copies:
        copy.start()
    for copy in copies:
        copy.wait()

    def chunk_out(index):
        return pltpu.make_async_copy(
            rounded_ref.at[index], weights_hbm.at[part(index, chunk), :], out_sems.at[index]
        )

    def weigh(index, carry):
        rows = part(index, chunk)
        protos = protos_ref[rows, :]
        folded = jnp.zeros((chunk, 128), jnp.float32)
        for start in range(0, crops_total, TILE):
            columns = slice(start, start + TILE)
            products = scores(protos, units_ref[columns, :])
            weights = jnp.exp2(products * teacher_rate + bias_ref[:, columns])
            weights_ref[rows, columns] = weights
            rounded_ref[index, :, columns] = weights.astype(jnp.bfloat16)
            folded = folded + lane_fold(weights, jnp.add)
        sums = jnp.sum(folded, axis=1, keepdims=True)
        scale_ref[rows, :] = jnp.broadcast_to(1.0 / (protos_total * sums), (chunk, 128))
        chunk_out(index).start()
        return carry

    lax.fori_loop(0, thin // chunk, weigh, 0)
    small = min(thin, 64)

    def add_up(index, totals):
        rows = part(index, small)
        scaled = weights_ref[rows, :] * jnp.tile(scale_ref[rows, :], (1, crops_total // 128))
        return totals + jnp.sum(scaled.reshape(-1, 8, crops_total), axis=0)

    totals = lax.fori_loop(0, thin // small, add_up, jnp.zeros((8, crops_total), jnp.float32))
    give_sums(copies_ref, jnp.sum(totals, axis=0, keepdims=True))
    for index in range(thin // chunk):
        chunk_out(index).wait()


def first_sweep(index, protos, mine, other, base, order, copies, thin, protos_total):
    width = protos.shape[1]
    crops_total = 2 * mine.shape[0]
    chunk = min(thin, 1024)
    return pl.pallas_call(
        skipping(functools.partial(first_sweep_kernel, chunk, protos_total), 5, len(order)),
        in_specs=[whole(pltpu.SMEM), whole(pl.ANY), whole(pl.ANY), whole(pl.ANY), whole()]
        + [whole(pl.ANY)] * len(order),
        out_specs=[whole(), whole(pl.ANY)],
        out_shape=[
            jax.ShapeDtypeStruct(sums_shape(copies, crops_total), jnp.bfloat16),
            pltpu.HBM((thin, crops_total), jnp.bfloat16),
        ],
        scratch_shapes=[
            pltpu.VMEM((thin, width), jnp.bfloat16),
            pltpu.VMEM((crops_total, width), jnp.bfloat16),
            pltpu.VMEM((thin, crops_total), jnp.float32),
            pltpu.VMEM((thin // chunk, chunk, crops_total), jnp.bfloat16),
            pltpu.VMEM((thin, 128), jnp.float32),
            pltpu.SemaphoreType.DMA((3,)),
            pltpu.SemaphoreType.DMA((thin // chunk,)),
        ],
        compiler_params=params(32 if crops_total <= 2048 else 56),
        cost_estimate=cost(2 * thin * width * crops_total, 2 * thin * crops_total, thin * crops_total),
        name="first_sweep",
    )(index, in_hbm(protos), mine, other, base, *order)


def fetch_rows(weights_hbm, weights_ref, sems):
    steps, chunk, _ = weights_ref.shape

    def rows_copy(index):
        return pltpu.make_async_copy(
            weights_hbm.at[part(index, chunk), :], weights_ref.at[index], sems.at[index]
        )

    for index in range(steps):
        rows_copy(index).start()
    return lambda index: rows_copy(index).wait()


def scaled_fold(weights_ref, index, scale_ref):
    _, chunk, crops_total = weights_ref.shape
    folds = []
    for row in range(0, chunk, 64):
        fold = None
        for start in range(0, crops_total, TILE):
            columns = slice(start, start + TILE)
            weights = weights_ref[index, row : row + 64, columns].astype(jnp.float32)
            scaled = lane_fold(weights * scale_ref[:, columns], jnp.add)
            fold = scaled if fold is None else fold + scaled
        folds.append(fold)
    return jnp.concatenate(folds, axis=0)


def next_sweep_kernel(
    protos_total, weights_hbm, parts_ref, copies_ref, weights_ref, scale_ref, pieces_ref, totals_ref, sems,
):
    steps, chunk, crops_total = weights_ref.shape
    arrived = fetch_rows(weights_hbm, weights_ref, sems)
    take_scales(parts_ref, scale_ref)
    totals_ref[...] = jnp.zeros(totals_ref.shape, jnp.float32)

    def weigh(index):
        return three_pieces(lane_scales(scaled_fold(weights_ref, index, scale_ref), protos_total))

    def add_up(index):
        return jnp.dot(pieces_ref[...], weights_ref[index], preferred_element_type=jnp.float32)

    arrived(0)
    pieces_ref[...] = weigh(0)

    def sweep(index, carry):
        arrived(index)
        sums = add_up(index - 1)
        pieces = weigh(index)
        totals_ref[...] += sums
        pieces_ref[...] = pieces
        return carry

    lax.fori_loop(1, steps, sweep, 0)
    totals = totals_ref[...] + add_up(steps - 1)
    give_sums(copies_ref, jnp.sum(totals, axis=0, keepdims=True))


def next_sweep(weights, parts, order, protos_total):
    thin, crops_total = weights.shape
    copies = parts.shape[0]
    chunk = min(thin, 256)
    return pl.pallas_call(
        skipping(functools.partial(next_sweep_kernel, protos_total), 2, len(order)),
        in_specs=[whole(pl.ANY), whole()] + [whole(pl.ANY)] * len(order),
        out_specs=whole(),
        out_shape=jax.ShapeDtypeStruct(sums_shape(copies, crops_total), jnp.bfloat16),
        scratch_shapes=[
            pltpu.VMEM((thin // chunk, chunk, crops_total), jnp.bfloat16),
            pltpu.VMEM((1, crops_total), jnp.float32),
            pltpu.VMEM((16, chunk), jnp.bfloat16),
            pltpu.VMEM((16, crops_total), jnp.float32),
            pltpu.SemaphoreType.DMA((thin // chunk,)),
        ],
        compiler_params=params(16 if crops_total <= 2048 else 50),
        cost_estimate=cost(8 * thin * crops_total, 2 * thin * crops_total),
        name="next_sweep",
    )(in_hbm(weights), parts, *order)


def last_scales_kernel(
    protos_total, weights_hbm, parts_ref, copies_ref, weights_ref, scale_ref, out_ref, sems,
):
    steps, chunk, crops_total = weights_ref.shape
    arrived = fetch_rows(weights_hbm, weights_ref, sems)
    take_scales(parts_ref, scale_ref)

    def weigh(index, carry):
        arrived(index)
        out_ref[:, part(index, chunk)] = lane_scales(
            scaled_fold(weights_ref, index, scale_ref), protos_total
        )
        return carry

    lax.fori_loop(0, steps, weigh, 0)
    copies_ref[...] = jnp.broadcast_to(out_ref[...][None], copies_ref.shape)


def last_scales(weights, parts, order, copies, protos_total):
    thin, crops_total = weights.shape
    chunk = min(thin, 256)
    return pl.pallas_call(
        skipping(functools.partial(last_scales_kernel, protos_total), 2, len(order)),
        in_specs=[whole(pl.ANY), whole()] + [whole(pl.ANY)] * len(order),
        out_specs=whole(),
        out_shape=jax.ShapeDtypeStruct((copies, 1, thin), jnp.float32),
        scratch_shapes=[
            pltpu.VMEM((thin // chunk, chunk, crops_total), jnp.bfloat16),
            pltpu.VMEM((1, crops_total), jnp.float32),
            pltpu.VMEM((1, thin), jnp.float32),
            pltpu.SemaphoreType.DMA((thin // chunk,)),
        ],
        compiler_params=params(16 if crops_total <= 2048 else 50),
        cost_estimate=cost(4 * thin * crops_total, 2 * thin * crops_total),
        name="last_scales",
    )(in_hbm(weights), parts, *order)


def student_front_kernel(
    index_ref, bias_ref, own_hbm, x_hbm, core_hbm, last_hbm, first_hbm, second_hbm, keep_ref, give_ref,
    first_ref, second_ref, rows_ref, sems,
):
    share = own_hbm.shape[0]
    copies = [
        pltpu.make_async_copy(source, rows_ref.at[slot * share : (slot + 1) * share, :], sems.at[slot])
        for slot, source in enumerate((own_hbm, x_hbm, core_hbm, last_hbm))
    ]
    copies.append(pltpu.make_async_copy(first_hbm, first_ref, sems.at[4]))
    second_copy = pltpu.make_async_copy(second_hbm, second_ref, sems.at[5])
    for copy in copies:
        copy.start()
    second_copy.start()
    hidden = first_ref.shape[1]
    bias = bias_ref[:, part(index_ref[0], hidden)]
    for copy in copies:
        copy.wait()
    h_first = gelu(
        jnp.dot(rows_ref[...], first_ref[...], preferred_element_type=jnp.float32) + bias
    ).astype(jnp.bfloat16)
    second_copy.wait()
    for start in range(0, second_ref.shape[1], 512):
        columns = slice(start, start + 512)
        product = jnp.dot(h_first, second_ref[:, columns], preferred_element_type=jnp.float32)
        keep_ref[:, columns] = product[: 2 * share]
        give_ref[:, columns] = product[2 * share :]


def student_front(index, bias, rows, first, second, order):
    share, features = rows[0].shape
    hidden, units = second.shape
    return pl.pallas_call(
        skipping(student_front_kernel, 8, len(order)),
        in_specs=[whole(pltpu.SMEM), whole()] + [whole(pl.ANY)] * (6 + len(order)),
        out_specs=[whole(), whole()],
        out_shape=[jax.ShapeDtypeStruct((2 * share, units), jnp.float32)] * 2,
        scratch_shapes=[
            pltpu.VMEM(first.shape, jnp.bfloat16),
            pltpu.VMEM(second.shape, jnp.bfloat16),
            pltpu.VMEM((4 * share, features), jnp.bfloat16),
            pltpu.SemaphoreType.DMA((6,)),
        ],
        compiler_params=params(16),
        cost_estimate=cost(8 * share * hidden * (features + units), 2 * hidden * (features + units)),
        name="student_front",
    )(index, in_hbm(bias.reshape(1, -1)), in_hbm(rows[0]), *rows[1:], in_hbm(first), in_hbm(second), *order)


def student_middle_kernel(
    index_ref, keep_ref, core_ref, x_ref, bias_ref, own_ref, partner_ref, other_ref, last_ref, last_bias_ref,
    unit_ref, emb_ref, lengths_ref, hidden_ref,
):
    share = x_ref.shape[0]
    block = own_ref.shape[0]
    sums = keep_ref[:share, :] + core_ref[:share, :] + x_ref[...]
    hidden_ref[...] = gelu(sums + bias_ref[...]).astype(jnp.bfloat16)
    index = index_ref[0]
    weights = ((0, own_ref[...]), (2, partner_ref[...]), (1, other_ref[...]), (3, last_ref[...]))
    bottleneck = jnp.broadcast_to(last_bias_ref[...], unit_ref.shape)
    for flip, weight in weights:
        bottleneck = bottleneck + jnp.dot(
            hidden_ref[:, part(index ^ flip, block)], weight, preferred_element_type=jnp.float32
        )
    unit, lengths = unit_rows(bottleneck)
    unit_ref[...] = unit
    emb_ref[...] = unit.astype(jnp.bfloat16)
    lengths_ref[...] = jnp.broadcast_to(lengths, lengths_ref.shape)


def student_middle(index, keep, core_rows, x_rows, bias, weights, last_bias):
    share, units = x_rows.shape
    width = weights[0].shape[1]
    return pl.pallas_call(
        student_middle_kernel,
        in_specs=[whole(pltpu.SMEM)] + [whole()] * 9,
        out_specs=[whole()] * 3,
        out_shape=[
            jax.ShapeDtypeStruct((share, width), jnp.float32),
            jax.ShapeDtypeStruct((share, width), jnp.bfloat16),
            jax.ShapeDtypeStruct((share, 128), jnp.float32),
        ],
        scratch_shapes=[pltpu.VMEM((share, units), jnp.bfloat16)],
        compiler_params=params(12),
        cost_estimate=cost(2 * share * units * width, 2 * units * width + 16 * share * units),
        name="student_middle",
    )(index, keep, core_rows, x_rows, in_hbm(bias.reshape(1, -1)), in_hbm(weights[0]), *weights[1:], in_hbm(last_bias.reshape(1, -1)))


def finish_kernel(unit_ref, lengths_ref, *rest):
    out_ref, blocks = rest[-1], rest[:-1]
    attracts, repels = blocks[: len(blocks) // 2], blocks[len(blocks) // 2 :]
    width = unit_ref.shape[1]
    row_top = functools.reduce(jnp.maximum, [ref[:, width + 128 :] for ref in attracts])
    attract_sum = repel_sum = 0.0
    row_sum = column_sum = 0.0
    for ref in attracts:
        fade = jnp.exp2((ref[:, width + 128 :] - row_top) * student_rate)
        row_sum = row_sum + ref[:, width : width + 128] * fade
        attract_sum = attract_sum + ref[:, :width] * jnp.tile(fade, (1, width // 128))
    for ref in repels:
        column_sum = column_sum + jnp.sum(ref[:, width:].astype(jnp.float32), axis=1, keepdims=True)
        repel_sum = repel_sum + ref[:, :width].astype(jnp.float32)
    emb_grad = (
        attract_sum / jnp.tile(row_sum, (1, width // 128))
        - repel_sum / column_sum
    ) / student_temp
    unit = unit_ref[...]
    along = jnp.sum(unit * emb_grad, axis=1, keepdims=True)
    out_ref[...] = (emb_grad - unit * along) / jnp.tile(lengths_ref[...], (1, width // 128))


def finish(unit, lengths, attracts, repels):
    return pl.pallas_call(
        finish_kernel,
        in_specs=[whole()] * (2 + len(attracts) + len(repels)),
        out_specs=whole(),
        out_shape=jax.ShapeDtypeStruct(unit.shape, jnp.float32),
        compiler_params=params(8),
        cost_estimate=cost(40 * unit.size, 40 * unit.size),
        name="finish",
    )(unit, lengths, *attracts, *repels)


def swap(values, axis, flip):
    return lax.ppermute(values, axis, [(i, i ^ flip) for i in range(lax.axis_size(axis))])


def bit_reversed(values, count):
    bits = count.bit_length() - 1
    split = values.reshape((2,) * bits + values.shape[1:])
    turned = jnp.transpose(split, tuple(reversed(range(bits))) + tuple(range(bits, split.ndim)))
    return turned.reshape(values.shape)


def gather_batch(values):
    step = lax.axis_size("batch") // 2
    stages = [values]
    while step:
        other = swap(values, "batch", step)
        upper = (lax.axis_index("batch") // step) % 2
        values = jnp.where(
            upper == 0, jnp.concatenate([values, other]), jnp.concatenate([other, values])
        )
        stages.append(values)
        step //= 2
    return stages


def send_blocks(blocks):
    flips = list(range(len(blocks) - 1, 0, -1))
    return [blocks[0]] + [swap(blocks[flip], "proto", flip) for flip in flips]


def all_to_all(copies, axes):
    return lax.all_to_all(copies, axes, 0, 0, tiled=True)


def body(crops, teacher_emb, w_first, b_first, w_second, b_second, w_third, b_third, protos):
    batch_index = lax.axis_index("batch")
    proto_index = lax.axis_index("proto")
    batch_size = lax.axis_size("batch")
    proto_size = lax.axis_size("proto")
    devices = batch_size * proto_size
    share_rows = crops.shape[0]
    group_rows = teacher_emb.shape[0]
    crops_total = group_rows * batch_size
    protos_total = protos.shape[0] * proto_size
    count, width = protos.shape
    thin = count // batch_size
    core = proto_index % 2
    proto_ref = proto_index.reshape(1)
    thin_ref = jnp.stack([batch_index, core])
    wide_ref = jnp.stack([batch_index, proto_index])

    own_unit, half = teacher_units(core.reshape(1), teacher_emb)
    stages = gather_batch(half)
    mine = stages[-1]
    other = swap(mine, "proto", 1)

    crops_x = swap(crops, "proto", 2)
    rows = [crops, crops_x, swap(crops, "proto", 1), swap(crops_x, "proto", 1)]
    third_x = swap(w_third, "proto", 2)
    thirds = [w_third, third_x, swap(w_third, "proto", 1), swap(third_x, "proto", 1)]
    top_copies = wide_tops(own_unit, protos, (stages[2],), devices, 8)
    keep, give = student_front(proto_ref, b_first, rows, w_first, w_second, (mine, third_x, top_copies))
    all_tops = all_to_all(top_copies, BOTH)
    tops = jnp.max(all_tops.reshape(batch_size, proto_size, 256)[:, :, :group_rows], axis=1)
    tops = bit_reversed(tops, batch_size).reshape(batch_size, 2, group_rows // 2)
    base = jnp.transpose(tops, (1, 0, 2)).reshape(1, crops_total) * -teacher_rate

    core_rows = swap(give, "proto", 1)
    x_sent = keep[share_rows:] + core_rows[share_rows:]
    x_rows = swap(x_sent, "proto", 2)
    unit, rounded, lengths = student_middle(
        proto_ref, keep, core_rows, x_rows, b_second, thirds, b_third
    )
    student_emb = jnp.concatenate([rounded] + [swap(rounded, "proto", flip) for flip in range(1, proto_size)])
    empty = jnp.concatenate(
        [jnp.zeros((group_rows, width + 128), jnp.float32), jnp.full((group_rows, 128), -1e30, jnp.float32)], axis=1
    )
    eighth = count // 8
    (state,) = attract(student_emb, empty, protos, 0, 5 * eighth, 5, 1)
    slots = attract(student_emb, state, protos, 5 * eighth, 3 * eighth, 3, proto_size)
    attract_parts = send_blocks(slots)

    copies, weights = first_sweep(thin_ref, protos, mine, other, base, (x_sent, *thirds[2:]), devices, thin, protos_total)
    for _ in range(ITERS - 2):
        copies = next_sweep(weights, all_to_all(copies, BOTH), (rounded,), protos_total)
    scale_copies = last_scales(weights, all_to_all(copies, BOTH), (state,), batch_size, protos_total)
    all_scale = all_to_all(scale_copies, "batch")
    repels = repel(wide_ref, own_unit, all_tops, all_scale, protos, (slots[0],), proto_size)
    return finish(unit, lengths, attract_parts, send_blocks(repels))


def solution(mesh):
    in_specs = (
        P(("batch", "proto"), None),
        P("batch", None),
        P(None, "proto"),
        P(),
        P("proto", None),
        P(),
        P("proto", None),
        P(),
        P("proto", None),
    )
    out_specs = P(("batch", "proto"), None)
    return jax.shard_map(body, mesh=mesh, in_specs=in_specs, out_specs=out_specs, check_vma=False)
```

```python
import functools
import math

import jax
import jax.numpy as jnp
from jax import lax
from jax.experimental import pallas as pl
from jax.experimental.pallas import tpu as pltpu
from jax.sharding import PartitionSpec as P

ITERS = 3

student_temp = 0.1
teacher_temp = 0.07
norm_eps = 1e-06
teacher_rate = math.log2(math.e) / teacher_temp
student_rate = math.log2(math.e) / student_temp

MIB = 1024 * 1024
BOTH = ("batch", "proto")
TILE = 256
WIDE = 512


def scores(left_rows, right_rows):
    return lax.dot_general(
        left_rows, right_rows, (((1,), (1,)), ((), ())), preferred_element_type=jnp.float32
    )


def unit_rows(values):
    lengths = jnp.sqrt(jnp.sum(values * values, axis=1, keepdims=True) + norm_eps)
    return (values / lengths, lengths)


def gelu(values):
    return 0.5 * values * (1.0 + lax.erf(values * math.sqrt(0.5)))


def whole(memory_space=pltpu.VMEM):
    return pl.BlockSpec(memory_space=memory_space)


def in_hbm(array):
    return pltpu.with_memory_space_constraint(array, pltpu.HBM)


def skipping(kernel, first, count):
    def trimmed(*refs):
        kernel(*refs[:first], *refs[first + count :])

    return trimmed


def part(index, size):
    return pl.ds(pl.multiple_of(index * size, size), size)


def lane_fold(values, combine):
    folded = values[:, :128]
    for start in range(128, values.shape[1], 128):
        folded = combine(folded, values[:, start : start + 128])
    return folded


def params(mib):
    return pltpu.CompilerParams(vmem_limit_bytes=mib * MIB)


def cost(flops, bytes_accessed, transcendentals=0):
    return pl.CostEstimate(
        flops=int(flops), bytes_accessed=int(bytes_accessed), transcendentals=int(transcendentals)
    )


def fetch(source, target, sems, first_row=0):
    count, rows = target.shape[:2]

    def chunk_copy(index):
        start = pl.multiple_of(first_row + index * rows, rows)
        return pltpu.make_async_copy(source.at[pl.ds(start, rows), :], target.at[index], sems.at[index])

    for index in range(count):
        chunk_copy(index).start()
    return lambda index: chunk_copy(index).wait()


def teacher_units_kernel(core_ref, emb_ref, unit_ref, half_ref):
    unit_ref[...] = unit_rows(emb_ref[...].astype(jnp.float32))[0].astype(jnp.bfloat16)
    half = half_ref.shape[0]
    half_ref[...] = unit_ref[part(core_ref[0], half), :]


def teacher_units(core, teacher_emb):
    rows, width = teacher_emb.shape
    return pl.pallas_call(
        teacher_units_kernel,
        in_specs=[whole(pltpu.SMEM), whole()],
        out_specs=[whole(), whole()],
        out_shape=[
            jax.ShapeDtypeStruct((rows, width), jnp.bfloat16),
            jax.ShapeDtypeStruct((rows // 2, width), jnp.bfloat16),
        ],
        compiler_params=params(4),
        cost_estimate=cost(4 * rows * width, 8 * rows * width),
        name="teacher_units",
    )(core, in_hbm(teacher_emb))


def front_kernel(
    index_ref, unit_ref, bias_ref, own_hbm, x_hbm, core_hbm, last_hbm, first_hbm, second_hbm, protos_hbm,
    tops_ref, keep_ref, give_ref, first_ref, second_ref, rows_ref, protos_ref, top_ref, sems, chunk_sems,
):
    rows = unit_ref.shape[0]
    steps, block = protos_ref.shape[:2]
    wide = min(WIDE, block)
    share = own_hbm.shape[0]
    arrived = fetch(protos_hbm, protos_ref, chunk_sems)
    copies = [
        pltpu.make_async_copy(source, rows_ref.at[slot * share : (slot + 1) * share, :], sems.at[slot])
        for slot, source in enumerate((own_hbm, x_hbm, core_hbm, last_hbm))
    ]
    copies.append(pltpu.make_async_copy(first_hbm, first_ref, sems.at[4]))
    copies.append(pltpu.make_async_copy(second_hbm, second_ref, sems.at[5]))
    for copy in copies:
        copy.start()
    top_ref[...] = jnp.full(top_ref.shape, -jnp.inf, jnp.float32)

    def step(index, carry):
        arrived(index)
        top = top_ref[:rows, :]
        for start in range(0, block, wide):
            products = scores(unit_ref[...], protos_ref[index, start : start + wide, :])
            top = jnp.maximum(top, lane_fold(products, jnp.maximum))
        top_ref[:rows, :] = top
        return carry

    lax.fori_loop(0, steps, step, 0)
    tops = jnp.max(jnp.transpose(top_ref[...]), axis=0, keepdims=True)
    tops_ref[...] = jnp.broadcast_to(tops[None], tops_ref.shape)
    for copy in copies:
        copy.wait()
    hidden = first_ref.shape[1]
    bias = bias_ref[:, part(index_ref[0], hidden)]
    h_first = gelu(
        jnp.dot(rows_ref[...], first_ref[...], preferred_element_type=jnp.float32) + bias
    ).astype(jnp.bfloat16)
    for start in range(0, second_ref.shape[1], 512):
        columns = slice(start, start + 512)
        product = jnp.dot(h_first, second_ref[:, columns], preferred_element_type=jnp.float32)
        keep_ref[:, columns] = product[: 2 * share]
        give_ref[:, columns] = product[2 * share :]


def front(index, unit, bias, rows, first, second, protos, order, copies, steps):
    share, features = rows[0].shape
    hidden, units = second.shape
    count, width = protos.shape
    return pl.pallas_call(
        skipping(front_kernel, 10, len(order)),
        in_specs=[whole(pltpu.SMEM), whole(), whole()] + [whole(pl.ANY)] * (7 + len(order)),
        out_specs=[whole()] * 3,
        out_shape=[jax.ShapeDtypeStruct((copies, 1, 256), jnp.float32)]
        + [jax.ShapeDtypeStruct((2 * share, units), jnp.float32)] * 2,
        scratch_shapes=[
            pltpu.VMEM(first.shape, jnp.bfloat16),
            pltpu.VMEM(second.shape, jnp.bfloat16),
            pltpu.VMEM((4 * share, features), jnp.bfloat16),
            pltpu.VMEM((steps, count // steps, width), jnp.bfloat16),
            pltpu.VMEM((256, 128), jnp.float32),
            pltpu.SemaphoreType.DMA((6,)),
            pltpu.SemaphoreType.DMA((steps,)),
        ],
        compiler_params=params(26),
        cost_estimate=cost(
            2 * unit.size * count + 8 * share * hidden * (features + units), 2 * width * count
        ),
        name="front",
    )(
        index, unit, in_hbm(bias.reshape(1, -1)), in_hbm(rows[0]), *rows[1:],
        in_hbm(first), in_hbm(second), in_hbm(protos), *order,
    )


def repel_kernel(group, index_ref, unit_ref, tops_ref, scale_ref, protos_hbm, *rest):
    out_refs, (protos_ref, sems, acc_ref, sum_ref, bias_ref) = rest[:-5], rest[-5:]
    rows, width = unit_ref.shape
    steps, block = protos_ref.shape[:2]
    wide = min(WIDE, block)
    arrived = fetch(protos_hbm, protos_ref, sems)
    first = index_ref[0] * group
    top = tops_ref[first]
    for other in range(1, group):
        top = jnp.maximum(top, tops_ref[first + other])
    bias_ref[...] = jnp.transpose(jnp.broadcast_to(top, (128, 256)))[:rows, :] * -teacher_rate
    acc_ref[...] = jnp.zeros(acc_ref.shape, jnp.float32)
    sum_ref[...] = jnp.zeros(sum_ref.shape, jnp.float32)

    def step(index, carry):
        arrived(index)
        bias = bias_ref[...]
        total = sum_ref[...]
        acc = acc_ref[...]
        for start in range(0, block, wide):
            protos = protos_ref[index, start : start + wide, :]
            products = scores(unit_ref[...], protos)
            pieces = []
            for lane in range(0, wide, 128):
                scaled = jnp.exp2(products[:, lane : lane + 128] * teacher_rate + bias)
                scaled = scaled * scale_ref[index, :, start + lane : start + lane + 128]
                total = total + scaled
                pieces.append(scaled.astype(jnp.bfloat16))
            acc = acc + jnp.dot(
                jnp.concatenate(pieces, axis=1), protos, preferred_element_type=jnp.float32
            )
        sum_ref[...] = total
        acc_ref[...] = acc
        return carry

    lax.fori_loop(0, steps, step, 0)
    total = jnp.sum(sum_ref[...], axis=1, keepdims=True)
    lanes = lax.broadcasted_iota(jnp.int32, sum_ref.shape, 1)
    sum_ref[...] = jnp.broadcast_to(total, sum_ref.shape)
    share = out_refs[0].shape[0]
    lanes = lanes[:share, :]
    for flip, out_ref in enumerate(out_refs):
        span = part(index_ref[1] ^ flip, share)
        total = sum_ref[span, :]
        out_ref[:, :width] = acc_ref[span, :].astype(out_ref.dtype)
        if flip == 0:
            out_ref[:, width:] = jnp.where(lanes == 0, total, 0.0)
        else:
            high = total.astype(jnp.bfloat16).astype(jnp.float32)
            middle = (total - high).astype(jnp.bfloat16).astype(jnp.float32)
            pieces = jnp.where(lanes == 0, high, jnp.where(lanes == 1, middle, total - high - middle))
            out_ref[:, width:] = jnp.where(lanes < 3, pieces, 0.0).astype(jnp.bfloat16)


def repel(index, unit, tops, scale, protos, order, proto_size):
    rows, width = unit.shape
    count = protos.shape[0]
    steps, _, block = scale.shape
    return pl.pallas_call(
        skipping(functools.partial(repel_kernel, proto_size), 5, len(order)),
        in_specs=[whole(pltpu.SMEM), whole(), whole(), whole(), whole(pl.ANY)] + [whole(pl.ANY)] * len(order),
        out_specs=[whole()] * proto_size,
        out_shape=[
            jax.ShapeDtypeStruct((rows // proto_size, width + 128), jnp.bfloat16 if flip else jnp.float32)
            for flip in range(proto_size)
        ],
        scratch_shapes=[
            pltpu.VMEM((steps, block, width), jnp.bfloat16),
            pltpu.SemaphoreType.DMA((steps,)),
            pltpu.VMEM((rows, width), jnp.float32),
            pltpu.VMEM((rows, 128), jnp.float32),
            pltpu.VMEM((rows, 128), jnp.float32),
        ],
        compiler_params=params(16),
        cost_estimate=cost(4 * rows * width * count, 2 * width * count, rows * count),
        name="repel",
    )(index, unit, tops, scale, in_hbm(protos), *order)


def attract_kernel(first_row, last, emb_ref, state_ref, protos_hbm, *rest):
    out_refs, scratch = rest[:-6], rest[-6:]
    protos_ref, sems, products_ref, acc_ref, sum_ref, top_ref = scratch
    width = emb_ref.shape[1]
    steps, block = protos_ref.shape[:2]
    arrived = fetch(protos_hbm, protos_ref, sems, first_row)
    old_top = state_ref[:, width + 128 :]
    top_ref[...] = old_top

    def first(index, carry):
        arrived(index)
        top = top_ref[...]
        for start in range(0, block, TILE):
            products = scores(emb_ref[...], protos_ref[index, start : start + TILE, :])
            products_ref[index, :, start : start + TILE] = products
            top = jnp.maximum(top, lane_fold(products, jnp.maximum))
        top_ref[...] = top
        return carry

    lax.fori_loop(0, steps, first, 0)
    top = jnp.broadcast_to(jnp.max(top_ref[...], axis=1, keepdims=True), top_ref.shape)
    fade = jnp.exp2((old_top - top) * student_rate)
    top_ref[...] = top
    sum_ref[...] = state_ref[:, width : width + 128] * fade
    acc_ref[...] = state_ref[:, :width] * jnp.tile(fade, (1, width // 128))

    def second(index, carry):
        top = top_ref[...]
        total = sum_ref[...]
        acc = acc_ref[...]
        for start in range(0, block, TILE):
            pieces = []
            for lane in range(start, start + TILE, 128):
                shifted = jnp.exp2((products_ref[index, :, lane : lane + 128] - top) * student_rate)
                total = total + shifted
                pieces.append(shifted.astype(jnp.bfloat16))
            acc = acc + jnp.dot(
                jnp.concatenate(pieces, axis=1),
                protos_ref[index, start : start + TILE, :],
                preferred_element_type=jnp.float32,
            )
        sum_ref[...] = total
        acc_ref[...] = acc
        return carry

    lax.fori_loop(0, steps, second, 0)
    if last:
        total = jnp.sum(sum_ref[...], axis=1, keepdims=True)
        sum_ref[...] = jnp.broadcast_to(total, sum_ref.shape)
    share = out_refs[0].shape[0]
    for slot, out_ref in enumerate(out_refs):
        rows = pl.ds(slot * share, share)
        out_ref[:, :width] = acc_ref[rows, :]
        out_ref[:, width : width + 128] = sum_ref[rows, :]
        out_ref[:, width + 128 :] = top_ref[rows, :]


def attract(emb, state, protos, first_row, count, steps, outputs):
    rows, width = emb.shape
    block = count // steps
    return pl.pallas_call(
        functools.partial(attract_kernel, first_row, outputs > 1),
        in_specs=[whole(), whole(), whole(pl.ANY)],
        out_specs=[whole()] * outputs,
        out_shape=[jax.ShapeDtypeStruct((rows // outputs, width + 256), jnp.float32)] * outputs,
        scratch_shapes=[
            pltpu.VMEM((steps, block, width), jnp.bfloat16),
            pltpu.SemaphoreType.DMA((steps,)),
            pltpu.VMEM((steps, rows, block), jnp.float32),
            pltpu.VMEM((rows, width), jnp.float32),
            pltpu.VMEM((rows, 128), jnp.float32),
            pltpu.VMEM((rows, 128), jnp.float32),
        ],
        compiler_params=params(24),
        cost_estimate=cost(4 * rows * width * count, 2 * width * count, rows * count),
        name="attract",
    )(emb, state, in_hbm(protos))


def three_pieces(values):
    high = values.astype(jnp.bfloat16)
    rest = values - high.astype(jnp.float32)
    middle = rest.astype(jnp.bfloat16)
    low = (rest - middle.astype(jnp.float32)).astype(jnp.bfloat16)
    return jnp.concatenate([high, middle, low, jnp.zeros((13, values.shape[1]), jnp.bfloat16)], axis=0)


def lane_scales(folded, protos_total):
    sums = [
        jnp.sum(jnp.transpose(folded[start : start + 128, :]), axis=0, keepdims=True)
        for start in range(0, folded.shape[0], 128)
    ]
    return 1.0 / (protos_total * jnp.concatenate(sums, axis=1))


def give_sums(copies_ref, totals):
    rows = [totals[:, start : start + 128] for start in range(0, totals.shape[1], 128)]
    spare = copies_ref.shape[1] - len(rows)
    if spare:
        rows.append(jnp.zeros((spare, 128), jnp.float32))
    packed = jnp.concatenate(rows, axis=0).astype(jnp.bfloat16)
    copies_ref[...] = jnp.broadcast_to(packed[None], copies_ref.shape)


def take_scales(parts_ref, scale_ref):
    crops_total = scale_ref.shape[1]
    sums = jnp.sum(parts_ref[...].astype(jnp.float32), axis=0)
    for row in range(crops_total // 128):
        scale_ref[:, row * 128 : row * 128 + 128] = 1.0 / (crops_total * sums[row : row + 1, :])


def sums_shape(copies, crops_total):
    return (copies, -(-crops_total // 2048) * 16, 128)


def lane_order(tops_ref, group, crops_total):
    batches = tops_ref.shape[0] // group
    rows = crops_total // batches
    bits = batches.bit_length() - 1
    tops = []
    for batch in range(batches):
        source = int(format(batch, "b").zfill(bits)[::-1], 2) if bits else 0
        tops.append(
            functools.reduce(jnp.maximum, [tops_ref[source * group + other] for other in range(group)])
        )
    halves = [top[:, core * rows // 2 : (core + 1) * rows // 2] for core in range(2) for top in tops]
    return jnp.concatenate(halves, axis=1)


def first_sweep_kernel(
    chunk, protos_total, group, index_ref, protos_hbm, mine_hbm, other_hbm, tops_ref, copies_ref, weights_hbm,
    protos_ref, units_ref, weights_ref, rounded_ref, scale_ref, bias_ref, sems, out_sems,
):
    thin, crops_total = weights_ref.shape
    half = mine_hbm.shape[0]
    core = index_ref[1]
    copies = (
        pltpu.make_async_copy(protos_hbm.at[part(index_ref[0], thin), :], protos_ref, sems.at[0]),
        pltpu.make_async_copy(mine_hbm, units_ref.at[part(core, half), :], sems.at[1]),
        pltpu.make_async_copy(other_hbm, units_ref.at[part(1 - core, half), :], sems.at[2]),
    )
    for copy in copies:
        copy.start()
    bias_ref[...] = lane_order(tops_ref, group, crops_total) * -teacher_rate
    for copy in copies:
        copy.wait()

    def chunk_out(index):
        return pltpu.make_async_copy(
            rounded_ref.at[index], weights_hbm.at[part(index, chunk), :], out_sems.at[index]
        )

    def weigh(index, carry):
        rows = part(index, chunk)
        protos = protos_ref[rows, :]
        folded = jnp.zeros((chunk, 128), jnp.float32)
        for start in range(0, crops_total, TILE):
            columns = slice(start, start + TILE)
            products = scores(protos, units_ref[columns, :])
            weights = jnp.exp2(products * teacher_rate + bias_ref[:, columns])
            weights_ref[rows, columns] = weights
            rounded_ref[index, :, columns] = weights.astype(jnp.bfloat16)
            folded = folded + lane_fold(weights, jnp.add)
        sums = jnp.sum(folded, axis=1, keepdims=True)
        scale_ref[rows, :] = jnp.broadcast_to(1.0 / (protos_total * sums), (chunk, 128))
        chunk_out(index).start()
        return carry

    lax.fori_loop(0, thin // chunk, weigh, 0)
    small = min(thin, 64)

    def add_up(index, totals):
        rows = part(index, small)
        scaled = weights_ref[rows, :] * jnp.tile(scale_ref[rows, :], (1, crops_total // 128))
        return totals + jnp.sum(scaled.reshape(-1, 8, crops_total), axis=0)

    totals = lax.fori_loop(0, thin // small, add_up, jnp.zeros((8, crops_total), jnp.float32))
    give_sums(copies_ref, jnp.sum(totals, axis=0, keepdims=True))
    for index in range(thin // chunk):
        chunk_out(index).wait()


def first_sweep(index, protos, mine, other, tops, order, copies, thin, protos_total):
    width = protos.shape[1]
    crops_total = 2 * mine.shape[0]
    chunk = min(thin, 1024)
    return pl.pallas_call(
        skipping(functools.partial(first_sweep_kernel, chunk, protos_total, protos_total // protos.shape[0]), 5, len(order)),
        in_specs=[whole(pltpu.SMEM), whole(pl.ANY), whole(pl.ANY), whole(pl.ANY), whole()]
        + [whole(pl.ANY)] * len(order),
        out_specs=[whole(), whole(pl.ANY)],
        out_shape=[
            jax.ShapeDtypeStruct(sums_shape(copies, crops_total), jnp.bfloat16),
            pltpu.HBM((thin, crops_total), jnp.bfloat16),
        ],
        scratch_shapes=[
            pltpu.VMEM((thin, width), jnp.bfloat16),
            pltpu.VMEM((crops_total, width), jnp.bfloat16),
            pltpu.VMEM((thin, crops_total), jnp.float32),
            pltpu.VMEM((thin // chunk, chunk, crops_total), jnp.bfloat16),
            pltpu.VMEM((thin, 128), jnp.float32),
            pltpu.VMEM((1, crops_total), jnp.float32),
            pltpu.SemaphoreType.DMA((3,)),
            pltpu.SemaphoreType.DMA((thin // chunk,)),
        ],
        compiler_params=params(32 if crops_total <= 2048 else 56),
        cost_estimate=cost(2 * thin * width * crops_total, 2 * thin * crops_total, thin * crops_total),
        name="first_sweep",
    )(index, in_hbm(protos), mine, other, tops, *order)


def fetch_rows(weights_hbm, weights_ref, sems):
    steps, chunk, _ = weights_ref.shape

    def rows_copy(index):
        return pltpu.make_async_copy(
            weights_hbm.at[part(index, chunk), :], weights_ref.at[index], sems.at[index]
        )

    for index in range(steps):
        rows_copy(index).start()
    return lambda index: rows_copy(index).wait()


def scaled_fold(weights_ref, index, scale_ref):
    _, chunk, crops_total = weights_ref.shape
    folds = []
    for row in range(0, chunk, 64):
        fold = None
        for start in range(0, crops_total, TILE):
            columns = slice(start, start + TILE)
            weights = weights_ref[index, row : row + 64, columns].astype(jnp.float32)
            scaled = lane_fold(weights * scale_ref[:, columns], jnp.add)
            fold = scaled if fold is None else fold + scaled
        folds.append(fold)
    return jnp.concatenate(folds, axis=0)


def next_sweep_kernel(
    protos_total, weights_hbm, parts_ref, copies_ref, weights_ref, scale_ref, pieces_ref, totals_ref, sems,
):
    steps, chunk, crops_total = weights_ref.shape
    arrived = fetch_rows(weights_hbm, weights_ref, sems)
    take_scales(parts_ref, scale_ref)
    totals_ref[...] = jnp.zeros(totals_ref.shape, jnp.float32)

    def weigh(index):
        return three_pieces(lane_scales(scaled_fold(weights_ref, index, scale_ref), protos_total))

    def add_up(index):
        return jnp.dot(pieces_ref[...], weights_ref[index], preferred_element_type=jnp.float32)

    arrived(0)
    pieces_ref[...] = weigh(0)

    def sweep(index, carry):
        arrived(index)
        sums = add_up(index - 1)
        pieces = weigh(index)
        totals_ref[...] += sums
        pieces_ref[...] = pieces
        return carry

    lax.fori_loop(1, steps, sweep, 0)
    totals = totals_ref[...] + add_up(steps - 1)
    give_sums(copies_ref, jnp.sum(totals, axis=0, keepdims=True))


def next_sweep(weights, parts, order, protos_total):
    thin, crops_total = weights.shape
    copies = parts.shape[0]
    chunk = min(thin, 256)
    return pl.pallas_call(
        skipping(functools.partial(next_sweep_kernel, protos_total), 2, len(order)),
        in_specs=[whole(pl.ANY), whole()] + [whole(pl.ANY)] * len(order),
        out_specs=whole(),
        out_shape=jax.ShapeDtypeStruct(sums_shape(copies, crops_total), jnp.bfloat16),
        scratch_shapes=[
            pltpu.VMEM((thin // chunk, chunk, crops_total), jnp.bfloat16),
            pltpu.VMEM((1, crops_total), jnp.float32),
            pltpu.VMEM((16, chunk), jnp.bfloat16),
            pltpu.VMEM((16, crops_total), jnp.float32),
            pltpu.SemaphoreType.DMA((thin // chunk,)),
        ],
        compiler_params=params(16 if crops_total <= 2048 else 50),
        cost_estimate=cost(8 * thin * crops_total, 2 * thin * crops_total),
        name="next_sweep",
    )(in_hbm(weights), parts, *order)


def last_scales_kernel(
    protos_total, weights_hbm, parts_ref, copies_ref, weights_ref, scale_ref, out_ref, sems,
):
    steps, chunk, crops_total = weights_ref.shape
    arrived = fetch_rows(weights_hbm, weights_ref, sems)
    take_scales(parts_ref, scale_ref)

    def weigh(index, carry):
        arrived(index)
        out_ref[:, part(index, chunk)] = lane_scales(
            scaled_fold(weights_ref, index, scale_ref), protos_total
        )
        return carry

    lax.fori_loop(0, steps, weigh, 0)
    copies_ref[...] = jnp.broadcast_to(out_ref[...][None], copies_ref.shape)


def last_scales(weights, parts, order, copies, protos_total):
    thin, crops_total = weights.shape
    chunk = min(thin, 256)
    return pl.pallas_call(
        skipping(functools.partial(last_scales_kernel, protos_total), 2, len(order)),
        in_specs=[whole(pl.ANY), whole()] + [whole(pl.ANY)] * len(order),
        out_specs=whole(),
        out_shape=jax.ShapeDtypeStruct((copies, 1, thin), jnp.float32),
        scratch_shapes=[
            pltpu.VMEM((thin // chunk, chunk, crops_total), jnp.bfloat16),
            pltpu.VMEM((1, crops_total), jnp.float32),
            pltpu.VMEM((1, thin), jnp.float32),
            pltpu.SemaphoreType.DMA((thin // chunk,)),
        ],
        compiler_params=params(16 if crops_total <= 2048 else 50),
        cost_estimate=cost(4 * thin * crops_total, 2 * thin * crops_total),
        name="last_scales",
    )(in_hbm(weights), parts, *order)


def student_middle_kernel(
    index_ref, keep_ref, core_ref, x_ref, bias_ref, own_ref, partner_ref, other_ref, last_ref, last_bias_ref,
    unit_ref, emb_ref, lengths_ref, hidden_ref,
):
    share = x_ref.shape[0]
    block = own_ref.shape[0]
    sums = keep_ref[:share, :] + core_ref[:share, :] + x_ref[...]
    hidden_ref[...] = gelu(sums + bias_ref[...]).astype(jnp.bfloat16)
    index = index_ref[0]
    weights = ((0, own_ref[...]), (2, partner_ref[...]), (1, other_ref[...]), (3, last_ref[...]))
    bottleneck = jnp.broadcast_to(last_bias_ref[...], unit_ref.shape)
    for flip, weight in weights:
        bottleneck = bottleneck + jnp.dot(
            hidden_ref[:, part(index ^ flip, block)], weight, preferred_element_type=jnp.float32
        )
    unit, lengths = unit_rows(bottleneck)
    unit_ref[...] = unit
    emb_ref[...] = unit.astype(jnp.bfloat16)
    lengths_ref[...] = jnp.broadcast_to(lengths, lengths_ref.shape)


def student_middle(index, keep, core_rows, x_rows, bias, weights, last_bias):
    share, units = x_rows.shape
    width = weights[0].shape[1]
    return pl.pallas_call(
        student_middle_kernel,
        in_specs=[whole(pltpu.SMEM)] + [whole()] * 9,
        out_specs=[whole()] * 3,
        out_shape=[
            jax.ShapeDtypeStruct((share, width), jnp.float32),
            jax.ShapeDtypeStruct((share, width), jnp.bfloat16),
            jax.ShapeDtypeStruct((share, 128), jnp.float32),
        ],
        scratch_shapes=[pltpu.VMEM((share, units), jnp.bfloat16)],
        compiler_params=params(12),
        cost_estimate=cost(2 * share * units * width, 2 * units * width + 16 * share * units),
        name="student_middle",
    )(index, keep, core_rows, x_rows, in_hbm(bias.reshape(1, -1)), in_hbm(weights[0]), *weights[1:], in_hbm(last_bias.reshape(1, -1)))


def finish_kernel(unit_ref, lengths_ref, *rest):
    out_ref, blocks = rest[-1], rest[:-1]
    attracts, repels = blocks[: len(blocks) // 2], blocks[len(blocks) // 2 :]
    width = unit_ref.shape[1]
    row_top = functools.reduce(jnp.maximum, [ref[:, width + 128 :] for ref in attracts])
    attract_sum = repel_sum = 0.0
    row_sum = column_sum = 0.0
    for ref in attracts:
        fade = jnp.exp2((ref[:, width + 128 :] - row_top) * student_rate)
        row_sum = row_sum + ref[:, width : width + 128] * fade
        attract_sum = attract_sum + ref[:, :width] * jnp.tile(fade, (1, width // 128))
    for ref in repels:
        column_sum = column_sum + jnp.sum(ref[:, width:].astype(jnp.float32), axis=1, keepdims=True)
        repel_sum = repel_sum + ref[:, :width].astype(jnp.float32)
    emb_grad = (
        attract_sum / jnp.tile(row_sum, (1, width // 128))
        - repel_sum / column_sum
    ) / student_temp
    unit = unit_ref[...]
    along = jnp.sum(unit * emb_grad, axis=1, keepdims=True)
    out_ref[...] = (emb_grad - unit * along) / jnp.tile(lengths_ref[...], (1, width // 128))


def finish(unit, lengths, attracts, repels):
    return pl.pallas_call(
        finish_kernel,
        in_specs=[whole()] * (2 + len(attracts) + len(repels)),
        out_specs=whole(),
        out_shape=jax.ShapeDtypeStruct(unit.shape, jnp.float32),
        compiler_params=params(8),
        cost_estimate=cost(40 * unit.size, 40 * unit.size),
        name="finish",
    )(unit, lengths, *attracts, *repels)


def swap(values, axis, flip):
    return lax.ppermute(values, axis, [(i, i ^ flip) for i in range(lax.axis_size(axis))])


def bit_reversed(values, count):
    bits = count.bit_length() - 1
    split = values.reshape((2,) * bits + values.shape[1:])
    turned = jnp.transpose(split, tuple(reversed(range(bits))) + tuple(range(bits, split.ndim)))
    return turned.reshape(values.shape)


def gather_batch(values):
    step = lax.axis_size("batch") // 2
    stages = [values]
    while step:
        other = swap(values, "batch", step)
        upper = (lax.axis_index("batch") // step) % 2
        values = jnp.where(
            upper == 0, jnp.concatenate([values, other]), jnp.concatenate([other, values])
        )
        stages.append(values)
        step //= 2
    return stages


def send_blocks(blocks):
    flips = list(range(len(blocks) - 1, 0, -1))
    return [blocks[0]] + [swap(blocks[flip], "proto", flip) for flip in flips]


def all_to_all(copies, axes):
    return lax.all_to_all(copies, axes, 0, 0, tiled=True)


def body(crops, teacher_emb, w_first, b_first, w_second, b_second, w_third, b_third, protos):
    batch_index = lax.axis_index("batch")
    proto_index = lax.axis_index("proto")
    batch_size = lax.axis_size("batch")
    proto_size = lax.axis_size("proto")
    devices = batch_size * proto_size
    share_rows = crops.shape[0]
    group_rows = teacher_emb.shape[0]
    crops_total = group_rows * batch_size
    protos_total = protos.shape[0] * proto_size
    count, width = protos.shape
    thin = count // batch_size
    core = proto_index % 2
    proto_ref = proto_index.reshape(1)
    thin_ref = jnp.stack([batch_index, core])
    wide_ref = jnp.stack([batch_index, proto_index])

    own_unit, half = teacher_units(core.reshape(1), teacher_emb)
    stages = gather_batch(half)
    mine = stages[-1]
    other = swap(mine, "proto", 1)

    crops_x = swap(crops, "proto", 2)
    rows = [crops, crops_x, swap(crops, "proto", 1), swap(crops_x, "proto", 1)]
    third_x = swap(w_third, "proto", 2)
    thirds = [w_third, third_x, swap(w_third, "proto", 1), swap(third_x, "proto", 1)]
    top_copies, keep, give = front(
        proto_ref, own_unit, b_first, rows, w_first, w_second, protos, (stages[2], third_x), devices, 8
    )
    all_tops = all_to_all(top_copies, BOTH)
    core_rows = swap(give, "proto", 1)
    x_sent = keep[share_rows:] + core_rows[share_rows:]
    x_rows = swap(x_sent, "proto", 2)
    unit, rounded, lengths = student_middle(
        proto_ref, keep, core_rows, x_rows, b_second, thirds, b_third
    )
    student_emb = jnp.concatenate([rounded] + [swap(rounded, "proto", flip) for flip in range(1, proto_size)])
    empty = jnp.concatenate(
        [jnp.zeros((group_rows, width + 128), jnp.float32), jnp.full((group_rows, 128), -1e30, jnp.float32)], axis=1
    )
    eighth = count // 8
    (state,) = attract(student_emb, empty, protos, 0, 5 * eighth, 5, 1)
    slots = attract(student_emb, state, protos, 5 * eighth, 3 * eighth, 3, proto_size)
    attract_parts = send_blocks(slots)

    copies, weights = first_sweep(thin_ref, protos, mine, other, all_tops, (x_sent, *thirds[2:]), devices, thin, protos_total)
    for _ in range(ITERS - 2):
        copies = next_sweep(weights, all_to_all(copies, BOTH), (rounded,), protos_total)
    scale_copies = last_scales(weights, all_to_all(copies, BOTH), (state,), batch_size, protos_total)
    all_scale = all_to_all(scale_copies, "batch")
    repels = repel(wide_ref, own_unit, all_tops, all_scale, protos, (slots[0],), proto_size)
    return finish(unit, lengths, attract_parts, send_blocks(repels))


def solution(mesh):
    in_specs = (
        P(("batch", "proto"), None),
        P("batch", None),
        P(None, "proto"),
        P(),
        P("proto", None),
        P(),
        P("proto", None),
        P(),
        P("proto", None),
    )
    out_specs = P(("batch", "proto"), None)
    return jax.shard_map(body, mesh=mesh, in_specs=in_specs, out_specs=out_specs, check_vma=False)
```

```python
import functools
import math

import jax
import jax.numpy as jnp
from jax import lax
from jax.experimental import pallas as pl
from jax.experimental.pallas import tpu as pltpu
from jax.sharding import PartitionSpec as P

ITERS = 3

student_temp = 0.1
teacher_temp = 0.07
norm_eps = 1e-06
teacher_rate = math.log2(math.e) / teacher_temp
student_rate = math.log2(math.e) / student_temp

MIB = 1024 * 1024
BOTH = ("batch", "proto")
TILE = 256
WIDE = 512


def scores(left_rows, right_rows):
    return lax.dot_general(
        left_rows, right_rows, (((1,), (1,)), ((), ())), preferred_element_type=jnp.float32
    )


def unit_rows(values):
    lengths = jnp.sqrt(jnp.sum(values * values, axis=1, keepdims=True) + norm_eps)
    return (values / lengths, lengths)


def gelu(values):
    return 0.5 * values * (1.0 + lax.erf(values * math.sqrt(0.5)))


def whole(memory_space=pltpu.VMEM):
    return pl.BlockSpec(memory_space=memory_space)


def in_hbm(array):
    return pltpu.with_memory_space_constraint(array, pltpu.HBM)


def skipping(kernel, first, count):
    def trimmed(*refs):
        kernel(*refs[:first], *refs[first + count :])

    return trimmed


def part(index, size):
    return pl.ds(pl.multiple_of(index * size, size), size)


def lane_fold(values, combine):
    folded = values[:, :128]
    for start in range(128, values.shape[1], 128):
        folded = combine(folded, values[:, start : start + 128])
    return folded


def params(mib):
    return pltpu.CompilerParams(vmem_limit_bytes=mib * MIB)


def cost(flops, bytes_accessed, transcendentals=0):
    return pl.CostEstimate(
        flops=int(flops), bytes_accessed=int(bytes_accessed), transcendentals=int(transcendentals)
    )


def fetch(source, target, sems, first_row=0):
    count, rows = target.shape[:2]

    def chunk_copy(index):
        start = pl.multiple_of(first_row + index * rows, rows)
        return pltpu.make_async_copy(source.at[pl.ds(start, rows), :], target.at[index], sems.at[index])

    for index in range(count):
        chunk_copy(index).start()
    return lambda index: chunk_copy(index).wait()


def teacher_units_kernel(core_ref, emb_ref, unit_ref, half_ref):
    unit_ref[...] = unit_rows(emb_ref[...].astype(jnp.float32))[0].astype(jnp.bfloat16)
    half = half_ref.shape[0]
    half_ref[...] = unit_ref[part(core_ref[0], half), :]


def teacher_units(core, teacher_emb):
    rows, width = teacher_emb.shape
    return pl.pallas_call(
        teacher_units_kernel,
        in_specs=[whole(pltpu.SMEM), whole()],
        out_specs=[whole(), whole()],
        out_shape=[
            jax.ShapeDtypeStruct((rows, width), jnp.bfloat16),
            jax.ShapeDtypeStruct((rows // 2, width), jnp.bfloat16),
        ],
        compiler_params=params(4),
        cost_estimate=cost(4 * rows * width, 8 * rows * width),
        name="teacher_units",
    )(core, in_hbm(teacher_emb))


def front_kernel(
    index_ref, unit_ref, bias_ref, own_hbm, x_hbm, core_hbm, last_hbm, first_hbm, second_hbm, protos_hbm,
    tops_ref, keep_ref, give_ref, first_ref, second_ref, rows_ref, protos_ref, padded_ref, top_ref, sems, chunk_sems,
):
    rows = unit_ref.shape[0]
    steps, block = protos_ref.shape[:2]
    wide = min(WIDE, block)
    share = own_hbm.shape[0]
    arrived = fetch(protos_hbm, protos_ref, chunk_sems)
    copies = [
        pltpu.make_async_copy(source, rows_ref.at[slot * share : (slot + 1) * share, :], sems.at[slot])
        for slot, source in enumerate((own_hbm, x_hbm, core_hbm, last_hbm))
    ]
    copies.append(pltpu.make_async_copy(first_hbm, first_ref, sems.at[4]))
    copies.append(pltpu.make_async_copy(second_hbm, second_ref, sems.at[5]))
    for copy in copies:
        copy.start()
    padded_ref[...] = jnp.zeros(padded_ref.shape, jnp.bfloat16)
    padded_ref[:rows, :] = unit_ref[...]
    top_ref[...] = jnp.full(top_ref.shape, -jnp.inf, jnp.float32)

    def step(index, carry):
        arrived(index)
        top = top_ref[...]
        for start in range(0, block, wide):
            products = scores(protos_ref[index, start : start + wide, :], padded_ref[...])
            top = jnp.maximum(top, jnp.max(products.reshape(-1, 8, products.shape[1]), axis=0))
        top_ref[...] = top
        return carry

    lax.fori_loop(0, steps, step, 0)
    tops = jnp.max(top_ref[...], axis=0, keepdims=True)
    tops_ref[...] = jnp.broadcast_to(tops[None], tops_ref.shape)
    for copy in copies:
        copy.wait()
    hidden = first_ref.shape[1]
    bias = bias_ref[:, part(index_ref[0], hidden)]
    h_first = gelu(
        jnp.dot(rows_ref[...], first_ref[...], preferred_element_type=jnp.float32) + bias
    ).astype(jnp.bfloat16)
    for start in range(0, second_ref.shape[1], 512):
        columns = slice(start, start + 512)
        product = jnp.dot(h_first, second_ref[:, columns], preferred_element_type=jnp.float32)
        keep_ref[:, columns] = product[: 2 * share]
        give_ref[:, columns] = product[2 * share :]


def front(index, unit, bias, rows, first, second, protos, order, copies, steps):
    share, features = rows[0].shape
    hidden, units = second.shape
    count, width = protos.shape
    return pl.pallas_call(
        skipping(front_kernel, 10, len(order)),
        in_specs=[whole(pltpu.SMEM), whole(), whole()] + [whole(pl.ANY)] * (7 + len(order)),
        out_specs=[whole()] * 3,
        out_shape=[jax.ShapeDtypeStruct((copies, 1, 256), jnp.float32)]
        + [jax.ShapeDtypeStruct((2 * share, units), jnp.float32)] * 2,
        scratch_shapes=[
            pltpu.VMEM(first.shape, jnp.bfloat16),
            pltpu.VMEM(second.shape, jnp.bfloat16),
            pltpu.VMEM((4 * share, features), jnp.bfloat16),
            pltpu.VMEM((steps, count // steps, width), jnp.bfloat16),
            pltpu.VMEM((256, width), jnp.bfloat16),
            pltpu.VMEM((8, 256), jnp.float32),
            pltpu.SemaphoreType.DMA((6,)),
            pltpu.SemaphoreType.DMA((steps,)),
        ],
        compiler_params=params(26),
        cost_estimate=cost(
            2 * unit.size * count + 8 * share * hidden * (features + units), 2 * width * count
        ),
        name="front",
    )(
        index, unit, in_hbm(bias.reshape(1, -1)), in_hbm(rows[0]), *rows[1:],
        in_hbm(first), in_hbm(second), in_hbm(protos), *order,
    )


def repel_kernel(group, index_ref, unit_ref, tops_ref, scale_ref, protos_hbm, *rest):
    out_refs, (protos_ref, sems, acc_ref, sum_ref, bias_ref) = rest[:-5], rest[-5:]
    rows, width = unit_ref.shape
    steps, block = protos_ref.shape[:2]
    wide = min(WIDE, block)
    arrived = fetch(protos_hbm, protos_ref, sems)
    first = index_ref[0] * group
    top = tops_ref[first]
    for other in range(1, group):
        top = jnp.maximum(top, tops_ref[first + other])
    bias_ref[...] = jnp.transpose(jnp.broadcast_to(top, (128, 256)))[:rows, :] * -teacher_rate
    acc_ref[...] = jnp.zeros(acc_ref.shape, jnp.float32)
    sum_ref[...] = jnp.zeros(sum_ref.shape, jnp.float32)

    def step(index, carry):
        arrived(index)
        bias = bias_ref[...]
        total = sum_ref[...]
        acc = acc_ref[...]
        for start in range(0, block, wide):
            protos = protos_ref[index, start : start + wide, :]
            products = scores(unit_ref[...], protos)
            pieces = []
            for lane in range(0, wide, 128):
                scaled = jnp.exp2(products[:, lane : lane + 128] * teacher_rate + bias)
                scaled = scaled * scale_ref[index, :, start + lane : start + lane + 128]
                total = total + scaled
                pieces.append(scaled.astype(jnp.bfloat16))
            acc = acc + jnp.dot(
                jnp.concatenate(pieces, axis=1), protos, preferred_element_type=jnp.float32
            )
        sum_ref[...] = total
        acc_ref[...] = acc
        return carry

    lax.fori_loop(0, steps, step, 0)
    total = jnp.sum(sum_ref[...], axis=1, keepdims=True)
    lanes = lax.broadcasted_iota(jnp.int32, sum_ref.shape, 1)
    sum_ref[...] = jnp.broadcast_to(total, sum_ref.shape)
    share = out_refs[0].shape[0]
    lanes = lanes[:share, :]
    for flip, out_ref in enumerate(out_refs):
        span = part(index_ref[1] ^ flip, share)
        total = sum_ref[span, :]
        out_ref[:, :width] = acc_ref[span, :].astype(out_ref.dtype)
        if flip == 0:
            out_ref[:, width:] = jnp.where(lanes == 0, total, 0.0)
        else:
            high = total.astype(jnp.bfloat16).astype(jnp.float32)
            middle = (total - high).astype(jnp.bfloat16).astype(jnp.float32)
            pieces = jnp.where(lanes == 0, high, jnp.where(lanes == 1, middle, total - high - middle))
            out_ref[:, width:] = jnp.where(lanes < 3, pieces, 0.0).astype(jnp.bfloat16)


def repel(index, unit, tops, scale, protos, order, proto_size):
    rows, width = unit.shape
    count = protos.shape[0]
    steps, _, block = scale.shape
    return pl.pallas_call(
        skipping(functools.partial(repel_kernel, proto_size), 5, len(order)),
        in_specs=[whole(pltpu.SMEM), whole(), whole(), whole(), whole(pl.ANY)] + [whole(pl.ANY)] * len(order),
        out_specs=[whole()] * proto_size,
        out_shape=[
            jax.ShapeDtypeStruct((rows // proto_size, width + 128), jnp.bfloat16 if flip else jnp.float32)
            for flip in range(proto_size)
        ],
        scratch_shapes=[
            pltpu.VMEM((steps, block, width), jnp.bfloat16),
            pltpu.SemaphoreType.DMA((steps,)),
            pltpu.VMEM((rows, width), jnp.float32),
            pltpu.VMEM((rows, 128), jnp.float32),
            pltpu.VMEM((rows, 128), jnp.float32),
        ],
        compiler_params=params(16),
        cost_estimate=cost(4 * rows * width * count, 2 * width * count, rows * count),
        name="repel",
    )(index, unit, tops, scale, in_hbm(protos), *order)


def attract_kernel(first_row, last, emb_ref, state_ref, protos_hbm, *rest):
    out_refs, scratch = rest[:-6], rest[-6:]
    protos_ref, sems, products_ref, acc_ref, sum_ref, top_ref = scratch
    width = emb_ref.shape[1]
    steps, block = protos_ref.shape[:2]
    arrived = fetch(protos_hbm, protos_ref, sems, first_row)
    old_top = state_ref[:, width + 128 :]
    top_ref[...] = old_top

    def first(index, carry):
        arrived(index)
        top = top_ref[...]
        for start in range(0, block, TILE):
            products = scores(emb_ref[...], protos_ref[index, start : start + TILE, :])
            products_ref[index, :, start : start + TILE] = products
            top = jnp.maximum(top, lane_fold(products, jnp.maximum))
        top_ref[...] = top
        return carry

    lax.fori_loop(0, steps, first, 0)
    top = jnp.broadcast_to(jnp.max(top_ref[...], axis=1, keepdims=True), top_ref.shape)
    fade = jnp.exp2((old_top - top) * student_rate)
    top_ref[...] = top
    sum_ref[...] = state_ref[:, width : width + 128] * fade
    acc_ref[...] = state_ref[:, :width] * jnp.tile(fade, (1, width // 128))

    def second(index, carry):
        top = top_ref[...]
        total = sum_ref[...]
        acc = acc_ref[...]
        for start in range(0, block, TILE):
            pieces = []
            for lane in range(start, start + TILE, 128):
                shifted = jnp.exp2((products_ref[index, :, lane : lane + 128] - top) * student_rate)
                total = total + shifted
                pieces.append(shifted.astype(jnp.bfloat16))
            acc = acc + jnp.dot(
                jnp.concatenate(pieces, axis=1),
                protos_ref[index, start : start + TILE, :],
                preferred_element_type=jnp.float32,
            )
        sum_ref[...] = total
        acc_ref[...] = acc
        return carry

    lax.fori_loop(0, steps, second, 0)
    if last:
        total = jnp.sum(sum_ref[...], axis=1, keepdims=True)
        sum_ref[...] = jnp.broadcast_to(total, sum_ref.shape)
    share = out_refs[0].shape[0]
    for slot, out_ref in enumerate(out_refs):
        rows = pl.ds(slot * share, share)
        out_ref[:, :width] = acc_ref[rows, :]
        out_ref[:, width : width + 128] = sum_ref[rows, :]
        out_ref[:, width + 128 :] = top_ref[rows, :]


def attract(emb, state, protos, first_row, count, steps, outputs):
    rows, width = emb.shape
    block = count // steps
    return pl.pallas_call(
        functools.partial(attract_kernel, first_row, outputs > 1),
        in_specs=[whole(), whole(), whole(pl.ANY)],
        out_specs=[whole()] * outputs,
        out_shape=[jax.ShapeDtypeStruct((rows // outputs, width + 256), jnp.float32)] * outputs,
        scratch_shapes=[
            pltpu.VMEM((steps, block, width), jnp.bfloat16),
            pltpu.SemaphoreType.DMA((steps,)),
            pltpu.VMEM((steps, rows, block), jnp.float32),
            pltpu.VMEM((rows, width), jnp.float32),
            pltpu.VMEM((rows, 128), jnp.float32),
            pltpu.VMEM((rows, 128), jnp.float32),
        ],
        compiler_params=params(24),
        cost_estimate=cost(4 * rows * width * count, 2 * width * count, rows * count),
        name="attract",
    )(emb, state, in_hbm(protos))


def three_pieces(values):
    high = values.astype(jnp.bfloat16)
    rest = values - high.astype(jnp.float32)
    middle = rest.astype(jnp.bfloat16)
    low = (rest - middle.astype(jnp.float32)).astype(jnp.bfloat16)
    return jnp.concatenate([high, middle, low, jnp.zeros((13, values.shape[1]), jnp.bfloat16)], axis=0)


def lane_scales(folded, protos_total):
    sums = [
        jnp.sum(jnp.transpose(folded[start : start + 128, :]), axis=0, keepdims=True)
        for start in range(0, folded.shape[0], 128)
    ]
    return 1.0 / (protos_total * jnp.concatenate(sums, axis=1))


def give_sums(copies_ref, totals):
    rows = [totals[:, start : start + 128] for start in range(0, totals.shape[1], 128)]
    spare = copies_ref.shape[1] - len(rows)
    if spare:
        rows.append(jnp.zeros((spare, 128), jnp.float32))
    packed = jnp.concatenate(rows, axis=0).astype(jnp.bfloat16)
    copies_ref[...] = jnp.broadcast_to(packed[None], copies_ref.shape)


def take_scales(parts_ref, scale_ref):
    crops_total = scale_ref.shape[1]
    sums = jnp.sum(parts_ref[...].astype(jnp.float32), axis=0)
    for row in range(crops_total // 128):
        scale_ref[:, row * 128 : row * 128 + 128] = 1.0 / (crops_total * sums[row : row + 1, :])


def sums_shape(copies, crops_total):
    return (copies, -(-crops_total // 2048) * 16, 128)


def lane_order(tops_ref, group, crops_total):
    batches = tops_ref.shape[0] // group
    rows = crops_total // batches
    bits = batches.bit_length() - 1
    tops = []
    for batch in range(batches):
        source = int(format(batch, "b").zfill(bits)[::-1], 2) if bits else 0
        tops.append(
            functools.reduce(jnp.maximum, [tops_ref[source * group + other] for other in range(group)])
        )
    halves = [top[:, core * rows // 2 : (core + 1) * rows // 2] for core in range(2) for top in tops]
    return jnp.concatenate(halves, axis=1)


def first_sweep_kernel(
    chunk, protos_total, group, index_ref, protos_hbm, mine_hbm, other_hbm, tops_ref, copies_ref, weights_hbm,
    protos_ref, units_ref, weights_ref, rounded_ref, scale_ref, bias_ref, sems, out_sems,
):
    thin, crops_total = weights_ref.shape
    half = mine_hbm.shape[0]
    core = index_ref[1]
    copies = (
        pltpu.make_async_copy(protos_hbm.at[part(index_ref[0], thin), :], protos_ref, sems.at[0]),
        pltpu.make_async_copy(mine_hbm, units_ref.at[part(core, half), :], sems.at[1]),
        pltpu.make_async_copy(other_hbm, units_ref.at[part(1 - core, half), :], sems.at[2]),
    )
    for copy in copies:
        copy.start()
    bias_ref[...] = lane_order(tops_ref, group, crops_total) * -teacher_rate
    for copy in copies:
        copy.wait()

    def chunk_out(index):
        return pltpu.make_async_copy(
            rounded_ref.at[index], weights_hbm.at[part(index, chunk), :], out_sems.at[index]
        )

    def weigh(index, carry):
        rows = part(index, chunk)
        protos = protos_ref[rows, :]
        folded = jnp.zeros((chunk, 128), jnp.float32)
        for start in range(0, crops_total, TILE):
            columns = slice(start, start + TILE)
            products = scores(protos, units_ref[columns, :])
            weights = jnp.exp2(products * teacher_rate + bias_ref[:, columns])
            weights_ref[rows, columns] = weights
            rounded_ref[index, :, columns] = weights.astype(jnp.bfloat16)
            folded = folded + lane_fold(weights, jnp.add)
        sums = jnp.sum(folded, axis=1, keepdims=True)
        scale_ref[rows, :] = jnp.broadcast_to(1.0 / (protos_total * sums), (chunk, 128))
        chunk_out(index).start()
        return carry

    lax.fori_loop(0, thin // chunk, weigh, 0)
    small = min(thin, 64)

    def add_up(index, totals):
        rows = part(index, small)
        scaled = weights_ref[rows, :] * jnp.tile(scale_ref[rows, :], (1, crops_total // 128))
        return totals + jnp.sum(scaled.reshape(-1, 8, crops_total), axis=0)

    totals = lax.fori_loop(0, thin // small, add_up, jnp.zeros((8, crops_total), jnp.float32))
    give_sums(copies_ref, jnp.sum(totals, axis=0, keepdims=True))
    for index in range(thin // chunk):
        chunk_out(index).wait()


def first_sweep(index, protos, mine, other, tops, order, copies, thin, protos_total):
    width = protos.shape[1]
    crops_total = 2 * mine.shape[0]
    chunk = min(thin, 1024)
    return pl.pallas_call(
        skipping(functools.partial(first_sweep_kernel, chunk, protos_total, protos_total // protos.shape[0]), 5, len(order)),
        in_specs=[whole(pltpu.SMEM), whole(pl.ANY), whole(pl.ANY), whole(pl.ANY), whole()]
        + [whole(pl.ANY)] * len(order),
        out_specs=[whole(), whole(pl.ANY)],
        out_shape=[
            jax.ShapeDtypeStruct(sums_shape(copies, crops_total), jnp.bfloat16),
            pltpu.HBM((thin, crops_total), jnp.bfloat16),
        ],
        scratch_shapes=[
            pltpu.VMEM((thin, width), jnp.bfloat16),
            pltpu.VMEM((crops_total, width), jnp.bfloat16),
            pltpu.VMEM((thin, crops_total), jnp.float32),
            pltpu.VMEM((thin // chunk, chunk, crops_total), jnp.bfloat16),
            pltpu.VMEM((thin, 128), jnp.float32),
            pltpu.VMEM((1, crops_total), jnp.float32),
            pltpu.SemaphoreType.DMA((3,)),
            pltpu.SemaphoreType.DMA((thin // chunk,)),
        ],
        compiler_params=params(32 if crops_total <= 2048 else 56),
        cost_estimate=cost(2 * thin * width * crops_total, 2 * thin * crops_total, thin * crops_total),
        name="first_sweep",
    )(index, in_hbm(protos), mine, other, tops, *order)


def fetch_rows(weights_hbm, weights_ref, sems):
    steps, chunk, _ = weights_ref.shape

    def rows_copy(index):
        return pltpu.make_async_copy(
            weights_hbm.at[part(index, chunk), :], weights_ref.at[index], sems.at[index]
        )

    for index in range(steps):
        rows_copy(index).start()
    return lambda index: rows_copy(index).wait()


def scaled_fold(weights_ref, index, scale_ref):
    _, chunk, crops_total = weights_ref.shape
    folds = []
    for row in range(0, chunk, 64):
        fold = None
        for start in range(0, crops_total, TILE):
            columns = slice(start, start + TILE)
            weights = weights_ref[index, row : row + 64, columns].astype(jnp.float32)
            scaled = lane_fold(weights * scale_ref[:, columns], jnp.add)
            fold = scaled if fold is None else fold + scaled
        folds.append(fold)
    return jnp.concatenate(folds, axis=0)


def next_sweep_kernel(
    protos_total, weights_hbm, parts_ref, copies_ref, weights_ref, scale_ref, pieces_ref, totals_ref, sems,
):
    steps, chunk, crops_total = weights_ref.shape
    arrived = fetch_rows(weights_hbm, weights_ref, sems)
    take_scales(parts_ref, scale_ref)
    totals_ref[...] = jnp.zeros(totals_ref.shape, jnp.float32)

    def weigh(index):
        return three_pieces(lane_scales(scaled_fold(weights_ref, index, scale_ref), protos_total))

    def add_up(index):
        return jnp.dot(pieces_ref[...], weights_ref[index], preferred_element_type=jnp.float32)

    arrived(0)
    pieces_ref[...] = weigh(0)

    def sweep(index, carry):
        arrived(index)
        sums = add_up(index - 1)
        pieces = weigh(index)
        totals_ref[...] += sums
        pieces_ref[...] = pieces
        return carry

    lax.fori_loop(1, steps, sweep, 0)
    totals = totals_ref[...] + add_up(steps - 1)
    give_sums(copies_ref, jnp.sum(totals, axis=0, keepdims=True))


def next_sweep(weights, parts, order, protos_total):
    thin, crops_total = weights.shape
    copies = parts.shape[0]
    chunk = min(thin, 256)
    return pl.pallas_call(
        skipping(functools.partial(next_sweep_kernel, protos_total), 2, len(order)),
        in_specs=[whole(pl.ANY), whole()] + [whole(pl.ANY)] * len(order),
        out_specs=whole(),
        out_shape=jax.ShapeDtypeStruct(sums_shape(copies, crops_total), jnp.bfloat16),
        scratch_shapes=[
            pltpu.VMEM((thin // chunk, chunk, crops_total), jnp.bfloat16),
            pltpu.VMEM((1, crops_total), jnp.float32),
            pltpu.VMEM((16, chunk), jnp.bfloat16),
            pltpu.VMEM((16, crops_total), jnp.float32),
            pltpu.SemaphoreType.DMA((thin // chunk,)),
        ],
        compiler_params=params(16 if crops_total <= 2048 else 50),
        cost_estimate=cost(8 * thin * crops_total, 2 * thin * crops_total),
        name="next_sweep",
    )(in_hbm(weights), parts, *order)


def last_scales_kernel(
    protos_total, weights_hbm, parts_ref, copies_ref, weights_ref, scale_ref, out_ref, sems,
):
    steps, chunk, crops_total = weights_ref.shape
    arrived = fetch_rows(weights_hbm, weights_ref, sems)
    take_scales(parts_ref, scale_ref)

    def weigh(index, carry):
        arrived(index)
        out_ref[:, part(index, chunk)] = lane_scales(
            scaled_fold(weights_ref, index, scale_ref), protos_total
        )
        return carry

    lax.fori_loop(0, steps, weigh, 0)
    copies_ref[...] = jnp.broadcast_to(out_ref[...][None], copies_ref.shape)


def last_scales(weights, parts, order, copies, protos_total):
    thin, crops_total = weights.shape
    chunk = min(thin, 256)
    return pl.pallas_call(
        skipping(functools.partial(last_scales_kernel, protos_total), 2, len(order)),
        in_specs=[whole(pl.ANY), whole()] + [whole(pl.ANY)] * len(order),
        out_specs=whole(),
        out_shape=jax.ShapeDtypeStruct((copies, 1, thin), jnp.float32),
        scratch_shapes=[
            pltpu.VMEM((thin // chunk, chunk, crops_total), jnp.bfloat16),
            pltpu.VMEM((1, crops_total), jnp.float32),
            pltpu.VMEM((1, thin), jnp.float32),
            pltpu.SemaphoreType.DMA((thin // chunk,)),
        ],
        compiler_params=params(16 if crops_total <= 2048 else 50),
        cost_estimate=cost(4 * thin * crops_total, 2 * thin * crops_total),
        name="last_scales",
    )(in_hbm(weights), parts, *order)


def student_middle_kernel(
    index_ref, keep_ref, core_ref, x_ref, bias_ref, own_ref, partner_ref, other_ref, last_ref, last_bias_ref,
    unit_ref, emb_ref, lengths_ref, hidden_ref,
):
    share = x_ref.shape[0]
    block = own_ref.shape[0]
    sums = keep_ref[:share, :] + core_ref[:share, :] + x_ref[...]
    hidden_ref[...] = gelu(sums + bias_ref[...]).astype(jnp.bfloat16)
    index = index_ref[0]
    weights = ((0, own_ref[...]), (2, partner_ref[...]), (1, other_ref[...]), (3, last_ref[...]))
    bottleneck = jnp.broadcast_to(last_bias_ref[...], unit_ref.shape)
    for flip, weight in weights:
        bottleneck = bottleneck + jnp.dot(
            hidden_ref[:, part(index ^ flip, block)], weight, preferred_element_type=jnp.float32
        )
    unit, lengths = unit_rows(bottleneck)
    unit_ref[...] = unit
    emb_ref[...] = unit.astype(jnp.bfloat16)
    lengths_ref[...] = jnp.broadcast_to(lengths, lengths_ref.shape)


def student_middle(index, keep, core_rows, x_rows, bias, weights, last_bias):
    share, units = x_rows.shape
    width = weights[0].shape[1]
    return pl.pallas_call(
        student_middle_kernel,
        in_specs=[whole(pltpu.SMEM)] + [whole()] * 9,
        out_specs=[whole()] * 3,
        out_shape=[
            jax.ShapeDtypeStruct((share, width), jnp.float32),
            jax.ShapeDtypeStruct((share, width), jnp.bfloat16),
            jax.ShapeDtypeStruct((share, 128), jnp.float32),
        ],
        scratch_shapes=[pltpu.VMEM((share, units), jnp.bfloat16)],
        compiler_params=params(12),
        cost_estimate=cost(2 * share * units * width, 2 * units * width + 16 * share * units),
        name="student_middle",
    )(index, keep, core_rows, x_rows, in_hbm(bias.reshape(1, -1)), in_hbm(weights[0]), *weights[1:], in_hbm(last_bias.reshape(1, -1)))


def finish_kernel(unit_ref, lengths_ref, *rest):
    out_ref, blocks = rest[-1], rest[:-1]
    attracts, repels = blocks[: len(blocks) // 2], blocks[len(blocks) // 2 :]
    width = unit_ref.shape[1]
    row_top = functools.reduce(jnp.maximum, [ref[:, width + 128 :] for ref in attracts])
    attract_sum = repel_sum = 0.0
    row_sum = column_sum = 0.0
    for ref in attracts:
        fade = jnp.exp2((ref[:, width + 128 :] - row_top) * student_rate)
        row_sum = row_sum + ref[:, width : width + 128] * fade
        attract_sum = attract_sum + ref[:, :width] * jnp.tile(fade, (1, width // 128))
    for ref in repels:
        column_sum = column_sum + jnp.sum(ref[:, width:].astype(jnp.float32), axis=1, keepdims=True)
        repel_sum = repel_sum + ref[:, :width].astype(jnp.float32)
    emb_grad = (
        attract_sum / jnp.tile(row_sum, (1, width // 128))
        - repel_sum / column_sum
    ) / student_temp
    unit = unit_ref[...]
    along = jnp.sum(unit * emb_grad, axis=1, keepdims=True)
    out_ref[...] = (emb_grad - unit * along) / jnp.tile(lengths_ref[...], (1, width // 128))


def finish(unit, lengths, attracts, repels):
    return pl.pallas_call(
        finish_kernel,
        in_specs=[whole()] * (2 + len(attracts) + len(repels)),
        out_specs=whole(),
        out_shape=jax.ShapeDtypeStruct(unit.shape, jnp.float32),
        compiler_params=params(8),
        cost_estimate=cost(40 * unit.size, 40 * unit.size),
        name="finish",
    )(unit, lengths, *attracts, *repels)


def swap(values, axis, flip):
    return lax.ppermute(values, axis, [(i, i ^ flip) for i in range(lax.axis_size(axis))])


def bit_reversed(values, count):
    bits = count.bit_length() - 1
    split = values.reshape((2,) * bits + values.shape[1:])
    turned = jnp.transpose(split, tuple(reversed(range(bits))) + tuple(range(bits, split.ndim)))
    return turned.reshape(values.shape)


def gather_batch(values):
    step = lax.axis_size("batch") // 2
    stages = [values]
    while step:
        other = swap(values, "batch", step)
        upper = (lax.axis_index("batch") // step) % 2
        values = jnp.where(
            upper == 0, jnp.concatenate([values, other]), jnp.concatenate([other, values])
        )
        stages.append(values)
        step //= 2
    return stages


def send_blocks(blocks):
    flips = list(range(len(blocks) - 1, 0, -1))
    return [blocks[0]] + [swap(blocks[flip], "proto", flip) for flip in flips]


def all_to_all(copies, axes):
    return lax.all_to_all(copies, axes, 0, 0, tiled=True)


def body(crops, teacher_emb, w_first, b_first, w_second, b_second, w_third, b_third, protos):
    batch_index = lax.axis_index("batch")
    proto_index = lax.axis_index("proto")
    batch_size = lax.axis_size("batch")
    proto_size = lax.axis_size("proto")
    devices = batch_size * proto_size
    share_rows = crops.shape[0]
    group_rows = teacher_emb.shape[0]
    crops_total = group_rows * batch_size
    protos_total = protos.shape[0] * proto_size
    count, width = protos.shape
    thin = count // batch_size
    core = proto_index % 2
    proto_ref = proto_index.reshape(1)
    thin_ref = jnp.stack([batch_index, core])
    wide_ref = jnp.stack([batch_index, proto_index])

    own_unit, half = teacher_units(core.reshape(1), teacher_emb)
    stages = gather_batch(half)
    mine = stages[-1]
    other = swap(mine, "proto", 1)

    crops_x = swap(crops, "proto", 2)
    rows = [crops, crops_x, swap(crops, "proto", 1), swap(crops_x, "proto", 1)]
    third_x = swap(w_third, "proto", 2)
    thirds = [w_third, third_x, swap(w_third, "proto", 1), swap(third_x, "proto", 1)]
    top_copies, keep, give = front(
        proto_ref, own_unit, b_first, rows, w_first, w_second, protos, (stages[2], third_x), devices, 8
    )
    all_tops = all_to_all(top_copies, BOTH)
    core_rows = swap(give, "proto", 1)
    x_sent = keep[share_rows:] + core_rows[share_rows:]
    x_rows = swap(x_sent, "proto", 2)
    unit, rounded, lengths = student_middle(
        proto_ref, keep, core_rows, x_rows, b_second, thirds, b_third
    )
    student_emb = jnp.concatenate([rounded] + [swap(rounded, "proto", flip) for flip in range(1, proto_size)])
    empty = jnp.concatenate(
        [jnp.zeros((group_rows, width + 128), jnp.float32), jnp.full((group_rows, 128), -1e30, jnp.float32)], axis=1
    )
    eighth = count // 8
    (state,) = attract(student_emb, empty, protos, 0, 5 * eighth, 5, 1)
    slots = attract(student_emb, state, protos, 5 * eighth, 3 * eighth, 3, proto_size)
    attract_parts = send_blocks(slots)

    copies, weights = first_sweep(thin_ref, protos, mine, other, all_tops, (x_sent, *thirds[2:]), devices, thin, protos_total)
    for _ in range(ITERS - 2):
        copies = next_sweep(weights, all_to_all(copies, BOTH), (rounded,), protos_total)
    scale_copies = last_scales(weights, all_to_all(copies, BOTH), (state,), batch_size, protos_total)
    all_scale = all_to_all(scale_copies, "batch")
    repels = repel(wide_ref, own_unit, all_tops, all_scale, protos, (slots[0],), proto_size)
    return finish(unit, lengths, attract_parts, send_blocks(repels))


def solution(mesh):
    in_specs = (
        P(("batch", "proto"), None),
        P("batch", None),
        P(None, "proto"),
        P(),
        P("proto", None),
        P(),
        P("proto", None),
        P(),
        P("proto", None),
    )
    out_specs = P(("batch", "proto"), None)
    return jax.shard_map(body, mesh=mesh, in_specs=in_specs, out_specs=out_specs, check_vma=False)
```

```python
import functools
import math

import jax
import jax.numpy as jnp
from jax import lax
from jax.experimental import pallas as pl
from jax.experimental.pallas import tpu as pltpu
from jax.sharding import PartitionSpec as P

ITERS = 3

student_temp = 0.1
teacher_temp = 0.07
norm_eps = 1e-06
teacher_rate = math.log2(math.e) / teacher_temp
student_rate = math.log2(math.e) / student_temp

MIB = 1024 * 1024
BOTH = ("batch", "proto")
TILE = 256
WIDE = 512


def scores(left_rows, right_rows):
    return lax.dot_general(
        left_rows, right_rows, (((1,), (1,)), ((), ())), preferred_element_type=jnp.float32
    )


def unit_rows(values):
    lengths = jnp.sqrt(jnp.sum(values * values, axis=1, keepdims=True) + norm_eps)
    return (values / lengths, lengths)


def gelu(values):
    return 0.5 * values * (1.0 + lax.erf(values * math.sqrt(0.5)))


def whole(memory_space=pltpu.VMEM):
    return pl.BlockSpec(memory_space=memory_space)


def in_hbm(array):
    return pltpu.with_memory_space_constraint(array, pltpu.HBM)


def skipping(kernel, first, count):
    def trimmed(*refs):
        kernel(*refs[:first], *refs[first + count :])

    return trimmed


def part(index, size):
    return pl.ds(pl.multiple_of(index * size, size), size)


def lane_fold(values, combine):
    folded = values[:, :128]
    for start in range(128, values.shape[1], 128):
        folded = combine(folded, values[:, start : start + 128])
    return folded


def params(mib):
    return pltpu.CompilerParams(vmem_limit_bytes=mib * MIB)


def cost(flops, bytes_accessed, transcendentals=0):
    return pl.CostEstimate(
        flops=int(flops), bytes_accessed=int(bytes_accessed), transcendentals=int(transcendentals)
    )


def fetch(source, target, sems, first_row=0):
    count, rows = target.shape[:2]

    def chunk_copy(index):
        start = pl.multiple_of(first_row + index * rows, rows)
        return pltpu.make_async_copy(source.at[pl.ds(start, rows), :], target.at[index], sems.at[index])

    for index in range(count):
        chunk_copy(index).start()
    return lambda index: chunk_copy(index).wait()


def teacher_units_kernel(core_ref, emb_ref, unit_ref, half_ref):
    unit_ref[...] = unit_rows(emb_ref[...].astype(jnp.float32))[0].astype(jnp.bfloat16)
    half = half_ref.shape[0]
    half_ref[...] = unit_ref[part(core_ref[0], half), :]


def teacher_units(core, teacher_emb):
    rows, width = teacher_emb.shape
    return pl.pallas_call(
        teacher_units_kernel,
        in_specs=[whole(pltpu.SMEM), whole()],
        out_specs=[whole(), whole()],
        out_shape=[
            jax.ShapeDtypeStruct((rows, width), jnp.bfloat16),
            jax.ShapeDtypeStruct((rows // 2, width), jnp.bfloat16),
        ],
        compiler_params=params(4),
        cost_estimate=cost(4 * rows * width, 8 * rows * width),
        name="teacher_units",
    )(core, in_hbm(teacher_emb))


def front_kernel(
    index_ref, unit_ref, bias_ref, own_hbm, x_hbm, core_hbm, last_hbm, first_hbm, second_hbm, protos_hbm,
    tops_ref, keep_ref, give_ref, first_ref, second_ref, rows_ref, protos_ref, padded_ref, top_ref, sems, chunk_sems,
):
    rows = unit_ref.shape[0]
    steps, block = protos_ref.shape[:2]
    wide = min(2 * WIDE, block)
    share = own_hbm.shape[0]
    arrived = fetch(protos_hbm, protos_ref, chunk_sems)
    copies = [
        pltpu.make_async_copy(source, rows_ref.at[slot * share : (slot + 1) * share, :], sems.at[slot])
        for slot, source in enumerate((own_hbm, x_hbm, core_hbm, last_hbm))
    ]
    copies.append(pltpu.make_async_copy(first_hbm, first_ref, sems.at[4]))
    copies.append(pltpu.make_async_copy(second_hbm, second_ref, sems.at[5]))
    for copy in copies:
        copy.start()
    padded_ref[...] = jnp.zeros(padded_ref.shape, jnp.bfloat16)
    padded_ref[:rows, :] = unit_ref[...]
    top_ref[...] = jnp.full(top_ref.shape, -jnp.inf, jnp.float32)

    def step(index, carry):
        arrived(index)
        top = top_ref[...]
        for start in range(0, block, wide):
            products = scores(protos_ref[index, start : start + wide, :], padded_ref[...])
            top = jnp.maximum(top, jnp.max(products.reshape(-1, 8, products.shape[1]), axis=0))
        top_ref[...] = top
        return carry

    lax.fori_loop(0, steps, step, 0)
    tops = jnp.max(top_ref[...], axis=0, keepdims=True)
    tops_ref[...] = jnp.broadcast_to(tops[None], tops_ref.shape)
    for copy in copies:
        copy.wait()
    hidden = first_ref.shape[1]
    bias = bias_ref[:, part(index_ref[0], hidden)]
    h_first = gelu(
        jnp.dot(rows_ref[...], first_ref[...], preferred_element_type=jnp.float32) + bias
    ).astype(jnp.bfloat16)
    for start in range(0, second_ref.shape[1], 512):
        columns = slice(start, start + 512)
        product = jnp.dot(h_first, second_ref[:, columns], preferred_element_type=jnp.float32)
        keep_ref[:, columns] = product[: 2 * share]
        give_ref[:, columns] = product[2 * share :]


def front(index, unit, bias, rows, first, second, protos, order, copies, steps):
    share, features = rows[0].shape
    hidden, units = second.shape
    count, width = protos.shape
    return pl.pallas_call(
        skipping(front_kernel, 10, len(order)),
        in_specs=[whole(pltpu.SMEM), whole(), whole()] + [whole(pl.ANY)] * (7 + len(order)),
        out_specs=[whole()] * 3,
        out_shape=[jax.ShapeDtypeStruct((copies, 1, 256), jnp.float32)]
        + [jax.ShapeDtypeStruct((2 * share, units), jnp.float32)] * 2,
        scratch_shapes=[
            pltpu.VMEM(first.shape, jnp.bfloat16),
            pltpu.VMEM(second.shape, jnp.bfloat16),
            pltpu.VMEM((4 * share, features), jnp.bfloat16),
            pltpu.VMEM((steps, count // steps, width), jnp.bfloat16),
            pltpu.VMEM((256, width), jnp.bfloat16),
            pltpu.VMEM((8, 256), jnp.float32),
            pltpu.SemaphoreType.DMA((6,)),
            pltpu.SemaphoreType.DMA((steps,)),
        ],
        compiler_params=params(26),
        cost_estimate=cost(
            2 * unit.size * count + 8 * share * hidden * (features + units), 2 * width * count
        ),
        name="front",
    )(
        index, unit, in_hbm(bias.reshape(1, -1)), in_hbm(rows[0]), *rows[1:],
        in_hbm(first), in_hbm(second), in_hbm(protos), *order,
    )


def repel_kernel(group, index_ref, unit_ref, tops_ref, scale_ref, protos_hbm, *rest):
    out_refs, (protos_ref, sems, acc_ref, sum_ref, bias_ref) = rest[:-5], rest[-5:]
    rows, width = unit_ref.shape
    steps, block = protos_ref.shape[:2]
    wide = min(WIDE, block)
    arrived = fetch(protos_hbm, protos_ref, sems)
    first = index_ref[0] * group
    top = tops_ref[first]
    for other in range(1, group):
        top = jnp.maximum(top, tops_ref[first + other])
    bias_ref[...] = jnp.transpose(jnp.broadcast_to(top, (128, 256)))[:rows, :] * -teacher_rate
    acc_ref[...] = jnp.zeros(acc_ref.shape, jnp.float32)
    sum_ref[...] = jnp.zeros(sum_ref.shape, jnp.float32)

    def step(index, carry):
        arrived(index)
        bias = bias_ref[...]
        total = sum_ref[...]
        acc = acc_ref[...]
        for start in range(0, block, wide):
            protos = protos_ref[index, start : start + wide, :]
            products = scores(unit_ref[...], protos)
            pieces = []
            for lane in range(0, wide, 128):
                scaled = jnp.exp2(products[:, lane : lane + 128] * teacher_rate + bias)
                scaled = scaled * scale_ref[index, :, start + lane : start + lane + 128]
                total = total + scaled
                pieces.append(scaled.astype(jnp.bfloat16))
            acc = acc + jnp.dot(
                jnp.concatenate(pieces, axis=1), protos, preferred_element_type=jnp.float32
            )
        sum_ref[...] = total
        acc_ref[...] = acc
        return carry

    lax.fori_loop(0, steps, step, 0)
    total = jnp.sum(sum_ref[...], axis=1, keepdims=True)
    lanes = lax.broadcasted_iota(jnp.int32, sum_ref.shape, 1)
    sum_ref[...] = jnp.broadcast_to(total, sum_ref.shape)
    share = out_refs[0].shape[0]
    lanes = lanes[:share, :]
    for flip, out_ref in enumerate(out_refs):
        span = part(index_ref[1] ^ flip, share)
        total = sum_ref[span, :]
        out_ref[:, :width] = acc_ref[span, :].astype(out_ref.dtype)
        if flip == 0:
            out_ref[:, width:] = jnp.where(lanes == 0, total, 0.0)
        else:
            high = total.astype(jnp.bfloat16).astype(jnp.float32)
            middle = (total - high).astype(jnp.bfloat16).astype(jnp.float32)
            pieces = jnp.where(lanes == 0, high, jnp.where(lanes == 1, middle, total - high - middle))
            out_ref[:, width:] = jnp.where(lanes < 3, pieces, 0.0).astype(jnp.bfloat16)


def repel(index, unit, tops, scale, protos, order, proto_size):
    rows, width = unit.shape
    count = protos.shape[0]
    steps, _, block = scale.shape
    return pl.pallas_call(
        skipping(functools.partial(repel_kernel, proto_size), 5, len(order)),
        in_specs=[whole(pltpu.SMEM), whole(), whole(), whole(), whole(pl.ANY)] + [whole(pl.ANY)] * len(order),
        out_specs=[whole()] * proto_size,
        out_shape=[
            jax.ShapeDtypeStruct((rows // proto_size, width + 128), jnp.bfloat16 if flip else jnp.float32)
            for flip in range(proto_size)
        ],
        scratch_shapes=[
            pltpu.VMEM((steps, block, width), jnp.bfloat16),
            pltpu.SemaphoreType.DMA((steps,)),
            pltpu.VMEM((rows, width), jnp.float32),
            pltpu.VMEM((rows, 128), jnp.float32),
            pltpu.VMEM((rows, 128), jnp.float32),
        ],
        compiler_params=params(16),
        cost_estimate=cost(4 * rows * width * count, 2 * width * count, rows * count),
        name="repel",
    )(index, unit, tops, scale, in_hbm(protos), *order)


def attract_kernel(first_row, last, emb_ref, state_ref, protos_hbm, *rest):
    out_refs, scratch = rest[:-6], rest[-6:]
    protos_ref, sems, products_ref, acc_ref, sum_ref, top_ref = scratch
    width = emb_ref.shape[1]
    steps, block = protos_ref.shape[:2]
    arrived = fetch(protos_hbm, protos_ref, sems, first_row)
    old_top = state_ref[:, width + 128 :]
    top_ref[...] = old_top

    def first(index, carry):
        arrived(index)
        top = top_ref[...]
        for start in range(0, block, TILE):
            products = scores(emb_ref[...], protos_ref[index, start : start + TILE, :])
            products_ref[index, :, start : start + TILE] = products
            top = jnp.maximum(top, lane_fold(products, jnp.maximum))
        top_ref[...] = top
        return carry

    lax.fori_loop(0, steps, first, 0)
    top = jnp.broadcast_to(jnp.max(top_ref[...], axis=1, keepdims=True), top_ref.shape)
    fade = jnp.exp2((old_top - top) * student_rate)
    top_ref[...] = top
    sum_ref[...] = state_ref[:, width : width + 128] * fade
    acc_ref[...] = state_ref[:, :width] * jnp.tile(fade, (1, width // 128))

    def second(index, carry):
        top = top_ref[...]
        total = sum_ref[...]
        acc = acc_ref[...]
        for start in range(0, block, TILE):
            pieces = []
            for lane in range(start, start + TILE, 128):
                shifted = jnp.exp2((products_ref[index, :, lane : lane + 128] - top) * student_rate)
                total = total + shifted
                pieces.append(shifted.astype(jnp.bfloat16))
            acc = acc + jnp.dot(
                jnp.concatenate(pieces, axis=1),
                protos_ref[index, start : start + TILE, :],
                preferred_element_type=jnp.float32,
            )
        sum_ref[...] = total
        acc_ref[...] = acc
        return carry

    lax.fori_loop(0, steps, second, 0)
    if last:
        total = jnp.sum(sum_ref[...], axis=1, keepdims=True)
        sum_ref[...] = jnp.broadcast_to(total, sum_ref.shape)
    share = out_refs[0].shape[0]
    for slot, out_ref in enumerate(out_refs):
        rows = pl.ds(slot * share, share)
        out_ref[:, :width] = acc_ref[rows, :]
        out_ref[:, width : width + 128] = sum_ref[rows, :]
        out_ref[:, width + 128 :] = top_ref[rows, :]


def attract(emb, state, protos, first_row, count, steps, outputs):
    rows, width = emb.shape
    block = count // steps
    return pl.pallas_call(
        functools.partial(attract_kernel, first_row, outputs > 1),
        in_specs=[whole(), whole(), whole(pl.ANY)],
        out_specs=[whole()] * outputs,
        out_shape=[jax.ShapeDtypeStruct((rows // outputs, width + 256), jnp.float32)] * outputs,
        scratch_shapes=[
            pltpu.VMEM((steps, block, width), jnp.bfloat16),
            pltpu.SemaphoreType.DMA((steps,)),
            pltpu.VMEM((steps, rows, block), jnp.float32),
            pltpu.VMEM((rows, width), jnp.float32),
            pltpu.VMEM((rows, 128), jnp.float32),
            pltpu.VMEM((rows, 128), jnp.float32),
        ],
        compiler_params=params(24),
        cost_estimate=cost(4 * rows * width * count, 2 * width * count, rows * count),
        name="attract",
    )(emb, state, in_hbm(protos))


def three_pieces(values):
    high = values.astype(jnp.bfloat16)
    rest = values - high.astype(jnp.float32)
    middle = rest.astype(jnp.bfloat16)
    low = (rest - middle.astype(jnp.float32)).astype(jnp.bfloat16)
    return jnp.concatenate([high, middle, low, jnp.zeros((13, values.shape[1]), jnp.bfloat16)], axis=0)


def lane_scales(folded, protos_total):
    sums = [
        jnp.sum(jnp.transpose(folded[start : start + 128, :]), axis=0, keepdims=True)
        for start in range(0, folded.shape[0], 128)
    ]
    return 1.0 / (protos_total * jnp.concatenate(sums, axis=1))


def give_sums(copies_ref, totals):
    rows = [totals[:, start : start + 128] for start in range(0, totals.shape[1], 128)]
    spare = copies_ref.shape[1] - len(rows)
    if spare:
        rows.append(jnp.zeros((spare, 128), jnp.float32))
    packed = jnp.concatenate(rows, axis=0).astype(jnp.bfloat16)
    copies_ref[...] = jnp.broadcast_to(packed[None], copies_ref.shape)


def take_scales(parts_ref, scale_ref):
    crops_total = scale_ref.shape[1]
    sums = jnp.sum(parts_ref[...].astype(jnp.float32), axis=0)
    for row in range(crops_total // 128):
        scale_ref[:, row * 128 : row * 128 + 128] = 1.0 / (crops_total * sums[row : row + 1, :])


def sums_shape(copies, crops_total):
    return (copies, -(-crops_total // 2048) * 16, 128)


def lane_order(tops_ref, group, crops_total):
    batches = tops_ref.shape[0] // group
    rows = crops_total // batches
    bits = batches.bit_length() - 1
    tops = []
    for batch in range(batches):
        source = int(format(batch, "b").zfill(bits)[::-1], 2) if bits else 0
        tops.append(
            functools.reduce(jnp.maximum, [tops_ref[source * group + other] for other in range(group)])
        )
    halves = [top[:, core * rows // 2 : (core + 1) * rows // 2] for core in range(2) for top in tops]
    return jnp.concatenate(halves, axis=1)


def first_sweep_kernel(
    chunk, protos_total, group, index_ref, protos_hbm, mine_hbm, other_hbm, tops_ref, copies_ref, weights_hbm,
    protos_ref, units_ref, weights_ref, rounded_ref, scale_ref, bias_ref, sems, out_sems,
):
    thin, crops_total = weights_ref.shape
    half = mine_hbm.shape[0]
    core = index_ref[1]
    copies = (
        pltpu.make_async_copy(protos_hbm.at[part(index_ref[0], thin), :], protos_ref, sems.at[0]),
        pltpu.make_async_copy(mine_hbm, units_ref.at[part(core, half), :], sems.at[1]),
        pltpu.make_async_copy(other_hbm, units_ref.at[part(1 - core, half), :], sems.at[2]),
    )
    for copy in copies:
        copy.start()
    bias_ref[...] = lane_order(tops_ref, group, crops_total) * -teacher_rate
    for copy in copies:
        copy.wait()

    def chunk_out(index):
        return pltpu.make_async_copy(
            rounded_ref.at[index], weights_hbm.at[part(index, chunk), :], out_sems.at[index]
        )

    def weigh(index, carry):
        rows = part(index, chunk)
        protos = protos_ref[rows, :]
        folded = jnp.zeros((chunk, 128), jnp.float32)
        for start in range(0, crops_total, TILE):
            columns = slice(start, start + TILE)
            products = scores(protos, units_ref[columns, :])
            weights = jnp.exp2(products * teacher_rate + bias_ref[:, columns])
            weights_ref[rows, columns] = weights
            rounded_ref[index, :, columns] = weights.astype(jnp.bfloat16)
            folded = folded + lane_fold(weights, jnp.add)
        sums = jnp.sum(folded, axis=1, keepdims=True)
        scale_ref[rows, :] = jnp.broadcast_to(1.0 / (protos_total * sums), (chunk, 128))
        chunk_out(index).start()
        return carry

    lax.fori_loop(0, thin // chunk, weigh, 0)
    small = min(thin, 64)

    def add_up(index, totals):
        rows = part(index, small)
        scaled = weights_ref[rows, :] * jnp.tile(scale_ref[rows, :], (1, crops_total // 128))
        return totals + jnp.sum(scaled.reshape(-1, 8, crops_total), axis=0)

    totals = lax.fori_loop(0, thin // small, add_up, jnp.zeros((8, crops_total), jnp.float32))
    give_sums(copies_ref, jnp.sum(totals, axis=0, keepdims=True))
    for index in range(thin // chunk):
        chunk_out(index).wait()


def first_sweep(index, protos, mine, other, tops, order, copies, thin, protos_total):
    width = protos.shape[1]
    crops_total = 2 * mine.shape[0]
    chunk = min(thin, 1024)
    return pl.pallas_call(
        skipping(functools.partial(first_sweep_kernel, chunk, protos_total, protos_total // protos.shape[0]), 5, len(order)),
        in_specs=[whole(pltpu.SMEM), whole(pl.ANY), whole(pl.ANY), whole(pl.ANY), whole()]
        + [whole(pl.ANY)] * len(order),
        out_specs=[whole(), whole(pl.ANY)],
        out_shape=[
            jax.ShapeDtypeStruct(sums_shape(copies, crops_total), jnp.bfloat16),
            pltpu.HBM((thin, crops_total), jnp.bfloat16),
        ],
        scratch_shapes=[
            pltpu.VMEM((thin, width), jnp.bfloat16),
            pltpu.VMEM((crops_total, width), jnp.bfloat16),
            pltpu.VMEM((thin, crops_total), jnp.float32),
            pltpu.VMEM((thin // chunk, chunk, crops_total), jnp.bfloat16),
            pltpu.VMEM((thin, 128), jnp.float32),
            pltpu.VMEM((1, crops_total), jnp.float32),
            pltpu.SemaphoreType.DMA((3,)),
            pltpu.SemaphoreType.DMA((thin // chunk,)),
        ],
        compiler_params=params(32 if crops_total <= 2048 else 56),
        cost_estimate=cost(2 * thin * width * crops_total, 2 * thin * crops_total, thin * crops_total),
        name="first_sweep",
    )(index, in_hbm(protos), mine, other, tops, *order)


def fetch_rows(weights_hbm, weights_ref, sems):
    steps, chunk, _ = weights_ref.shape

    def rows_copy(index):
        return pltpu.make_async_copy(
            weights_hbm.at[part(index, chunk), :], weights_ref.at[index], sems.at[index]
        )

    for index in range(steps):
        rows_copy(index).start()
    return lambda index: rows_copy(index).wait()


def scaled_fold(weights_ref, index, scale_ref):
    _, chunk, crops_total = weights_ref.shape
    folds = []
    for row in range(0, chunk, 64):
        fold = None
        for start in range(0, crops_total, TILE):
            columns = slice(start, start + TILE)
            weights = weights_ref[index, row : row + 64, columns].astype(jnp.float32)
            scaled = lane_fold(weights * scale_ref[:, columns], jnp.add)
            fold = scaled if fold is None else fold + scaled
        folds.append(fold)
    return jnp.concatenate(folds, axis=0)


def next_sweep_kernel(
    protos_total, weights_hbm, parts_ref, copies_ref, weights_ref, scale_ref, pieces_ref, totals_ref, sems,
):
    steps, chunk, crops_total = weights_ref.shape
    arrived = fetch_rows(weights_hbm, weights_ref, sems)
    take_scales(parts_ref, scale_ref)
    totals_ref[...] = jnp.zeros(totals_ref.shape, jnp.float32)

    def weigh(index):
        return three_pieces(lane_scales(scaled_fold(weights_ref, index, scale_ref), protos_total))

    def add_up(index):
        return jnp.dot(pieces_ref[...], weights_ref[index], preferred_element_type=jnp.float32)

    arrived(0)
    pieces_ref[...] = weigh(0)

    def sweep(index, carry):
        arrived(index)
        sums = add_up(index - 1)
        pieces = weigh(index)
        totals_ref[...] += sums
        pieces_ref[...] = pieces
        return carry

    lax.fori_loop(1, steps, sweep, 0)
    totals = totals_ref[...] + add_up(steps - 1)
    give_sums(copies_ref, jnp.sum(totals, axis=0, keepdims=True))


def next_sweep(weights, parts, order, protos_total):
    thin, crops_total = weights.shape
    copies = parts.shape[0]
    chunk = min(thin, 256)
    return pl.pallas_call(
        skipping(functools.partial(next_sweep_kernel, protos_total), 2, len(order)),
        in_specs=[whole(pl.ANY), whole()] + [whole(pl.ANY)] * len(order),
        out_specs=whole(),
        out_shape=jax.ShapeDtypeStruct(sums_shape(copies, crops_total), jnp.bfloat16),
        scratch_shapes=[
            pltpu.VMEM((thin // chunk, chunk, crops_total), jnp.bfloat16),
            pltpu.VMEM((1, crops_total), jnp.float32),
            pltpu.VMEM((16, chunk), jnp.bfloat16),
            pltpu.VMEM((16, crops_total), jnp.float32),
            pltpu.SemaphoreType.DMA((thin // chunk,)),
        ],
        compiler_params=params(16 if crops_total <= 2048 else 50),
        cost_estimate=cost(8 * thin * crops_total, 2 * thin * crops_total),
        name="next_sweep",
    )(in_hbm(weights), parts, *order)


def last_scales_kernel(
    protos_total, weights_hbm, parts_ref, copies_ref, weights_ref, scale_ref, out_ref, sems,
):
    steps, chunk, crops_total = weights_ref.shape
    arrived = fetch_rows(weights_hbm, weights_ref, sems)
    take_scales(parts_ref, scale_ref)

    def weigh(index, carry):
        arrived(index)
        out_ref[:, part(index, chunk)] = lane_scales(
            scaled_fold(weights_ref, index, scale_ref), protos_total
        )
        return carry

    lax.fori_loop(0, steps, weigh, 0)
    copies_ref[...] = jnp.broadcast_to(out_ref[...][None], copies_ref.shape)


def last_scales(weights, parts, order, copies, protos_total):
    thin, crops_total = weights.shape
    chunk = min(thin, 256)
    return pl.pallas_call(
        skipping(functools.partial(last_scales_kernel, protos_total), 2, len(order)),
        in_specs=[whole(pl.ANY), whole()] + [whole(pl.ANY)] * len(order),
        out_specs=whole(),
        out_shape=jax.ShapeDtypeStruct((copies, 1, thin), jnp.float32),
        scratch_shapes=[
            pltpu.VMEM((thin // chunk, chunk, crops_total), jnp.bfloat16),
            pltpu.VMEM((1, crops_total), jnp.float32),
            pltpu.VMEM((1, thin), jnp.float32),
            pltpu.SemaphoreType.DMA((thin // chunk,)),
        ],
        compiler_params=params(16 if crops_total <= 2048 else 50),
        cost_estimate=cost(4 * thin * crops_total, 2 * thin * crops_total),
        name="last_scales",
    )(in_hbm(weights), parts, *order)


def student_middle_kernel(
    index_ref, keep_ref, core_ref, x_ref, bias_ref, own_ref, partner_ref, other_ref, last_ref, last_bias_ref,
    unit_ref, emb_ref, lengths_ref, hidden_ref,
):
    share = x_ref.shape[0]
    block = own_ref.shape[0]
    sums = keep_ref[:share, :] + core_ref[:share, :] + x_ref[...]
    hidden_ref[...] = gelu(sums + bias_ref[...]).astype(jnp.bfloat16)
    index = index_ref[0]
    weights = ((0, own_ref[...]), (2, partner_ref[...]), (1, other_ref[...]), (3, last_ref[...]))
    bottleneck = jnp.broadcast_to(last_bias_ref[...], unit_ref.shape)
    for flip, weight in weights:
        bottleneck = bottleneck + jnp.dot(
            hidden_ref[:, part(index ^ flip, block)], weight, preferred_element_type=jnp.float32
        )
    unit, lengths = unit_rows(bottleneck)
    unit_ref[...] = unit
    emb_ref[...] = unit.astype(jnp.bfloat16)
    lengths_ref[...] = jnp.broadcast_to(lengths, lengths_ref.shape)


def student_middle(index, keep, core_rows, x_rows, bias, weights, last_bias):
    share, units = x_rows.shape
    width = weights[0].shape[1]
    return pl.pallas_call(
        student_middle_kernel,
        in_specs=[whole(pltpu.SMEM)] + [whole()] * 9,
        out_specs=[whole()] * 3,
        out_shape=[
            jax.ShapeDtypeStruct((share, width), jnp.float32),
            jax.ShapeDtypeStruct((share, width), jnp.bfloat16),
            jax.ShapeDtypeStruct((share, 128), jnp.float32),
        ],
        scratch_shapes=[pltpu.VMEM((share, units), jnp.bfloat16)],
        compiler_params=params(12),
        cost_estimate=cost(2 * share * units * width, 2 * units * width + 16 * share * units),
        name="student_middle",
    )(index, keep, core_rows, x_rows, in_hbm(bias.reshape(1, -1)), in_hbm(weights[0]), *weights[1:], in_hbm(last_bias.reshape(1, -1)))


def finish_kernel(unit_ref, lengths_ref, *rest):
    out_ref, blocks = rest[-1], rest[:-1]
    attracts, repels = blocks[: len(blocks) // 2], blocks[len(blocks) // 2 :]
    width = unit_ref.shape[1]
    row_top = functools.reduce(jnp.maximum, [ref[:, width + 128 :] for ref in attracts])
    attract_sum = repel_sum = 0.0
    row_sum = column_sum = 0.0
    for ref in attracts:
        fade = jnp.exp2((ref[:, width + 128 :] - row_top) * student_rate)
        row_sum = row_sum + ref[:, width : width + 128] * fade
        attract_sum = attract_sum + ref[:, :width] * jnp.tile(fade, (1, width // 128))
    for ref in repels:
        column_sum = column_sum + jnp.sum(ref[:, width:].astype(jnp.float32), axis=1, keepdims=True)
        repel_sum = repel_sum + ref[:, :width].astype(jnp.float32)
    emb_grad = (
        attract_sum / jnp.tile(row_sum, (1, width // 128))
        - repel_sum / column_sum
    ) / student_temp
    unit = unit_ref[...]
    along = jnp.sum(unit * emb_grad, axis=1, keepdims=True)
    out_ref[...] = (emb_grad - unit * along) / jnp.tile(lengths_ref[...], (1, width // 128))


def finish(unit, lengths, attracts, repels):
    return pl.pallas_call(
        finish_kernel,
        in_specs=[whole()] * (2 + len(attracts) + len(repels)),
        out_specs=whole(),
        out_shape=jax.ShapeDtypeStruct(unit.shape, jnp.float32),
        compiler_params=params(8),
        cost_estimate=cost(40 * unit.size, 40 * unit.size),
        name="finish",
    )(unit, lengths, *attracts, *repels)


def swap(values, axis, flip):
    return lax.ppermute(values, axis, [(i, i ^ flip) for i in range(lax.axis_size(axis))])


def bit_reversed(values, count):
    bits = count.bit_length() - 1
    split = values.reshape((2,) * bits + values.shape[1:])
    turned = jnp.transpose(split, tuple(reversed(range(bits))) + tuple(range(bits, split.ndim)))
    return turned.reshape(values.shape)


def gather_batch(values):
    step = lax.axis_size("batch") // 2
    stages = [values]
    while step:
        other = swap(values, "batch", step)
        upper = (lax.axis_index("batch") // step) % 2
        values = jnp.where(
            upper == 0, jnp.concatenate([values, other]), jnp.concatenate([other, values])
        )
        stages.append(values)
        step //= 2
    return stages


def send_blocks(blocks):
    flips = list(range(len(blocks) - 1, 0, -1))
    return [blocks[0]] + [swap(blocks[flip], "proto", flip) for flip in flips]


def all_to_all(copies, axes):
    return lax.all_to_all(copies, axes, 0, 0, tiled=True)


def body(crops, teacher_emb, w_first, b_first, w_second, b_second, w_third, b_third, protos):
    batch_index = lax.axis_index("batch")
    proto_index = lax.axis_index("proto")
    batch_size = lax.axis_size("batch")
    proto_size = lax.axis_size("proto")
    devices = batch_size * proto_size
    share_rows = crops.shape[0]
    group_rows = teacher_emb.shape[0]
    crops_total = group_rows * batch_size
    protos_total = protos.shape[0] * proto_size
    count, width = protos.shape
    thin = count // batch_size
    core = proto_index % 2
    proto_ref = proto_index.reshape(1)
    thin_ref = jnp.stack([batch_index, core])
    wide_ref = jnp.stack([batch_index, proto_index])

    own_unit, half = teacher_units(core.reshape(1), teacher_emb)
    stages = gather_batch(half)
    mine = stages[-1]
    other = swap(mine, "proto", 1)

    crops_x = swap(crops, "proto", 2)
    rows = [crops, crops_x, swap(crops, "proto", 1), swap(crops_x, "proto", 1)]
    third_x = swap(w_third, "proto", 2)
    thirds = [w_third, third_x, swap(w_third, "proto", 1), swap(third_x, "proto", 1)]
    top_copies, keep, give = front(
        proto_ref, own_unit, b_first, rows, w_first, w_second, protos, (stages[2], third_x), devices, 8
    )
    all_tops = all_to_all(top_copies, BOTH)
    core_rows = swap(give, "proto", 1)
    x_sent = keep[share_rows:] + core_rows[share_rows:]
    x_rows = swap(x_sent, "proto", 2)
    unit, rounded, lengths = student_middle(
        proto_ref, keep, core_rows, x_rows, b_second, thirds, b_third
    )
    student_emb = jnp.concatenate([rounded] + [swap(rounded, "proto", flip) for flip in range(1, proto_size)])
    empty = jnp.concatenate(
        [jnp.zeros((group_rows, width + 128), jnp.float32), jnp.full((group_rows, 128), -1e30, jnp.float32)], axis=1
    )
    eighth = count // 8
    (state,) = attract(student_emb, empty, protos, 0, 5 * eighth, 5, 1)
    slots = attract(student_emb, state, protos, 5 * eighth, 3 * eighth, 3, proto_size)
    attract_parts = send_blocks(slots)

    copies, weights = first_sweep(thin_ref, protos, mine, other, all_tops, (x_sent, *thirds[2:]), devices, thin, protos_total)
    for _ in range(ITERS - 2):
        copies = next_sweep(weights, all_to_all(copies, BOTH), (rounded,), protos_total)
    scale_copies = last_scales(weights, all_to_all(copies, BOTH), (state,), batch_size, protos_total)
    all_scale = all_to_all(scale_copies, "batch")
    repels = repel(wide_ref, own_unit, all_tops, all_scale, protos, (slots[0],), proto_size)
    return finish(unit, lengths, attract_parts, send_blocks(repels))


def solution(mesh):
    in_specs = (
        P(("batch", "proto"), None),
        P("batch", None),
        P(None, "proto"),
        P(),
        P("proto", None),
        P(),
        P("proto", None),
        P(),
        P("proto", None),
    )
    out_specs = P(("batch", "proto"), None)
    return jax.shard_map(body, mesh=mesh, in_specs=in_specs, out_specs=out_specs, check_vma=False)
```

```python
import functools
import math

import jax
import jax.numpy as jnp
from jax import lax
from jax.experimental import pallas as pl
from jax.experimental.pallas import tpu as pltpu
from jax.sharding import PartitionSpec as P

ITERS = 3

student_temp = 0.1
teacher_temp = 0.07
norm_eps = 1e-06
teacher_rate = math.log2(math.e) / teacher_temp
student_rate = math.log2(math.e) / student_temp

MIB = 1024 * 1024
BOTH = ("batch", "proto")
TILE = 256
WIDE = 512


def scores(left_rows, right_rows):
    return lax.dot_general(
        left_rows, right_rows, (((1,), (1,)), ((), ())), preferred_element_type=jnp.float32
    )


def unit_rows(values):
    lengths = jnp.sqrt(jnp.sum(values * values, axis=1, keepdims=True) + norm_eps)
    return (values / lengths, lengths)


def gelu(values):
    return 0.5 * values * (1.0 + lax.erf(values * math.sqrt(0.5)))


def whole(memory_space=pltpu.VMEM):
    return pl.BlockSpec(memory_space=memory_space)


def in_hbm(array):
    return pltpu.with_memory_space_constraint(array, pltpu.HBM)


def skipping(kernel, first, count):
    def trimmed(*refs):
        kernel(*refs[:first], *refs[first + count :])

    return trimmed


def part(index, size):
    return pl.ds(pl.multiple_of(index * size, size), size)


def lane_fold(values, combine):
    folded = values[:, :128]
    for start in range(128, values.shape[1], 128):
        folded = combine(folded, values[:, start : start + 128])
    return folded


def params(mib):
    return pltpu.CompilerParams(vmem_limit_bytes=mib * MIB)


def cost(flops, bytes_accessed, transcendentals=0):
    return pl.CostEstimate(
        flops=int(flops), bytes_accessed=int(bytes_accessed), transcendentals=int(transcendentals)
    )


def fetch(source, target, sems, first_row=0):
    count, rows = target.shape[:2]

    def chunk_copy(index):
        start = pl.multiple_of(first_row + index * rows, rows)
        return pltpu.make_async_copy(source.at[pl.ds(start, rows), :], target.at[index], sems.at[index])

    for index in range(count):
        chunk_copy(index).start()
    return lambda index: chunk_copy(index).wait()


def teacher_units_kernel(core_ref, emb_ref, unit_ref, half_ref):
    unit_ref[...] = unit_rows(emb_ref[...].astype(jnp.float32))[0].astype(jnp.bfloat16)
    half = half_ref.shape[0]
    half_ref[...] = unit_ref[part(core_ref[0], half), :]


def teacher_units(core, teacher_emb):
    rows, width = teacher_emb.shape
    return pl.pallas_call(
        teacher_units_kernel,
        in_specs=[whole(pltpu.SMEM), whole()],
        out_specs=[whole(), whole()],
        out_shape=[
            jax.ShapeDtypeStruct((rows, width), jnp.bfloat16),
            jax.ShapeDtypeStruct((rows // 2, width), jnp.bfloat16),
        ],
        compiler_params=params(4),
        cost_estimate=cost(4 * rows * width, 8 * rows * width),
        name="teacher_units",
    )(core, in_hbm(teacher_emb))


def front_kernel(
    index_ref, unit_ref, bias_ref, own_hbm, x_hbm, core_hbm, last_hbm, first_hbm, second_hbm, protos_hbm,
    tops_ref, keep_ref, give_ref, first_ref, second_ref, rows_ref, protos_ref, padded_ref, top_ref, sems, chunk_sems,
):
    rows = unit_ref.shape[0]
    steps, block = protos_ref.shape[:2]
    wide = min(2 * WIDE, block)
    share = own_hbm.shape[0]
    arrived = fetch(protos_hbm, protos_ref, chunk_sems)
    copies = [
        pltpu.make_async_copy(source, rows_ref.at[slot * share : (slot + 1) * share, :], sems.at[slot])
        for slot, source in enumerate((own_hbm, x_hbm, core_hbm, last_hbm))
    ]
    copies.append(pltpu.make_async_copy(first_hbm, first_ref, sems.at[4]))
    copies.append(pltpu.make_async_copy(second_hbm, second_ref, sems.at[5]))
    for copy in copies:
        copy.start()
    padded_ref[...] = jnp.zeros(padded_ref.shape, jnp.bfloat16)
    padded_ref[:rows, :] = unit_ref[...]
    top_ref[...] = jnp.full(top_ref.shape, -jnp.inf, jnp.float32)

    def step(index, carry):
        arrived(index)
        top = top_ref[...]
        for start in range(0, block, wide):
            products = scores(protos_ref[index, start : start + wide, :], padded_ref[...])
            top = jnp.maximum(top, jnp.max(products.reshape(-1, 8, products.shape[1]), axis=0))
        top_ref[...] = top
        return carry

    lax.fori_loop(0, steps, step, 0)
    tops = jnp.max(top_ref[...], axis=0, keepdims=True)
    tops_ref[...] = jnp.broadcast_to(tops[None], tops_ref.shape)
    for copy in copies:
        copy.wait()
    hidden = first_ref.shape[1]
    bias = bias_ref[:, part(index_ref[0], hidden)]
    h_first = gelu(
        jnp.dot(rows_ref[...], first_ref[...], preferred_element_type=jnp.float32) + bias
    ).astype(jnp.bfloat16)
    for start in range(0, second_ref.shape[1], 512):
        columns = slice(start, start + 512)
        product = jnp.dot(h_first, second_ref[:, columns], preferred_element_type=jnp.float32)
        keep_ref[:, columns] = product[: 2 * share]
        give_ref[:, columns] = product[2 * share :]


def front(index, unit, bias, rows, first, second, protos, order, copies, steps):
    share, features = rows[0].shape
    hidden, units = second.shape
    count, width = protos.shape
    return pl.pallas_call(
        skipping(front_kernel, 10, len(order)),
        in_specs=[whole(pltpu.SMEM), whole(), whole()] + [whole(pl.ANY)] * (7 + len(order)),
        out_specs=[whole()] * 3,
        out_shape=[jax.ShapeDtypeStruct((copies, 1, 256), jnp.float32)]
        + [jax.ShapeDtypeStruct((2 * share, units), jnp.float32)] * 2,
        scratch_shapes=[
            pltpu.VMEM(first.shape, jnp.bfloat16),
            pltpu.VMEM(second.shape, jnp.bfloat16),
            pltpu.VMEM((4 * share, features), jnp.bfloat16),
            pltpu.VMEM((steps, count // steps, width), jnp.bfloat16),
            pltpu.VMEM((256, width), jnp.bfloat16),
            pltpu.VMEM((8, 256), jnp.float32),
            pltpu.SemaphoreType.DMA((6,)),
            pltpu.SemaphoreType.DMA((steps,)),
        ],
        compiler_params=params(26),
        cost_estimate=cost(
            2 * unit.size * count + 8 * share * hidden * (features + units), 2 * width * count
        ),
        name="front",
    )(
        index, unit, in_hbm(bias.reshape(1, -1)), in_hbm(rows[0]), *rows[1:],
        in_hbm(first), in_hbm(second), in_hbm(protos), *order,
    )


def repel_kernel(group, index_ref, unit_ref, tops_ref, scale_ref, protos_hbm, *rest):
    out_refs, (protos_ref, sems, acc_ref, sum_ref, bias_ref) = rest[:-5], rest[-5:]
    rows, width = unit_ref.shape
    steps, block = protos_ref.shape[:2]
    wide = min(WIDE, block)
    arrived = fetch(protos_hbm, protos_ref, sems)
    first = index_ref[0] * group
    top = tops_ref[first]
    for other in range(1, group):
        top = jnp.maximum(top, tops_ref[first + other])
    bias_ref[...] = jnp.transpose(jnp.broadcast_to(top, (128, 256)))[:rows, :] * -teacher_rate
    acc_ref[...] = jnp.zeros(acc_ref.shape, jnp.float32)
    sum_ref[...] = jnp.zeros(sum_ref.shape, jnp.float32)

    def step(index, carry):
        arrived(index)
        bias = bias_ref[...]
        total = sum_ref[...]
        acc = acc_ref[...]
        for start in range(0, block, wide):
            protos = protos_ref[index, start : start + wide, :]
            products = scores(unit_ref[...], protos)
            pieces = []
            for lane in range(0, wide, 128):
                scaled = jnp.exp2(products[:, lane : lane + 128] * teacher_rate + bias)
                scaled = scaled * scale_ref[index, :, start + lane : start + lane + 128]
                total = total + scaled
                pieces.append(scaled.astype(jnp.bfloat16))
            acc = acc + jnp.dot(
                jnp.concatenate(pieces, axis=1), protos, preferred_element_type=jnp.float32
            )
        sum_ref[...] = total
        acc_ref[...] = acc
        return carry

    lax.fori_loop(0, steps, step, 0)
    total = jnp.sum(sum_ref[...], axis=1, keepdims=True)
    lanes = lax.broadcasted_iota(jnp.int32, sum_ref.shape, 1)
    sum_ref[...] = jnp.broadcast_to(total, sum_ref.shape)
    share = out_refs[0].shape[0]
    lanes = lanes[:share, :]
    for flip, out_ref in enumerate(out_refs):
        span = part(index_ref[1] ^ flip, share)
        total = sum_ref[span, :]
        out_ref[:, :width] = acc_ref[span, :].astype(out_ref.dtype)
        if flip == 0:
            out_ref[:, width:] = jnp.where(lanes == 0, total, 0.0)
        else:
            high = total.astype(jnp.bfloat16).astype(jnp.float32)
            middle = (total - high).astype(jnp.bfloat16).astype(jnp.float32)
            pieces = jnp.where(lanes == 0, high, jnp.where(lanes == 1, middle, total - high - middle))
            out_ref[:, width:] = jnp.where(lanes < 3, pieces, 0.0).astype(jnp.bfloat16)


def repel(index, unit, tops, scale, protos, order, proto_size):
    rows, width = unit.shape
    count = protos.shape[0]
    steps, _, block = scale.shape
    return pl.pallas_call(
        skipping(functools.partial(repel_kernel, proto_size), 5, len(order)),
        in_specs=[whole(pltpu.SMEM), whole(), whole(), whole(), whole(pl.ANY)] + [whole(pl.ANY)] * len(order),
        out_specs=[whole()] * proto_size,
        out_shape=[
            jax.ShapeDtypeStruct((rows // proto_size, width + 128), jnp.bfloat16 if flip else jnp.float32)
            for flip in range(proto_size)
        ],
        scratch_shapes=[
            pltpu.VMEM((steps, block, width), jnp.bfloat16),
            pltpu.SemaphoreType.DMA((steps,)),
            pltpu.VMEM((rows, width), jnp.float32),
            pltpu.VMEM((rows, 128), jnp.float32),
            pltpu.VMEM((rows, 128), jnp.float32),
        ],
        compiler_params=params(16),
        cost_estimate=cost(4 * rows * width * count, 2 * width * count, rows * count),
        name="repel",
    )(index, unit, tops, scale, in_hbm(protos), *order)


def attract_kernel(first_row, last, emb_ref, state_ref, protos_hbm, *rest):
    out_refs, scratch = rest[:-6], rest[-6:]
    protos_ref, sems, products_ref, acc_ref, sum_ref, top_ref = scratch
    width = emb_ref.shape[1]
    steps, block = protos_ref.shape[:2]
    arrived = fetch(protos_hbm, protos_ref, sems, first_row)
    old_top = state_ref[:, width + 128 :]
    top_ref[...] = old_top

    def first(index, carry):
        arrived(index)
        top = top_ref[...]
        for start in range(0, block, TILE):
            products = scores(emb_ref[...], protos_ref[index, start : start + TILE, :])
            products_ref[index, :, start : start + TILE] = products
            top = jnp.maximum(top, lane_fold(products, jnp.maximum))
        top_ref[...] = top
        return carry

    lax.fori_loop(0, steps, first, 0)
    top = jnp.broadcast_to(jnp.max(top_ref[...], axis=1, keepdims=True), top_ref.shape)
    fade = jnp.exp2((old_top - top) * student_rate)
    top_ref[...] = top
    sum_ref[...] = state_ref[:, width : width + 128] * fade
    acc_ref[...] = state_ref[:, :width] * jnp.tile(fade, (1, width // 128))

    def second(index, carry):
        top = top_ref[...]
        total = sum_ref[...]
        acc = acc_ref[...]
        for start in range(0, block, TILE):
            pieces = []
            for lane in range(start, start + TILE, 128):
                shifted = jnp.exp2((products_ref[index, :, lane : lane + 128] - top) * student_rate)
                total = total + shifted
                pieces.append(shifted.astype(jnp.bfloat16))
            acc = acc + jnp.dot(
                jnp.concatenate(pieces, axis=1),
                protos_ref[index, start : start + TILE, :],
                preferred_element_type=jnp.float32,
            )
        sum_ref[...] = total
        acc_ref[...] = acc
        return carry

    lax.fori_loop(0, steps, second, 0)
    if last:
        total = jnp.sum(sum_ref[...], axis=1, keepdims=True)
        sum_ref[...] = jnp.broadcast_to(total, sum_ref.shape)
    share = out_refs[0].shape[0]
    for slot, out_ref in enumerate(out_refs):
        rows = pl.ds(slot * share, share)
        out_ref[:, :width] = acc_ref[rows, :]
        out_ref[:, width : width + 128] = sum_ref[rows, :]
        out_ref[:, width + 128 :] = top_ref[rows, :]


def attract(emb, state, protos, first_row, count, steps, outputs):
    rows, width = emb.shape
    block = count // steps
    return pl.pallas_call(
        functools.partial(attract_kernel, first_row, outputs > 1),
        in_specs=[whole(), whole(), whole(pl.ANY)],
        out_specs=[whole()] * outputs,
        out_shape=[jax.ShapeDtypeStruct((rows // outputs, width + 256), jnp.float32)] * outputs,
        scratch_shapes=[
            pltpu.VMEM((steps, block, width), jnp.bfloat16),
            pltpu.SemaphoreType.DMA((steps,)),
            pltpu.VMEM((steps, rows, block), jnp.float32),
            pltpu.VMEM((rows, width), jnp.float32),
            pltpu.VMEM((rows, 128), jnp.float32),
            pltpu.VMEM((rows, 128), jnp.float32),
        ],
        compiler_params=params(24),
        cost_estimate=cost(4 * rows * width * count, 2 * width * count, rows * count),
        name="attract",
    )(emb, state, in_hbm(protos))


def three_pieces(values):
    high = values.astype(jnp.bfloat16)
    rest = values - high.astype(jnp.float32)
    middle = rest.astype(jnp.bfloat16)
    low = (rest - middle.astype(jnp.float32)).astype(jnp.bfloat16)
    return jnp.concatenate([high, middle, low, jnp.zeros((13, values.shape[1]), jnp.bfloat16)], axis=0)


def lane_scales(folded, protos_total):
    sums = [
        jnp.sum(jnp.transpose(folded[start : start + 128, :]), axis=0, keepdims=True)
        for start in range(0, folded.shape[0], 128)
    ]
    return 1.0 / (protos_total * jnp.concatenate(sums, axis=1))


def give_sums(copies_ref, totals):
    rows = [totals[:, start : start + 128] for start in range(0, totals.shape[1], 128)]
    spare = copies_ref.shape[1] - len(rows)
    if spare:
        rows.append(jnp.zeros((spare, 128), jnp.float32))
    packed = jnp.concatenate(rows, axis=0).astype(jnp.bfloat16)
    copies_ref[...] = jnp.broadcast_to(packed[None], copies_ref.shape)


def take_scales(parts_ref, scale_ref):
    crops_total = scale_ref.shape[1]
    sums = jnp.sum(parts_ref[...].astype(jnp.float32), axis=0)
    for row in range(crops_total // 128):
        scale_ref[:, row * 128 : row * 128 + 128] = 1.0 / (crops_total * sums[row : row + 1, :])


def sums_shape(copies, crops_total):
    return (copies, -(-crops_total // 2048) * 16, 128)


def lane_order(tops_ref, group, crops_total):
    batches = tops_ref.shape[0] // group
    rows = crops_total // batches
    bits = batches.bit_length() - 1
    tops = []
    for batch in range(batches):
        source = int(format(batch, "b").zfill(bits)[::-1], 2) if bits else 0
        tops.append(
            functools.reduce(jnp.maximum, [tops_ref[source * group + other] for other in range(group)])
        )
    halves = [top[:, core * rows // 2 : (core + 1) * rows // 2] for core in range(2) for top in tops]
    return jnp.concatenate(halves, axis=1)


def first_sweep_kernel(
    chunk, protos_total, group, index_ref, protos_hbm, mine_hbm, other_hbm, tops_ref, copies_ref, weights_hbm,
    protos_ref, units_ref, weights_ref, rounded_ref, scale_ref, bias_ref, sems, out_sems,
):
    thin, crops_total = weights_ref.shape
    half = mine_hbm.shape[0]
    core = index_ref[1]
    copies = (
        pltpu.make_async_copy(protos_hbm.at[part(index_ref[0], thin), :], protos_ref, sems.at[0]),
        pltpu.make_async_copy(mine_hbm, units_ref.at[part(core, half), :], sems.at[1]),
        pltpu.make_async_copy(other_hbm, units_ref.at[part(1 - core, half), :], sems.at[2]),
    )
    for copy in copies:
        copy.start()
    bias_ref[...] = lane_order(tops_ref, group, crops_total) * -teacher_rate
    for copy in copies:
        copy.wait()

    def chunk_out(index):
        return pltpu.make_async_copy(
            rounded_ref.at[index], weights_hbm.at[part(index, chunk), :], out_sems.at[index]
        )

    def weigh(index, carry):
        rows = part(index, chunk)
        protos = protos_ref[rows, :]
        folded = jnp.zeros((chunk, 128), jnp.float32)
        for start in range(0, crops_total, TILE):
            columns = slice(start, start + TILE)
            products = scores(protos, units_ref[columns, :])
            weights = jnp.exp2(products * teacher_rate + bias_ref[:, columns])
            weights_ref[rows, columns] = weights
            rounded_ref[index, :, columns] = weights.astype(jnp.bfloat16)
            folded = folded + lane_fold(weights, jnp.add)
        sums = jnp.sum(folded, axis=1, keepdims=True)
        scale_ref[rows, :] = jnp.broadcast_to(1.0 / (protos_total * sums), (chunk, 128))
        chunk_out(index).start()
        return carry

    lax.fori_loop(0, thin // chunk, weigh, 0)
    small = min(thin, 64)

    def add_up(index, totals):
        rows = part(index, small)
        scaled = weights_ref[rows, :] * jnp.tile(scale_ref[rows, :], (1, crops_total // 128))
        return totals + jnp.sum(scaled.reshape(-1, 8, crops_total), axis=0)

    totals = lax.fori_loop(0, thin // small, add_up, jnp.zeros((8, crops_total), jnp.float32))
    give_sums(copies_ref, jnp.sum(totals, axis=0, keepdims=True))
    for index in range(thin // chunk):
        chunk_out(index).wait()


def first_sweep(index, protos, mine, other, tops, order, copies, thin, protos_total):
    width = protos.shape[1]
    crops_total = 2 * mine.shape[0]
    chunk = min(thin, 1024)
    return pl.pallas_call(
        skipping(functools.partial(first_sweep_kernel, chunk, protos_total, protos_total // protos.shape[0]), 5, len(order)),
        in_specs=[whole(pltpu.SMEM), whole(pl.ANY), whole(pl.ANY), whole(pl.ANY), whole()]
        + [whole(pl.ANY)] * len(order),
        out_specs=[whole(), whole(pl.ANY)],
        out_shape=[
            jax.ShapeDtypeStruct(sums_shape(copies, crops_total), jnp.bfloat16),
            pltpu.HBM((thin, crops_total), jnp.bfloat16),
        ],
        scratch_shapes=[
            pltpu.VMEM((thin, width), jnp.bfloat16),
            pltpu.VMEM((crops_total, width), jnp.bfloat16),
            pltpu.VMEM((thin, crops_total), jnp.float32),
            pltpu.VMEM((thin // chunk, chunk, crops_total), jnp.bfloat16),
            pltpu.VMEM((thin, 128), jnp.float32),
            pltpu.VMEM((1, crops_total), jnp.float32),
            pltpu.SemaphoreType.DMA((3,)),
            pltpu.SemaphoreType.DMA((thin // chunk,)),
        ],
        compiler_params=params(32 if crops_total <= 2048 else 56),
        cost_estimate=cost(2 * thin * width * crops_total, 2 * thin * crops_total, thin * crops_total),
        name="first_sweep",
    )(index, in_hbm(protos), mine, other, tops, *order)


def fetch_rows(weights_hbm, weights_ref, sems):
    steps, chunk, _ = weights_ref.shape

    def rows_copy(index):
        return pltpu.make_async_copy(
            weights_hbm.at[part(index, chunk), :], weights_ref.at[index], sems.at[index]
        )

    for index in range(steps):
        rows_copy(index).start()
    return lambda index: rows_copy(index).wait()


def scaled_fold(weights_ref, index, scale_ref):
    _, chunk, crops_total = weights_ref.shape
    folds = []
    for row in range(0, chunk, 64):
        fold = None
        for start in range(0, crops_total, TILE):
            columns = slice(start, start + TILE)
            weights = weights_ref[index, row : row + 64, columns].astype(jnp.float32)
            scaled = lane_fold(weights * scale_ref[:, columns], jnp.add)
            fold = scaled if fold is None else fold + scaled
        folds.append(fold)
    return jnp.concatenate(folds, axis=0)


def next_sweep_kernel(
    protos_total, weights_hbm, parts_ref, copies_ref, weights_ref, scale_ref, pieces_ref, totals_ref, sems,
):
    steps, chunk, crops_total = weights_ref.shape
    arrived = fetch_rows(weights_hbm, weights_ref, sems)
    take_scales(parts_ref, scale_ref)
    totals_ref[...] = jnp.zeros(totals_ref.shape, jnp.float32)

    def weigh(index):
        return three_pieces(lane_scales(scaled_fold(weights_ref, index, scale_ref), protos_total))

    def add_up(index):
        return jnp.dot(pieces_ref[...], weights_ref[index], preferred_element_type=jnp.float32)

    arrived(0)
    pieces_ref[...] = weigh(0)

    def sweep(index, carry):
        arrived(index)
        sums = add_up(index - 1)
        pieces = weigh(index)
        totals_ref[...] += sums
        pieces_ref[...] = pieces
        return carry

    lax.fori_loop(1, steps, sweep, 0)
    totals = totals_ref[...] + add_up(steps - 1)
    give_sums(copies_ref, jnp.sum(totals, axis=0, keepdims=True))


def next_sweep(weights, parts, order, protos_total):
    thin, crops_total = weights.shape
    copies = parts.shape[0]
    chunk = min(thin, 256)
    return pl.pallas_call(
        skipping(functools.partial(next_sweep_kernel, protos_total), 2, len(order)),
        in_specs=[whole(pl.ANY), whole()] + [whole(pl.ANY)] * len(order),
        out_specs=whole(),
        out_shape=jax.ShapeDtypeStruct(sums_shape(copies, crops_total), jnp.bfloat16),
        scratch_shapes=[
            pltpu.VMEM((thin // chunk, chunk, crops_total), jnp.bfloat16),
            pltpu.VMEM((1, crops_total), jnp.float32),
            pltpu.VMEM((16, chunk), jnp.bfloat16),
            pltpu.VMEM((16, crops_total), jnp.float32),
            pltpu.SemaphoreType.DMA((thin // chunk,)),
        ],
        compiler_params=params(16 if crops_total <= 2048 else 50),
        cost_estimate=cost(8 * thin * crops_total, 2 * thin * crops_total),
        name="next_sweep",
    )(in_hbm(weights), parts, *order)


def last_scales_kernel(
    protos_total, weights_hbm, parts_ref, copies_ref, weights_ref, scale_ref, out_ref, sems,
):
    steps, chunk, crops_total = weights_ref.shape
    arrived = fetch_rows(weights_hbm, weights_ref, sems)
    take_scales(parts_ref, scale_ref)

    def weigh(index, carry):
        arrived(index)
        out_ref[:, part(index, chunk)] = lane_scales(
            scaled_fold(weights_ref, index, scale_ref), protos_total
        )
        return carry

    lax.fori_loop(0, steps, weigh, 0)
    copies_ref[...] = jnp.broadcast_to(out_ref[...][None], copies_ref.shape)


def last_scales(weights, parts, order, copies, protos_total):
    thin, crops_total = weights.shape
    chunk = min(thin, 256)
    return pl.pallas_call(
        skipping(functools.partial(last_scales_kernel, protos_total), 2, len(order)),
        in_specs=[whole(pl.ANY), whole()] + [whole(pl.ANY)] * len(order),
        out_specs=whole(),
        out_shape=jax.ShapeDtypeStruct((copies, 1, thin), jnp.float32),
        scratch_shapes=[
            pltpu.VMEM((thin // chunk, chunk, crops_total), jnp.bfloat16),
            pltpu.VMEM((1, crops_total), jnp.float32),
            pltpu.VMEM((1, thin), jnp.float32),
            pltpu.SemaphoreType.DMA((thin // chunk,)),
        ],
        compiler_params=params(16 if crops_total <= 2048 else 50),
        cost_estimate=cost(4 * thin * crops_total, 2 * thin * crops_total),
        name="last_scales",
    )(in_hbm(weights), parts, *order)


def student_middle_kernel(
    index_ref, keep_ref, core_ref, x_ref, bias_ref, own_ref, partner_ref, other_ref, last_ref, last_bias_ref,
    unit_ref, emb_ref, lengths_ref, hidden_ref,
):
    share = x_ref.shape[0]
    block = own_ref.shape[0]
    sums = keep_ref[:share, :] + core_ref[:share, :] + x_ref[...]
    hidden_ref[...] = gelu(sums + bias_ref[...]).astype(jnp.bfloat16)
    index = index_ref[0]
    weights = ((0, own_ref[...]), (2, partner_ref[...]), (1, other_ref[...]), (3, last_ref[...]))
    bottleneck = jnp.broadcast_to(last_bias_ref[...], unit_ref.shape)
    for flip, weight in weights:
        bottleneck = bottleneck + jnp.dot(
            hidden_ref[:, part(index ^ flip, block)], weight, preferred_element_type=jnp.float32
        )
    unit, lengths = unit_rows(bottleneck)
    unit_ref[...] = unit
    emb_ref[...] = unit.astype(jnp.bfloat16)
    lengths_ref[...] = jnp.broadcast_to(lengths, lengths_ref.shape)


def student_middle(index, keep, core_rows, x_rows, bias, weights, last_bias):
    share, units = x_rows.shape
    width = weights[0].shape[1]
    return pl.pallas_call(
        student_middle_kernel,
        in_specs=[whole(pltpu.SMEM)] + [whole()] * 9,
        out_specs=[whole()] * 3,
        out_shape=[
            jax.ShapeDtypeStruct((share, width), jnp.float32),
            jax.ShapeDtypeStruct((share, width), jnp.bfloat16),
            jax.ShapeDtypeStruct((share, 128), jnp.float32),
        ],
        scratch_shapes=[pltpu.VMEM((share, units), jnp.bfloat16)],
        compiler_params=params(12),
        cost_estimate=cost(2 * share * units * width, 2 * units * width + 16 * share * units),
        name="student_middle",
    )(index, keep, core_rows, x_rows, in_hbm(bias.reshape(1, -1)), in_hbm(weights[0]), *weights[1:], in_hbm(last_bias.reshape(1, -1)))


def finish_kernel(unit_ref, lengths_ref, *rest):
    out_ref, blocks = rest[-1], rest[:-1]
    attracts, repels = blocks[: len(blocks) // 2], blocks[len(blocks) // 2 :]
    width = unit_ref.shape[1]
    row_top = functools.reduce(jnp.maximum, [ref[:, width + 128 :] for ref in attracts])
    attract_sum = repel_sum = 0.0
    row_sum = column_sum = 0.0
    for ref in attracts:
        fade = jnp.exp2((ref[:, width + 128 :] - row_top) * student_rate)
        row_sum = row_sum + ref[:, width : width + 128] * fade
        attract_sum = attract_sum + ref[:, :width] * jnp.tile(fade, (1, width // 128))
    for ref in repels:
        column_sum = column_sum + jnp.sum(ref[:, width:].astype(jnp.float32), axis=1, keepdims=True)
        repel_sum = repel_sum + ref[:, :width].astype(jnp.float32)
    emb_grad = (
        attract_sum / jnp.tile(row_sum, (1, width // 128))
        - repel_sum / column_sum
    ) / student_temp
    unit = unit_ref[...]
    along = jnp.sum(unit * emb_grad, axis=1, keepdims=True)
    out_ref[...] = (emb_grad - unit * along) / jnp.tile(lengths_ref[...], (1, width // 128))


def finish(unit, lengths, attracts, repels):
    return pl.pallas_call(
        finish_kernel,
        in_specs=[whole()] * (2 + len(attracts) + len(repels)),
        out_specs=whole(),
        out_shape=jax.ShapeDtypeStruct(unit.shape, jnp.float32),
        compiler_params=params(8),
        cost_estimate=cost(40 * unit.size, 40 * unit.size),
        name="finish",
    )(unit, lengths, *attracts, *repels)


def swap(values, axis, flip):
    return lax.ppermute(values, axis, [(i, i ^ flip) for i in range(lax.axis_size(axis))])


def bit_reversed(values, count):
    bits = count.bit_length() - 1
    split = values.reshape((2,) * bits + values.shape[1:])
    turned = jnp.transpose(split, tuple(reversed(range(bits))) + tuple(range(bits, split.ndim)))
    return turned.reshape(values.shape)


def gather_batch(values):
    step = lax.axis_size("batch") // 2
    stages = [values]
    while step:
        other = swap(values, "batch", step)
        upper = (lax.axis_index("batch") // step) % 2
        values = jnp.where(
            upper == 0, jnp.concatenate([values, other]), jnp.concatenate([other, values])
        )
        stages.append(values)
        step //= 2
    return stages


def send_blocks(blocks):
    flips = list(range(len(blocks) - 1, 0, -1))
    return [blocks[0]] + [swap(blocks[flip], "proto", flip) for flip in flips]


def all_to_all(copies, axes):
    return lax.all_to_all(copies, axes, 0, 0, tiled=True)


def body(crops, teacher_emb, w_first, b_first, w_second, b_second, w_third, b_third, protos):
    batch_index = lax.axis_index("batch")
    proto_index = lax.axis_index("proto")
    batch_size = lax.axis_size("batch")
    proto_size = lax.axis_size("proto")
    devices = batch_size * proto_size
    share_rows = crops.shape[0]
    group_rows = teacher_emb.shape[0]
    crops_total = group_rows * batch_size
    protos_total = protos.shape[0] * proto_size
    count, width = protos.shape
    thin = count // batch_size
    core = proto_index % 2
    proto_ref = proto_index.reshape(1)
    thin_ref = jnp.stack([batch_index, core])
    wide_ref = jnp.stack([batch_index, proto_index])

    own_unit, half = teacher_units(core.reshape(1), teacher_emb)
    stages = gather_batch(half)
    mine = stages[-1]
    other = swap(mine, "proto", 1)

    crops_x = swap(crops, "proto", 2)
    rows = [crops, crops_x, swap(crops, "proto", 1), swap(crops_x, "proto", 1)]
    third_x = swap(w_third, "proto", 2)
    thirds = [w_third, third_x, swap(w_third, "proto", 1), swap(third_x, "proto", 1)]
    top_copies, keep, give = front(
        proto_ref, own_unit, b_first, rows, w_first, w_second, protos, (stages[2], third_x), devices, 8
    )
    all_tops = all_to_all(top_copies, BOTH)
    core_rows = swap(give, "proto", 1)
    x_sent = keep[share_rows:] + core_rows[share_rows:]
    x_rows = swap(x_sent, "proto", 2)
    unit, rounded, lengths = student_middle(
        proto_ref, keep, core_rows, x_rows, b_second, thirds, b_third
    )
    student_emb = jnp.concatenate([rounded] + [swap(rounded, "proto", flip) for flip in range(1, proto_size)])
    empty = jnp.concatenate(
        [jnp.zeros((group_rows, width + 128), jnp.float32), jnp.full((group_rows, 128), -1e30, jnp.float32)], axis=1
    )
    eighth = count // 8
    (state,) = attract(student_emb, empty, protos, 0, 6 * eighth, 6, 1)
    slots = attract(student_emb, state, protos, 6 * eighth, 2 * eighth, 2, proto_size)
    attract_parts = send_blocks(slots)

    copies, weights = first_sweep(thin_ref, protos, mine, other, all_tops, (x_sent, *thirds[2:]), devices, thin, protos_total)
    for _ in range(ITERS - 2):
        copies = next_sweep(weights, all_to_all(copies, BOTH), (rounded,), protos_total)
    scale_copies = last_scales(weights, all_to_all(copies, BOTH), (state,), batch_size, protos_total)
    all_scale = all_to_all(scale_copies, "batch")
    repels = repel(wide_ref, own_unit, all_tops, all_scale, protos, (slots[0],), proto_size)
    return finish(unit, lengths, attract_parts, send_blocks(repels))


def solution(mesh):
    in_specs = (
        P(("batch", "proto"), None),
        P("batch", None),
        P(None, "proto"),
        P(),
        P("proto", None),
        P(),
        P("proto", None),
        P(),
        P("proto", None),
    )
    out_specs = P(("batch", "proto"), None)
    return jax.shard_map(body, mesh=mesh, in_specs=in_specs, out_specs=out_specs, check_vma=False)
```

```python
import functools
import math

import jax
import jax.numpy as jnp
from jax import lax
from jax.experimental import pallas as pl
from jax.experimental.pallas import tpu as pltpu
from jax.sharding import PartitionSpec as P

ITERS = 3

student_temp = 0.1
teacher_temp = 0.07
norm_eps = 1e-06
teacher_rate = math.log2(math.e) / teacher_temp
student_rate = math.log2(math.e) / student_temp

MIB = 1024 * 1024
BOTH = ("batch", "proto")
TILE = 256
WIDE = 512


def scores(left_rows, right_rows):
    return lax.dot_general(
        left_rows, right_rows, (((1,), (1,)), ((), ())), preferred_element_type=jnp.float32
    )


def unit_rows(values):
    lengths = jnp.sqrt(jnp.sum(values * values, axis=1, keepdims=True) + norm_eps)
    return (values / lengths, lengths)


def gelu(values):
    return 0.5 * values * (1.0 + lax.erf(values * math.sqrt(0.5)))


def whole(memory_space=pltpu.VMEM):
    return pl.BlockSpec(memory_space=memory_space)


def in_hbm(array):
    return pltpu.with_memory_space_constraint(array, pltpu.HBM)


def skipping(kernel, first, count):
    def trimmed(*refs):
        kernel(*refs[:first], *refs[first + count :])

    return trimmed


def part(index, size):
    return pl.ds(pl.multiple_of(index * size, size), size)


def lane_fold(values, combine):
    folded = values[:, :128]
    for start in range(128, values.shape[1], 128):
        folded = combine(folded, values[:, start : start + 128])
    return folded


def params(mib):
    return pltpu.CompilerParams(vmem_limit_bytes=mib * MIB)


def cost(flops, bytes_accessed, transcendentals=0):
    return pl.CostEstimate(
        flops=int(flops), bytes_accessed=int(bytes_accessed), transcendentals=int(transcendentals)
    )


def fetch(source, target, sems, first_row=0):
    count, rows = target.shape[:2]

    def chunk_copy(index):
        start = pl.multiple_of(first_row + index * rows, rows)
        return pltpu.make_async_copy(source.at[pl.ds(start, rows), :], target.at[index], sems.at[index])

    for index in range(count):
        chunk_copy(index).start()
    return lambda index: chunk_copy(index).wait()


def teacher_units_kernel(core_ref, emb_ref, unit_ref, half_ref):
    unit_ref[...] = unit_rows(emb_ref[...].astype(jnp.float32))[0].astype(jnp.bfloat16)
    half = half_ref.shape[0]
    half_ref[...] = unit_ref[part(core_ref[0], half), :]


def teacher_units(core, teacher_emb):
    rows, width = teacher_emb.shape
    return pl.pallas_call(
        teacher_units_kernel,
        in_specs=[whole(pltpu.SMEM), whole()],
        out_specs=[whole(), whole()],
        out_shape=[
            jax.ShapeDtypeStruct((rows, width), jnp.bfloat16),
            jax.ShapeDtypeStruct((rows // 2, width), jnp.bfloat16),
        ],
        compiler_params=params(4),
        cost_estimate=cost(4 * rows * width, 8 * rows * width),
        name="teacher_units",
    )(core, in_hbm(teacher_emb))


def front_kernel(
    index_ref, unit_ref, bias_ref, own_hbm, x_hbm, core_hbm, last_hbm, first_hbm, second_hbm, protos_hbm,
    tops_ref, keep_ref, give_ref, first_ref, second_ref, rows_ref, protos_ref, padded_ref, top_ref, sems, chunk_sems,
):
    rows = unit_ref.shape[0]
    steps, block = protos_ref.shape[:2]
    wide = min(2 * WIDE, block)
    share = own_hbm.shape[0]
    arrived = fetch(protos_hbm, protos_ref, chunk_sems)
    copies = [
        pltpu.make_async_copy(source, rows_ref.at[slot * share : (slot + 1) * share, :], sems.at[slot])
        for slot, source in enumerate((own_hbm, x_hbm, core_hbm, last_hbm))
    ]
    copies.append(pltpu.make_async_copy(first_hbm, first_ref, sems.at[4]))
    copies.append(pltpu.make_async_copy(second_hbm, second_ref, sems.at[5]))
    for copy in copies:
        copy.start()
    padded_ref[...] = jnp.zeros(padded_ref.shape, jnp.bfloat16)
    padded_ref[:rows, :] = unit_ref[...]
    top_ref[...] = jnp.full(top_ref.shape, -jnp.inf, jnp.float32)

    def step(index, carry):
        arrived(index)
        top = top_ref[...]
        for start in range(0, block, wide):
            products = scores(protos_ref[index, start : start + wide, :], padded_ref[...])
            top = jnp.maximum(top, jnp.max(products.reshape(-1, 8, products.shape[1]), axis=0))
        top_ref[...] = top
        return carry

    lax.fori_loop(0, steps, step, 0)
    tops = jnp.max(top_ref[...], axis=0, keepdims=True)
    tops_ref[...] = jnp.broadcast_to(tops[None], tops_ref.shape)
    for copy in copies:
        copy.wait()
    hidden = first_ref.shape[1]
    bias = bias_ref[:, part(index_ref[0], hidden)]
    h_first = gelu(
        jnp.dot(rows_ref[...], first_ref[...], preferred_element_type=jnp.float32) + bias
    ).astype(jnp.bfloat16)
    for start in range(0, second_ref.shape[1], 512):
        columns = slice(start, start + 512)
        product = jnp.dot(h_first, second_ref[:, columns], preferred_element_type=jnp.float32)
        keep_ref[:, columns] = product[: 2 * share]
        give_ref[:, columns] = product[2 * share :]


def front(index, unit, bias, rows, first, second, protos, order, copies, steps):
    share, features = rows[0].shape
    hidden, units = second.shape
    count, width = protos.shape
    return pl.pallas_call(
        skipping(front_kernel, 10, len(order)),
        in_specs=[whole(pltpu.SMEM), whole(), whole()] + [whole(pl.ANY)] * (7 + len(order)),
        out_specs=[whole()] * 3,
        out_shape=[jax.ShapeDtypeStruct((copies, 1, 256), jnp.float32)]
        + [jax.ShapeDtypeStruct((2 * share, units), jnp.float32)] * 2,
        scratch_shapes=[
            pltpu.VMEM(first.shape, jnp.bfloat16),
            pltpu.VMEM(second.shape, jnp.bfloat16),
            pltpu.VMEM((4 * share, features), jnp.bfloat16),
            pltpu.VMEM((steps, count // steps, width), jnp.bfloat16),
            pltpu.VMEM((256, width), jnp.bfloat16),
            pltpu.VMEM((8, 256), jnp.float32),
            pltpu.SemaphoreType.DMA((6,)),
            pltpu.SemaphoreType.DMA((steps,)),
        ],
        compiler_params=params(26),
        cost_estimate=cost(
            2 * unit.size * count + 8 * share * hidden * (features + units), 2 * width * count
        ),
        name="front",
    )(
        index, unit, in_hbm(bias.reshape(1, -1)), in_hbm(rows[0]), *rows[1:],
        in_hbm(first), in_hbm(second), in_hbm(protos), *order,
    )


def repel_kernel(group, index_ref, unit_ref, tops_ref, scale_ref, protos_hbm, *rest):
    out_refs, (protos_ref, sems, acc_ref, sum_ref, bias_ref) = rest[:-5], rest[-5:]
    rows, width = unit_ref.shape
    steps, block = protos_ref.shape[:2]
    wide = min(WIDE, block)
    arrived = fetch(protos_hbm, protos_ref, sems)
    first = index_ref[0] * group
    top = tops_ref[first]
    for other in range(1, group):
        top = jnp.maximum(top, tops_ref[first + other])
    bias_ref[...] = jnp.transpose(jnp.broadcast_to(top, (128, 256)))[:rows, :] * -teacher_rate
    acc_ref[...] = jnp.zeros(acc_ref.shape, jnp.float32)
    sum_ref[...] = jnp.zeros(sum_ref.shape, jnp.float32)

    def step(index, carry):
        arrived(index)
        bias = bias_ref[...]
        total = sum_ref[...]
        acc = acc_ref[...]
        for start in range(0, block, wide):
            protos = protos_ref[index, start : start + wide, :]
            products = scores(unit_ref[...], protos)
            pieces = []
            for lane in range(0, wide, 128):
                scaled = jnp.exp2(products[:, lane : lane + 128] * teacher_rate + bias)
                scaled = scaled * scale_ref[index, :, start + lane : start + lane + 128]
                total = total + scaled
                pieces.append(scaled.astype(jnp.bfloat16))
            acc = acc + jnp.dot(
                jnp.concatenate(pieces, axis=1), protos, preferred_element_type=jnp.float32
            )
        sum_ref[...] = total
        acc_ref[...] = acc
        return carry

    lax.fori_loop(0, steps, step, 0)
    total = jnp.sum(sum_ref[...], axis=1, keepdims=True)
    lanes = lax.broadcasted_iota(jnp.int32, sum_ref.shape, 1)
    sum_ref[...] = jnp.broadcast_to(total, sum_ref.shape)
    share = out_refs[0].shape[0]
    lanes = lanes[:share, :]
    for flip, out_ref in enumerate(out_refs):
        span = part(index_ref[1] ^ flip, share)
        total = sum_ref[span, :]
        out_ref[:, :width] = acc_ref[span, :].astype(out_ref.dtype)
        if flip == 0:
            out_ref[:, width:] = jnp.where(lanes == 0, total, 0.0)
        else:
            high = total.astype(jnp.bfloat16).astype(jnp.float32)
            middle = (total - high).astype(jnp.bfloat16).astype(jnp.float32)
            pieces = jnp.where(lanes == 0, high, jnp.where(lanes == 1, middle, total - high - middle))
            out_ref[:, width:] = jnp.where(lanes < 3, pieces, 0.0).astype(jnp.bfloat16)


def repel(index, unit, tops, scale, protos, order, proto_size):
    rows, width = unit.shape
    count = protos.shape[0]
    steps, _, block = scale.shape
    return pl.pallas_call(
        skipping(functools.partial(repel_kernel, proto_size), 5, len(order)),
        in_specs=[whole(pltpu.SMEM), whole(), whole(), whole(), whole(pl.ANY)] + [whole(pl.ANY)] * len(order),
        out_specs=[whole()] * proto_size,
        out_shape=[
            jax.ShapeDtypeStruct((rows // proto_size, width + 128), jnp.bfloat16 if flip else jnp.float32)
            for flip in range(proto_size)
        ],
        scratch_shapes=[
            pltpu.VMEM((steps, block, width), jnp.bfloat16),
            pltpu.SemaphoreType.DMA((steps,)),
            pltpu.VMEM((rows, width), jnp.float32),
            pltpu.VMEM((rows, 128), jnp.float32),
            pltpu.VMEM((rows, 128), jnp.float32),
        ],
        compiler_params=params(16),
        cost_estimate=cost(4 * rows * width * count, 2 * width * count, rows * count),
        name="repel",
    )(index, unit, tops, scale, in_hbm(protos), *order)


def attract_kernel(first_row, last, emb_ref, state_ref, protos_hbm, *rest):
    out_refs, scratch = rest[:-6], rest[-6:]
    protos_ref, sems, products_ref, acc_ref, sum_ref, top_ref = scratch
    width = emb_ref.shape[1]
    steps, block = protos_ref.shape[:2]
    arrived = fetch(protos_hbm, protos_ref, sems, first_row)
    old_top = state_ref[:, width + 128 :]
    top_ref[...] = old_top

    def first(index, carry):
        arrived(index)
        top = top_ref[...]
        for start in range(0, block, TILE):
            products = scores(emb_ref[...], protos_ref[index, start : start + TILE, :])
            products_ref[index, :, start : start + TILE] = products
            top = jnp.maximum(top, lane_fold(products, jnp.maximum))
        top_ref[...] = top
        return carry

    lax.fori_loop(0, steps, first, 0)
    top = jnp.broadcast_to(jnp.max(top_ref[...], axis=1, keepdims=True), top_ref.shape)
    fade = jnp.exp2((old_top - top) * student_rate)
    top_ref[...] = top
    sum_ref[...] = state_ref[:, width : width + 128] * fade
    acc_ref[...] = state_ref[:, :width] * jnp.tile(fade, (1, width // 128))

    def second(index, carry):
        top = top_ref[...]
        total = sum_ref[...]
        acc = acc_ref[...]
        for start in range(0, block, TILE):
            pieces = []
            for lane in range(start, start + TILE, 128):
                shifted = jnp.exp2((products_ref[index, :, lane : lane + 128] - top) * student_rate)
                total = total + shifted
                pieces.append(shifted.astype(jnp.bfloat16))
            acc = acc + jnp.dot(
                jnp.concatenate(pieces, axis=1),
                protos_ref[index, start : start + TILE, :],
                preferred_element_type=jnp.float32,
            )
        sum_ref[...] = total
        acc_ref[...] = acc
        return carry

    lax.fori_loop(0, steps, second, 0)
    if last:
        total = jnp.sum(sum_ref[...], axis=1, keepdims=True)
        sum_ref[...] = jnp.broadcast_to(total, sum_ref.shape)
    share = out_refs[0].shape[0]
    for slot, out_ref in enumerate(out_refs):
        rows = pl.ds(slot * share, share)
        out_ref[:, :width] = acc_ref[rows, :]
        out_ref[:, width : width + 128] = sum_ref[rows, :]
        out_ref[:, width + 128 :] = top_ref[rows, :]


def attract(emb, state, protos, first_row, count, steps, outputs):
    rows, width = emb.shape
    block = count // steps
    return pl.pallas_call(
        functools.partial(attract_kernel, first_row, outputs > 1),
        in_specs=[whole(), whole(), whole(pl.ANY)],
        out_specs=[whole()] * outputs,
        out_shape=[jax.ShapeDtypeStruct((rows // outputs, width + 256), jnp.float32)] * outputs,
        scratch_shapes=[
            pltpu.VMEM((steps, block, width), jnp.bfloat16),
            pltpu.SemaphoreType.DMA((steps,)),
            pltpu.VMEM((steps, rows, block), jnp.float32),
            pltpu.VMEM((rows, width), jnp.float32),
            pltpu.VMEM((rows, 128), jnp.float32),
            pltpu.VMEM((rows, 128), jnp.float32),
        ],
        compiler_params=params(24),
        cost_estimate=cost(4 * rows * width * count, 2 * width * count, rows * count),
        name="attract",
    )(emb, state, in_hbm(protos))


def three_pieces(values):
    high = values.astype(jnp.bfloat16)
    rest = values - high.astype(jnp.float32)
    middle = rest.astype(jnp.bfloat16)
    low = (rest - middle.astype(jnp.float32)).astype(jnp.bfloat16)
    return jnp.concatenate([high, middle, low, jnp.zeros((13, values.shape[1]), jnp.bfloat16)], axis=0)


def lane_scales(folded, protos_total):
    sums = [
        jnp.sum(jnp.transpose(folded[start : start + 128, :]), axis=0, keepdims=True)
        for start in range(0, folded.shape[0], 128)
    ]
    return 1.0 / (protos_total * jnp.concatenate(sums, axis=1))


def give_sums(copies_ref, totals):
    rows = [totals[:, start : start + 128] for start in range(0, totals.shape[1], 128)]
    spare = copies_ref.shape[1] - len(rows)
    if spare:
        rows.append(jnp.zeros((spare, 128), jnp.float32))
    packed = jnp.concatenate(rows, axis=0).astype(jnp.bfloat16)
    copies_ref[...] = jnp.broadcast_to(packed[None], copies_ref.shape)


def take_scales(parts_ref, scale_ref):
    crops_total = scale_ref.shape[1]
    sums = jnp.sum(parts_ref[...].astype(jnp.float32), axis=0)
    for row in range(crops_total // 128):
        scale_ref[:, row * 128 : row * 128 + 128] = 1.0 / (crops_total * sums[row : row + 1, :])


def sums_shape(copies, crops_total):
    return (copies, -(-crops_total // 2048) * 16, 128)


def lane_order(tops_ref, group, crops_total):
    batches = tops_ref.shape[0] // group
    rows = crops_total // batches
    bits = batches.bit_length() - 1
    tops = []
    for batch in range(batches):
        source = int(format(batch, "b").zfill(bits)[::-1], 2) if bits else 0
        tops.append(
            functools.reduce(jnp.maximum, [tops_ref[source * group + other] for other in range(group)])
        )
    halves = [top[:, core * rows // 2 : (core + 1) * rows // 2] for core in range(2) for top in tops]
    return jnp.concatenate(halves, axis=1)


def first_sweep_kernel(
    chunk, protos_total, group, index_ref, protos_hbm, mine_hbm, other_hbm, tops_ref, copies_ref, weights_hbm,
    protos_ref, units_ref, weights_ref, rounded_ref, scale_ref, bias_ref, sems, out_sems,
):
    thin, crops_total = weights_ref.shape
    half = mine_hbm.shape[0]
    core = index_ref[1]
    copies = (
        pltpu.make_async_copy(protos_hbm.at[part(index_ref[0], thin), :], protos_ref, sems.at[0]),
        pltpu.make_async_copy(mine_hbm, units_ref.at[part(core, half), :], sems.at[1]),
        pltpu.make_async_copy(other_hbm, units_ref.at[part(1 - core, half), :], sems.at[2]),
    )
    for copy in copies:
        copy.start()
    bias_ref[...] = lane_order(tops_ref, group, crops_total) * -teacher_rate
    for copy in copies:
        copy.wait()

    def chunk_out(index):
        return pltpu.make_async_copy(
            rounded_ref.at[index], weights_hbm.at[part(index, chunk), :], out_sems.at[index]
        )

    def weigh(index, carry):
        rows = part(index, chunk)
        protos = protos_ref[rows, :]
        folded = jnp.zeros((chunk, 128), jnp.float32)
        for start in range(0, crops_total, TILE):
            columns = slice(start, start + TILE)
            products = scores(protos, units_ref[columns, :])
            weights = jnp.exp2(products * teacher_rate + bias_ref[:, columns])
            weights_ref[rows, columns] = weights
            rounded_ref[index, :, columns] = weights.astype(jnp.bfloat16)
            folded = folded + lane_fold(weights, jnp.add)
        sums = jnp.sum(folded, axis=1, keepdims=True)
        scale_ref[rows, :] = jnp.broadcast_to(1.0 / (protos_total * sums), (chunk, 128))
        chunk_out(index).start()
        return carry

    lax.fori_loop(0, thin // chunk, weigh, 0)
    small = min(thin, 64)

    def add_up(index, totals):
        rows = part(index, small)
        scaled = weights_ref[rows, :] * jnp.tile(scale_ref[rows, :], (1, crops_total // 128))
        return totals + jnp.sum(scaled.reshape(-1, 8, crops_total), axis=0)

    totals = lax.fori_loop(0, thin // small, add_up, jnp.zeros((8, crops_total), jnp.float32))
    give_sums(copies_ref, jnp.sum(totals, axis=0, keepdims=True))
    for index in range(thin // chunk):
        chunk_out(index).wait()


def first_sweep(index, protos, mine, other, tops, order, copies, thin, protos_total):
    width = protos.shape[1]
    crops_total = 2 * mine.shape[0]
    chunk = min(thin, 1024)
    return pl.pallas_call(
        skipping(functools.partial(first_sweep_kernel, chunk, protos_total, protos_total // protos.shape[0]), 5, len(order)),
        in_specs=[whole(pltpu.SMEM), whole(pl.ANY), whole(pl.ANY), whole(pl.ANY), whole()]
        + [whole(pl.ANY)] * len(order),
        out_specs=[whole(), whole(pl.ANY)],
        out_shape=[
            jax.ShapeDtypeStruct(sums_shape(copies, crops_total), jnp.bfloat16),
            pltpu.HBM((thin, crops_total), jnp.bfloat16),
        ],
        scratch_shapes=[
            pltpu.VMEM((thin, width), jnp.bfloat16),
            pltpu.VMEM((crops_total, width), jnp.bfloat16),
            pltpu.VMEM((thin, crops_total), jnp.float32),
            pltpu.VMEM((thin // chunk, chunk, crops_total), jnp.bfloat16),
            pltpu.VMEM((thin, 128), jnp.float32),
            pltpu.VMEM((1, crops_total), jnp.float32),
            pltpu.SemaphoreType.DMA((3,)),
            pltpu.SemaphoreType.DMA((thin // chunk,)),
        ],
        compiler_params=params(32 if crops_total <= 2048 else 56),
        cost_estimate=cost(2 * thin * width * crops_total, 2 * thin * crops_total, thin * crops_total),
        name="first_sweep",
    )(index, in_hbm(protos), mine, other, tops, *order)


def fetch_rows(weights_hbm, weights_ref, sems):
    steps, chunk, _ = weights_ref.shape

    def rows_copy(index):
        return pltpu.make_async_copy(
            weights_hbm.at[part(index, chunk), :], weights_ref.at[index], sems.at[index]
        )

    for index in range(steps):
        rows_copy(index).start()
    return lambda index: rows_copy(index).wait()


def scaled_fold(weights_ref, index, scale_ref):
    _, chunk, crops_total = weights_ref.shape
    folds = []
    for row in range(0, chunk, 64):
        fold = None
        for start in range(0, crops_total, TILE):
            columns = slice(start, start + TILE)
            weights = weights_ref[index, row : row + 64, columns].astype(jnp.float32)
            scaled = lane_fold(weights * scale_ref[:, columns], jnp.add)
            fold = scaled if fold is None else fold + scaled
        folds.append(fold)
    return jnp.concatenate(folds, axis=0)


def next_sweep_kernel(
    protos_total, weights_hbm, parts_ref, copies_ref, weights_ref, scale_ref, pieces_ref, totals_ref, sems,
):
    steps, chunk, crops_total = weights_ref.shape
    arrived = fetch_rows(weights_hbm, weights_ref, sems)
    take_scales(parts_ref, scale_ref)
    totals_ref[...] = jnp.zeros(totals_ref.shape, jnp.float32)

    def weigh(index):
        return three_pieces(lane_scales(scaled_fold(weights_ref, index, scale_ref), protos_total))

    def add_up(index):
        return jnp.dot(pieces_ref[...], weights_ref[index], preferred_element_type=jnp.float32)

    arrived(0)
    pieces_ref[...] = weigh(0)

    def sweep(index, carry):
        arrived(index)
        sums = add_up(index - 1)
        pieces = weigh(index)
        totals_ref[...] += sums
        pieces_ref[...] = pieces
        return carry

    lax.fori_loop(1, steps, sweep, 0)
    totals = totals_ref[...] + add_up(steps - 1)
    give_sums(copies_ref, jnp.sum(totals, axis=0, keepdims=True))


def next_sweep(weights, parts, order, protos_total):
    thin, crops_total = weights.shape
    copies = parts.shape[0]
    chunk = min(thin, 256)
    return pl.pallas_call(
        skipping(functools.partial(next_sweep_kernel, protos_total), 2, len(order)),
        in_specs=[whole(pl.ANY), whole()] + [whole(pl.ANY)] * len(order),
        out_specs=whole(),
        out_shape=jax.ShapeDtypeStruct(sums_shape(copies, crops_total), jnp.bfloat16),
        scratch_shapes=[
            pltpu.VMEM((thin // chunk, chunk, crops_total), jnp.bfloat16),
            pltpu.VMEM((1, crops_total), jnp.float32),
            pltpu.VMEM((16, chunk), jnp.bfloat16),
            pltpu.VMEM((16, crops_total), jnp.float32),
            pltpu.SemaphoreType.DMA((thin // chunk,)),
        ],
        compiler_params=params(16 if crops_total <= 2048 else 50),
        cost_estimate=cost(8 * thin * crops_total, 2 * thin * crops_total),
        name="next_sweep",
    )(in_hbm(weights), parts, *order)


def last_scales_kernel(
    protos_total, weights_hbm, parts_ref, copies_ref, weights_ref, scale_ref, out_ref, sems,
):
    steps, chunk, crops_total = weights_ref.shape
    arrived = fetch_rows(weights_hbm, weights_ref, sems)
    take_scales(parts_ref, scale_ref)

    def weigh(index, carry):
        arrived(index)
        out_ref[:, part(index, chunk)] = lane_scales(
            scaled_fold(weights_ref, index, scale_ref), protos_total
        )
        return carry

    lax.fori_loop(0, steps, weigh, 0)
    copies_ref[...] = jnp.broadcast_to(out_ref[...][None], copies_ref.shape)


def last_scales(weights, parts, order, copies, protos_total):
    thin, crops_total = weights.shape
    chunk = min(thin, 256)
    return pl.pallas_call(
        skipping(functools.partial(last_scales_kernel, protos_total), 2, len(order)),
        in_specs=[whole(pl.ANY), whole()] + [whole(pl.ANY)] * len(order),
        out_specs=whole(),
        out_shape=jax.ShapeDtypeStruct((copies, 1, thin), jnp.float32),
        scratch_shapes=[
            pltpu.VMEM((thin // chunk, chunk, crops_total), jnp.bfloat16),
            pltpu.VMEM((1, crops_total), jnp.float32),
            pltpu.VMEM((1, thin), jnp.float32),
            pltpu.SemaphoreType.DMA((thin // chunk,)),
        ],
        compiler_params=params(16 if crops_total <= 2048 else 50),
        cost_estimate=cost(4 * thin * crops_total, 2 * thin * crops_total),
        name="last_scales",
    )(in_hbm(weights), parts, *order)


def student_middle_kernel(
    index_ref, keep_ref, core_ref, x_ref, bias_ref, own_ref, partner_ref, other_ref, last_ref, last_bias_ref,
    unit_ref, emb_ref, lengths_ref, hidden_ref,
):
    share = x_ref.shape[0]
    block = own_ref.shape[0]
    sums = keep_ref[:share, :] + core_ref[:share, :] + x_ref[...]
    hidden_ref[...] = gelu(sums + bias_ref[...]).astype(jnp.bfloat16)
    index = index_ref[0]
    weights = ((0, own_ref[...]), (2, partner_ref[...]), (1, other_ref[...]), (3, last_ref[...]))
    bottleneck = jnp.broadcast_to(last_bias_ref[...], unit_ref.shape)
    for flip, weight in weights:
        bottleneck = bottleneck + jnp.dot(
            hidden_ref[:, part(index ^ flip, block)], weight, preferred_element_type=jnp.float32
        )
    unit, lengths = unit_rows(bottleneck)
    unit_ref[...] = unit
    emb_ref[...] = unit.astype(jnp.bfloat16)
    lengths_ref[...] = jnp.broadcast_to(lengths, lengths_ref.shape)


def student_middle(index, keep, core_rows, x_rows, bias, weights, last_bias):
    share, units = x_rows.shape
    width = weights[0].shape[1]
    return pl.pallas_call(
        student_middle_kernel,
        in_specs=[whole(pltpu.SMEM)] + [whole()] * 9,
        out_specs=[whole()] * 3,
        out_shape=[
            jax.ShapeDtypeStruct((share, width), jnp.float32),
            jax.ShapeDtypeStruct((share, width), jnp.bfloat16),
            jax.ShapeDtypeStruct((share, 128), jnp.float32),
        ],
        scratch_shapes=[pltpu.VMEM((share, units), jnp.bfloat16)],
        compiler_params=params(12),
        cost_estimate=cost(2 * share * units * width, 2 * units * width + 16 * share * units),
        name="student_middle",
    )(index, keep, core_rows, x_rows, in_hbm(bias.reshape(1, -1)), in_hbm(weights[0]), *weights[1:], in_hbm(last_bias.reshape(1, -1)))


def finish_kernel(unit_ref, lengths_ref, *rest):
    out_ref, blocks = rest[-1], rest[:-1]
    attracts, repels = blocks[: len(blocks) // 2], blocks[len(blocks) // 2 :]
    width = unit_ref.shape[1]
    row_top = functools.reduce(jnp.maximum, [ref[:, width + 128 :] for ref in attracts])
    attract_sum = repel_sum = 0.0
    row_sum = column_sum = 0.0
    for ref in attracts:
        fade = jnp.exp2((ref[:, width + 128 :] - row_top) * student_rate)
        row_sum = row_sum + ref[:, width : width + 128] * fade
        attract_sum = attract_sum + ref[:, :width] * jnp.tile(fade, (1, width // 128))
    for ref in repels:
        column_sum = column_sum + jnp.sum(ref[:, width:].astype(jnp.float32), axis=1, keepdims=True)
        repel_sum = repel_sum + ref[:, :width].astype(jnp.float32)
    emb_grad = (
        attract_sum / jnp.tile(row_sum, (1, width // 128))
        - repel_sum / column_sum
    ) / student_temp
    unit = unit_ref[...]
    along = jnp.sum(unit * emb_grad, axis=1, keepdims=True)
    out_ref[...] = (emb_grad - unit * along) / jnp.tile(lengths_ref[...], (1, width // 128))


def finish(unit, lengths, attracts, repels):
    return pl.pallas_call(
        finish_kernel,
        in_specs=[whole()] * (2 + len(attracts) + len(repels)),
        out_specs=whole(),
        out_shape=jax.ShapeDtypeStruct(unit.shape, jnp.float32),
        compiler_params=params(8),
        cost_estimate=cost(40 * unit.size, 40 * unit.size),
        name="finish",
    )(unit, lengths, *attracts, *repels)


def swap(values, axis, flip):
    return lax.ppermute(values, axis, [(i, i ^ flip) for i in range(lax.axis_size(axis))])


def bit_reversed(values, count):
    bits = count.bit_length() - 1
    split = values.reshape((2,) * bits + values.shape[1:])
    turned = jnp.transpose(split, tuple(reversed(range(bits))) + tuple(range(bits, split.ndim)))
    return turned.reshape(values.shape)


def gather_batch(values):
    step = lax.axis_size("batch") // 2
    stages = [values]
    while step:
        other = swap(values, "batch", step)
        upper = (lax.axis_index("batch") // step) % 2
        values = jnp.where(
            upper == 0, jnp.concatenate([values, other]), jnp.concatenate([other, values])
        )
        stages.append(values)
        step //= 2
    return stages


def send_blocks(blocks):
    flips = list(range(len(blocks) - 1, 0, -1))
    return [blocks[0]] + [swap(blocks[flip], "proto", flip) for flip in flips]


def all_to_all(copies, axes):
    return lax.all_to_all(copies, axes, 0, 0, tiled=True)


def body(crops, teacher_emb, w_first, b_first, w_second, b_second, w_third, b_third, protos):
    batch_index = lax.axis_index("batch")
    proto_index = lax.axis_index("proto")
    batch_size = lax.axis_size("batch")
    proto_size = lax.axis_size("proto")
    devices = batch_size * proto_size
    share_rows = crops.shape[0]
    group_rows = teacher_emb.shape[0]
    crops_total = group_rows * batch_size
    protos_total = protos.shape[0] * proto_size
    count, width = protos.shape
    thin = count // batch_size
    core = proto_index % 2
    proto_ref = proto_index.reshape(1)
    thin_ref = jnp.stack([batch_index, core])
    wide_ref = jnp.stack([batch_index, proto_index])

    own_unit, half = teacher_units(core.reshape(1), teacher_emb)
    stages = gather_batch(half)
    mine = stages[-1]
    other = swap(mine, "proto", 1)

    crops_x = swap(crops, "proto", 2)
    rows = [crops, crops_x, swap(crops, "proto", 1), swap(crops_x, "proto", 1)]
    third_x = swap(w_third, "proto", 2)
    thirds = [w_third, third_x, swap(w_third, "proto", 1), swap(third_x, "proto", 1)]
    top_copies, keep, give = front(
        proto_ref, own_unit, b_first, rows, w_first, w_second, protos, (stages[2], third_x), devices, 8
    )
    all_tops = all_to_all(top_copies, BOTH)
    core_rows = swap(give, "proto", 1)
    x_sent = keep[share_rows:] + core_rows[share_rows:]
    x_rows = swap(x_sent, "proto", 2)
    unit, rounded, lengths = student_middle(
        proto_ref, keep, core_rows, x_rows, b_second, thirds, b_third
    )
    student_emb = jnp.concatenate([rounded] + [swap(rounded, "proto", flip) for flip in range(1, proto_size)])
    empty = jnp.concatenate(
        [jnp.zeros((group_rows, width + 128), jnp.float32), jnp.full((group_rows, 128), -1e30, jnp.float32)], axis=1
    )
    eighth = count // 8
    (state,) = attract(student_emb, empty, protos, 0, 6 * eighth, 6, 1)
    slots = attract(student_emb, state, protos, 6 * eighth, 2 * eighth, 2, proto_size)
    attract_parts = send_blocks(slots)

    copies, weights = first_sweep(thin_ref, protos, mine, other, all_tops, (x_sent,), devices, thin, protos_total)
    for _ in range(ITERS - 2):
        copies = next_sweep(weights, all_to_all(copies, BOTH), (rounded,), protos_total)
    scale_copies = last_scales(weights, all_to_all(copies, BOTH), (state,), batch_size, protos_total)
    all_scale = all_to_all(scale_copies, "batch")
    repels = repel(wide_ref, own_unit, all_tops, all_scale, protos, (slots[0],), proto_size)
    return finish(unit, lengths, attract_parts, send_blocks(repels))


def solution(mesh):
    in_specs = (
        P(("batch", "proto"), None),
        P("batch", None),
        P(None, "proto"),
        P(),
        P("proto", None),
        P(),
        P("proto", None),
        P(),
        P("proto", None),
    )
    out_specs = P(("batch", "proto"), None)
    return jax.shard_map(body, mesh=mesh, in_specs=in_specs, out_specs=out_specs, check_vma=False)
```
